32 devices in a mesh: groups: 2 (over y), seq: 4 (over z), cuts: 4 (over x, core).
Axes of the slice: x: 2, y: 2, z: 4, core: 2. Of those that a mesh axis runs over, the one named last changes fastest.
Arguments:
- queries: bfloat16 [2048, 2048], P(('groups', 'seq'), 'cuts'), parts along dimension 0, may hold values from -56 to 56
- keyvals: bfloat16 [2048, 1024], P(('groups', 'seq'), 'cuts'), parts along dimension 0, may hold values from -5 to 5
- preceding_keyvalues: bfloat16 [256, 1024], P('groups', 'cuts'), parts along dimension 0, may hold values from -5 to 5
- attention_sink_logits: float32 [32], P('cuts'), may hold values from 3 to 7
- residual: bfloat16 [2048, 2880], P(('groups', 'seq'), 'cuts'), parts along dimension 0, may hold values from -24 to 24
- w_out: bfloat16 [2048, 2880], P(None, 'cuts'), may hold values from -0.75 to 0.75
- norm_gain: float32 [2880], replicated, may hold values from 0.5 to 1.5
- expert_ids: int32 [2048, 4], P(('groups', 'seq')), parts along dimension 0, may hold values from 0 to 127, all different within a row; in each aligned block of 256 rows (0 to 255, 256 to 511, ...) at most 16 rows name the same one
- route_weights: float32 [2048, 4], P(('groups', 'seq')), parts along dimension 0, may hold values from 0.1 to 1
- w_gate: bfloat16 [4, 2880, 1440], P('seq', None, 'cuts'), may hold values from -0.109375 to 0.109375
- w_up: bfloat16 [4, 2880, 1440], P('seq', None, 'cuts'), may hold values from -0.109375 to 0.109375
- w_down: bfloat16 [4, 1440, 2880], P('seq', 'cuts'), may hold values from -0.15625 to 0.15625
Outputs:
- layer_out: bfloat16 [2048, 2880], P(('groups', 'seq'), 'cuts'), parts along dimension 0
The draws below stay inside these ranges and needn't reach their ends.
There are 2 independent parts, one for each index of `groups`. The reference program is written for one: setup_inputs(seed, part) draws one part's arguments, and reference() takes and returns one part's arrays. A program takes and returns all parts, laid end to end along the dimension named above; an argument that names none is the same for every part. Nothing has to cross between parts.
Inputs may be any that keep to these rules, and one draw needn't show every extreme that they name: `expert_ids`: the 4 experts of a token differ. Among the 256 rows of one device no expert is named by more than 16 rows, and in every draw some expert is named by exactly 16 rows of some device.
All inputs are finite; a program needn't handle non-finite values.
Results may differ from the reference program's by a relative error of at most 0.0038.
Values may be sent and summed in bfloat16 or wider, within the bound.
No kernel may reach another device: no remote copies, remote signals or barrier semaphores. Data moves between devices by JAX's collectives and lax.ppermute only.
A program may use at most 64 MiB of HBM per device.

```python
import math
import jax
import jax.numpy as jnp
import numpy as np
from jax import lax

D = 2880
QUERY_HEADS = 32
KEYVALUE_HEADS = 8
HEAD_SIZE = 64
KEYS_SEEN = 128
TOP = 4
EXPERTS = 128
FF_WIN = 1440
TOK_DEV = 256
PROMPT_TOKENS = 1024
EXP_LIVE = 4
CAP = 16
N_SEQ = 4
N_CUTS = 4


def draw_keyvals(key, part):
    key = jax.random.fold_in(key, 5)
    key_portion, value_portion = jax.random.split(key)
    unrotated_keys = jnp.clip(jax.random.normal(key_portion, (PROMPT_TOKENS, KEYVALUE_HEADS, HEAD_SIZE), jnp.float32), -5.0, 5.0)
    joined_values = jnp.clip(jax.random.normal(value_portion, (PROMPT_TOKENS, KEYVALUE_HEADS, HEAD_SIZE), jnp.float32), -5.0, 5.0)
    return jnp.stack([unrotated_keys, joined_values], axis=2).reshape(PROMPT_TOKENS, KEYVALUE_HEADS * 2 * HEAD_SIZE).astype(jnp.bfloat16)


def draw_queries(key, part):
    key = jax.random.fold_in(key, 7)
    drawn_rows = jnp.clip(jax.random.normal(key, (PROMPT_TOKENS, QUERY_HEADS, HEAD_SIZE), jnp.float32), -5.0, 5.0)
    return drawn_rows.reshape(PROMPT_TOKENS, QUERY_HEADS * HEAD_SIZE).astype(jnp.bfloat16)


def draw_residual(key, part):
    key = jax.random.fold_in(key, 11)
    base_key, column_key = jax.random.split(key, 2)
    ramp = 0.6 + 1.2 * jnp.arange(D, dtype=jnp.int32).astype(jnp.float32) / D
    column_scale = jnp.exp(jax.random.uniform(column_key, (D,), jnp.float32, -1.2, 1.2)) * ramp
    base_rows = jnp.clip(jax.random.normal(base_key, (PROMPT_TOKENS, D), jnp.float32), -5.0, 5.0)
    return jnp.clip(base_rows * column_scale[None, :], -24.0, 24.0).astype(jnp.bfloat16)


def shard_levels(rng, dims, cuts, smallest, top_value):
    def one(position, shards_of):
        steps = jax.random.uniform(jax.random.fold_in(jax.random.fold_in(rng, 6), position), (shards_of,), jnp.float32, smallest / len(cuts), top_value / len(cuts))
        return jnp.repeat(jnp.exp(steps), dims[position] // shards_of).reshape((-1,) + (1,) * (len(dims) - position - 1))

    factor_of = one(*cuts[0])
    for cut in cuts[1:]:
        factor_of = factor_of * one(*cut)
    return factor_of


def deal_out(own_key, own, number, rows, count, top, reach, lean):
    order = jax.random.permutation(own_key, count)
    heavy_load, usual = load_shares(count, rows * top, reach, lean, True), load_shares(count, rows * top, reach, lean, False)
    places = jnp.arange(count)

    def named(tallies, rotation):
        used = int((tallies > 0).sum())
        fixed = max(1, used // 4)
        shifted = fixed + (places - fixed + rotation * (used - fixed)) % max(1, count - fixed)
        return jnp.zeros((count,), jnp.int32).at[order[jnp.where(places < fixed, places, shifted)]].set(jnp.asarray(tallies, jnp.int32))

    tallies = jnp.where(number % 4 == 0, named(heavy_load, number // 4), named(usual, number - number // 4 - 1))
    mixed = jax.random.permutation(jax.random.fold_in(own, 3), count)
    source_of, taker = mixed[0:count // 2 * 2:2], mixed[1:count // 2 * 2:2]
    margin = jnp.minimum(tallies[source_of] - 1, reach - tallies[taker]) // 2
    margin = jnp.where((source_of == order[0]) | (taker == order[0]) | (tallies[taker] == 0), 0, jnp.maximum(margin, 0))
    shifted = jax.random.randint(jax.random.fold_in(own, 4), (count // 2,), 0, 1 << 20) % (margin + 1)
    tallies = tallies.at[source_of].add(-shifted).at[taker].add(shifted)
    labels = jnp.searchsorted(jnp.cumsum(tallies), jnp.arange(rows * top), side="right").astype(jnp.int32)
    table = labels.reshape(top, rows).T
    table = table[jax.random.permutation(jax.random.fold_in(own, 1), rows)]
    rotation = jax.random.randint(jax.random.fold_in(own, 2), (rows, 1), 0, top)
    return jnp.take_along_axis(table, (jnp.arange(top)[None, :] + rotation) % top, axis=1)


def load_shares(amount, total, bound, lean, full):
    loads = [(1 << 20) // math.isqrt(standing ** lean) + 1 for standing in range(1, amount + 1)]
    largest = bound if full else min(bound, max(-(-total // amount), total * loads[0] // sum(loads)))
    least = 1 if total - largest >= amount - 1 else 0
    counts, spare = [largest] + [least] * (amount - 1), total - largest - least * (amount - 1)
    while spare > 0:
        movable = [i for i in range(1, amount) if counts[i] < largest] or [i for i in range(1, amount) if counts[i] < bound]
        pool, left = sum([loads[i] for i in movable]), spare
        for i in movable:
            more = min(bound - counts[i], max(1, left * loads[i] // pool), spare)
            counts[i] = counts[i] + more
            spare = spare - more
    return np.array(counts)


def noise(key, dims, scale, most, cuts=(), held_as=jnp.bfloat16):
    entries = jax.random.normal(key, dims, jnp.float32) * scale
    if len(cuts) > 0:
        entries = shard_levels(key, dims, cuts, -0.22, 0.18) * entries
    return jnp.clip(entries, min=-most, max=most).astype(held_as)


def setup_inputs(seed: int = 0, part: int = 0) -> dict:
    seeds = jax.random.split(jax.random.key(seed), 13)
    own_keys = jax.random.split(jax.random.fold_in(seeds[12], part), 13)
    queries = draw_queries(jax.random.fold_in(jax.random.fold_in(seeds[12], part), 71), part)
    keyvals = draw_keyvals(jax.random.fold_in(jax.random.fold_in(seeds[12], part), 71), part)
    preceding_keyvalues = noise(own_keys[2], (KEYS_SEEN, KEYVALUE_HEADS * 2 * HEAD_SIZE), 1.0, 5.0, ((1, 4),))
    attention_sink_logits = jnp.clip(3.0 + 4.0 * jax.random.uniform(seeds[3], (QUERY_HEADS,), jnp.float32) ** shard_levels(seeds[3], (QUERY_HEADS,), ((0, 4),), -0.2, 0.2), 3.0, 7.0)
    residual = draw_residual(jax.random.fold_in(jax.random.fold_in(seeds[12], part), 71), part)
    w_out = noise(seeds[5], (QUERY_HEADS * HEAD_SIZE, D), (QUERY_HEADS * HEAD_SIZE // 32) ** -0.5, 0.75, ((1, 4),))
    norm_gain = jnp.clip(1.0 + 0.1 * jax.random.normal(seeds[6], (D,), jnp.float32), 0.5, 1.5)
    expert_ids_keys = jax.random.split(jax.random.fold_in(own_keys[7], 1), PROMPT_TOKENS // TOK_DEV)
    expert_ids_turns = jax.random.permutation(jax.random.fold_in(own_keys[7], 3), PROMPT_TOKENS // TOK_DEV)
    expert_ids = jax.vmap(lambda own, number: deal_out(jax.random.fold_in(own_keys[7], 2), own, number, TOK_DEV, EXPERTS, TOP, CAP, 2))(expert_ids_keys, expert_ids_turns).reshape((PROMPT_TOKENS, TOP))
    route_weights = jnp.clip(jnp.exp(math.log(1.0) - 2.3025851 * jax.random.uniform(own_keys[8], (PROMPT_TOKENS, TOP), jnp.float32) ** shard_levels(own_keys[8], (PROMPT_TOKENS, TOP), ((0, 4),), -0.2, 0.2)), 0.1, 1.0)
    w_gate = noise(seeds[9], (EXP_LIVE, D, FF_WIN), D ** -0.5, 0.109375, ((0, 4), (2, 4)))
    w_up = noise(seeds[10], (EXP_LIVE, D, FF_WIN), D ** -0.5, 0.109375, ((0, 4), (2, 4)))
    w_down = noise(seeds[11], (EXP_LIVE, FF_WIN, D), FF_WIN ** -0.5, 0.15625, ((0, 4), (1, 4)))
    return dict(queries=queries, keyvals=keyvals, preceding_keyvalues=preceding_keyvalues, attention_sink_logits=attention_sink_logits, residual=residual, w_out=w_out, norm_gain=norm_gain, expert_ids=expert_ids, route_weights=route_weights, w_gate=w_gate, w_up=w_up, w_down=w_down)


norm_eps = 1e-05
glu_alpha = 1.702

def attention_all(queries, keyvals, preceding_keyvalues, attention_sink_logits):
    queries_per_group = QUERY_HEADS // KEYVALUE_HEADS
    head_scale = HEAD_SIZE ** (-0.5)
    joined_keys = jnp.concatenate([preceding_keyvalues, keyvals], axis=0).reshape(KEYS_SEEN + PROMPT_TOKENS, KEYVALUE_HEADS, 2, HEAD_SIZE)
    query_head_rows = queries.reshape(PROMPT_TOKENS // KEYS_SEEN, KEYS_SEEN, KEYVALUE_HEADS, queries_per_group, HEAD_SIZE)
    row_ids = jnp.arange(KEYS_SEEN, dtype=jnp.int32)[:, None]
    col_ids = jnp.arange(2 * KEYS_SEEN, dtype=jnp.int32)[None, :]
    allowed = (col_ids > row_ids) & (col_ids <= row_ids + KEYS_SEEN)
    local_sink_logit = attention_sink_logits.reshape(KEYVALUE_HEADS, queries_per_group)[:, :, None]

    def one_block(block_index):
        block_q = lax.dynamic_index_in_dim(query_head_rows, block_index, 0, keepdims=False).astype(jnp.float32)
        block_kv = lax.dynamic_slice_in_dim(joined_keys, block_index * KEYS_SEEN, 2 * KEYS_SEEN, 0).astype(jnp.float32)
        scores = jnp.einsum('tkgd,skd->kgts', block_q, block_kv[:, :, 0, :], precision=lax.Precision.HIGHEST) * head_scale
        scores = jnp.where(allowed[None, None, :, :], scores, -jnp.inf)
        peak = jnp.maximum(lax.optimization_barrier(jnp.max(scores, axis=3)), local_sink_logit)
        exp_terms = jnp.exp(scores - peak[..., None])
        denom = lax.optimization_barrier(jnp.sum(exp_terms, axis=3)) + jnp.exp(local_sink_logit - peak)
        probs = (exp_terms / denom[..., None]).astype(jnp.bfloat16)
        outputs = jnp.einsum('kgts,skd->tkgd', probs.astype(jnp.float32), block_kv[:, :, 1, :], precision=lax.Precision.HIGHEST)
        return outputs.astype(jnp.bfloat16).reshape(KEYS_SEEN, QUERY_HEADS * HEAD_SIZE)
    blocks = lax.map(one_block, jnp.arange(PROMPT_TOKENS // KEYS_SEEN, dtype=jnp.int32))
    return blocks.reshape(PROMPT_TOKENS, QUERY_HEADS * HEAD_SIZE)

def run_expert(operands):
    rows_here, gate_w, up_w, down_w = operands
    gate_sum = jnp.dot(rows_here, gate_w, preferred_element_type=jnp.float32)
    up_sum = jnp.dot(rows_here, up_w, preferred_element_type=jnp.float32)
    activated = ((up_sum + 1.0) * gate_sum * jax.nn.sigmoid(glu_alpha * gate_sum)).astype(jnp.bfloat16)
    width_part = FF_WIN // N_CUTS
    totals = jnp.zeros((rows_here.shape[0], D), jnp.float32)
    for group_ix in range(N_CUTS):
        lower = group_ix * width_part
        part_sum = jnp.dot(activated[:, lower:lower + width_part], down_w[lower:lower + width_part], preferred_element_type=jnp.float32)
        totals = totals + lax.optimization_barrier(part_sum.astype(jnp.bfloat16)).astype(jnp.float32)
    return totals.astype(jnp.bfloat16)

def reference(queries, keyvals, preceding_keyvalues, attention_sink_logits, residual, w_out, norm_gain, expert_ids, route_weights, w_gate, w_up, w_down):
    attended = attention_all(queries, keyvals, preceding_keyvalues, attention_sink_logits)
    projected = jnp.dot(attended, w_out, preferred_element_type=jnp.float32)
    resid = (residual.astype(jnp.float32) + projected).astype(jnp.bfloat16)
    wide_rows = resid.astype(jnp.float32)
    normed = (wide_rows * lax.rsqrt(lax.optimization_barrier(jnp.mean(wide_rows * wide_rows, axis=1, keepdims=True)) + norm_eps) * norm_gain[None, :]).astype(jnp.bfloat16)
    id_blocks = expert_ids.reshape(N_SEQ, TOK_DEV, TOP)
    experts_held = jnp.arange(EXP_LIVE, dtype=jnp.int32)
    is_named = id_blocks[..., None] == experts_held[None, None, None, :]
    chosen = jnp.any(is_named, axis=2).astype(jnp.int32)
    before = jnp.cumsum(chosen, axis=1, dtype=jnp.int32) - chosen
    ranking = lax.optimization_barrier(jnp.sum(jnp.where(is_named, before[:, :, None, :], 0), axis=3, dtype=jnp.int32))
    live_mask = id_blocks < EXP_LIVE
    block_ix = jnp.arange(N_SEQ, dtype=jnp.int32)[:, None, None]
    token_ix = block_ix * TOK_DEV + jnp.arange(TOK_DEV, dtype=jnp.int32)[None, :, None] + jnp.zeros((1, 1, TOP), jnp.int32)
    slot_count = EXP_LIVE * N_SEQ * CAP
    flat_slot = jnp.where(live_mask, id_blocks * (N_SEQ * CAP) + block_ix * CAP + ranking, slot_count).astype(jnp.int32)
    slot_token = jnp.full((slot_count,), PROMPT_TOKENS, jnp.int32).at[flat_slot.reshape(-1)].set(token_ix.reshape(-1), mode='drop')
    padded = jnp.concatenate([normed, jnp.zeros((1, D), jnp.bfloat16)], axis=0)
    expert_rows = jnp.take(padded, slot_token, axis=0).reshape(EXP_LIVE, N_SEQ * CAP, D)
    expert_out = lax.map(run_expert, (expert_rows, w_gate, w_up, w_down))
    expert_flat = expert_out.reshape(slot_count, D)
    safe_slot = jnp.where(live_mask, flat_slot, 0).reshape(PROMPT_TOKENS, TOP).astype(jnp.int32)
    weights_live = jnp.where(live_mask.reshape(PROMPT_TOKENS, TOP), route_weights, 0.0)
    mixed_in = jnp.zeros((PROMPT_TOKENS, D), jnp.float32)
    for pick_ix in range(TOP):
        mixed_in = mixed_in + weights_live[:, pick_ix:pick_ix + 1] * jnp.take(expert_flat, safe_slot[:, pick_ix], axis=0).astype(jnp.float32)
    return (resid.astype(jnp.float32) + mixed_in).astype(jnp.bfloat16)
```

```python
import functools

import jax
import jax.numpy as jnp
from jax import lax
from jax.experimental import pallas as pl
from jax.experimental.pallas import tpu as pltpu
from jax.sharding import PartitionSpec as P

HEAD_SIZE = 64
KEYS_SEEN = 128
CAP = 16
CORES = 2

norm_eps = 1e-05
glu_alpha = 1.702

NT = (((1,), (1,)), ((), ()))
NN = (((1,), (0,)), ((), ()))
TN = (((0,), (0,)), ((), ()))
VMEM_LIMIT = 40 * 1024 * 1024


def dot(a, b, dims):
    return lax.dot_general(a, b, dims, preferred_element_type=jnp.float32)


def call(kernel, outs, scratch=(), smem=(), n_in=0, flops=0, moved=0):
    specs = [
        pl.BlockSpec(memory_space=pltpu.SMEM if i in smem else pltpu.VMEM) for i in range(n_in)
    ]
    return pl.pallas_call(
        kernel,
        out_shape=outs,
        in_specs=specs,
        out_specs=jax.tree.map(lambda _: pl.BlockSpec(memory_space=pltpu.VMEM), outs),
        scratch_shapes=list(scratch),
        compiler_params=pltpu.CompilerParams(vmem_limit_bytes=VMEM_LIMIT),
        cost_estimate=pl.CostEstimate(flops=flops, bytes_accessed=moved, transcendentals=0),
    )


def bf16(*shape):
    return jax.ShapeDtypeStruct(shape, jnp.bfloat16)


def tables_kernel(live, ids_ref, weights_ref, placing_ref, mix_hi_ref, mix_lo_ref):
    top, toks = ids_ref.shape
    ids = ids_ref[...]
    weights = weights_ref[...]
    chosen = jnp.concatenate(
        [jnp.max((ids == e).astype(jnp.float32), axis=0, keepdims=True) for e in range(live)], axis=0
    )
    earlier = lax.broadcasted_iota(jnp.int32, (toks, toks), 0)
    later = lax.broadcasted_iota(jnp.int32, (toks, toks), 1)
    strict = (earlier < later).astype(jnp.bfloat16)
    before = dot(chosen.astype(jnp.bfloat16), strict, NN)
    slot = lax.broadcasted_iota(jnp.int32, (CAP, toks), 0).astype(jnp.float32)
    for e in range(live):
        weight = jnp.sum(jnp.where(ids == e, weights, 0.0), axis=0, keepdims=True)
        fills = (before[e : e + 1] == slot) & (chosen[e : e + 1] > 0.0)
        mix = jnp.where(fills, weight, 0.0)
        hi = mix.astype(jnp.bfloat16)
        rows = slice(e * CAP, (e + 1) * CAP)
        placing_ref[rows] = fills.astype(jnp.bfloat16)
        mix_hi_ref[rows] = hi
        mix_lo_ref[rows] = (mix - hi.astype(jnp.float32)).astype(jnp.bfloat16)


def attend_kernel(q_ref, kv_ref, before_ref, rim_ref, sinks_ref, out_ref, joined_ref):
    toks = q_ref.shape[0]
    groups = kv_ref.shape[1] // (2 * HEAD_SIZE)
    pairs = q_ref.shape[1] // (2 * HEAD_SIZE)
    per_group = pairs // groups
    first = lax.axis_index("seq") == 0
    joined_ref[:KEYS_SEEN] = jnp.where(first, before_ref[...], rim_ref[...])
    joined_ref[KEYS_SEEN:] = kv_ref[...]
    span = 2 * KEYS_SEEN
    row = lax.broadcasted_iota(jnp.int32, (KEYS_SEEN, span), 0)
    col = lax.broadcasted_iota(jnp.int32, (KEYS_SEEN, span), 1)
    allowed = (col > row) & (col <= row + KEYS_SEEN)
    low = lax.broadcasted_iota(jnp.int32, (span, 2 * HEAD_SIZE), 1) < HEAD_SIZE
    for g in range(groups):
        for b in range(toks // KEYS_SEEN):
            lanes = slice(g * 2 * HEAD_SIZE, (g + 1) * 2 * HEAD_SIZE)
            both = joined_ref[b * KEYS_SEEN : b * KEYS_SEEN + span, lanes].astype(jnp.float32)
            turned = pltpu.roll(both, HEAD_SIZE, 1)
            keys = jnp.concatenate([jnp.where(low, both, 0.0), jnp.where(low, 0.0, turned)], axis=0)
            values = jnp.concatenate([jnp.where(low, turned, 0.0), jnp.where(low, 0.0, both)], axis=0)
            keys = keys.astype(jnp.bfloat16)
            values = values.astype(jnp.bfloat16)
            for p in range(g * per_group, (g + 1) * per_group):
                rows = slice(b * KEYS_SEEN, (b + 1) * KEYS_SEEN)
                heads = slice(p * 2 * HEAD_SIZE, (p + 1) * 2 * HEAD_SIZE)
                scores = dot(q_ref[rows, heads], keys, NT) * (HEAD_SIZE**-0.5)
                probs = []
                for i in range(2):
                    sink = sinks_ref[2 * p + i]
                    part = jnp.where(allowed, scores[:, i * span : (i + 1) * span], -jnp.inf)
                    peak = jnp.maximum(jnp.max(part, axis=1, keepdims=True), sink)
                    terms = jnp.exp(part - peak)
                    denom = jnp.sum(terms, axis=1, keepdims=True) + jnp.exp(sink - peak)
                    probs.append((terms / denom).astype(jnp.bfloat16))
                mixed = dot(jnp.concatenate(probs, axis=1), values, NN)
                out_ref[rows, heads] = mixed.astype(jnp.bfloat16)


def origin(k, steps, sibling):
    me = lax.axis_index("cuts")
    chip = lax.rem(lax.div(me, CORES) - k + steps, steps)
    core = lax.rem(me, CORES)
    return chip * CORES + (1 - core if sibling else core)


def project_kernel(steps, *refs):
    mine, theirs = refs[:steps], refs[steps : 2 * steps]
    w_ref, residual_ref, placing_ref, resid_ref = refs[2 * steps : 2 * steps + 4]
    outgoing = refs[2 * steps + 4 : -1]
    rows_ref = refs[-1]
    width = mine[0].shape[1]
    total = residual_ref[...].astype(jnp.float32)
    for k in range(steps):
        for sibling in (False, True):
            block = (theirs if sibling else mine)[k][...]
            at = pl.multiple_of(origin(k, steps, sibling) * width, 128)
            total += dot(w_ref[:, pl.ds(at, width)], block, NT)
    resid = total.astype(jnp.bfloat16)
    resid_ref[...] = resid
    live = len(outgoing)
    rows = dot(placing_ref[...], resid, NT).astype(jnp.bfloat16)
    rows_ref[...] = rows.reshape(rows_ref.shape)
    me = lax.axis_index("seq")
    for k in range(live):
        outgoing[k][...] = rows_ref[lax.rem(me + k, live)]


def expert_kernel(steps, *refs):
    mine, theirs = refs[:steps], refs[steps : 2 * steps]
    gain_ref, gate_ref, up_ref, down_ref, kept_ref, given_ref, blocks_ref, rows_ref = refs[2 * steps :]
    cuts = CORES * steps
    width = mine[0].shape[1]
    for k in range(steps):
        blocks_ref[origin(k, steps, False)] = mine[k][...]
        blocks_ref[origin(k, steps, True)] = theirs[k][...]
    blocks = [blocks_ref[p].astype(jnp.float32) for p in range(cuts)]
    squares = sum(jnp.sum(b * b, axis=1, keepdims=True) for b in blocks)
    scale = lax.rsqrt(squares / (cuts * width) + norm_eps)
    gain = gain_ref[...].reshape(1, cuts * width)
    wide = jnp.concatenate(blocks, axis=1)
    rows_ref[...] = (wide * scale * gain).astype(jnp.bfloat16)
    rows = rows_ref[...]
    gate = dot(rows, gate_ref[...], NT)
    up = dot(rows, up_ref[...], NT)
    activated = ((up + 1.0) * gate * jax.nn.sigmoid(glu_alpha * gate)).astype(jnp.bfloat16)
    out = dot(activated, down_ref[...], NN).astype(jnp.bfloat16)
    for p in range(cuts):
        blocks_ref[p] = out[:, p * width : (p + 1) * width]
    for k in range(steps):
        kept_ref[k] = blocks_ref[origin(k, steps, False)]
        given_ref[k] = blocks_ref[origin(k, steps, True)]


def add_pair_kernel(kept_ref, given_ref, *out_refs):
    for k, out_ref in enumerate(out_refs):
        total = kept_ref[k].astype(jnp.float32) + given_ref[k].astype(jnp.float32)
        out_ref[...] = total.astype(jnp.bfloat16)


def add_chips_kernel(steps, *refs):
    total = sum(r[...].astype(jnp.float32) for r in refs[:steps])
    for k, out_ref in enumerate(refs[steps:]):
        out_ref[...] = total[k * CAP : (k + 1) * CAP].astype(jnp.bfloat16)


def combine_kernel(live, *refs):
    blocks = refs[:live]
    mix_hi_ref, mix_lo_ref, resid_ref, out_ref, rows_ref = refs[live:]
    me = lax.axis_index("seq")
    for k in range(live):
        rows_ref[lax.rem(me + k, live)] = blocks[k][...]
    rows = rows_ref[...].reshape(live * CAP, -1)
    mixed = dot(rows, mix_hi_ref[...], TN) + dot(rows, mix_lo_ref[...], TN)
    out_ref[...] = (resid_ref[...].astype(jnp.float32) + mixed).astype(jnp.bfloat16)


def shift_seq(block, distance):
    size = lax.axis_size("seq")
    return lax.ppermute(block, "seq", [(i, (i + distance) % size) for i in range(size)])


def shift_chips(block, distance):
    size = lax.axis_size("cuts")
    return lax.ppermute(block, "cuts", [(i, (i + CORES * distance) % size) for i in range(size)])


def swap_cores(block):
    return lax.ppermute(block, "cuts", [(i, i ^ 1) for i in range(lax.axis_size("cuts"))])


def gather_cuts(block):
    steps = lax.axis_size("cuts") // CORES
    mine = [block] + [shift_chips(block, k) for k in range(1, steps)]
    return mine, [swap_cores(b) for b in mine]


def shards(
    queries,
    keyvals,
    preceding_keyvalues,
    attention_sink_logits,
    residual,
    w_out,
    norm_gain,
    expert_ids,
    route_weights,
    w_gate,
    w_up,
    w_down,
):
    toks, feats = residual.shape
    live = w_gate.shape[0] * lax.axis_size("seq")
    cuts = lax.axis_size("cuts")
    steps = cuts // CORES
    slots = live * CAP
    hidden = w_gate.shape[2]
    width = norm_gain.shape[0]

    size = lax.axis_size("seq")
    rim = lax.ppermute(keyvals[toks - KEYS_SEEN :], "seq", [(i, i + 1) for i in range(size - 1)])
    placing, mix_hi, mix_lo = call(
        functools.partial(tables_kernel, live), (bf16(slots, toks),) * 3, n_in=2
    )(expert_ids.T, route_weights.T)
    attended = call(
        attend_kernel,
        bf16(*queries.shape),
        scratch=[pltpu.VMEM((KEYS_SEEN + toks, keyvals.shape[1]), jnp.bfloat16)],
        smem=(4,),
        n_in=5,
    )(queries, keyvals, preceding_keyvalues, rim, attention_sink_logits)
    mine, theirs = gather_cuts(attended)
    resid, *outgoing = call(
        functools.partial(project_kernel, steps),
        (bf16(feats, toks),) + (bf16(CAP, feats),) * live,
        scratch=[pltpu.VMEM((live, CAP, feats), jnp.bfloat16)],
        n_in=2 * steps + 3,
    )(*mine, *theirs, w_out.T, residual.T, placing)
    arrived = [outgoing[0]] + [shift_seq(outgoing[k], k) for k in range(1, live)]
    mine, theirs = gather_cuts(jnp.concatenate(arrived, axis=0))
    kept, given = call(
        functools.partial(expert_kernel, steps),
        (bf16(steps, slots, feats),) * 2,
        scratch=[
            pltpu.VMEM((cuts, slots, feats), jnp.bfloat16),
            pltpu.VMEM((slots, width), jnp.bfloat16),
        ],
        n_in=2 * steps + 4,
    )(*mine, *theirs, norm_gain, w_gate[0].T, w_up[0].T, w_down[0])
    sums = call(add_pair_kernel, (bf16(slots, feats),) * steps, n_in=2)(kept, swap_cores(given))
    sums = [sums[0]] + [shift_chips(sums[k], steps - k) for k in range(1, steps)]
    returned = call(
        functools.partial(add_chips_kernel, steps),
        (bf16(CAP, feats),) * live,
        n_in=steps,
    )(*sums)
    returned = [returned[0]] + [shift_seq(returned[k], live - k) for k in range(1, live)]
    out = call(
        functools.partial(combine_kernel, live),
        bf16(feats, toks),
        scratch=[pltpu.VMEM((live, CAP, feats), jnp.bfloat16)],
        n_in=live + 3,
    )(*returned, mix_hi, mix_lo, resid)
    return out.T


def solution(mesh):
    placed = (
        P(("groups", "seq"), "cuts"),
        P(("groups", "seq"), "cuts"),
        P("groups", "cuts"),
        P("cuts"),
        P(("groups", "seq"), "cuts"),
        P(None, "cuts"),
        P(),
        P(("groups", "seq"), None),
        P(("groups", "seq"), None),
        P("seq", None, "cuts"),
        P("seq", None, "cuts"),
        P("seq", "cuts", None),
    )
    return jax.shard_map(
        shards, mesh=mesh, in_specs=placed, out_specs=P(("groups", "seq"), "cuts"), check_vma=False
    )
```

```python
import functools
import math

import jax
import jax.numpy as jnp
from jax import lax
from jax.experimental import pallas as pl
from jax.experimental.pallas import tpu as pltpu
from jax.sharding import PartitionSpec as P

HEAD_SIZE = 64
KEYS_SEEN = 128
PAIR = 2 * HEAD_SIZE
SPAN = 2 * KEYS_SEEN
CAP = 16
CORES = 2

norm_eps = 1e-05
glu_alpha = 1.702

NT = (((1,), (1,)), ((), ()))
NN = (((1,), (0,)), ((), ()))
TN = (((0,), (0,)), ((), ()))
VMEM_LIMIT = 32 * 1024 * 1024


def dot(a, b, dims):
    return lax.dot_general(a, b, dims, preferred_element_type=jnp.float32)


def call(kernel, outs, n_in, scratch=(), hbm=(), smem=(), flops=0, moved=0):
    spaces = [pltpu.HBM if i in hbm else pltpu.SMEM if i in smem else pltpu.VMEM for i in range(n_in)]
    return pl.pallas_call(
        kernel,
        out_shape=outs,
        in_specs=[pl.BlockSpec(memory_space=space) for space in spaces],
        out_specs=jax.tree.map(lambda _: pl.BlockSpec(memory_space=pltpu.VMEM), outs),
        scratch_shapes=list(scratch),
        compiler_params=pltpu.CompilerParams(vmem_limit_bytes=VMEM_LIMIT),
        cost_estimate=pl.CostEstimate(flops=flops, bytes_accessed=moved, transcendentals=0),
    )


def bf16(*shape):
    return jax.ShapeDtypeStruct(shape, jnp.bfloat16)


def visible():
    key = lax.broadcasted_iota(jnp.int32, (SPAN, KEYS_SEEN), 0)
    query = lax.broadcasted_iota(jnp.int32, (SPAN, KEYS_SEEN), 1)
    return (key > query) & (key <= query + KEYS_SEEN)


def attend_block(pairs, both, sinks, allowed):
    both = both.astype(jnp.float32)
    low = lax.broadcasted_iota(jnp.int32, both.shape, 1) < HEAD_SIZE
    turned = pltpu.roll(both, HEAD_SIZE, 1)
    keys = jnp.concatenate([jnp.where(low, both, 0.0), jnp.where(low, 0.0, turned)], axis=0)
    values = jnp.concatenate([jnp.where(low, turned, 0.0), jnp.where(low, 0.0, both)], axis=0)
    keys, values = keys.astype(jnp.bfloat16), values.astype(jnp.bfloat16)
    scores = dot(keys, jnp.concatenate(pairs, axis=0), NT) * (HEAD_SIZE**-0.5 * math.log2(math.e))
    allowed = jnp.concatenate([allowed] * len(pairs), axis=1)
    probs = []
    for i in range(2):
        sink = jnp.concatenate([sinks[2 * p + i] for p in range(len(pairs))], axis=1)
        part = jnp.where(allowed, scores[i * SPAN : (i + 1) * SPAN], -jnp.inf)
        peak = jnp.maximum(jnp.max(part, axis=0, keepdims=True), sink)
        terms = jnp.exp2(part - peak)
        denom = jnp.sum(terms, axis=0, keepdims=True) + jnp.exp2(sink - peak)
        probs.append((terms * (1.0 / denom)).astype(jnp.bfloat16))
    mixed = dot(values, jnp.concatenate(probs, axis=0), TN).astype(jnp.bfloat16)
    return [mixed[:, p * KEYS_SEEN : (p + 1) * KEYS_SEEN] for p in range(len(pairs))]


def attend_tokens(block, q_ref, rows_of, sinks, out_ref, lanes):
    groups = len(rows_of)
    per_group = q_ref.shape[1] // PAIR // groups
    allowed = visible()
    toks = slice(block * KEYS_SEEN, (block + 1) * KEYS_SEEN)
    for g, both in enumerate(rows_of):
        first = g * per_group
        pairs = [q_ref[toks, (first + p) * PAIR : (first + p + 1) * PAIR] for p in range(per_group)]
        outs = attend_block(pairs, both, sinks[2 * first : 2 * (first + per_group)], allowed)
        for p, out in enumerate(outs):
            out_ref[(first + p) * PAIR : (first + p + 1) * PAIR, lanes] = out


def fill_tables(live, ids, weights, placing_ref, mix_hi_ref, mix_lo_ref):
    toks = ids.shape[1]
    chosen = jnp.concatenate(
        [jnp.max((ids == e).astype(jnp.float32), axis=0, keepdims=True) for e in range(live)], axis=0
    )
    earlier = lax.broadcasted_iota(jnp.int32, (toks, toks), 0)
    later = lax.broadcasted_iota(jnp.int32, (toks, toks), 1)
    strict = (earlier < later).astype(jnp.bfloat16)
    before = dot(chosen.astype(jnp.bfloat16), strict, NN)
    slot = lax.broadcasted_iota(jnp.int32, (CAP, toks), 0).astype(jnp.float32)
    for e in range(live):
        weight = jnp.sum(jnp.where(ids == e, weights, 0.0), axis=0, keepdims=True)
        fills = (before[e : e + 1] == slot) & (chosen[e : e + 1] > 0.0)
        mix = jnp.where(fills, weight, 0.0)
        hi = mix.astype(jnp.bfloat16)
        rows = slice(e * CAP, (e + 1) * CAP)
        placing_ref[rows] = fills.astype(jnp.bfloat16)
        mix_hi_ref[rows] = hi
        mix_lo_ref[rows] = (mix - hi.astype(jnp.float32)).astype(jnp.bfloat16)


def first_kernel(live, sinks_ref, *refs):
    loaded, (ids_ref, weights_ref) = refs[:5], refs[5:7]
    held = refs[7:12]
    placing_ref, mix_hi_ref, mix_lo_ref, sinks_out, late_ref, ids_vmem, weights_vmem, sems = refs[12:]
    copies = [
        pltpu.make_async_copy(source, target, sems.at[i])
        for i, (source, target) in enumerate(
            zip((*loaded[:2], ids_ref, weights_ref, *loaded[2:]), (*held[:2], ids_vmem, weights_vmem, *held[2:]))
        )
    ]
    for copy in copies:
        copy.start()
    q_ref, kv_ref = held[:2]
    heads = sinks_ref.shape[0]
    sinks = [jnp.full((1, KEYS_SEEN), sinks_ref[h], jnp.float32) * math.log2(math.e) for h in range(heads)]
    sinks_out[...] = jnp.concatenate(sinks, axis=0)
    for copy in copies[2:4]:
        copy.wait()
    fill_tables(live, ids_vmem[...], weights_vmem[...], placing_ref, mix_hi_ref, mix_lo_ref)
    for copy in copies[:2]:
        copy.wait()
    groups = kv_ref.shape[1] // PAIR
    for b in range(1, q_ref.shape[0] // KEYS_SEEN):
        span = slice((b - 1) * KEYS_SEEN, (b + 1) * KEYS_SEEN)
        rows_of = [kv_ref[span, g * PAIR : (g + 1) * PAIR] for g in range(groups)]
        attend_tokens(b, q_ref, rows_of, sinks, late_ref, slice((b - 1) * KEYS_SEEN, b * KEYS_SEEN))
    for copy in copies[4:]:
        copy.wait()


def second_kernel(q_ref, kv_ref, before_ref, rim_ref, sinks_ref, late_ref, placing_ref, all_ref, rows_ref):
    first = lax.axis_index("seq") == 0
    rim = jnp.where(first, before_ref[...], rim_ref[...])
    groups = kv_ref.shape[1] // PAIR
    rows_of = []
    for g in range(groups):
        lanes = slice(g * PAIR, (g + 1) * PAIR)
        rows_of.append(jnp.concatenate([rim[:, lanes], kv_ref[:KEYS_SEEN, lanes]], axis=0))
    sinks = [sinks_ref[h : h + 1] for h in range(sinks_ref.shape[0])]
    attend_tokens(0, q_ref, rows_of, sinks, all_ref, slice(0, KEYS_SEEN))
    all_ref[:, KEYS_SEEN:] = late_ref[...]
    rows_ref[...] = dot(placing_ref[...], all_ref[...], NT).astype(jnp.bfloat16)


def origin(k, sibling):
    me = lax.axis_index("cuts")
    return lax.bitwise_xor(me, CORES * k + (1 if sibling else 0))


def project_rows_kernel(steps, *refs):
    blocks = refs[: 2 * steps]
    w_ref, residual_ref, placing_ref = refs[2 * steps : 2 * steps + 3]
    outgoing, rows_ref = refs[2 * steps + 3 : -1], refs[-1]
    width = blocks[0].shape[1]
    total = dot(placing_ref[...], residual_ref[...], NT)
    for i, block in enumerate(blocks):
        at = pl.multiple_of(origin(i % steps, i >= steps) * width, 128)
        total += dot(block[...], w_ref[:, pl.ds(at, width)], NT)
    rows_ref[...] = total.astype(jnp.bfloat16).reshape(rows_ref.shape)
    me = lax.axis_index("seq")
    for k, out_ref in enumerate(outgoing):
        out_ref[...] = rows_ref[lax.bitwise_xor(me, k)]


def project_kernel(steps, *refs):
    blocks = refs[: 2 * steps]
    w_ref, residual_ref, resid_ref = refs[2 * steps :]
    width = blocks[0].shape[0]
    total = residual_ref[...].astype(jnp.float32)
    for i, block in enumerate(blocks):
        at = pl.multiple_of(origin(i % steps, i >= steps) * width, 128)
        total += dot(w_ref[:, pl.ds(at, width)], block[...], NN)
    resid_ref[...] = total.astype(jnp.bfloat16)


def expert_kernel(steps, *refs):
    blocks = refs[: 2 * steps]
    gain_ref, gate_ref, up_ref, down_ref, kept_ref, given_ref, blocks_ref, rows_ref = refs[2 * steps :]
    cuts = CORES * steps
    width = blocks[0].shape[1]
    for i, block in enumerate(blocks):
        blocks_ref[origin(i % steps, i >= steps)] = block[...]
    wide = [blocks_ref[p].astype(jnp.float32) for p in range(cuts)]
    squares = sum(jnp.sum(b * b, axis=1, keepdims=True) for b in wide)
    scale = lax.rsqrt(squares / (cuts * width) + norm_eps)
    gain = gain_ref[...].reshape(1, cuts * width)
    rows_ref[...] = (jnp.concatenate(wide, axis=1) * scale * gain).astype(jnp.bfloat16)
    rows = rows_ref[...]
    gate = dot(rows, gate_ref[...], NT)
    up = dot(rows, up_ref[...], NT)
    activated = ((up + 1.0) * gate * jax.nn.sigmoid(glu_alpha * gate)).astype(jnp.bfloat16)
    out = dot(activated, down_ref[...], NN).astype(jnp.bfloat16)
    for p in range(cuts):
        blocks_ref[p] = out[:, p * width : (p + 1) * width]
    for k in range(steps):
        kept_ref[k] = blocks_ref[origin(k, False)]
        given_ref[k] = blocks_ref[origin(k, True)]


def add_cores_kernel(kept_ref, given_ref, *out_refs):
    for k, out_ref in enumerate(out_refs):
        total = kept_ref[k].astype(jnp.float32) + given_ref[k].astype(jnp.float32)
        out_ref[...] = total.astype(jnp.bfloat16)


def add_chips_kernel(steps, *refs):
    total = sum(r[...].astype(jnp.float32) for r in refs[:steps])
    for k, out_ref in enumerate(refs[steps:]):
        out_ref[...] = total[k * CAP : (k + 1) * CAP].astype(jnp.bfloat16)


def combine_kernel(live, *refs):
    blocks = refs[:live]
    mix_hi_ref, mix_lo_ref, resid_ref, out_ref, rows_ref = refs[live:]
    me = lax.axis_index("seq")
    for k in range(live):
        rows_ref[lax.bitwise_xor(me, k)] = blocks[k][...]
    rows = rows_ref[...].reshape(live * CAP, -1)
    mixed = dot(rows, mix_hi_ref[...], TN) + dot(rows, mix_lo_ref[...], TN)
    out_ref[...] = (resid_ref[...].astype(jnp.float32) + mixed).astype(jnp.bfloat16)


def swap(block, axis, mask):
    return lax.ppermute(block, axis, [(i, i ^ mask) for i in range(lax.axis_size(axis))])


def gather_cuts(block):
    steps = lax.axis_size("cuts") // CORES
    mine = [block] + [swap(block, "cuts", CORES * k) for k in range(1, steps)]
    return mine + [swap(b, "cuts", 1) for b in mine]


def shards(
    queries,
    keyvals,
    preceding_keyvalues,
    attention_sink_logits,
    residual,
    w_out,
    norm_gain,
    expert_ids,
    route_weights,
    w_gate,
    w_up,
    w_down,
):
    toks, feats = residual.shape
    size = lax.axis_size("seq")
    live = w_gate.shape[0] * size
    cuts = lax.axis_size("cuts")
    steps = cuts // CORES
    slots = live * CAP
    head_rows = queries.shape[1]
    heads = head_rows // HEAD_SIZE
    width = norm_gain.shape[0]

    rim = lax.ppermute(keyvals[toks - KEYS_SEEN :], "seq", [(i, i + 1) for i in range(size - 1)])
    loads = (queries, keyvals, preceding_keyvalues, w_out.T, residual.T)
    q, kv, before, w_t, residual_t, placing, mix_hi, mix_lo, sinks, late = call(
        functools.partial(first_kernel, live),
        (
            *(bf16(*a.shape) for a in loads),
            *(bf16(slots, toks),) * 3,
            jax.ShapeDtypeStruct((heads, KEYS_SEEN), jnp.float32),
            bf16(head_rows, toks - KEYS_SEEN),
        ),
        n_in=8,
        scratch=[
            pltpu.VMEM(expert_ids.T.shape, jnp.int32),
            pltpu.VMEM(expert_ids.T.shape, jnp.float32),
            pltpu.SemaphoreType.DMA((7,)),
        ],
        smem=(0,),
        hbm=range(1, 8),
        flops=4 * toks * SPAN * head_rows,
        moved=2 * (w_out.size + residual.size + queries.size),
    )(attention_sink_logits, *loads, expert_ids.T, route_weights.T)
    attended, rows = call(
        second_kernel,
        (bf16(head_rows, toks), bf16(slots, head_rows)),
        n_in=7,
        flops=2 * toks * SPAN * head_rows,
        moved=2 * queries.size,
    )(q, kv, before, rim, sinks, late, placing)

    outgoing = call(
        functools.partial(project_rows_kernel, steps),
        (bf16(CAP, feats),) * live,
        n_in=cuts + 3,
        scratch=[pltpu.VMEM((live, CAP, feats), jnp.bfloat16)],
        flops=2 * slots * w_out.size,
        moved=2 * w_out.size,
    )(*gather_cuts(rows), w_t, residual_t, placing)
    arrived = [outgoing[0]] + [swap(outgoing[k], "seq", k) for k in range(1, live)]

    resid = call(
        functools.partial(project_kernel, steps),
        bf16(feats, toks),
        n_in=cuts + 2,
        flops=2 * toks * w_out.size,
        moved=2 * w_out.size,
    )(*gather_cuts(attended), w_t, residual_t)

    kept, given = call(
        functools.partial(expert_kernel, steps),
        (bf16(steps, slots, feats),) * 2,
        n_in=cuts + 4,
        scratch=[
            pltpu.VMEM((cuts, slots, feats), jnp.bfloat16),
            pltpu.VMEM((slots, width), jnp.bfloat16),
        ],
        flops=6 * slots * w_gate.size,
        moved=6 * w_gate.size,
    )(*gather_cuts(jnp.concatenate(arrived, axis=0)), norm_gain, w_gate[0].T, w_up[0].T, w_down[0])
    sums = call(add_cores_kernel, (bf16(slots, feats),) * steps, n_in=2)(kept, swap(given, "cuts", 1))
    sums = [sums[0]] + [swap(sums[k], "cuts", CORES * k) for k in range(1, steps)]
    returned = call(functools.partial(add_chips_kernel, steps), (bf16(CAP, feats),) * live, n_in=steps)(*sums)
    returned = [returned[0]] + [swap(returned[k], "seq", k) for k in range(1, live)]
    out = call(
        functools.partial(combine_kernel, live),
        bf16(feats, toks),
        n_in=live + 3,
        scratch=[pltpu.VMEM((live, CAP, feats), jnp.bfloat16)],
    )(*returned, mix_hi, mix_lo, resid)
    return out.T


def solution(mesh):
    placed = (
        P(("groups", "seq"), "cuts"),
        P(("groups", "seq"), "cuts"),
        P("groups", "cuts"),
        P("cuts"),
        P(("groups", "seq"), "cuts"),
        P(None, "cuts"),
        P(),
        P(("groups", "seq"), None),
        P(("groups", "seq"), None),
        P("seq", None, "cuts"),
        P("seq", None, "cuts"),
        P("seq", "cuts", None),
    )
    return jax.shard_map(
        shards, mesh=mesh, in_specs=placed, out_specs=P(("groups", "seq"), "cuts"), check_vma=False
    )
```

```python
import functools
import math

import jax
import jax.numpy as jnp
from jax import lax
from jax.experimental import pallas as pl
from jax.experimental.pallas import tpu as pltpu
from jax.sharding import PartitionSpec as P

HEAD_SIZE = 64
KEYS_SEEN = 128
PAIR = 2 * HEAD_SIZE
SPAN = 2 * KEYS_SEEN
CAP = 16
CORES = 2

norm_eps = 1e-05
glu_alpha = 1.702

NT = (((1,), (1,)), ((), ()))
NN = (((1,), (0,)), ((), ()))
TN = (((0,), (0,)), ((), ()))
VMEM_LIMIT = 32 * 1024 * 1024


def dot(a, b, dims):
    return lax.dot_general(a, b, dims, preferred_element_type=jnp.float32)


def call(kernel, outs, n_in, scratch=(), hbm=(), smem=(), flops=0, moved=0):
    spaces = [pltpu.HBM if i in hbm else pltpu.SMEM if i in smem else pltpu.VMEM for i in range(n_in)]
    return pl.pallas_call(
        kernel,
        out_shape=outs,
        in_specs=[pl.BlockSpec(memory_space=space) for space in spaces],
        out_specs=jax.tree.map(lambda _: pl.BlockSpec(memory_space=pltpu.VMEM), outs),
        scratch_shapes=list(scratch),
        compiler_params=pltpu.CompilerParams(vmem_limit_bytes=VMEM_LIMIT),
        cost_estimate=pl.CostEstimate(flops=flops, bytes_accessed=moved, transcendentals=0),
    )


def in_hbm(array):
    return pltpu.with_memory_space_constraint(array, pltpu.HBM)


def bf16(*shape):
    return jax.ShapeDtypeStruct(shape, jnp.bfloat16)


def visible():
    key = lax.broadcasted_iota(jnp.int32, (SPAN, KEYS_SEEN), 0)
    query = lax.broadcasted_iota(jnp.int32, (SPAN, KEYS_SEEN), 1)
    return (key > query) & (key <= query + KEYS_SEEN)


def attend_block(pairs, both, sinks, allowed):
    both = both.astype(jnp.float32)
    low = lax.broadcasted_iota(jnp.int32, both.shape, 1) < HEAD_SIZE
    turned = pltpu.roll(both, HEAD_SIZE, 1)
    keys = jnp.concatenate([jnp.where(low, both, 0.0), jnp.where(low, 0.0, turned)], axis=0)
    values = jnp.concatenate([jnp.where(low, turned, 0.0), jnp.where(low, 0.0, both)], axis=0)
    keys, values = keys.astype(jnp.bfloat16), values.astype(jnp.bfloat16)
    scores = dot(keys, jnp.concatenate(pairs, axis=0), NT) * (HEAD_SIZE**-0.5 * math.log2(math.e))
    allowed = jnp.concatenate([allowed] * len(pairs), axis=1)
    probs = []
    for i in range(2):
        sink = jnp.concatenate([sinks[2 * p + i] for p in range(len(pairs))], axis=1)
        part = jnp.where(allowed, scores[i * SPAN : (i + 1) * SPAN], -jnp.inf)
        peak = jnp.maximum(jnp.max(part, axis=0, keepdims=True), sink)
        terms = jnp.exp2(part - peak)
        denom = jnp.sum(terms, axis=0, keepdims=True) + jnp.exp2(sink - peak)
        probs.append((terms * (1.0 / denom)).astype(jnp.bfloat16))
    mixed = dot(values, jnp.concatenate(probs, axis=0), TN).astype(jnp.bfloat16)
    return [mixed[:, p * KEYS_SEEN : (p + 1) * KEYS_SEEN] for p in range(len(pairs))]


def attend_tokens(block, q_ref, rows_of, sinks, out_ref, lanes):
    groups = len(rows_of)
    per_group = q_ref.shape[1] // PAIR // groups
    allowed = visible()
    toks = slice(block * KEYS_SEEN, (block + 1) * KEYS_SEEN)
    for g, both in enumerate(rows_of):
        first = g * per_group
        pairs = [q_ref[toks, (first + p) * PAIR : (first + p + 1) * PAIR] for p in range(per_group)]
        outs = attend_block(pairs, both, sinks[2 * first : 2 * (first + per_group)], allowed)
        for p, out in enumerate(outs):
            out_ref[(first + p) * PAIR : (first + p + 1) * PAIR, lanes] = out


def fill_tables(live, ids, weights, placing_ref, mix_hi_ref, mix_lo_ref):
    toks = ids.shape[1]
    chosen = jnp.concatenate(
        [jnp.max((ids == e).astype(jnp.float32), axis=0, keepdims=True) for e in range(live)], axis=0
    )
    earlier = lax.broadcasted_iota(jnp.int32, (toks, toks), 0)
    later = lax.broadcasted_iota(jnp.int32, (toks, toks), 1)
    strict = (earlier < later).astype(jnp.bfloat16)
    before = dot(chosen.astype(jnp.bfloat16), strict, NN)
    slot = lax.broadcasted_iota(jnp.int32, (CAP, toks), 0).astype(jnp.float32)
    for e in range(live):
        weight = jnp.sum(jnp.where(ids == e, weights, 0.0), axis=0, keepdims=True)
        fills = (before[e : e + 1] == slot) & (chosen[e : e + 1] > 0.0)
        mix = jnp.where(fills, weight, 0.0)
        hi = mix.astype(jnp.bfloat16)
        rows = slice(e * CAP, (e + 1) * CAP)
        placing_ref[rows] = fills.astype(jnp.bfloat16)
        mix_hi_ref[rows] = hi
        mix_lo_ref[rows] = (mix - hi.astype(jnp.float32)).astype(jnp.bfloat16)


def first_kernel(live, sinks_ref, *refs):
    loaded, (ids_ref, weights_ref) = refs[:5], refs[5:7]
    held = refs[7:12]
    placing_ref, mix_hi_ref, mix_lo_ref, sinks_out, late_ref, ids_vmem, weights_vmem, sems = refs[12:]
    copies = [
        pltpu.make_async_copy(source, target, sems.at[i])
        for i, (source, target) in enumerate(
            zip((*loaded[:2], ids_ref, weights_ref, *loaded[2:]), (*held[:2], ids_vmem, weights_vmem, *held[2:]))
        )
    ]
    for copy in copies:
        copy.start()
    q_ref, kv_ref = held[:2]
    heads = sinks_ref.shape[0]
    sinks = [jnp.full((1, KEYS_SEEN), sinks_ref[h], jnp.float32) * math.log2(math.e) for h in range(heads)]
    sinks_out[...] = jnp.concatenate(sinks, axis=0)
    for copy in copies[2:4]:
        copy.wait()
    fill_tables(live, ids_vmem[...], weights_vmem[...], placing_ref, mix_hi_ref, mix_lo_ref)
    for copy in copies[:2]:
        copy.wait()
    groups = kv_ref.shape[1] // PAIR
    for b in range(1, q_ref.shape[0] // KEYS_SEEN):
        span = slice((b - 1) * KEYS_SEEN, (b + 1) * KEYS_SEEN)
        rows_of = [kv_ref[span, g * PAIR : (g + 1) * PAIR] for g in range(groups)]
        attend_tokens(b, q_ref, rows_of, sinks, late_ref, slice((b - 1) * KEYS_SEEN, b * KEYS_SEEN))
    for copy in copies[4:]:
        copy.wait()


def second_kernel(q_ref, kv_ref, before_ref, rim_ref, sinks_ref, late_ref, placing_ref, all_ref, rows_ref):
    first = lax.axis_index("seq") == 0
    rim = jnp.where(first, before_ref[...], rim_ref[rim_ref.shape[0] - KEYS_SEEN :])
    groups = kv_ref.shape[1] // PAIR
    rows_of = []
    for g in range(groups):
        lanes = slice(g * PAIR, (g + 1) * PAIR)
        rows_of.append(jnp.concatenate([rim[:, lanes], kv_ref[:KEYS_SEEN, lanes]], axis=0))
    sinks = [sinks_ref[h : h + 1] for h in range(sinks_ref.shape[0])]
    attend_tokens(0, q_ref, rows_of, sinks, all_ref, slice(0, KEYS_SEEN))
    all_ref[:, KEYS_SEEN:] = late_ref[...]
    rows_ref[...] = dot(placing_ref[...], all_ref[...], NT).astype(jnp.bfloat16)


def origin(k, sibling):
    me = lax.axis_index("cuts")
    return lax.bitwise_xor(me, CORES * k + (1 if sibling else 0))


def add_products(total, first, blocks, w_ref, steps, dims, swapped=False):
    width = blocks[0].shape[0 if swapped else 1] if blocks else 0
    for i, block in enumerate(blocks, first):
        at = pl.multiple_of(origin(i % steps, i >= steps) * width, 128)
        w = w_ref[:, pl.ds(at, width)]
        total += dot(w, block[...], dims) if swapped else dot(block[...], w, dims)
    return total


def rows_near_kernel(steps, mine_ref, theirs_ref, w_ref, residual_ref, placing_ref, total_ref):
    total = dot(placing_ref[...], residual_ref[...], NT)
    total = add_products(total, 0, [mine_ref], w_ref, steps, NT)
    total_ref[...] = add_products(total, steps, [theirs_ref], w_ref, steps, NT)


def rows_chips_kernel(steps, *refs):
    blocks, (before_ref, w_ref, total_ref) = refs[: steps - 1], refs[steps - 1 :]
    total_ref[...] = add_products(before_ref[...], 1, blocks, w_ref, steps, NT)


def rows_last_kernel(steps, *refs):
    blocks, (before_ref, w_ref) = refs[: steps - 1], refs[steps - 1 : steps + 1]
    outgoing, rows_ref = refs[steps + 1 : -1], refs[-1]
    total = add_products(before_ref[...], steps + 1, blocks, w_ref, steps, NT)
    rows_ref[...] = total.astype(jnp.bfloat16).reshape(rows_ref.shape)
    me = lax.axis_index("seq")
    for k, out_ref in enumerate(outgoing):
        out_ref[...] = rows_ref[lax.bitwise_xor(me, k)]


def stack_kernel(*refs):
    for i, block in enumerate(refs[:-1]):
        refs[-1][i * CAP : (i + 1) * CAP] = block[...]


def project_kernel(steps, *refs):
    blocks = refs[: 2 * steps]
    w_ref, residual_ref, resid_ref = refs[2 * steps :]
    total = add_products(residual_ref[...].astype(jnp.float32), 0, blocks, w_ref, steps, NN, True)
    resid_ref[...] = total.astype(jnp.bfloat16)


def expert_kernel(live, steps, *refs):
    cuts = CORES * steps
    most, rest = refs[:cuts], refs[cuts : 2 * cuts]
    gain_ref, gate_ref, up_ref, down_ref, kept_ref, given_ref, blocks_ref, rows_ref = refs[2 * cuts :]
    width = most[0].shape[1]
    far = (live - 2) * CAP
    for i in range(cuts):
        p = origin(i % steps, i >= steps)
        blocks_ref[p, :far] = most[i][:far]
        blocks_ref[p, far : far + CAP] = rest[i][...]
        blocks_ref[p, far + CAP :] = most[i][far:]
    wide = [blocks_ref[p].astype(jnp.float32) for p in range(cuts)]
    squares = sum(jnp.sum(b * b, axis=1, keepdims=True) for b in wide)
    scale = lax.rsqrt(squares / (cuts * width) + norm_eps)
    gain = gain_ref[...].reshape(1, cuts * width)
    rows_ref[...] = (jnp.concatenate(wide, axis=1) * scale * gain).astype(jnp.bfloat16)
    rows = rows_ref[...]
    gate = dot(rows, gate_ref[...], NT)
    up = dot(rows, up_ref[...], NT)
    activated = ((up + 1.0) * gate * jax.nn.sigmoid(glu_alpha * gate)).astype(jnp.bfloat16)
    out = dot(activated, down_ref[...], NN).astype(jnp.bfloat16)
    for p in range(cuts):
        blocks_ref[p] = out[:, p * width : (p + 1) * width]
    for k in range(steps):
        kept_ref[k] = blocks_ref[origin(k, False)]
        given_ref[k] = blocks_ref[origin(k, True)]


def add_cores_kernel(kept_ref, given_ref, *out_refs):
    half = out_refs[0].shape[0]
    for i, out_ref in enumerate(out_refs):
        rows = slice(i % 2 * half, (i % 2 + 1) * half)
        total = kept_ref[i // 2, rows].astype(jnp.float32) + given_ref[i // 2, rows].astype(jnp.float32)
        out_ref[...] = total.astype(jnp.bfloat16)


def add_chips_kernel(steps, *refs):
    total = sum(r[...].astype(jnp.float32) for r in refs[:steps])
    for k, out_ref in enumerate(refs[steps:]):
        out_ref[...] = total[k * CAP : (k + 1) * CAP].astype(jnp.bfloat16)


def combine_kernel(live, *refs):
    blocks = refs[:live]
    mix_hi_ref, mix_lo_ref, resid_ref, out_ref, rows_ref = refs[live:]
    me = lax.axis_index("seq")
    for k in range(live):
        rows_ref[lax.bitwise_xor(me, live - 1 - k)] = blocks[k][...]
    rows = rows_ref[...].reshape(live * CAP, -1)
    mixed = dot(rows, mix_hi_ref[...], TN) + dot(rows, mix_lo_ref[...], TN)
    out_ref[...] = (resid_ref[...].astype(jnp.float32) + mixed).astype(jnp.bfloat16)


def swap(block, axis, mask):
    return lax.ppermute(block, axis, [(i, i ^ mask) for i in range(lax.axis_size(axis))])


def gather_cuts(block):
    steps = lax.axis_size("cuts") // CORES
    mine = [block] + [swap(block, "cuts", CORES * k) for k in range(1, steps)]
    return mine, [swap(b, "cuts", 1) for b in mine]


def shards(
    queries,
    keyvals,
    preceding_keyvalues,
    attention_sink_logits,
    residual,
    w_out,
    norm_gain,
    expert_ids,
    route_weights,
    w_gate,
    w_up,
    w_down,
):
    toks, feats = residual.shape
    size = lax.axis_size("seq")
    live = w_gate.shape[0] * size
    cuts = lax.axis_size("cuts")
    steps = cuts // CORES
    slots = live * CAP
    head_rows = queries.shape[1]
    heads = head_rows // HEAD_SIZE
    width = norm_gain.shape[0]

    rim = lax.ppermute(keyvals, "seq", [(i, i + 1) for i in range(size - 1)])
    loads = (queries, keyvals, preceding_keyvalues, w_out.T, residual.T)
    q, kv, before, w_t, residual_t, placing, mix_hi, mix_lo, sinks, late = call(
        functools.partial(first_kernel, live),
        (
            *(bf16(*a.shape) for a in loads),
            *(bf16(slots, toks),) * 3,
            jax.ShapeDtypeStruct((heads, KEYS_SEEN), jnp.float32),
            bf16(head_rows, toks - KEYS_SEEN),
        ),
        n_in=8,
        scratch=[
            pltpu.VMEM(expert_ids.T.shape, jnp.int32),
            pltpu.VMEM(expert_ids.T.shape, jnp.float32),
            pltpu.SemaphoreType.DMA((7,)),
        ],
        smem=(0,),
        hbm=range(1, 8),
        flops=4 * toks * SPAN * head_rows,
        moved=2 * (w_out.size + residual.size + queries.size),
    )(attention_sink_logits, *(in_hbm(a) for a in (*loads, expert_ids.T, route_weights.T)))
    attended, rows = call(
        second_kernel,
        (bf16(head_rows, toks), bf16(slots, head_rows)),
        n_in=7,
        flops=2 * toks * SPAN * head_rows,
        moved=2 * queries.size,
    )(q, kv, before, rim, sinks, late, placing)

    mine, theirs = gather_cuts(rows)
    total = jax.ShapeDtypeStruct((slots, feats), jnp.float32)
    part = dict(flops=slots * w_out.size // 2, moved=w_out.size // 2)
    near = call(functools.partial(rows_near_kernel, steps), total, n_in=5, **part)(
        mine[0], theirs[0], w_t, residual_t, placing
    )
    chips = call(functools.partial(rows_chips_kernel, steps), total, n_in=steps + 1, **part)(
        *mine[1:], near, w_t
    )
    outgoing = call(
        functools.partial(rows_last_kernel, steps),
        (bf16(CAP, feats),) * live,
        n_in=steps + 1,
        scratch=[pltpu.VMEM((live, CAP, feats), jnp.bfloat16)],
        **part,
    )(*theirs[1:], chips, w_t)

    arrived = [swap(outgoing[k], "seq", k) for k in range(live - 1, 0, -1)] + [outgoing[0]]
    most = call(stack_kernel, bf16(slots - CAP, feats), n_in=live - 1)(*arrived[:-2], arrived[-1])
    most_mine, most_theirs = gather_cuts(most)
    rest_mine, rest_theirs = gather_cuts(arrived[-2])

    mine, theirs = gather_cuts(attended)
    resid = call(
        functools.partial(project_kernel, steps),
        bf16(feats, toks),
        n_in=cuts + 2,
        flops=2 * toks * w_out.size,
        moved=2 * w_out.size,
    )(*mine, *theirs, w_t, residual_t)

    kept, given = call(
        functools.partial(expert_kernel, live, steps),
        (bf16(steps, slots, feats),) * 2,
        n_in=2 * cuts + 4,
        scratch=[
            pltpu.VMEM((cuts, slots, feats), jnp.bfloat16),
            pltpu.VMEM((slots, width), jnp.bfloat16),
        ],
        flops=6 * slots * w_gate.size,
        moved=6 * w_gate.size,
    )(*most_mine, *most_theirs, *rest_mine, *rest_theirs, norm_gain, w_gate[0].T, w_up[0].T, w_down[0])
    sums = call(add_cores_kernel, (bf16(slots // 2, feats),) * (2 * steps), n_in=2)(
        kept, swap(given, "cuts", 1)
    )
    returned = []
    for half in range(2):
        parts = [sums[half]] + [swap(sums[2 * k + half], "cuts", CORES * k) for k in range(1, steps)]
        blocks = call(functools.partial(add_chips_kernel, steps), (bf16(CAP, feats),) * (live // 2), n_in=steps)(
            *parts
        )
        for block in blocks:
            k = live - 1 - len(returned)
            returned.append(swap(block, "seq", k) if k else block)
    out = call(
        functools.partial(combine_kernel, live),
        bf16(feats, toks),
        n_in=live + 3,
        scratch=[pltpu.VMEM((live, CAP, feats), jnp.bfloat16)],
    )(*returned, mix_hi, mix_lo, resid)
    return out.T


def solution(mesh):
    placed = (
        P(("groups", "seq"), "cuts"),
        P(("groups", "seq"), "cuts"),
        P("groups", "cuts"),
        P("cuts"),
        P(("groups", "seq"), "cuts"),
        P(None, "cuts"),
        P(),
        P(("groups", "seq"), None),
        P(("groups", "seq"), None),
        P("seq", None, "cuts"),
        P("seq", None, "cuts"),
        P("seq", "cuts", None),
    )
    return jax.shard_map(
        shards, mesh=mesh, in_specs=placed, out_specs=P(("groups", "seq"), "cuts"), check_vma=False
    )
```

```python
import functools
import math

import jax
import jax.numpy as jnp
from jax import lax
from jax.experimental import pallas as pl
from jax.experimental.pallas import tpu as pltpu
from jax.sharding import PartitionSpec as P

HEAD_SIZE = 64
KEYS_SEEN = 128
PAIR = 2 * HEAD_SIZE
SPAN = 2 * KEYS_SEEN
CAP = 16
CORES = 2

norm_eps = 1e-05
glu_alpha = 1.702

NT = (((1,), (1,)), ((), ()))
NN = (((1,), (0,)), ((), ()))
TN = (((0,), (0,)), ((), ()))
VMEM_LIMIT = 32 * 1024 * 1024


def dot(a, b, dims):
    return lax.dot_general(a, b, dims, preferred_element_type=jnp.float32)


def call(kernel, outs, n_in, scratch=(), hbm=(), smem=(), flops=0, moved=0):
    spaces = [pltpu.HBM if i in hbm else pltpu.SMEM if i in smem else pltpu.VMEM for i in range(n_in)]
    return pl.pallas_call(
        kernel,
        out_shape=outs,
        in_specs=[pl.BlockSpec(memory_space=space) for space in spaces],
        out_specs=jax.tree.map(lambda _: pl.BlockSpec(memory_space=pltpu.VMEM), outs),
        scratch_shapes=list(scratch),
        compiler_params=pltpu.CompilerParams(vmem_limit_bytes=VMEM_LIMIT),
        cost_estimate=pl.CostEstimate(flops=flops, bytes_accessed=moved, transcendentals=0),
    )


def in_hbm(array):
    return pltpu.with_memory_space_constraint(array, pltpu.HBM)


def bf16(*shape):
    return jax.ShapeDtypeStruct(shape, jnp.bfloat16)


def visible():
    key = lax.broadcasted_iota(jnp.int32, (SPAN, KEYS_SEEN), 0)
    query = lax.broadcasted_iota(jnp.int32, (SPAN, KEYS_SEEN), 1)
    return (key > query) & (key <= query + KEYS_SEEN)


def attend_block(pairs, both, sinks, allowed):
    both = both.astype(jnp.float32)
    low = lax.broadcasted_iota(jnp.int32, both.shape, 1) < HEAD_SIZE
    turned = pltpu.roll(both, HEAD_SIZE, 1)
    keys = jnp.concatenate([jnp.where(low, both, 0.0), jnp.where(low, 0.0, turned)], axis=0)
    values = jnp.concatenate([jnp.where(low, turned, 0.0), jnp.where(low, 0.0, both)], axis=0)
    keys, values = keys.astype(jnp.bfloat16), values.astype(jnp.bfloat16)
    scores = dot(keys, jnp.concatenate(pairs, axis=0), NT) * (HEAD_SIZE**-0.5 * math.log2(math.e))
    allowed = jnp.concatenate([allowed] * len(pairs), axis=1)
    probs = []
    for i in range(2):
        sink = jnp.concatenate([sinks[2 * p + i] for p in range(len(pairs))], axis=1)
        part = jnp.where(allowed, scores[i * SPAN : (i + 1) * SPAN], -jnp.inf)
        peak = jnp.maximum(jnp.max(part, axis=0, keepdims=True), sink)
        terms = jnp.exp2(part - peak)
        denom = jnp.sum(terms, axis=0, keepdims=True) + jnp.exp2(sink - peak)
        probs.append((terms * (1.0 / denom)).astype(jnp.bfloat16))
    mixed = dot(values, jnp.concatenate(probs, axis=0), TN).astype(jnp.bfloat16)
    return [mixed[:, p * KEYS_SEEN : (p + 1) * KEYS_SEEN] for p in range(len(pairs))]


def attend_tokens(block, q_ref, rows_of, sinks, out_ref, lanes):
    groups = len(rows_of)
    per_group = q_ref.shape[1] // PAIR // groups
    allowed = visible()
    toks = slice(block * KEYS_SEEN, (block + 1) * KEYS_SEEN)
    for g, both in enumerate(rows_of):
        first = g * per_group
        pairs = [q_ref[toks, (first + p) * PAIR : (first + p + 1) * PAIR] for p in range(per_group)]
        outs = attend_block(pairs, both, sinks[2 * first : 2 * (first + per_group)], allowed)
        for p, out in enumerate(outs):
            out_ref[(first + p) * PAIR : (first + p + 1) * PAIR, lanes] = out


def fill_tables(live, ids, weights, placing_ref, mix_hi_ref, mix_lo_ref):
    toks = ids.shape[1]
    chosen = jnp.concatenate(
        [jnp.max((ids == e).astype(jnp.float32), axis=0, keepdims=True) for e in range(live)], axis=0
    )
    earlier = lax.broadcasted_iota(jnp.int32, (toks, toks), 0)
    later = lax.broadcasted_iota(jnp.int32, (toks, toks), 1)
    strict = (earlier < later).astype(jnp.bfloat16)
    before = dot(chosen.astype(jnp.bfloat16), strict, NN)
    slot = lax.broadcasted_iota(jnp.int32, (CAP, toks), 0).astype(jnp.float32)
    for e in range(live):
        weight = jnp.sum(jnp.where(ids == e, weights, 0.0), axis=0, keepdims=True)
        fills = (before[e : e + 1] == slot) & (chosen[e : e + 1] > 0.0)
        mix = jnp.where(fills, weight, 0.0)
        hi = mix.astype(jnp.bfloat16)
        rows = slice(e * CAP, (e + 1) * CAP)
        placing_ref[rows] = fills.astype(jnp.bfloat16)
        mix_hi_ref[rows] = hi
        mix_lo_ref[rows] = (mix - hi.astype(jnp.float32)).astype(jnp.bfloat16)


def first_kernel(live, *refs):
    loaded, held = refs[:8], refs[8:13]
    placing_ref, mix_hi_ref, mix_lo_ref, sinks_out, late_ref, ids_ref, weights_ref, sinks_ref, sems = refs[13:]
    targets = (ids_ref, weights_ref, sinks_ref, *held)
    copies = [pltpu.make_async_copy(*pair, sems.at[i]) for i, pair in enumerate(zip(loaded, targets))]
    for copy in copies:
        copy.start()
    q_ref, kv_ref = held[:2]
    for copy in copies[:2]:
        copy.wait()
    fill_tables(live, ids_ref[...], weights_ref[...], placing_ref, mix_hi_ref, mix_lo_ref)
    for copy in copies[2:5]:
        copy.wait()
    heads = sinks_ref.shape[0]
    sinks = [jnp.full((1, KEYS_SEEN), sinks_ref[h], jnp.float32) * math.log2(math.e) for h in range(heads)]
    sinks_out[...] = jnp.concatenate(sinks, axis=0)
    groups = kv_ref.shape[1] // PAIR
    for b in range(1, q_ref.shape[0] // KEYS_SEEN):
        span = slice((b - 1) * KEYS_SEEN, (b + 1) * KEYS_SEEN)
        rows_of = [kv_ref[span, g * PAIR : (g + 1) * PAIR] for g in range(groups)]
        attend_tokens(b, q_ref, rows_of, sinks, late_ref, slice((b - 1) * KEYS_SEEN, b * KEYS_SEEN))
    for copy in copies[5:]:
        copy.wait()


def second_kernel(
    q_ref, kv_ref, before_ref, to_even_ref, to_odd_ref, sinks_ref, late_ref, placing_ref, all_ref, rows_ref
):
    first = lax.axis_index("seq") == 0
    odd = lax.rem(lax.axis_index("seq"), 2) == 1
    rim = jnp.where(first, before_ref[...], jnp.where(odd, to_odd_ref[...], to_even_ref[...]))
    groups = kv_ref.shape[1] // PAIR
    rows_of = []
    for g in range(groups):
        lanes = slice(g * PAIR, (g + 1) * PAIR)
        rows_of.append(jnp.concatenate([rim[:, lanes], kv_ref[:KEYS_SEEN, lanes]], axis=0))
    sinks = [sinks_ref[h : h + 1] for h in range(sinks_ref.shape[0])]
    attend_tokens(0, q_ref, rows_of, sinks, all_ref, slice(0, KEYS_SEEN))
    all_ref[:, KEYS_SEEN:] = late_ref[...]
    rows_ref[...] = dot(placing_ref[...], all_ref[...], NT).astype(jnp.bfloat16)


def origin(k, sibling):
    me = lax.axis_index("cuts")
    return lax.bitwise_xor(me, CORES * k + (1 if sibling else 0))


def add_products(total, first, blocks, w_ref, steps, dims, swapped=False):
    width = blocks[0].shape[0 if swapped else 1] if blocks else 0
    for i, block in enumerate(blocks, first):
        at = pl.multiple_of(origin(i % steps, i >= steps) * width, 128)
        w = w_ref[:, pl.ds(at, width)]
        total += dot(w, block[...], dims) if swapped else dot(block[...], w, dims)
    return total


def rows_near_kernel(steps, mine_ref, theirs_ref, w_ref, residual_ref, placing_ref, total_ref):
    total = dot(placing_ref[...], residual_ref[...], NT)
    total = add_products(total, 0, [mine_ref], w_ref, steps, NT)
    total_ref[...] = add_products(total, steps, [theirs_ref], w_ref, steps, NT)


def rows_chips_kernel(steps, *refs):
    blocks, (before_ref, w_ref, total_ref) = refs[: steps - 1], refs[steps - 1 :]
    total_ref[...] = add_products(before_ref[...], 1, blocks, w_ref, steps, NT)


def rows_last_kernel(steps, *refs):
    blocks, (before_ref, w_ref) = refs[: steps - 1], refs[steps - 1 : steps + 1]
    outgoing, rows_ref = refs[steps + 1 : -1], refs[-1]
    total = add_products(before_ref[...], steps + 1, blocks, w_ref, steps, NT)
    rows_ref[...] = total.astype(jnp.bfloat16).reshape(rows_ref.shape)
    me = lax.axis_index("seq")
    for k, out_ref in enumerate(outgoing):
        out_ref[...] = rows_ref[lax.bitwise_xor(me, k)]


def stack_kernel(*refs):
    for i, block in enumerate(refs[:-1]):
        refs[-1][i * CAP : (i + 1) * CAP] = block[...]


def project_kernel(steps, *refs):
    blocks = refs[: 2 * steps]
    w_ref, residual_ref, resid_ref = refs[2 * steps :]
    total = add_products(residual_ref[...].astype(jnp.float32), 0, blocks, w_ref, steps, NN, True)
    resid_ref[...] = total.astype(jnp.bfloat16)


def expert_kernel(steps, *refs):
    cuts = CORES * steps
    gain_ref, gate_ref, up_ref, down_ref, kept_ref, given_ref, blocks_ref, rows_ref = refs[cuts:]
    width = refs[0].shape[1]
    for i in range(cuts):
        blocks_ref[origin(i % steps, i >= steps)] = refs[i][...]
    wide = [blocks_ref[p].astype(jnp.float32) for p in range(cuts)]
    squares = sum(jnp.sum(b * b, axis=1, keepdims=True) for b in wide)
    scale = lax.rsqrt(squares / (cuts * width) + norm_eps)
    gain = gain_ref[...].reshape(1, cuts * width)
    rows_ref[...] = (jnp.concatenate(wide, axis=1) * scale * gain).astype(jnp.bfloat16)
    rows = rows_ref[...]
    gate = dot(rows, gate_ref[...], NT)
    up = dot(rows, up_ref[...], NT)
    activated = ((up + 1.0) * gate * jax.nn.sigmoid(glu_alpha * gate)).astype(jnp.bfloat16)
    out = dot(activated, down_ref[...], NN).astype(jnp.bfloat16)
    for p in range(cuts):
        blocks_ref[p] = out[:, p * width : (p + 1) * width]
    for k in range(steps):
        kept_ref[k] = blocks_ref[origin(k, False)]
        given_ref[k] = blocks_ref[origin(k, True)]


def add_cores_kernel(kept_ref, given_ref, *out_refs):
    half = out_refs[0].shape[0]
    for i, out_ref in enumerate(out_refs):
        rows = slice(i % 2 * half, (i % 2 + 1) * half)
        total = kept_ref[i // 2, rows].astype(jnp.float32) + given_ref[i // 2, rows].astype(jnp.float32)
        out_ref[...] = total.astype(jnp.bfloat16)


def add_chips_kernel(steps, *refs):
    total = sum(r[...].astype(jnp.float32) for r in refs[:steps])
    for k, out_ref in enumerate(refs[steps:]):
        out_ref[...] = total[k * CAP : (k + 1) * CAP].astype(jnp.bfloat16)


def combine_kernel(live, *refs):
    blocks = refs[:live]
    mix_hi_ref, mix_lo_ref, resid_ref, out_ref, rows_ref = refs[live:]
    me = lax.axis_index("seq")
    for k in range(live):
        rows_ref[lax.bitwise_xor(me, live - 1 - k)] = blocks[k][...]
    rows = rows_ref[...].reshape(live * CAP, -1)
    mixed = dot(rows, mix_hi_ref[...], TN) + dot(rows, mix_lo_ref[...], TN)
    out_ref[...] = (resid_ref[...].astype(jnp.float32) + mixed).astype(jnp.bfloat16)


def swap(block, axis, mask):
    return lax.ppermute(block, axis, [(i, i ^ mask) for i in range(lax.axis_size(axis))])


def gather_cuts(block):
    steps = lax.axis_size("cuts") // CORES
    mine = [block] + [swap(block, "cuts", CORES * k) for k in range(1, steps)]
    return mine, [swap(b, "cuts", 1) for b in mine]


def shards(
    queries,
    keyvals,
    preceding_keyvalues,
    attention_sink_logits,
    residual,
    w_out,
    norm_gain,
    expert_ids,
    route_weights,
    w_gate,
    w_up,
    w_down,
):
    toks, feats = residual.shape
    size = lax.axis_size("seq")
    live = w_gate.shape[0] * size
    cuts = lax.axis_size("cuts")
    steps = cuts // CORES
    slots = live * CAP
    head_rows = queries.shape[1]
    heads = head_rows // HEAD_SIZE
    width = norm_gain.shape[0]

    tail = keyvals[toks - KEYS_SEEN :]
    rims = [lax.ppermute(tail, "seq", [(i, i + 1) for i in range(odd, size - 1, 2)]) for odd in (1, 0)]
    loads = (queries, keyvals, preceding_keyvalues, w_out.T, residual.T)
    q, kv, before, w_t, residual_t, placing, mix_hi, mix_lo, sinks, late = call(
        functools.partial(first_kernel, live),
        (
            *(bf16(*a.shape) for a in loads),
            *(bf16(slots, toks),) * 3,
            jax.ShapeDtypeStruct((heads, KEYS_SEEN), jnp.float32),
            bf16(head_rows, toks - KEYS_SEEN),
        ),
        n_in=8,
        scratch=[
            pltpu.VMEM(expert_ids.T.shape, jnp.int32),
            pltpu.VMEM(expert_ids.T.shape, jnp.float32),
            pltpu.SMEM(attention_sink_logits.shape, jnp.float32),
            pltpu.SemaphoreType.DMA((8,)),
        ],
        hbm=range(8),
        flops=4 * toks * SPAN * head_rows,
        moved=2 * (w_out.size + residual.size + queries.size),
    )(*(in_hbm(a) for a in (expert_ids.T, route_weights.T, attention_sink_logits, *loads)))
    attended, rows = call(
        second_kernel,
        (bf16(head_rows, toks), bf16(slots, head_rows)),
        n_in=8,
        flops=2 * toks * SPAN * head_rows,
        moved=2 * queries.size,
    )(q, kv, before, *rims, sinks, late, placing)

    mine, theirs = gather_cuts(rows)
    total = jax.ShapeDtypeStruct((slots, feats), jnp.float32)
    part = dict(flops=slots * w_out.size // 2, moved=w_out.size // 2)
    near = call(functools.partial(rows_near_kernel, steps), total, n_in=5, **part)(
        mine[0], theirs[0], w_t, residual_t, placing
    )
    chips = call(functools.partial(rows_chips_kernel, steps), total, n_in=steps + 1, **part)(
        *mine[1:], near, w_t
    )
    outgoing = call(
        functools.partial(rows_last_kernel, steps),
        (bf16(CAP, feats),) * live,
        n_in=steps + 1,
        scratch=[pltpu.VMEM((live, CAP, feats), jnp.bfloat16)],
        **part,
    )(*theirs[1:], chips, w_t)

    arrived = [swap(outgoing[k], "seq", k) for k in range(live - 1, 0, -1)] + [outgoing[0]]
    stacked = call(stack_kernel, bf16(slots, feats), n_in=live)(*arrived)
    expert_mine, expert_theirs = gather_cuts(stacked)

    attended, _ = lax.optimization_barrier((attended, chips))
    mine, theirs = gather_cuts(attended)
    resid = call(
        functools.partial(project_kernel, steps),
        bf16(feats, toks),
        n_in=cuts + 2,
        flops=2 * toks * w_out.size,
        moved=2 * w_out.size,
    )(*mine, *theirs, w_t, residual_t)

    kept, given = call(
        functools.partial(expert_kernel, steps),
        (bf16(steps, slots, feats),) * 2,
        n_in=cuts + 4,
        scratch=[
            pltpu.VMEM((cuts, slots, feats), jnp.bfloat16),
            pltpu.VMEM((slots, width), jnp.bfloat16),
        ],
        flops=6 * slots * w_gate.size,
        moved=6 * w_gate.size,
    )(*expert_mine, *expert_theirs, norm_gain, w_gate[0].T, w_up[0].T, w_down[0])
    sums = call(add_cores_kernel, (bf16(slots // 2, feats),) * (2 * steps), n_in=2)(
        kept, swap(given, "cuts", 1)
    )
    returned = []
    for half in range(2):
        parts = [sums[half]] + [swap(sums[2 * k + half], "cuts", CORES * k) for k in range(1, steps)]
        blocks = call(functools.partial(add_chips_kernel, steps), (bf16(CAP, feats),) * (live // 2), n_in=steps)(
            *parts
        )
        for block in blocks:
            k = live - 1 - len(returned)
            returned.append(swap(block, "seq", k) if k else block)
    out = call(
        functools.partial(combine_kernel, live),
        bf16(feats, toks),
        n_in=live + 3,
        scratch=[pltpu.VMEM((live, CAP, feats), jnp.bfloat16)],
    )(*returned, mix_hi, mix_lo, resid)
    return out.T


def solution(mesh):
    placed = (
        P(("groups", "seq"), "cuts"),
        P(("groups", "seq"), "cuts"),
        P("groups", "cuts"),
        P("cuts"),
        P(("groups", "seq"), "cuts"),
        P(None, "cuts"),
        P(),
        P(("groups", "seq"), None),
        P(("groups", "seq"), None),
        P("seq", None, "cuts"),
        P("seq", None, "cuts"),
        P("seq", "cuts", None),
    )
    return jax.shard_map(
        shards, mesh=mesh, in_specs=placed, out_specs=P(("groups", "seq"), "cuts"), check_vma=False
    )
```

```python
import functools
import math

import jax
import jax.numpy as jnp
from jax import lax
from jax.experimental import pallas as pl
from jax.experimental.pallas import tpu as pltpu
from jax.sharding import PartitionSpec as P

HEAD_SIZE = 64
KEYS_SEEN = 128
PAIR = 2 * HEAD_SIZE
SPAN = 2 * KEYS_SEEN
CAP = 16
CORES = 2

norm_eps = 1e-05
glu_alpha = 1.702

NT = (((1,), (1,)), ((), ()))
NN = (((1,), (0,)), ((), ()))
TN = (((0,), (0,)), ((), ()))
VMEM_LIMIT = 32 * 1024 * 1024


def dot(a, b, dims):
    return lax.dot_general(a, b, dims, preferred_element_type=jnp.float32)


def call(kernel, outs, n_in, scratch=(), hbm=(), smem=(), flops=0, moved=0):
    spaces = [pltpu.HBM if i in hbm else pltpu.SMEM if i in smem else pltpu.VMEM for i in range(n_in)]
    return pl.pallas_call(
        kernel,
        out_shape=outs,
        in_specs=[pl.BlockSpec(memory_space=space) for space in spaces],
        out_specs=jax.tree.map(lambda _: pl.BlockSpec(memory_space=pltpu.VMEM), outs),
        scratch_shapes=list(scratch),
        compiler_params=pltpu.CompilerParams(vmem_limit_bytes=VMEM_LIMIT),
        cost_estimate=pl.CostEstimate(flops=flops, bytes_accessed=moved, transcendentals=0),
    )


def in_hbm(array):
    return pltpu.with_memory_space_constraint(array, pltpu.HBM)


def bf16(*shape):
    return jax.ShapeDtypeStruct(shape, jnp.bfloat16)


def visible():
    key = lax.broadcasted_iota(jnp.int32, (SPAN, KEYS_SEEN), 0)
    query = lax.broadcasted_iota(jnp.int32, (SPAN, KEYS_SEEN), 1)
    return (key > query) & (key <= query + KEYS_SEEN)


def attend_block(pairs, both, sinks, allowed):
    both = both.astype(jnp.float32)
    low = lax.broadcasted_iota(jnp.int32, both.shape, 1) < HEAD_SIZE
    turned = pltpu.roll(both, HEAD_SIZE, 1)
    keys = jnp.concatenate([jnp.where(low, both, 0.0), jnp.where(low, 0.0, turned)], axis=0)
    values = jnp.concatenate([jnp.where(low, turned, 0.0), jnp.where(low, 0.0, both)], axis=0)
    keys, values = keys.astype(jnp.bfloat16), values.astype(jnp.bfloat16)
    scores = dot(keys, jnp.concatenate(pairs, axis=0), NT) * (HEAD_SIZE**-0.5 * math.log2(math.e))
    allowed = jnp.concatenate([allowed] * len(pairs), axis=1)
    probs = []
    for i in range(2):
        sink = jnp.concatenate([sinks[2 * p + i] for p in range(len(pairs))], axis=1)
        part = jnp.where(allowed, scores[i * SPAN : (i + 1) * SPAN], -jnp.inf)
        peak = jnp.maximum(jnp.max(part, axis=0, keepdims=True), sink)
        terms = jnp.exp2(part - peak)
        denom = jnp.sum(terms, axis=0, keepdims=True) + jnp.exp2(sink - peak)
        probs.append((terms * (1.0 / denom)).astype(jnp.bfloat16))
    mixed = dot(values, jnp.concatenate(probs, axis=0), TN).astype(jnp.bfloat16)
    return [mixed[:, p * KEYS_SEEN : (p + 1) * KEYS_SEEN] for p in range(len(pairs))]


def attend_tokens(block, q_ref, rows_of, sinks, out_ref, lanes):
    groups = len(rows_of)
    per_group = q_ref.shape[1] // PAIR // groups
    allowed = visible()
    toks = slice(block * KEYS_SEEN, (block + 1) * KEYS_SEEN)
    for g, both in enumerate(rows_of):
        first = g * per_group
        pairs = [q_ref[toks, (first + p) * PAIR : (first + p + 1) * PAIR] for p in range(per_group)]
        outs = attend_block(pairs, both, sinks[2 * first : 2 * (first + per_group)], allowed)
        for p, out in enumerate(outs):
            out_ref[(first + p) * PAIR : (first + p + 1) * PAIR, lanes] = out


def fill_tables(live, ids, weights, placing_ref, mix_hi_ref, mix_lo_ref):
    toks = ids.shape[1]
    chosen = jnp.concatenate(
        [jnp.max((ids == e).astype(jnp.float32), axis=0, keepdims=True) for e in range(live)], axis=0
    )
    earlier = lax.broadcasted_iota(jnp.int32, (toks, toks), 0)
    later = lax.broadcasted_iota(jnp.int32, (toks, toks), 1)
    strict = (earlier < later).astype(jnp.bfloat16)
    before = dot(chosen.astype(jnp.bfloat16), strict, NN)
    slot = lax.broadcasted_iota(jnp.int32, (CAP, toks), 0).astype(jnp.float32)
    for e in range(live):
        weight = jnp.sum(jnp.where(ids == e, weights, 0.0), axis=0, keepdims=True)
        fills = (before[e : e + 1] == slot) & (chosen[e : e + 1] > 0.0)
        mix = jnp.where(fills, weight, 0.0)
        hi = mix.astype(jnp.bfloat16)
        rows = slice(e * CAP, (e + 1) * CAP)
        placing_ref[rows] = fills.astype(jnp.bfloat16)
        mix_hi_ref[rows] = hi
        mix_lo_ref[rows] = (mix - hi.astype(jnp.float32)).astype(jnp.bfloat16)


def first_kernel(live, *refs):
    loaded, held = refs[:8], refs[8:13]
    placing_ref, mix_hi_ref, mix_lo_ref, sinks_out, late_ref, ids_ref, weights_ref, sinks_ref, sems = refs[13:]
    targets = (ids_ref, weights_ref, sinks_ref, *held)
    copies = [pltpu.make_async_copy(*pair, sems.at[i]) for i, pair in enumerate(zip(loaded, targets))]
    for copy in copies:
        copy.start()
    q_ref, kv_ref = held[:2]
    for copy in copies[:2]:
        copy.wait()
    fill_tables(live, ids_ref[...], weights_ref[...], placing_ref, mix_hi_ref, mix_lo_ref)
    for copy in copies[2:5]:
        copy.wait()
    heads = sinks_ref.shape[0]
    sinks = [jnp.full((1, KEYS_SEEN), sinks_ref[h], jnp.float32) * math.log2(math.e) for h in range(heads)]
    sinks_out[...] = jnp.concatenate(sinks, axis=0)
    groups = kv_ref.shape[1] // PAIR
    for b in range(1, q_ref.shape[0] // KEYS_SEEN):
        span = slice((b - 1) * KEYS_SEEN, (b + 1) * KEYS_SEEN)
        rows_of = [kv_ref[span, g * PAIR : (g + 1) * PAIR] for g in range(groups)]
        attend_tokens(b, q_ref, rows_of, sinks, late_ref, slice((b - 1) * KEYS_SEEN, b * KEYS_SEEN))
    for copy in copies[5:]:
        copy.wait()


def second_kernel(q_ref, kv_ref, before_ref, rim_ref, sinks_ref, late_ref, placing_ref, all_ref, rows_ref):
    first = lax.axis_index("seq") == 0
    rim = jnp.where(first, before_ref[...], rim_ref[...])
    groups = kv_ref.shape[1] // PAIR
    rows_of = []
    for g in range(groups):
        lanes = slice(g * PAIR, (g + 1) * PAIR)
        rows_of.append(jnp.concatenate([rim[:, lanes], kv_ref[:KEYS_SEEN, lanes]], axis=0))
    sinks = [sinks_ref[h : h + 1] for h in range(sinks_ref.shape[0])]
    attend_tokens(0, q_ref, rows_of, sinks, all_ref, slice(0, KEYS_SEEN))
    all_ref[:, KEYS_SEEN:] = late_ref[...]
    rows_ref[...] = dot(placing_ref[...], all_ref[...], NT).astype(jnp.bfloat16)


def origin(k, sibling):
    me = lax.axis_index("cuts")
    return lax.bitwise_xor(me, CORES * k + (1 if sibling else 0))


def add_products(total, first, blocks, w_ref, steps, dims, swapped=False):
    width = blocks[0].shape[0 if swapped else 1] if blocks else 0
    for i, block in enumerate(blocks, first):
        at = pl.multiple_of(origin(i % steps, i >= steps) * width, 128)
        w = w_ref[:, pl.ds(at, width)]
        total += dot(w, block[...], dims) if swapped else dot(block[...], w, dims)
    return total


def rows_near_kernel(steps, mine_ref, theirs_ref, w_ref, residual_ref, placing_ref, total_ref):
    total = dot(placing_ref[...], residual_ref[...], NT)
    total = add_products(total, 0, [mine_ref], w_ref, steps, NT)
    total_ref[...] = add_products(total, steps, [theirs_ref], w_ref, steps, NT)


def rows_chips_kernel(steps, *refs):
    blocks, (before_ref, w_ref, total_ref) = refs[: steps - 1], refs[steps - 1 :]
    total_ref[...] = add_products(before_ref[...], 1, blocks, w_ref, steps, NT)


def rows_last_kernel(steps, *refs):
    blocks, (before_ref, w_ref) = refs[: steps - 1], refs[steps - 1 : steps + 1]
    outgoing, rows_ref = refs[steps + 1 : -1], refs[-1]
    total = add_products(before_ref[...], steps + 1, blocks, w_ref, steps, NT)
    rows_ref[...] = total.astype(jnp.bfloat16).reshape(rows_ref.shape)
    me = lax.axis_index("seq")
    for k, out_ref in enumerate(outgoing):
        out_ref[...] = rows_ref[lax.bitwise_xor(me, k)]


def stack_kernel(*refs):
    for i, block in enumerate(refs[:-1]):
        refs[-1][i * CAP : (i + 1) * CAP] = block[...]


def project_kernel(steps, *refs):
    blocks = refs[: 2 * steps]
    w_ref, residual_ref, resid_ref = refs[2 * steps :]
    total = add_products(residual_ref[...].astype(jnp.float32), 0, blocks, w_ref, steps, NN, True)
    resid_ref[...] = total.astype(jnp.bfloat16)


def expert_kernel(steps, *refs):
    cuts = CORES * steps
    gain_ref, gate_ref, up_ref, down_ref, kept_ref, given_ref, blocks_ref, rows_ref = refs[cuts:]
    width = refs[0].shape[1]
    for i in range(cuts):
        blocks_ref[origin(i % steps, i >= steps)] = refs[i][...]
    wide = [blocks_ref[p].astype(jnp.float32) for p in range(cuts)]
    squares = sum(jnp.sum(b * b, axis=1, keepdims=True) for b in wide)
    scale = lax.rsqrt(squares / (cuts * width) + norm_eps)
    gain = gain_ref[...].reshape(1, cuts * width)
    rows_ref[...] = (jnp.concatenate(wide, axis=1) * scale * gain).astype(jnp.bfloat16)
    rows = rows_ref[...]
    gate = dot(rows, gate_ref[...], NT)
    up = dot(rows, up_ref[...], NT)
    activated = ((up + 1.0) * gate * jax.nn.sigmoid(glu_alpha * gate)).astype(jnp.bfloat16)
    out = dot(activated, down_ref[...], NN).astype(jnp.bfloat16)
    for p in range(cuts):
        blocks_ref[p] = out[:, p * width : (p + 1) * width]
    for k in range(steps):
        kept_ref[k] = blocks_ref[origin(k, False)]
        given_ref[k] = blocks_ref[origin(k, True)]


def add_cores_kernel(kept_ref, given_ref, *out_refs):
    half = out_refs[0].shape[0]
    for i, out_ref in enumerate(out_refs):
        rows = slice(i % 2 * half, (i % 2 + 1) * half)
        total = kept_ref[i // 2, rows].astype(jnp.float32) + given_ref[i // 2, rows].astype(jnp.float32)
        out_ref[...] = total.astype(jnp.bfloat16)


def add_chips_kernel(steps, *refs):
    total = sum(r[...].astype(jnp.float32) for r in refs[:steps])
    for k, out_ref in enumerate(refs[steps:]):
        out_ref[...] = total[k * CAP : (k + 1) * CAP].astype(jnp.bfloat16)


def combine_kernel(live, *refs):
    blocks = refs[:live]
    mix_hi_ref, mix_lo_ref, resid_ref, out_ref, rows_ref = refs[live:]
    me = lax.axis_index("seq")
    for k in range(live):
        rows_ref[lax.bitwise_xor(me, live - 1 - k)] = blocks[k][...]
    rows = rows_ref[...].reshape(live * CAP, -1)
    mixed = dot(rows, mix_hi_ref[...], TN) + dot(rows, mix_lo_ref[...], TN)
    out_ref[...] = (resid_ref[...].astype(jnp.float32) + mixed).astype(jnp.bfloat16)


def swap(block, axis, mask):
    return lax.ppermute(block, axis, [(i, i ^ mask) for i in range(lax.axis_size(axis))])


def gather_cuts(block):
    steps = lax.axis_size("cuts") // CORES
    mine = [block] + [swap(block, "cuts", CORES * k) for k in range(1, steps)]
    return mine, [swap(b, "cuts", 1) for b in mine]


def shards(
    queries,
    keyvals,
    preceding_keyvalues,
    attention_sink_logits,
    residual,
    w_out,
    norm_gain,
    expert_ids,
    route_weights,
    w_gate,
    w_up,
    w_down,
):
    toks, feats = residual.shape
    size = lax.axis_size("seq")
    live = w_gate.shape[0] * size
    cuts = lax.axis_size("cuts")
    steps = cuts // CORES
    slots = live * CAP
    head_rows = queries.shape[1]
    heads = head_rows // HEAD_SIZE
    width = norm_gain.shape[0]

    tail = keyvals[toks - KEYS_SEEN :]
    rim = lax.ppermute(tail, "seq", [(i, (i + 1) % size) for i in range(size)])
    loads = (queries, keyvals, preceding_keyvalues, w_out.T, residual.T)
    q, kv, before, w_t, residual_t, placing, mix_hi, mix_lo, sinks, late = call(
        functools.partial(first_kernel, live),
        (
            *(bf16(*a.shape) for a in loads),
            *(bf16(slots, toks),) * 3,
            jax.ShapeDtypeStruct((heads, KEYS_SEEN), jnp.float32),
            bf16(head_rows, toks - KEYS_SEEN),
        ),
        n_in=8,
        scratch=[
            pltpu.VMEM(expert_ids.T.shape, jnp.int32),
            pltpu.VMEM(expert_ids.T.shape, jnp.float32),
            pltpu.SMEM(attention_sink_logits.shape, jnp.float32),
            pltpu.SemaphoreType.DMA((8,)),
        ],
        hbm=range(8),
        flops=4 * toks * SPAN * head_rows,
        moved=2 * (w_out.size + residual.size + queries.size),
    )(*(in_hbm(a) for a in (expert_ids.T, route_weights.T, attention_sink_logits, *loads)))
    attended, rows = call(
        second_kernel,
        (bf16(head_rows, toks), bf16(slots, head_rows)),
        n_in=7,
        flops=2 * toks * SPAN * head_rows,
        moved=2 * queries.size,
    )(q, kv, before, rim, sinks, late, placing)

    mine, theirs = gather_cuts(rows)
    total = jax.ShapeDtypeStruct((slots, feats), jnp.float32)
    part = dict(flops=slots * w_out.size // 2, moved=w_out.size // 2)
    near = call(functools.partial(rows_near_kernel, steps), total, n_in=5, **part)(
        mine[0], theirs[0], w_t, residual_t, placing
    )
    chips = call(functools.partial(rows_chips_kernel, steps), total, n_in=steps + 1, **part)(
        *mine[1:], near, w_t
    )
    outgoing = call(
        functools.partial(rows_last_kernel, steps),
        (bf16(CAP, feats),) * live,
        n_in=steps + 1,
        scratch=[pltpu.VMEM((live, CAP, feats), jnp.bfloat16)],
        **part,
    )(*theirs[1:], chips, w_t)

    arrived = [swap(outgoing[k], "seq", k) for k in range(live - 1, 0, -1)] + [outgoing[0]]
    stacked = call(stack_kernel, bf16(slots, feats), n_in=live)(*arrived)
    expert_mine, expert_theirs = gather_cuts(stacked)

    attended, _ = lax.optimization_barrier((attended, arrived[0]))
    mine, theirs = gather_cuts(attended)
    resid = call(
        functools.partial(project_kernel, steps),
        bf16(feats, toks),
        n_in=cuts + 2,
        flops=2 * toks * w_out.size,
        moved=2 * w_out.size,
    )(*mine, *theirs, w_t, residual_t)

    kept, given = call(
        functools.partial(expert_kernel, steps),
        (bf16(steps, slots, feats),) * 2,
        n_in=cuts + 4,
        scratch=[
            pltpu.VMEM((cuts, slots, feats), jnp.bfloat16),
            pltpu.VMEM((slots, width), jnp.bfloat16),
        ],
        flops=6 * slots * w_gate.size,
        moved=6 * w_gate.size,
    )(*expert_mine, *expert_theirs, norm_gain, w_gate[0].T, w_up[0].T, w_down[0])
    sums = call(add_cores_kernel, (bf16(slots // 2, feats),) * (2 * steps), n_in=2)(
        kept, swap(given, "cuts", 1)
    )
    returned = []
    for half in range(2):
        parts = [sums[half]] + [swap(sums[2 * k + half], "cuts", CORES * k) for k in range(1, steps)]
        blocks = call(functools.partial(add_chips_kernel, steps), (bf16(CAP, feats),) * (live // 2), n_in=steps)(
            *parts
        )
        for block in blocks:
            k = live - 1 - len(returned)
            returned.append(swap(block, "seq", k) if k else block)
    out = call(
        functools.partial(combine_kernel, live),
        bf16(feats, toks),
        n_in=live + 3,
        scratch=[pltpu.VMEM((live, CAP, feats), jnp.bfloat16)],
    )(*returned, mix_hi, mix_lo, resid)
    return out.T


def solution(mesh):
    placed = (
        P(("groups", "seq"), "cuts"),
        P(("groups", "seq"), "cuts"),
        P("groups", "cuts"),
        P("cuts"),
        P(("groups", "seq"), "cuts"),
        P(None, "cuts"),
        P(),
        P(("groups", "seq"), None),
        P(("groups", "seq"), None),
        P("seq", None, "cuts"),
        P("seq", None, "cuts"),
        P("seq", "cuts", None),
    )
    return jax.shard_map(
        shards, mesh=mesh, in_specs=placed, out_specs=P(("groups", "seq"), "cuts"), check_vma=False
    )
```

```python
import functools
import math

import jax
import jax.numpy as jnp
from jax import lax
from jax.experimental import pallas as pl
from jax.experimental.pallas import tpu as pltpu
from jax.sharding import PartitionSpec as P

HEAD_SIZE = 64
KEYS_SEEN = 128
PAIR = 2 * HEAD_SIZE
SPAN = 2 * KEYS_SEEN
CAP = 16
CORES = 2

norm_eps = 1e-05
glu_alpha = 1.702

NT = (((1,), (1,)), ((), ()))
NN = (((1,), (0,)), ((), ()))
TN = (((0,), (0,)), ((), ()))
VMEM_LIMIT = 32 * 1024 * 1024


def dot(a, b, dims):
    return lax.dot_general(a, b, dims, preferred_element_type=jnp.float32)


def call(kernel, outs, n_in, scratch=(), hbm=(), smem=(), flops=0, moved=0):
    spaces = [pltpu.HBM if i in hbm else pltpu.SMEM if i in smem else pltpu.VMEM for i in range(n_in)]
    return pl.pallas_call(
        kernel,
        out_shape=outs,
        in_specs=[pl.BlockSpec(memory_space=space) for space in spaces],
        out_specs=jax.tree.map(lambda _: pl.BlockSpec(memory_space=pltpu.VMEM), outs),
        scratch_shapes=list(scratch),
        compiler_params=pltpu.CompilerParams(vmem_limit_bytes=VMEM_LIMIT),
        cost_estimate=pl.CostEstimate(flops=flops, bytes_accessed=moved, transcendentals=0),
    )


def in_hbm(array):
    return pltpu.with_memory_space_constraint(array, pltpu.HBM)


def bf16(*shape):
    return jax.ShapeDtypeStruct(shape, jnp.bfloat16)


def visible():
    key = lax.broadcasted_iota(jnp.int32, (SPAN, KEYS_SEEN), 0)
    query = lax.broadcasted_iota(jnp.int32, (SPAN, KEYS_SEEN), 1)
    return (key > query) & (key <= query + KEYS_SEEN)


def attend_block(pairs, both, sinks, allowed):
    both = both.astype(jnp.float32)
    low = lax.broadcasted_iota(jnp.int32, both.shape, 1) < HEAD_SIZE
    turned = pltpu.roll(both, HEAD_SIZE, 1)
    keys = jnp.concatenate([jnp.where(low, both, 0.0), jnp.where(low, 0.0, turned)], axis=0)
    values = jnp.concatenate([jnp.where(low, turned, 0.0), jnp.where(low, 0.0, both)], axis=0)
    keys, values = keys.astype(jnp.bfloat16), values.astype(jnp.bfloat16)
    scores = dot(keys, jnp.concatenate(pairs, axis=0), NT) * (HEAD_SIZE**-0.5 * math.log2(math.e))
    allowed = jnp.concatenate([allowed] * len(pairs), axis=1)
    probs = []
    for i in range(2):
        sink = jnp.concatenate([sinks[2 * p + i] for p in range(len(pairs))], axis=1)
        part = jnp.where(allowed, scores[i * SPAN : (i + 1) * SPAN], -jnp.inf)
        peak = jnp.maximum(jnp.max(part, axis=0, keepdims=True), sink)
        terms = jnp.exp2(part - peak)
        denom = jnp.sum(terms, axis=0, keepdims=True) + jnp.exp2(sink - peak)
        probs.append((terms * (1.0 / denom)).astype(jnp.bfloat16))
    mixed = dot(values, jnp.concatenate(probs, axis=0), TN).astype(jnp.bfloat16)
    return [mixed[:, p * KEYS_SEEN : (p + 1) * KEYS_SEEN] for p in range(len(pairs))]


def attend_tokens(block, q_ref, rows_of, sinks, out_ref, lanes):
    groups = len(rows_of)
    per_group = q_ref.shape[1] // PAIR // groups
    allowed = visible()
    toks = slice(block * KEYS_SEEN, (block + 1) * KEYS_SEEN)
    for g, both in enumerate(rows_of):
        first = g * per_group
        pairs = [q_ref[toks, (first + p) * PAIR : (first + p + 1) * PAIR] for p in range(per_group)]
        outs = attend_block(pairs, both, sinks[2 * first : 2 * (first + per_group)], allowed)
        for p, out in enumerate(outs):
            out_ref[(first + p) * PAIR : (first + p + 1) * PAIR, lanes] = out


def fill_tables(live, ids, weights, placing_ref, mix_hi_ref, mix_lo_ref):
    toks = ids.shape[1]
    chosen = jnp.concatenate(
        [jnp.max((ids == e).astype(jnp.float32), axis=0, keepdims=True) for e in range(live)], axis=0
    )
    earlier = lax.broadcasted_iota(jnp.int32, (toks, toks), 0)
    later = lax.broadcasted_iota(jnp.int32, (toks, toks), 1)
    strict = (earlier < later).astype(jnp.bfloat16)
    before = dot(chosen.astype(jnp.bfloat16), strict, NN)
    slot = lax.broadcasted_iota(jnp.int32, (CAP, toks), 0).astype(jnp.float32)
    for e in range(live):
        weight = jnp.sum(jnp.where(ids == e, weights, 0.0), axis=0, keepdims=True)
        fills = (before[e : e + 1] == slot) & (chosen[e : e + 1] > 0.0)
        mix = jnp.where(fills, weight, 0.0)
        hi = mix.astype(jnp.bfloat16)
        rows = slice(e * CAP, (e + 1) * CAP)
        placing_ref[rows] = fills.astype(jnp.bfloat16)
        mix_hi_ref[rows] = hi
        mix_lo_ref[rows] = (mix - hi.astype(jnp.float32)).astype(jnp.bfloat16)


def first_kernel(live, *refs):
    loaded, held = refs[:8], refs[8:13]
    placing_ref, mix_hi_ref, mix_lo_ref, sinks_out, late_ref, ids_ref, weights_ref, sinks_ref, sems = refs[13:]
    targets = (ids_ref, weights_ref, sinks_ref, *held)
    copies = [pltpu.make_async_copy(*pair, sems.at[i]) for i, pair in enumerate(zip(loaded, targets))]
    for copy in copies:
        copy.start()
    q_ref, kv_ref = held[:2]
    for copy in copies[:2]:
        copy.wait()
    fill_tables(live, ids_ref[...], weights_ref[...], placing_ref, mix_hi_ref, mix_lo_ref)
    for copy in copies[2:5]:
        copy.wait()
    heads = sinks_ref.shape[0]
    sinks = [jnp.full((1, KEYS_SEEN), sinks_ref[h], jnp.float32) * math.log2(math.e) for h in range(heads)]
    sinks_out[...] = jnp.concatenate(sinks, axis=0)
    groups = kv_ref.shape[1] // PAIR
    for b in range(1, q_ref.shape[0] // KEYS_SEEN):
        span = slice((b - 1) * KEYS_SEEN, (b + 1) * KEYS_SEEN)
        rows_of = [kv_ref[span, g * PAIR : (g + 1) * PAIR] for g in range(groups)]
        attend_tokens(b, q_ref, rows_of, sinks, late_ref, slice((b - 1) * KEYS_SEEN, b * KEYS_SEEN))
    for copy in copies[5:]:
        copy.wait()


def second_kernel(q_ref, kv_ref, before_ref, rim_ref, sinks_ref, late_ref, placing_ref, all_ref, rows_ref):
    first = lax.axis_index("seq") == 0
    rim = jnp.where(first, before_ref[...], rim_ref[...])
    groups = kv_ref.shape[1] // PAIR
    rows_of = []
    for g in range(groups):
        lanes = slice(g * PAIR, (g + 1) * PAIR)
        rows_of.append(jnp.concatenate([rim[:, lanes], kv_ref[:KEYS_SEEN, lanes]], axis=0))
    sinks = [sinks_ref[h : h + 1] for h in range(sinks_ref.shape[0])]
    attend_tokens(0, q_ref, rows_of, sinks, all_ref, slice(0, KEYS_SEEN))
    all_ref[:, KEYS_SEEN:] = late_ref[...]
    rows_ref[...] = dot(placing_ref[...], all_ref[...], NT).astype(jnp.bfloat16)


def origin(k, sibling):
    me = lax.axis_index("cuts")
    return lax.bitwise_xor(me, CORES * k + (1 if sibling else 0))


def add_products(total, first, blocks, w_ref, steps, dims, swapped=False):
    width = blocks[0].shape[0 if swapped else 1] if blocks else 0
    for i, block in enumerate(blocks, first):
        at = pl.multiple_of(origin(i % steps, i >= steps) * width, 128)
        w = w_ref[:, pl.ds(at, width)]
        total += dot(w, block[...], dims) if swapped else dot(block[...], w, dims)
    return total


def rows_near_kernel(steps, mine_ref, theirs_ref, w_ref, residual_ref, placing_ref, total_ref):
    total = dot(placing_ref[...], residual_ref[...], NT)
    total = add_products(total, 0, [mine_ref], w_ref, steps, NT)
    total_ref[...] = add_products(total, steps, [theirs_ref], w_ref, steps, NT)


def rows_chips_kernel(steps, *refs):
    blocks, (before_ref, w_ref, total_ref) = refs[: steps - 1], refs[steps - 1 :]
    total_ref[...] = add_products(before_ref[...], 1, blocks, w_ref, steps, NT)


def rows_last_kernel(steps, *refs):
    blocks, (before_ref, w_ref) = refs[: steps - 1], refs[steps - 1 : steps + 1]
    outgoing, rows_ref = refs[steps + 1 : -1], refs[-1]
    total = add_products(before_ref[...], steps + 1, blocks, w_ref, steps, NT)
    rows_ref[...] = total.astype(jnp.bfloat16).reshape(rows_ref.shape)
    me = lax.axis_index("seq")
    for k, out_ref in enumerate(outgoing):
        out_ref[...] = rows_ref[lax.bitwise_xor(me, k)]


def stack_kernel(*refs):
    for i, block in enumerate(refs[:-1]):
        refs[-1][i * CAP : (i + 1) * CAP] = block[...]


def project_kernel(steps, *refs):
    blocks = refs[: 2 * steps]
    w_ref, residual_ref, resid_ref = refs[2 * steps :]
    total = add_products(residual_ref[...].astype(jnp.float32), 0, blocks, w_ref, steps, NN, True)
    resid_ref[...] = total.astype(jnp.bfloat16)


def weights_kernel(gate_ref, up_ref, down_ref, gain_ref, gates_ref, ups_ref, downs_ref, gains_ref, *scratch):
    held, sems = scratch[:3], scratch[3]
    copies = [
        pltpu.make_async_copy(source, target, sems.at[i])
        for i, (source, target) in enumerate(zip((gate_ref, up_ref, down_ref), held))
    ]
    for copy in copies:
        copy.start()
    cuts, _, width = gates_ref.shape
    gain = gain_ref[...].reshape(1, cuts * width)
    for p in range(cuts):
        gains_ref[p] = gain[:, p * width : (p + 1) * width]
    for copy, source, target in zip(copies, held, (gates_ref, ups_ref, downs_ref)):
        copy.wait()
        for p in range(cuts):
            target[p] = source[:, p * width : (p + 1) * width]


def add_features(sums, first, blocks, gains_ref, gates_ref, ups_ref, steps):
    gate, up, squares = sums
    for i, block in enumerate(blocks, first):
        p = origin(i % steps, i >= steps)
        wide = block[...].astype(jnp.float32)
        squares += jnp.sum(wide * wide, axis=1, keepdims=True)
        rows = (wide * gains_ref[p]).astype(jnp.bfloat16)
        gate += dot(rows, gates_ref[p], NT)
        up += dot(rows, ups_ref[p], NT)
    return gate, up, squares


def store_sums(sums, refs):
    for ref, value in zip(refs, sums):
        ref[...] = jnp.broadcast_to(value, ref.shape)


def expert_near_kernel(steps, mine_ref, theirs_ref, gains_ref, gates_ref, ups_ref, *out_refs):
    zeros = jnp.zeros(out_refs[0].shape, jnp.float32)
    sums = (zeros, zeros, jnp.zeros((zeros.shape[0], 1), jnp.float32))
    for first, block in ((0, mine_ref), (steps, theirs_ref)):
        sums = add_features(sums, first, [block], gains_ref, gates_ref, ups_ref, steps)
    store_sums(sums, out_refs)


def expert_chips_kernel(steps, *refs):
    blocks, refs = refs[: steps - 1], refs[steps - 1 :]
    sums = (refs[0][...], refs[1][...], refs[2][:, :1])
    store_sums(add_features(sums, 1, blocks, *refs[3:6], steps), refs[6:])


def expert_last_kernel(steps, *refs):
    blocks, refs = refs[: steps - 1], refs[steps - 1 :]
    sums = (refs[0][...], refs[1][...], refs[2][:, :1])
    gains_ref, gates_ref, ups_ref, downs_ref, given_ref, activated_ref = refs[3:]
    gate, up, squares = add_features(sums, steps + 1, blocks, gains_ref, gates_ref, ups_ref, steps)
    cuts, _, width = gates_ref.shape
    scale = lax.rsqrt(squares / (cuts * width) + norm_eps)
    gate, up = gate * scale, up * scale
    activated = ((up + 1.0) * gate * jax.nn.sigmoid(glu_alpha * gate)).astype(jnp.bfloat16)
    activated_ref[...] = activated
    for k in range(steps):
        given_ref[k] = dot(activated, downs_ref[origin(k, True)], NN).astype(jnp.bfloat16)


def expert_kept_kernel(activated_ref, downs_ref, kept_ref):
    for k in range(kept_ref.shape[0]):
        kept_ref[k] = dot(activated_ref[...], downs_ref[origin(k, False)], NN).astype(jnp.bfloat16)


def add_cores_kernel(kept_ref, given_ref, *out_refs):
    half = out_refs[0].shape[0]
    for i, out_ref in enumerate(out_refs):
        rows = slice(i % 2 * half, (i % 2 + 1) * half)
        total = kept_ref[i // 2, rows].astype(jnp.float32) + given_ref[i // 2, rows].astype(jnp.float32)
        out_ref[...] = total.astype(jnp.bfloat16)


def add_chips_kernel(steps, *refs):
    total = sum(r[...].astype(jnp.float32) for r in refs[:steps])
    for k, out_ref in enumerate(refs[steps:]):
        out_ref[...] = total[k * CAP : (k + 1) * CAP].astype(jnp.bfloat16)


def combine_kernel(live, *refs):
    blocks = refs[:live]
    mix_hi_ref, mix_lo_ref, resid_ref, out_ref, rows_ref = refs[live:]
    me = lax.axis_index("seq")
    for k in range(live):
        rows_ref[lax.bitwise_xor(me, live - 1 - k)] = blocks[k][...]
    rows = rows_ref[...].reshape(live * CAP, -1)
    mixed = dot(rows, mix_hi_ref[...], TN) + dot(rows, mix_lo_ref[...], TN)
    out_ref[...] = (resid_ref[...].astype(jnp.float32) + mixed).astype(jnp.bfloat16)


def swap(block, axis, mask):
    return lax.ppermute(block, axis, [(i, i ^ mask) for i in range(lax.axis_size(axis))])


def from_chips(block):
    return [swap(block, "cuts", CORES * k) for k in range(1, lax.axis_size("cuts") // CORES)]


def from_sibling(block):
    return swap(block, "cuts", 1)


def after(arrays, others):
    return lax.optimization_barrier((arrays, others))[0]


def shards(
    queries,
    keyvals,
    preceding_keyvalues,
    attention_sink_logits,
    residual,
    w_out,
    norm_gain,
    expert_ids,
    route_weights,
    w_gate,
    w_up,
    w_down,
):
    toks, feats = residual.shape
    size = lax.axis_size("seq")
    live = w_gate.shape[0] * size
    cuts = lax.axis_size("cuts")
    steps = cuts // CORES
    slots = live * CAP
    head_rows = queries.shape[1]
    heads = head_rows // HEAD_SIZE
    width = norm_gain.shape[0]
    hidden = w_gate.shape[2]

    tail = keyvals[toks - KEYS_SEEN :]
    rim = lax.ppermute(tail, "seq", [(i, (i + 1) % size) for i in range(size)])
    loads = (queries, keyvals, preceding_keyvalues, w_out.T, residual.T)
    q, kv, before, w_t, residual_t, placing, mix_hi, mix_lo, sinks, late = call(
        functools.partial(first_kernel, live),
        (
            *(bf16(*a.shape) for a in loads),
            *(bf16(slots, toks),) * 3,
            jax.ShapeDtypeStruct((heads, KEYS_SEEN), jnp.float32),
            bf16(head_rows, toks - KEYS_SEEN),
        ),
        n_in=8,
        scratch=[
            pltpu.VMEM(expert_ids.T.shape, jnp.int32),
            pltpu.VMEM(expert_ids.T.shape, jnp.float32),
            pltpu.SMEM(attention_sink_logits.shape, jnp.float32),
            pltpu.SemaphoreType.DMA((8,)),
        ],
        hbm=range(8),
        flops=4 * toks * SPAN * head_rows,
        moved=2 * (w_out.size + residual.size + queries.size),
    )(*(in_hbm(a) for a in (expert_ids.T, route_weights.T, attention_sink_logits, *loads)))
    attended, rows = call(
        second_kernel,
        (bf16(head_rows, toks), bf16(slots, head_rows)),
        n_in=7,
        flops=2 * toks * SPAN * head_rows,
        moved=2 * queries.size,
    )(q, kv, before, rim, sinks, late, placing)

    chip_rows = from_chips(rows)
    sibling_rows = from_sibling(rows)
    total = jax.ShapeDtypeStruct((slots, feats), jnp.float32)
    part = dict(flops=slots * w_out.size // 2, moved=w_out.size // 2)
    near = call(functools.partial(rows_near_kernel, steps), total, n_in=5, **part)(
        rows, sibling_rows, w_t, residual_t, placing
    )
    chip_rows = after(chip_rows, near)
    relayed_rows = [from_sibling(b) for b in chip_rows]
    chips = call(functools.partial(rows_chips_kernel, steps), total, n_in=steps + 1, **part)(
        *chip_rows, near, w_t
    )
    outgoing = call(
        functools.partial(rows_last_kernel, steps),
        (bf16(CAP, feats),) * live,
        n_in=steps + 1,
        scratch=[pltpu.VMEM((live, CAP, feats), jnp.bfloat16)],
        **part,
    )(*relayed_rows, chips, w_t)

    arrived = [swap(outgoing[k], "seq", k) for k in range(live - 1, 0, -1)] + [outgoing[0]]

    w_gate_t, w_up_t, w_down_t, _ = lax.optimization_barrier((w_gate[0].T, w_up[0].T, w_down[0], outgoing[0]))
    weights = call(
        weights_kernel,
        (*(bf16(cuts, hidden, feats),) * 3, jax.ShapeDtypeStruct((cuts, 1, feats), jnp.float32)),
        n_in=4,
        hbm=range(3),
        scratch=[*(pltpu.VMEM((hidden, width), jnp.bfloat16),) * 3, pltpu.SemaphoreType.DMA((3,))],
        moved=6 * w_gate.size,
    )(in_hbm(w_gate_t), in_hbm(w_up_t), in_hbm(w_down_t), norm_gain)
    gates, ups, downs, gains = weights
    sums = (
        *(jax.ShapeDtypeStruct((slots, hidden), jnp.float32),) * 2,
        jax.ShapeDtypeStruct((slots, KEYS_SEEN), jnp.float32),
    )
    part = dict(flops=slots * w_gate.size, moved=w_gate.size)
    stacked = call(stack_kernel, bf16(slots, feats), n_in=live)(*after(arrived, gains))
    chip_rows = from_chips(stacked)
    near = call(functools.partial(expert_near_kernel, steps), sums, n_in=5, **part)(
        stacked, from_sibling(stacked), gains, gates, ups
    )
    chip_rows = after(chip_rows, near)
    relayed_rows = [from_sibling(b) for b in chip_rows]
    chips = call(functools.partial(expert_chips_kernel, steps), sums, n_in=steps + 5, **part)(
        *chip_rows, *near, gains, gates, ups
    )
    given, activated = call(
        functools.partial(expert_last_kernel, steps),
        (bf16(steps, slots, feats), bf16(slots, hidden)),
        n_in=steps + 6,
        **part,
    )(*relayed_rows, *chips, gains, gates, ups, downs)
    kept = call(expert_kept_kernel, bf16(steps, slots, feats), n_in=2, **part)(activated, downs)
    chip_blocks = from_chips(attended)
    blocks = [attended, *chip_blocks, *(from_sibling(b) for b in (attended, *chip_blocks))]
    resid = call(
        functools.partial(project_kernel, steps),
        bf16(feats, toks),
        n_in=cuts + 2,
        flops=2 * toks * w_out.size,
        moved=2 * w_out.size,
    )(*blocks, w_t, residual_t)

    sums = call(add_cores_kernel, (bf16(slots // 2, feats),) * (2 * steps), n_in=2)(
        kept, swap(given, "cuts", 1)
    )
    returned = []
    for half in range(2):
        parts = [sums[half]] + [swap(sums[2 * k + half], "cuts", CORES * k) for k in range(1, steps)]
        blocks = call(functools.partial(add_chips_kernel, steps), (bf16(CAP, feats),) * (live // 2), n_in=steps)(
            *parts
        )
        for block in blocks:
            k = live - 1 - len(returned)
            returned.append(swap(block, "seq", k) if k else block)
    out = call(
        functools.partial(combine_kernel, live),
        bf16(feats, toks),
        n_in=live + 3,
        scratch=[pltpu.VMEM((live, CAP, feats), jnp.bfloat16)],
    )(*returned, mix_hi, mix_lo, resid)
    return out.T


def solution(mesh):
    placed = (
        P(("groups", "seq"), "cuts"),
        P(("groups", "seq"), "cuts"),
        P("groups", "cuts"),
        P("cuts"),
        P(("groups", "seq"), "cuts"),
        P(None, "cuts"),
        P(),
        P(("groups", "seq"), None),
        P(("groups", "seq"), None),
        P("seq", None, "cuts"),
        P("seq", None, "cuts"),
        P("seq", "cuts", None),
    )
    return jax.shard_map(
        shards, mesh=mesh, in_specs=placed, out_specs=P(("groups", "seq"), "cuts"), check_vma=False
    )
```

```python
import functools
import math

import jax
import jax.numpy as jnp
from jax import lax
from jax.experimental import pallas as pl
from jax.experimental.pallas import tpu as pltpu
from jax.sharding import PartitionSpec as P

HEAD_SIZE = 64
KEYS_SEEN = 128
PAIR = 2 * HEAD_SIZE
SPAN = 2 * KEYS_SEEN
CAP = 16
CORES = 2

norm_eps = 1e-05
glu_alpha = 1.702

NT = (((1,), (1,)), ((), ()))
NN = (((1,), (0,)), ((), ()))
TN = (((0,), (0,)), ((), ()))
VMEM_LIMIT = 32 * 1024 * 1024


def dot(a, b, dims):
    return lax.dot_general(a, b, dims, preferred_element_type=jnp.float32)


def call(kernel, outs, n_in, scratch=(), hbm=(), smem=(), flops=0, moved=0):
    spaces = [pltpu.HBM if i in hbm else pltpu.SMEM if i in smem else pltpu.VMEM for i in range(n_in)]
    return pl.pallas_call(
        kernel,
        out_shape=outs,
        in_specs=[pl.BlockSpec(memory_space=space) for space in spaces],
        out_specs=jax.tree.map(lambda _: pl.BlockSpec(memory_space=pltpu.VMEM), outs),
        scratch_shapes=list(scratch),
        compiler_params=pltpu.CompilerParams(vmem_limit_bytes=VMEM_LIMIT),
        cost_estimate=pl.CostEstimate(flops=flops, bytes_accessed=moved, transcendentals=0),
    )


def in_hbm(array):
    return pltpu.with_memory_space_constraint(array, pltpu.HBM)


def bf16(*shape):
    return jax.ShapeDtypeStruct(shape, jnp.bfloat16)


def visible():
    key = lax.broadcasted_iota(jnp.int32, (SPAN, KEYS_SEEN), 0)
    query = lax.broadcasted_iota(jnp.int32, (SPAN, KEYS_SEEN), 1)
    return (key > query) & (key <= query + KEYS_SEEN)


def attend_block(pairs, both, sinks, allowed):
    both = both.astype(jnp.float32)
    low = lax.broadcasted_iota(jnp.int32, both.shape, 1) < HEAD_SIZE
    turned = pltpu.roll(both, HEAD_SIZE, 1)
    keys = jnp.concatenate([jnp.where(low, both, 0.0), jnp.where(low, 0.0, turned)], axis=0)
    values = jnp.concatenate([jnp.where(low, turned, 0.0), jnp.where(low, 0.0, both)], axis=0)
    keys, values = keys.astype(jnp.bfloat16), values.astype(jnp.bfloat16)
    scores = dot(keys, jnp.concatenate(pairs, axis=0), NT) * (HEAD_SIZE**-0.5 * math.log2(math.e))
    allowed = jnp.concatenate([allowed] * len(pairs), axis=1)
    probs = []
    for i in range(2):
        sink = jnp.concatenate([sinks[2 * p + i] for p in range(len(pairs))], axis=1)
        part = jnp.where(allowed, scores[i * SPAN : (i + 1) * SPAN], -jnp.inf)
        peak = jnp.maximum(jnp.max(part, axis=0, keepdims=True), sink)
        terms = jnp.exp2(part - peak)
        denom = jnp.sum(terms, axis=0, keepdims=True) + jnp.exp2(sink - peak)
        probs.append((terms * (1.0 / denom)).astype(jnp.bfloat16))
    mixed = dot(values, jnp.concatenate(probs, axis=0), TN).astype(jnp.bfloat16)
    return [mixed[:, p * KEYS_SEEN : (p + 1) * KEYS_SEEN] for p in range(len(pairs))]


def attend_tokens(block, q_ref, rows_of, sinks, out_ref, lanes):
    groups = len(rows_of)
    per_group = q_ref.shape[1] // PAIR // groups
    allowed = visible()
    toks = slice(block * KEYS_SEEN, (block + 1) * KEYS_SEEN)
    for g, both in enumerate(rows_of):
        first = g * per_group
        pairs = [q_ref[toks, (first + p) * PAIR : (first + p + 1) * PAIR] for p in range(per_group)]
        outs = attend_block(pairs, both, sinks[2 * first : 2 * (first + per_group)], allowed)
        for p, out in enumerate(outs):
            out_ref[(first + p) * PAIR : (first + p + 1) * PAIR, lanes] = out


def fill_tables(live, ids, weights, placing_ref, mix_hi_ref, mix_lo_ref):
    toks = ids.shape[1]
    chosen = jnp.concatenate(
        [jnp.max((ids == e).astype(jnp.float32), axis=0, keepdims=True) for e in range(live)], axis=0
    )
    earlier = lax.broadcasted_iota(jnp.int32, (toks, toks), 0)
    later = lax.broadcasted_iota(jnp.int32, (toks, toks), 1)
    strict = (earlier < later).astype(jnp.bfloat16)
    before = dot(chosen.astype(jnp.bfloat16), strict, NN)
    slot = lax.broadcasted_iota(jnp.int32, (CAP, toks), 0).astype(jnp.float32)
    for e in range(live):
        weight = jnp.sum(jnp.where(ids == e, weights, 0.0), axis=0, keepdims=True)
        fills = (before[e : e + 1] == slot) & (chosen[e : e + 1] > 0.0)
        mix = jnp.where(fills, weight, 0.0)
        hi = mix.astype(jnp.bfloat16)
        rows = slice(e * CAP, (e + 1) * CAP)
        placing_ref[rows] = fills.astype(jnp.bfloat16)
        mix_hi_ref[rows] = hi
        mix_lo_ref[rows] = (mix - hi.astype(jnp.float32)).astype(jnp.bfloat16)


def first_kernel(live, *refs):
    loaded, held = refs[:8], refs[8:13]
    placing_ref, mix_hi_ref, mix_lo_ref, sinks_out, late_ref, ids_ref, weights_ref, sinks_ref, sems = refs[13:]
    targets = (ids_ref, weights_ref, sinks_ref, *held)
    copies = [pltpu.make_async_copy(*pair, sems.at[i]) for i, pair in enumerate(zip(loaded, targets))]
    for copy in copies:
        copy.start()
    q_ref, kv_ref = held[:2]
    for copy in copies[:2]:
        copy.wait()
    fill_tables(live, ids_ref[...], weights_ref[...], placing_ref, mix_hi_ref, mix_lo_ref)
    for copy in copies[2:5]:
        copy.wait()
    heads = sinks_ref.shape[0]
    sinks = [jnp.full((1, KEYS_SEEN), sinks_ref[h], jnp.float32) * math.log2(math.e) for h in range(heads)]
    sinks_out[...] = jnp.concatenate(sinks, axis=0)
    groups = kv_ref.shape[1] // PAIR
    for b in range(1, q_ref.shape[0] // KEYS_SEEN):
        span = slice((b - 1) * KEYS_SEEN, (b + 1) * KEYS_SEEN)
        rows_of = [kv_ref[span, g * PAIR : (g + 1) * PAIR] for g in range(groups)]
        attend_tokens(b, q_ref, rows_of, sinks, late_ref, slice((b - 1) * KEYS_SEEN, b * KEYS_SEEN))
    for copy in copies[5:]:
        copy.wait()


def second_kernel(q_ref, kv_ref, before_ref, rim_ref, sinks_ref, late_ref, placing_ref, all_ref, rows_ref):
    first = lax.axis_index("seq") == 0
    rim = jnp.where(first, before_ref[...], rim_ref[...])
    groups = kv_ref.shape[1] // PAIR
    rows_of = []
    for g in range(groups):
        lanes = slice(g * PAIR, (g + 1) * PAIR)
        rows_of.append(jnp.concatenate([rim[:, lanes], kv_ref[:KEYS_SEEN, lanes]], axis=0))
    sinks = [sinks_ref[h : h + 1] for h in range(sinks_ref.shape[0])]
    attend_tokens(0, q_ref, rows_of, sinks, all_ref, slice(0, KEYS_SEEN))
    all_ref[:, KEYS_SEEN:] = late_ref[...]
    rows_ref[...] = dot(placing_ref[...], all_ref[...], NT).astype(jnp.bfloat16)


def origin(k, sibling):
    me = lax.axis_index("cuts")
    return lax.bitwise_xor(me, CORES * k + (1 if sibling else 0))


def add_products(total, places, blocks, w_ref, steps, dims, swapped=False):
    width = blocks[0].shape[0 if swapped else 1] if blocks else 0
    for i, block in zip(places, blocks):
        at = pl.multiple_of(origin(i % steps, i >= steps) * width, 128)
        w = w_ref[:, pl.ds(at, width)]
        total += dot(w, block[...], dims) if swapped else dot(block[...], w, dims)
    return total


def rows_own_kernel(steps, rows_ref, w_ref, residual_ref, placing_ref, total_ref):
    total = dot(placing_ref[...], residual_ref[...], NT)
    total_ref[...] = add_products(total, [0], [rows_ref], w_ref, steps, NT)


def rows_more_kernel(places, steps, *refs):
    blocks, (before_ref, w_ref, total_ref) = refs[:-3], refs[-3:]
    total_ref[...] = add_products(before_ref[...], places, blocks, w_ref, steps, NT)


def rows_last_kernel(steps, *refs):
    blocks, (before_ref, w_ref) = refs[: steps - 1], refs[steps - 1 : steps + 1]
    outgoing, rows_ref = refs[steps + 1 : -1], refs[-1]
    total = add_products(before_ref[...], range(steps + 1, 2 * steps), blocks, w_ref, steps, NT)
    rows_ref[...] = total.astype(jnp.bfloat16).reshape(rows_ref.shape)
    me = lax.axis_index("seq")
    for k, out_ref in enumerate(outgoing):
        out_ref[...] = rows_ref[lax.bitwise_xor(me, k)]


def stack_kernel(*refs):
    for i, block in enumerate(refs[:-1]):
        refs[-1][i * CAP : (i + 1) * CAP] = block[...]


def project_kernel(steps, *refs):
    blocks = refs[: 2 * steps]
    w_ref, residual_ref, resid_ref = refs[2 * steps :]
    total = residual_ref[...].astype(jnp.float32)
    total = add_products(total, range(2 * steps), blocks, w_ref, steps, NN, True)
    resid_ref[...] = total.astype(jnp.bfloat16)


def spread_kernel(source_ref, blocks_ref):
    cuts, _, width = blocks_ref.shape
    for p in range(cuts):
        blocks_ref[p] = source_ref[:, p * width : (p + 1) * width]


def spread_gain_kernel(gain_ref, blocks_ref):
    cuts, _, width = blocks_ref.shape
    gain = gain_ref[...].reshape(1, cuts * width)
    for p in range(cuts):
        blocks_ref[p] = gain[:, p * width : (p + 1) * width]


def add_features(sums, places, blocks, gains_ref, gates_ref, ups_ref, steps):
    gate, up, squares = sums
    for i, block in zip(places, blocks):
        p = origin(i % steps, i >= steps)
        wide = block[...].astype(jnp.float32)
        squares += jnp.sum(wide * wide, axis=1, keepdims=True)
        rows = (wide * gains_ref[p]).astype(jnp.bfloat16)
        gate += dot(rows, gates_ref[p], NT)
        up += dot(rows, ups_ref[p], NT)
    return gate, up, squares


def store_sums(sums, refs):
    for ref, value in zip(refs, sums):
        ref[...] = jnp.broadcast_to(value, ref.shape)


def expert_own_kernel(steps, block_ref, gains_ref, gates_ref, ups_ref, *out_refs):
    zeros = jnp.zeros(out_refs[0].shape, jnp.float32)
    sums = (zeros, zeros, jnp.zeros((zeros.shape[0], 1), jnp.float32))
    store_sums(add_features(sums, [0], [block_ref], gains_ref, gates_ref, ups_ref, steps), out_refs)


def expert_more_kernel(places, steps, *refs):
    blocks, refs = refs[:-9], refs[-9:]
    sums = (refs[0][...], refs[1][...], refs[2][:, :1])
    store_sums(add_features(sums, places, blocks, *refs[3:6], steps), refs[6:])


def expert_last_kernel(steps, *refs):
    blocks, refs = refs[: steps - 1], refs[steps - 1 :]
    sums = (refs[0][...], refs[1][...], refs[2][:, :1])
    gains_ref, gates_ref, ups_ref, downs_ref, given_ref, activated_ref = refs[3:]
    places = range(steps + 1, 2 * steps)
    gate, up, squares = add_features(sums, places, blocks, gains_ref, gates_ref, ups_ref, steps)
    cuts, _, width = gates_ref.shape
    scale = lax.rsqrt(squares / (cuts * width) + norm_eps)
    gate, up = gate * scale, up * scale
    activated = ((up + 1.0) * gate * jax.nn.sigmoid(glu_alpha * gate)).astype(jnp.bfloat16)
    activated_ref[...] = activated
    for k in range(steps):
        given_ref[k] = dot(activated, downs_ref[origin(k, True)], NN).astype(jnp.bfloat16)


def expert_kept_kernel(activated_ref, downs_ref, kept_ref):
    for k in range(kept_ref.shape[0]):
        kept_ref[k] = dot(activated_ref[...], downs_ref[origin(k, False)], NN).astype(jnp.bfloat16)


def add_cores_kernel(kept_ref, given_ref, *out_refs):
    half = out_refs[0].shape[0]
    for i, out_ref in enumerate(out_refs):
        rows = slice(i % 2 * half, (i % 2 + 1) * half)
        total = kept_ref[i // 2, rows].astype(jnp.float32) + given_ref[i // 2, rows].astype(jnp.float32)
        out_ref[...] = total.astype(jnp.bfloat16)


def add_chips_kernel(steps, *refs):
    total = sum(r[...].astype(jnp.float32) for r in refs[:steps])
    for k, out_ref in enumerate(refs[steps:]):
        out_ref[...] = total[k * CAP : (k + 1) * CAP].astype(jnp.bfloat16)


def combine_kernel(live, *refs):
    blocks = refs[:live]
    mix_hi_ref, mix_lo_ref, resid_ref, out_ref, rows_ref = refs[live:]
    me = lax.axis_index("seq")
    for k in range(live):
        rows_ref[lax.bitwise_xor(me, live - 1 - k)] = blocks[k][...]
    rows = rows_ref[...].reshape(live * CAP, -1)
    mixed = dot(rows, mix_hi_ref[...], TN) + dot(rows, mix_lo_ref[...], TN)
    out_ref[...] = (resid_ref[...].astype(jnp.float32) + mixed).astype(jnp.bfloat16)


def swap(block, axis, mask):
    return lax.ppermute(block, axis, [(i, i ^ mask) for i in range(lax.axis_size(axis))])


def from_chips(block):
    return [swap(block, "cuts", CORES * k) for k in range(1, lax.axis_size("cuts") // CORES)]


def from_sibling(block):
    return swap(block, "cuts", 1)


def after(arrays, others):
    return lax.optimization_barrier((arrays, others))[0]


def shards(
    queries,
    keyvals,
    preceding_keyvalues,
    attention_sink_logits,
    residual,
    w_out,
    norm_gain,
    expert_ids,
    route_weights,
    w_gate,
    w_up,
    w_down,
):
    toks, feats = residual.shape
    size = lax.axis_size("seq")
    live = w_gate.shape[0] * size
    cuts = lax.axis_size("cuts")
    steps = cuts // CORES
    slots = live * CAP
    head_rows = queries.shape[1]
    heads = head_rows // HEAD_SIZE
    width = norm_gain.shape[0]
    hidden = w_gate.shape[2]

    tail = keyvals[toks - KEYS_SEEN :]
    rim = lax.ppermute(tail, "seq", [(i, (i + 1) % size) for i in range(size)])
    loads = (queries, keyvals, preceding_keyvalues, w_out.T, residual.T)
    q, kv, before, w_t, residual_t, placing, mix_hi, mix_lo, sinks, late = call(
        functools.partial(first_kernel, live),
        (
            *(bf16(*a.shape) for a in loads),
            *(bf16(slots, toks),) * 3,
            jax.ShapeDtypeStruct((heads, KEYS_SEEN), jnp.float32),
            bf16(head_rows, toks - KEYS_SEEN),
        ),
        n_in=8,
        scratch=[
            pltpu.VMEM(expert_ids.T.shape, jnp.int32),
            pltpu.VMEM(expert_ids.T.shape, jnp.float32),
            pltpu.SMEM(attention_sink_logits.shape, jnp.float32),
            pltpu.SemaphoreType.DMA((8,)),
        ],
        hbm=range(8),
        flops=4 * toks * SPAN * head_rows,
        moved=2 * (w_out.size + residual.size + queries.size),
    )(*(in_hbm(a) for a in (expert_ids.T, route_weights.T, attention_sink_logits, *loads)))
    attended, rows = call(
        second_kernel,
        (bf16(head_rows, toks), bf16(slots, head_rows)),
        n_in=7,
        flops=2 * toks * SPAN * head_rows,
        moved=2 * queries.size,
    )(q, kv, before, rim, sinks, late, placing)

    chip_rows = from_chips(rows)
    total = jax.ShapeDtypeStruct((slots, feats), jnp.float32)
    part = dict(flops=slots * w_out.size // 2, moved=w_out.size // 2)
    own = call(functools.partial(rows_own_kernel, steps), total, n_in=4, **part)(
        rows, w_t, residual_t, placing
    )
    sibling_rows = from_sibling(rows)
    places = [steps, *range(1, steps)]
    spread = functools.partial(
        call, spread_kernel, bf16(cuts, hidden, feats), n_in=1, moved=4 * w_gate.size
    )
    gates = spread()(after(w_gate[0].T, rows))
    chip_rows = after(chip_rows, (own, gates))
    relayed_rows = [from_sibling(b) for b in chip_rows]
    chips = call(functools.partial(rows_more_kernel, places, steps), total, n_in=steps + 2, **part)(
        sibling_rows, *chip_rows, own, w_t
    )
    outgoing = call(
        functools.partial(rows_last_kernel, steps),
        (bf16(CAP, feats),) * live,
        n_in=steps + 1,
        scratch=[pltpu.VMEM((live, CAP, feats), jnp.bfloat16)],
        **part,
    )(*relayed_rows, chips, w_t)

    arrived = [swap(outgoing[k], "seq", k) for k in range(live - 1, 0, -1)] + [outgoing[0]]

    ups = spread()(after(w_up[0].T, outgoing[0]))
    gains = call(spread_gain_kernel, jax.ShapeDtypeStruct((cuts, 1, feats), jnp.float32), n_in=1)(norm_gain)
    sums = (
        *(jax.ShapeDtypeStruct((slots, hidden), jnp.float32),) * 2,
        jax.ShapeDtypeStruct((slots, KEYS_SEEN), jnp.float32),
    )
    part = dict(flops=slots * w_gate.size, moved=w_gate.size)
    stacked = call(stack_kernel, bf16(slots, feats), n_in=live)(*after(arrived, (ups, gains)))
    chip_rows = from_chips(stacked)
    own = call(functools.partial(expert_own_kernel, steps), sums, n_in=4, **part)(stacked, gains, gates, ups)
    sibling_rows = from_sibling(stacked)
    downs = spread()(after(w_down[0], stacked))
    chip_blocks = from_chips(after(attended, gates))
    blocks = [attended, *chip_blocks]
    blocks += [from_sibling(b) for b in blocks]
    chip_rows = after(chip_rows, (own, downs))
    relayed_rows = [from_sibling(b) for b in chip_rows]
    chips = call(functools.partial(expert_more_kernel, places, steps), sums, n_in=steps + 6, **part)(
        sibling_rows, *chip_rows, *own, gains, gates, ups
    )
    given, activated = call(
        functools.partial(expert_last_kernel, steps),
        (bf16(steps, slots, feats), bf16(slots, hidden)),
        n_in=steps + 6,
        **part,
    )(*relayed_rows, *chips, gains, gates, ups, downs)
    kept = call(expert_kept_kernel, bf16(steps, slots, feats), n_in=2, **part)(activated, downs)
    resid = call(
        functools.partial(project_kernel, steps),
        bf16(feats, toks),
        n_in=cuts + 2,
        flops=2 * toks * w_out.size,
        moved=2 * w_out.size,
    )(*blocks, w_t, residual_t)

    sums = call(add_cores_kernel, (bf16(slots // 2, feats),) * (2 * steps), n_in=2)(
        kept, swap(given, "cuts", 1)
    )
    returned = []
    for half in range(2):
        parts = [sums[half]] + [swap(sums[2 * k + half], "cuts", CORES * k) for k in range(1, steps)]
        blocks = call(functools.partial(add_chips_kernel, steps), (bf16(CAP, feats),) * (live // 2), n_in=steps)(
            *parts
        )
        for block in blocks:
            k = live - 1 - len(returned)
            returned.append(swap(block, "seq", k) if k else block)
    out = call(
        functools.partial(combine_kernel, live),
        bf16(feats, toks),
        n_in=live + 3,
        scratch=[pltpu.VMEM((live, CAP, feats), jnp.bfloat16)],
    )(*returned, mix_hi, mix_lo, resid)
    return out.T


def solution(mesh):
    placed = (
        P(("groups", "seq"), "cuts"),
        P(("groups", "seq"), "cuts"),
        P("groups", "cuts"),
        P("cuts"),
        P(("groups", "seq"), "cuts"),
        P(None, "cuts"),
        P(),
        P(("groups", "seq"), None),
        P(("groups", "seq"), None),
        P("seq", None, "cuts"),
        P("seq", None, "cuts"),
        P("seq", "cuts", None),
    )
    return jax.shard_map(
        shards, mesh=mesh, in_specs=placed, out_specs=P(("groups", "seq"), "cuts"), check_vma=False
    )
```

```python
import functools
import math

import jax
import jax.numpy as jnp
from jax import lax
from jax.experimental import pallas as pl
from jax.experimental.pallas import tpu as pltpu
from jax.sharding import PartitionSpec as P

HEAD_SIZE = 64
KEYS_SEEN = 128
PAIR = 2 * HEAD_SIZE
SPAN = 2 * KEYS_SEEN
CAP = 16
CORES = 2

norm_eps = 1e-05
glu_alpha = 1.702

NT = (((1,), (1,)), ((), ()))
NN = (((1,), (0,)), ((), ()))
TN = (((0,), (0,)), ((), ()))
VMEM_LIMIT = 32 * 1024 * 1024


def dot(a, b, dims):
    return lax.dot_general(a, b, dims, preferred_element_type=jnp.float32)


def call(kernel, outs, n_in, scratch=(), hbm=(), smem=(), flops=0, moved=0):
    spaces = [pltpu.HBM if i in hbm else pltpu.SMEM if i in smem else pltpu.VMEM for i in range(n_in)]
    return pl.pallas_call(
        kernel,
        out_shape=outs,
        in_specs=[pl.BlockSpec(memory_space=space) for space in spaces],
        out_specs=jax.tree.map(lambda _: pl.BlockSpec(memory_space=pltpu.VMEM), outs),
        scratch_shapes=list(scratch),
        compiler_params=pltpu.CompilerParams(vmem_limit_bytes=VMEM_LIMIT),
        cost_estimate=pl.CostEstimate(flops=flops, bytes_accessed=moved, transcendentals=0),
    )


def in_hbm(array):
    return pltpu.with_memory_space_constraint(array, pltpu.HBM)


def bf16(*shape):
    return jax.ShapeDtypeStruct(shape, jnp.bfloat16)


def visible():
    key = lax.broadcasted_iota(jnp.int32, (SPAN, KEYS_SEEN), 0)
    query = lax.broadcasted_iota(jnp.int32, (SPAN, KEYS_SEEN), 1)
    return (key > query) & (key <= query + KEYS_SEEN)


def attend_block(pairs, both, sinks, allowed):
    both = both.astype(jnp.float32)
    low = lax.broadcasted_iota(jnp.int32, both.shape, 1) < HEAD_SIZE
    turned = pltpu.roll(both, HEAD_SIZE, 1)
    keys = jnp.concatenate([jnp.where(low, both, 0.0), jnp.where(low, 0.0, turned)], axis=0)
    values = jnp.concatenate([jnp.where(low, turned, 0.0), jnp.where(low, 0.0, both)], axis=0)
    keys, values = keys.astype(jnp.bfloat16), values.astype(jnp.bfloat16)
    scores = dot(keys, jnp.concatenate(pairs, axis=0), NT) * (HEAD_SIZE**-0.5 * math.log2(math.e))
    allowed = jnp.concatenate([allowed] * len(pairs), axis=1)
    probs = []
    for i in range(2):
        sink = jnp.concatenate([sinks[2 * p + i] for p in range(len(pairs))], axis=1)
        part = jnp.where(allowed, scores[i * SPAN : (i + 1) * SPAN], -jnp.inf)
        peak = jnp.maximum(jnp.max(part, axis=0, keepdims=True), sink)
        terms = jnp.exp2(part - peak)
        denom = jnp.sum(terms, axis=0, keepdims=True) + jnp.exp2(sink - peak)
        probs.append((terms * (1.0 / denom)).astype(jnp.bfloat16))
    mixed = dot(values, jnp.concatenate(probs, axis=0), TN).astype(jnp.bfloat16)
    return [mixed[:, p * KEYS_SEEN : (p + 1) * KEYS_SEEN] for p in range(len(pairs))]


def attend_tokens(block, q_ref, rows_of, sinks, out_ref, lanes):
    groups = len(rows_of)
    per_group = q_ref.shape[1] // PAIR // groups
    allowed = visible()
    toks = slice(block * KEYS_SEEN, (block + 1) * KEYS_SEEN)
    for g, both in enumerate(rows_of):
        first = g * per_group
        pairs = [q_ref[toks, (first + p) * PAIR : (first + p + 1) * PAIR] for p in range(per_group)]
        outs = attend_block(pairs, both, sinks[2 * first : 2 * (first + per_group)], allowed)
        for p, out in enumerate(outs):
            out_ref[(first + p) * PAIR : (first + p + 1) * PAIR, lanes] = out


def fill_tables(live, ids, weights, placing_ref, mix_hi_ref, mix_lo_ref):
    toks = ids.shape[1]
    chosen = jnp.concatenate(
        [jnp.max((ids == e).astype(jnp.float32), axis=0, keepdims=True) for e in range(live)], axis=0
    )
    earlier = lax.broadcasted_iota(jnp.int32, (toks, toks), 0)
    later = lax.broadcasted_iota(jnp.int32, (toks, toks), 1)
    strict = (earlier < later).astype(jnp.bfloat16)
    before = dot(chosen.astype(jnp.bfloat16), strict, NN)
    slot = lax.broadcasted_iota(jnp.int32, (CAP, toks), 0).astype(jnp.float32)
    for e in range(live):
        weight = jnp.sum(jnp.where(ids == e, weights, 0.0), axis=0, keepdims=True)
        fills = (before[e : e + 1] == slot) & (chosen[e : e + 1] > 0.0)
        mix = jnp.where(fills, weight, 0.0)
        hi = mix.astype(jnp.bfloat16)
        rows = slice(e * CAP, (e + 1) * CAP)
        placing_ref[rows] = fills.astype(jnp.bfloat16)
        mix_hi_ref[rows] = hi
        mix_lo_ref[rows] = (mix - hi.astype(jnp.float32)).astype(jnp.bfloat16)


def first_kernel(live, *refs):
    loaded, held = refs[:8], refs[8:13]
    placing_ref, mix_hi_ref, mix_lo_ref, sinks_out, late_ref, ids_ref, weights_ref, sinks_ref, sems = refs[13:]
    targets = (ids_ref, weights_ref, sinks_ref, *held)
    copies = [pltpu.make_async_copy(*pair, sems.at[i]) for i, pair in enumerate(zip(loaded, targets))]
    for copy in copies:
        copy.start()
    q_ref, kv_ref = held[:2]
    for copy in copies[:2]:
        copy.wait()
    fill_tables(live, ids_ref[...], weights_ref[...], placing_ref, mix_hi_ref, mix_lo_ref)
    for copy in copies[2:5]:
        copy.wait()
    heads = sinks_ref.shape[0]
    sinks = [jnp.full((1, KEYS_SEEN), sinks_ref[h], jnp.float32) * math.log2(math.e) for h in range(heads)]
    sinks_out[...] = jnp.concatenate(sinks, axis=0)
    groups = kv_ref.shape[1] // PAIR
    for b in range(1, q_ref.shape[0] // KEYS_SEEN):
        span = slice((b - 1) * KEYS_SEEN, (b + 1) * KEYS_SEEN)
        rows_of = [kv_ref[span, g * PAIR : (g + 1) * PAIR] for g in range(groups)]
        attend_tokens(b, q_ref, rows_of, sinks, late_ref, slice((b - 1) * KEYS_SEEN, b * KEYS_SEEN))
    for copy in copies[5:]:
        copy.wait()


def second_kernel(q_ref, kv_ref, before_ref, rim_ref, sinks_ref, late_ref, placing_ref, all_ref, rows_ref):
    first = lax.axis_index("seq") == 0
    rim = jnp.where(first, before_ref[...], rim_ref[...])
    groups = kv_ref.shape[1] // PAIR
    rows_of = []
    for g in range(groups):
        lanes = slice(g * PAIR, (g + 1) * PAIR)
        rows_of.append(jnp.concatenate([rim[:, lanes], kv_ref[:KEYS_SEEN, lanes]], axis=0))
    sinks = [sinks_ref[h : h + 1] for h in range(sinks_ref.shape[0])]
    attend_tokens(0, q_ref, rows_of, sinks, all_ref, slice(0, KEYS_SEEN))
    all_ref[:, KEYS_SEEN:] = late_ref[...]
    rows_ref[...] = dot(placing_ref[...], all_ref[...], NT).astype(jnp.bfloat16)


def origin(k, sibling):
    me = lax.axis_index("cuts")
    return lax.bitwise_xor(me, CORES * k + (1 if sibling else 0))


def add_products(total, places, blocks, w_ref, steps, dims, swapped=False):
    width = blocks[0].shape[0 if swapped else 1] if blocks else 0
    for i, block in zip(places, blocks):
        at = pl.multiple_of(origin(i % steps, i >= steps) * width, 128)
        w = w_ref[:, pl.ds(at, width)]
        total += dot(w, block[...], dims) if swapped else dot(block[...], w, dims)
    return total


def rows_own_kernel(steps, rows_ref, w_ref, residual_ref, placing_ref, total_ref):
    total = dot(placing_ref[...], residual_ref[...], NT)
    total_ref[...] = add_products(total, [0], [rows_ref], w_ref, steps, NT)


def rows_more_kernel(places, steps, *refs):
    blocks, (before_ref, w_ref, total_ref) = refs[:-3], refs[-3:]
    total_ref[...] = add_products(before_ref[...], places, blocks, w_ref, steps, NT)


def rows_last_kernel(steps, *refs):
    blocks, (before_ref, w_ref) = refs[: steps - 1], refs[steps - 1 : steps + 1]
    outgoing, rows_ref = refs[steps + 1 : -1], refs[-1]
    total = add_products(before_ref[...], range(steps + 1, 2 * steps), blocks, w_ref, steps, NT)
    rows_ref[...] = total.astype(jnp.bfloat16).reshape(rows_ref.shape)
    me = lax.axis_index("seq")
    for k, out_ref in enumerate(outgoing):
        out_ref[...] = rows_ref[lax.bitwise_xor(me, k)]


def stack_kernel(*refs):
    for i, block in enumerate(refs[:-1]):
        refs[-1][i * CAP : (i + 1) * CAP] = block[...]


def project_kernel(steps, *refs):
    blocks = refs[: 2 * steps]
    w_ref, residual_ref, resid_ref = refs[2 * steps :]
    total = residual_ref[...].astype(jnp.float32)
    total = add_products(total, range(2 * steps), blocks, w_ref, steps, NN, True)
    resid_ref[...] = total.astype(jnp.bfloat16)


def spread_kernel(*refs):
    sources, targets = refs[:CORES], refs[CORES:]
    steps, _, width = targets[0].shape
    chip, core = lax.div(lax.axis_index("cuts"), CORES), lax.rem(lax.axis_index("cuts"), CORES)
    for value in range(CORES):

        @pl.when(core == value)
        def _():
            for source, target in zip(sources, targets):
                for p in range(value, CORES * steps, CORES):
                    target[lax.bitwise_xor(chip, p // CORES)] = source[:, p * width : (p + 1) * width]


def spread_gain_kernel(gain_ref, blocks_ref):
    cuts, _, width = blocks_ref.shape
    gain = gain_ref[...].reshape(1, cuts * width)
    for p in range(cuts):
        blocks_ref[p] = gain[:, p * width : (p + 1) * width]


def add_features(totals, k, block, gains_ref, weights):
    wide = block[...].astype(jnp.float32)
    rows = (wide * gains_ref[origin(k, False)]).astype(jnp.bfloat16)
    totals = [total + dot(rows, w[k], NT) for total, w in zip(totals, weights)] + totals[len(weights) :]
    totals[-1] += jnp.sum(wide * wide, axis=1, keepdims=True)
    return totals


def expert_own_kernel(block_ref, gains_ref, *refs):
    weights, totals_ref = refs[:-1], refs[-1]
    totals = [jnp.zeros(totals_ref.shape[1:], jnp.float32)] * totals_ref.shape[0]
    for i, total in enumerate(add_features(totals, 0, block_ref, gains_ref, weights)):
        totals_ref[i] = total


def expert_chips_kernel(steps, *refs):
    blocks, refs = refs[: steps - 1], refs[steps - 1 :]
    before_ref, gains_ref, *weights, totals_ref, sums_ref, squares_ref = refs
    totals = [before_ref[i] for i in range(totals_ref.shape[0])]
    for k, block in enumerate(blocks, 1):
        totals = add_features(totals, k, block, gains_ref, weights)
    for i, total in enumerate(totals):
        totals_ref[i] = total
    for i in range(2 * CORES):
        sums_ref[i] = totals[i].astype(jnp.bfloat16)
    squares_ref[...] = totals[-1][:, : squares_ref.shape[1]]


def expert_last_kernel(features, mine_ref, sums_ref, squares_ref, down_mine_ref, down_theirs_ref, *out_refs):
    gates = [mine_ref[i] + sums_ref[1 - i].astype(jnp.float32) for i in range(CORES)]
    ups = [mine_ref[CORES + i] + sums_ref[CORES + 1 - i].astype(jnp.float32) for i in range(CORES)]
    squares = mine_ref[2 * CORES][:, :1] + squares_ref[:, :1]
    scale = lax.rsqrt(squares / features + norm_eps)
    activated = []
    for gate, up in zip(gates, ups):
        gate, up = gate * scale, up * scale
        activated.append(((up + 1.0) * gate * jax.nn.sigmoid(glu_alpha * gate)).astype(jnp.bfloat16))
    for i in range(CORES):
        out_refs[i][...] = activated[i]
    store_products(range(1, down_mine_ref.shape[0]), out_refs[:CORES], down_mine_ref, down_theirs_ref, out_refs[CORES:])


def store_products(chips, activated, down_mine_ref, down_theirs_ref, out_refs):
    half = out_refs[0].shape[0]
    for k, firsts in zip(chips, range(0, len(out_refs), 2)):
        out = dot(activated[0][...], down_mine_ref[k], NN) + dot(activated[1][...], down_theirs_ref[k], NN)
        for i in range(2):
            out_refs[firsts + i][...] = out[i * half : (i + 1) * half].astype(jnp.bfloat16)


def expert_kept_kernel(mine_ref, theirs_ref, down_mine_ref, down_theirs_ref, *out_refs):
    store_products([0], (mine_ref, theirs_ref), down_mine_ref, down_theirs_ref, out_refs)


def add_chips_kernel(steps, *refs):
    total = sum(r[...].astype(jnp.float32) for r in refs[:steps])
    for k, out_ref in enumerate(refs[steps:]):
        out_ref[...] = total[k * CAP : (k + 1) * CAP].astype(jnp.bfloat16)


def combine_kernel(live, *refs):
    blocks = refs[:live]
    mix_hi_ref, mix_lo_ref, resid_ref, out_ref, rows_ref = refs[live:]
    me = lax.axis_index("seq")
    for k in range(live):
        rows_ref[lax.bitwise_xor(me, live - 1 - k)] = blocks[k][...]
    rows = rows_ref[...].reshape(live * CAP, -1)
    mix = jnp.concatenate([mix_hi_ref[...], mix_lo_ref[...]], axis=0)
    mixed = dot(jnp.concatenate([rows, rows], axis=0), mix, TN)
    out_ref[...] = (resid_ref[...].astype(jnp.float32) + mixed).astype(jnp.bfloat16)


def swap(block, axis, mask):
    return lax.ppermute(block, axis, [(i, i ^ mask) for i in range(lax.axis_size(axis))])


def from_chips(block):
    return [swap(block, "cuts", CORES * k) for k in range(1, lax.axis_size("cuts") // CORES)]


def from_sibling(block):
    return swap(block, "cuts", 1)


def after(arrays, others):
    return lax.optimization_barrier((arrays, others))[0]


def shards(
    queries,
    keyvals,
    preceding_keyvalues,
    attention_sink_logits,
    residual,
    w_out,
    norm_gain,
    expert_ids,
    route_weights,
    w_gate,
    w_up,
    w_down,
):
    toks, feats = residual.shape
    size = lax.axis_size("seq")
    live = w_gate.shape[0] * size
    cuts = lax.axis_size("cuts")
    steps = cuts // CORES
    slots = live * CAP
    head_rows = queries.shape[1]
    heads = head_rows // HEAD_SIZE
    width = norm_gain.shape[0]
    hidden = w_gate.shape[2]

    tail = keyvals[toks - KEYS_SEEN :]
    rim = lax.ppermute(tail, "seq", [(i, (i + 1) % size) for i in range(size)])
    loads = (queries, keyvals, preceding_keyvalues, w_out.T, residual.T)
    q, kv, before, w_t, residual_t, placing, mix_hi, mix_lo, sinks, late = call(
        functools.partial(first_kernel, live),
        (
            *(bf16(*a.shape) for a in loads),
            *(bf16(slots, toks),) * 3,
            jax.ShapeDtypeStruct((heads, KEYS_SEEN), jnp.float32),
            bf16(head_rows, toks - KEYS_SEEN),
        ),
        n_in=8,
        scratch=[
            pltpu.VMEM(expert_ids.T.shape, jnp.int32),
            pltpu.VMEM(expert_ids.T.shape, jnp.float32),
            pltpu.SMEM(attention_sink_logits.shape, jnp.float32),
            pltpu.SemaphoreType.DMA((8,)),
        ],
        hbm=range(8),
        flops=4 * toks * SPAN * head_rows,
        moved=2 * (w_out.size + residual.size + queries.size),
    )(*(in_hbm(a) for a in (expert_ids.T, route_weights.T, attention_sink_logits, *loads)))
    pairs = [(w, from_sibling(w)) for w in (w_gate[0].T, w_up[0].T, w_down[0])]
    spread = call(spread_kernel, (bf16(steps, hidden, feats),) * CORES, n_in=CORES, moved=4 * w_gate.size)
    attended, rows = call(
        second_kernel,
        (bf16(head_rows, toks), bf16(slots, head_rows)),
        n_in=7,
        flops=2 * toks * SPAN * head_rows,
        moved=2 * queries.size,
    )(q, kv, before, rim, sinks, late, placing)

    gate_pair, up_pair, down_pair = pairs
    rows, attended = after((rows, attended), pairs)
    chip_rows = from_chips(rows)
    total = jax.ShapeDtypeStruct((slots, feats), jnp.float32)
    part = dict(flops=slots * w_out.size // 2, moved=w_out.size // 2)
    own = call(functools.partial(rows_own_kernel, steps), total, n_in=4, **part)(
        rows, w_t, residual_t, placing
    )
    sibling_rows = from_sibling(rows)
    places = [steps, *range(1, steps)]
    gates = spread(*after(gate_pair, rows))
    chip_rows = after(chip_rows, (own, gates))
    relayed_rows = [from_sibling(b) for b in chip_rows]
    chips = call(functools.partial(rows_more_kernel, places, steps), total, n_in=steps + 2, **part)(
        sibling_rows, *chip_rows, own, w_t
    )
    outgoing = call(
        functools.partial(rows_last_kernel, steps),
        (bf16(CAP, feats),) * live,
        n_in=steps + 1,
        scratch=[pltpu.VMEM((live, CAP, feats), jnp.bfloat16)],
        **part,
    )(*relayed_rows, chips, w_t)

    arrived = [swap(outgoing[k], "seq", k) for k in range(live - 1, 0, -1)] + [outgoing[0]]

    gains = call(spread_gain_kernel, jax.ShapeDtypeStruct((cuts, 1, feats), jnp.float32), n_in=1)(norm_gain)
    ups = spread(*after(up_pair, outgoing[0]))
    weights = (*gates, *ups)
    totals = jax.ShapeDtypeStruct((2 * CORES + 1, slots, hidden), jnp.float32)
    part = dict(flops=4 * slots * hidden * feats, moved=8 * hidden * feats)
    chip_blocks = from_chips(after(attended, outgoing[0]))
    stacked = call(stack_kernel, bf16(slots, feats), n_in=live)(*after(arrived, (gains, ups)))
    chip_rows = from_chips(stacked)
    own = call(expert_own_kernel, totals, n_in=6, **part)(stacked, gains, *weights)
    blocks = [attended, *chip_blocks]
    blocks += [from_sibling(b) for b in after(blocks, stacked)]
    downs = spread(*after(down_pair, stacked))
    chip_rows = after(chip_rows, (own, downs))
    chips, *theirs = call(
        functools.partial(expert_chips_kernel, steps),
        (totals, bf16(2 * CORES, slots, hidden), jax.ShapeDtypeStruct((slots, KEYS_SEEN), jnp.float32)),
        n_in=steps + 5,
        **part,
    )(
        *chip_rows, own, gains, *weights
    )
    half = bf16(slots // 2, feats)
    act_mine, act_theirs, *sums = call(
        functools.partial(expert_last_kernel, width),
        (*(bf16(slots, hidden),) * CORES, *(half,) * (2 * steps - 2)),
        n_in=5,
    )(chips, *(from_sibling(a) for a in theirs), *downs)
    kept = call(expert_kept_kernel, (half,) * 2, n_in=4)(act_mine, act_theirs, *downs)
    sums = [*kept, *sums]
    resid = call(
        functools.partial(project_kernel, steps),
        bf16(feats, toks),
        n_in=cuts + 2,
        flops=2 * toks * w_out.size,
        moved=2 * w_out.size,
    )(*blocks, w_t, residual_t)

    returned = []
    for half in range(2):
        parts = [sums[half]] + [swap(sums[2 * k + half], "cuts", CORES * k) for k in range(1, steps)]
        blocks = call(functools.partial(add_chips_kernel, steps), (bf16(CAP, feats),) * (live // 2), n_in=steps)(
            *parts
        )
        for block in blocks:
            k = live - 1 - len(returned)
            returned.append(swap(block, "seq", k) if k else block)
    out = call(
        functools.partial(combine_kernel, live),
        bf16(feats, toks),
        n_in=live + 3,
        scratch=[pltpu.VMEM((live, CAP, feats), jnp.bfloat16)],
    )(*returned, mix_hi, mix_lo, resid)
    return out.T


def solution(mesh):
    placed = (
        P(("groups", "seq"), "cuts"),
        P(("groups", "seq"), "cuts"),
        P("groups", "cuts"),
        P("cuts"),
        P(("groups", "seq"), "cuts"),
        P(None, "cuts"),
        P(),
        P(("groups", "seq"), None),
        P(("groups", "seq"), None),
        P("seq", None, "cuts"),
        P("seq", None, "cuts"),
        P("seq", "cuts", None),
    )
    return jax.shard_map(
        shards, mesh=mesh, in_specs=placed, out_specs=P(("groups", "seq"), "cuts"), check_vma=False
    )
```

```python
import functools
import math

import jax
import jax.numpy as jnp
from jax import lax
from jax.experimental import pallas as pl
from jax.experimental.pallas import tpu as pltpu
from jax.sharding import PartitionSpec as P

HEAD_SIZE = 64
KEYS_SEEN = 128
PAIR = 2 * HEAD_SIZE
SPAN = 2 * KEYS_SEEN
CAP = 16
CORES = 2

norm_eps = 1e-05
glu_alpha = 1.702

NT = (((1,), (1,)), ((), ()))
NN = (((1,), (0,)), ((), ()))
TN = (((0,), (0,)), ((), ()))
VMEM_LIMIT = 32 * 1024 * 1024


def dot(a, b, dims):
    return lax.dot_general(a, b, dims, preferred_element_type=jnp.float32)


def call(kernel, outs, n_in, scratch=(), hbm=(), smem=(), flops=0, moved=0):
    spaces = [pltpu.HBM if i in hbm else pltpu.SMEM if i in smem else pltpu.VMEM for i in range(n_in)]
    return pl.pallas_call(
        kernel,
        out_shape=outs,
        in_specs=[pl.BlockSpec(memory_space=space) for space in spaces],
        out_specs=jax.tree.map(lambda _: pl.BlockSpec(memory_space=pltpu.VMEM), outs),
        scratch_shapes=list(scratch),
        compiler_params=pltpu.CompilerParams(vmem_limit_bytes=VMEM_LIMIT),
        cost_estimate=pl.CostEstimate(flops=flops, bytes_accessed=moved, transcendentals=0),
    )


def in_hbm(array):
    return pltpu.with_memory_space_constraint(array, pltpu.HBM)


def bf16(*shape):
    return jax.ShapeDtypeStruct(shape, jnp.bfloat16)


def visible():
    key = lax.broadcasted_iota(jnp.int32, (SPAN, KEYS_SEEN), 0)
    query = lax.broadcasted_iota(jnp.int32, (SPAN, KEYS_SEEN), 1)
    return (key > query) & (key <= query + KEYS_SEEN)


def attend_block(pairs, both, sinks, allowed):
    both = both.astype(jnp.float32)
    low = lax.broadcasted_iota(jnp.int32, both.shape, 1) < HEAD_SIZE
    turned = pltpu.roll(both, HEAD_SIZE, 1)
    keys = jnp.concatenate([jnp.where(low, both, 0.0), jnp.where(low, 0.0, turned)], axis=0)
    values = jnp.concatenate([jnp.where(low, turned, 0.0), jnp.where(low, 0.0, both)], axis=0)
    keys, values = keys.astype(jnp.bfloat16), values.astype(jnp.bfloat16)
    scores = dot(keys, jnp.concatenate(pairs, axis=0), NT) * (HEAD_SIZE**-0.5 * math.log2(math.e))
    allowed = jnp.concatenate([allowed] * len(pairs), axis=1)
    probs = []
    for i in range(2):
        sink = jnp.concatenate([sinks[2 * p + i] for p in range(len(pairs))], axis=1)
        part = jnp.where(allowed, scores[i * SPAN : (i + 1) * SPAN], -jnp.inf)
        peak = jnp.maximum(jnp.max(part, axis=0, keepdims=True), sink)
        terms = jnp.exp2(part - peak)
        denom = jnp.sum(terms, axis=0, keepdims=True) + jnp.exp2(sink - peak)
        probs.append((terms * (1.0 / denom)).astype(jnp.bfloat16))
    mixed = dot(values, jnp.concatenate(probs, axis=0), TN).astype(jnp.bfloat16)
    return [mixed[:, p * KEYS_SEEN : (p + 1) * KEYS_SEEN] for p in range(len(pairs))]


def attend_tokens(block, q_ref, rows_of, sinks, out_ref, lanes):
    groups = len(rows_of)
    per_group = q_ref.shape[1] // PAIR // groups
    allowed = visible()
    toks = slice(block * KEYS_SEEN, (block + 1) * KEYS_SEEN)
    for g, both in enumerate(rows_of):
        first = g * per_group
        pairs = [q_ref[toks, (first + p) * PAIR : (first + p + 1) * PAIR] for p in range(per_group)]
        outs = attend_block(pairs, both, sinks[2 * first : 2 * (first + per_group)], allowed)
        for p, out in enumerate(outs):
            out_ref[(first + p) * PAIR : (first + p + 1) * PAIR, lanes] = out


def fill_tables(live, ids, weights, placing_ref, mix_hi_ref, mix_lo_ref):
    toks = ids.shape[1]
    chosen = jnp.concatenate(
        [jnp.max((ids == e).astype(jnp.float32), axis=0, keepdims=True) for e in range(live)], axis=0
    )
    earlier = lax.broadcasted_iota(jnp.int32, (toks, toks), 0)
    later = lax.broadcasted_iota(jnp.int32, (toks, toks), 1)
    strict = (earlier < later).astype(jnp.bfloat16)
    before = dot(chosen.astype(jnp.bfloat16), strict, NN)
    slot = lax.broadcasted_iota(jnp.int32, (CAP, toks), 0).astype(jnp.float32)
    for e in range(live):
        weight = jnp.sum(jnp.where(ids == e, weights, 0.0), axis=0, keepdims=True)
        fills = (before[e : e + 1] == slot) & (chosen[e : e + 1] > 0.0)
        mix = jnp.where(fills, weight, 0.0)
        hi = mix.astype(jnp.bfloat16)
        rows = slice(e * CAP, (e + 1) * CAP)
        placing_ref[rows] = fills.astype(jnp.bfloat16)
        mix_hi_ref[rows] = hi
        mix_lo_ref[rows] = (mix - hi.astype(jnp.float32)).astype(jnp.bfloat16)


def first_kernel(live, *refs):
    loaded, held = refs[:8], refs[8:13]
    placing_ref, mix_hi_ref, mix_lo_ref, sinks_out, late_ref, ids_ref, weights_ref, sinks_ref, sems = refs[13:]
    targets = (ids_ref, weights_ref, sinks_ref, *held)
    copies = [pltpu.make_async_copy(*pair, sems.at[i]) for i, pair in enumerate(zip(loaded, targets))]
    for copy in copies:
        copy.start()
    q_ref, kv_ref = held[:2]
    for copy in copies[:2]:
        copy.wait()
    fill_tables(live, ids_ref[...], weights_ref[...], placing_ref, mix_hi_ref, mix_lo_ref)
    for copy in copies[2:5]:
        copy.wait()
    heads = sinks_ref.shape[0]
    sinks = [jnp.full((1, KEYS_SEEN), sinks_ref[h], jnp.float32) * math.log2(math.e) for h in range(heads)]
    sinks_out[...] = jnp.concatenate(sinks, axis=0)
    groups = kv_ref.shape[1] // PAIR
    for b in range(1, q_ref.shape[0] // KEYS_SEEN):
        span = slice((b - 1) * KEYS_SEEN, (b + 1) * KEYS_SEEN)
        rows_of = [kv_ref[span, g * PAIR : (g + 1) * PAIR] for g in range(groups)]
        attend_tokens(b, q_ref, rows_of, sinks, late_ref, slice((b - 1) * KEYS_SEEN, b * KEYS_SEEN))
    for copy in copies[5:]:
        copy.wait()


def second_kernel(q_ref, kv_ref, before_ref, rim_ref, sinks_ref, late_ref, placing_ref, all_ref, rows_ref):
    first = lax.axis_index("seq") == 0
    rim = jnp.where(first, before_ref[...], rim_ref[...])
    groups = kv_ref.shape[1] // PAIR
    rows_of = []
    for g in range(groups):
        lanes = slice(g * PAIR, (g + 1) * PAIR)
        rows_of.append(jnp.concatenate([rim[:, lanes], kv_ref[:KEYS_SEEN, lanes]], axis=0))
    sinks = [sinks_ref[h : h + 1] for h in range(sinks_ref.shape[0])]
    attend_tokens(0, q_ref, rows_of, sinks, all_ref, slice(0, KEYS_SEEN))
    all_ref[:, KEYS_SEEN:] = late_ref[...]
    rows_ref[...] = dot(placing_ref[...], all_ref[...], NT).astype(jnp.bfloat16)


def origin(k, sibling):
    me = lax.axis_index("cuts")
    return lax.bitwise_xor(me, CORES * k + (1 if sibling else 0))


def add_products(total, places, blocks, w_ref, steps, dims, swapped=False):
    width = blocks[0].shape[0 if swapped else 1] if blocks else 0
    for i, block in zip(places, blocks):
        at = pl.multiple_of(origin(i % steps, i >= steps) * width, 128)
        w = w_ref[:, pl.ds(at, width)]
        total += dot(w, block[...], dims) if swapped else dot(block[...], w, dims)
    return total


def rows_own_kernel(steps, rows_ref, w_ref, residual_ref, placing_ref, total_ref):
    total = dot(placing_ref[...], residual_ref[...], NT)
    total_ref[...] = add_products(total, [0], [rows_ref], w_ref, steps, NT)


def rows_more_kernel(places, steps, *refs):
    blocks, (before_ref, w_ref, total_ref) = refs[:-3], refs[-3:]
    total_ref[...] = add_products(before_ref[...], places, blocks, w_ref, steps, NT)


def rows_last_kernel(steps, *refs):
    blocks, (before_ref, w_ref) = refs[: steps - 1], refs[steps - 1 : steps + 1]
    outgoing, rows_ref = refs[steps + 1 : -1], refs[-1]
    total = add_products(before_ref[...], range(steps + 1, 2 * steps), blocks, w_ref, steps, NT)
    rows_ref[...] = total.astype(jnp.bfloat16).reshape(rows_ref.shape)
    me = lax.axis_index("seq")
    for k, out_ref in enumerate(outgoing):
        out_ref[...] = rows_ref[lax.bitwise_xor(me, k)]


def stack_kernel(*refs):
    for i, block in enumerate(refs[:-1]):
        refs[-1][i * CAP : (i + 1) * CAP] = block[...]


def project_kernel(steps, *refs):
    blocks = refs[: 2 * steps]
    w_ref, residual_ref, resid_ref = refs[2 * steps :]
    total = residual_ref[...].astype(jnp.float32)
    total = add_products(total, range(2 * steps), blocks, w_ref, steps, NN, True)
    resid_ref[...] = total.astype(jnp.bfloat16)


def spread_kernel(source_ref, blocks_ref):
    cuts, _, width = blocks_ref.shape
    for p in range(cuts):
        blocks_ref[p] = source_ref[:, p * width : (p + 1) * width]


def spread_gain_kernel(gain_ref, blocks_ref):
    cuts, _, width = blocks_ref.shape
    gain = gain_ref[...].reshape(1, cuts * width)
    for p in range(cuts):
        blocks_ref[p] = gain[:, p * width : (p + 1) * width]


def add_features(sums, places, blocks, gains_ref, gates_ref, ups_ref, steps):
    gate, up, squares = sums
    for i, block in zip(places, blocks):
        p = origin(i % steps, i >= steps)
        wide = block[...].astype(jnp.float32)
        squares += jnp.sum(wide * wide, axis=1, keepdims=True)
        rows = (wide * gains_ref[p]).astype(jnp.bfloat16)
        gate += dot(rows, gates_ref[p], NT)
        up += dot(rows, ups_ref[p], NT)
    return gate, up, squares


def store_sums(sums, refs):
    for ref, value in zip(refs, sums):
        ref[...] = jnp.broadcast_to(value, ref.shape)


def expert_own_kernel(steps, block_ref, gains_ref, gates_ref, ups_ref, *out_refs):
    zeros = jnp.zeros(out_refs[0].shape, jnp.float32)
    sums = (zeros, zeros, jnp.zeros((zeros.shape[0], 1), jnp.float32))
    store_sums(add_features(sums, [0], [block_ref], gains_ref, gates_ref, ups_ref, steps), out_refs)


def expert_more_kernel(places, steps, *refs):
    blocks, refs = refs[:-9], refs[-9:]
    sums = (refs[0][...], refs[1][...], refs[2][:, :1])
    store_sums(add_features(sums, places, blocks, *refs[3:6], steps), refs[6:])


def expert_last_kernel(steps, *refs):
    blocks, refs = refs[: steps - 1], refs[steps - 1 :]
    sums = (refs[0][...], refs[1][...], refs[2][:, :1])
    gains_ref, gates_ref, ups_ref, downs_ref, given_ref, activated_ref = refs[3:]
    places = range(steps + 1, 2 * steps)
    gate, up, squares = add_features(sums, places, blocks, gains_ref, gates_ref, ups_ref, steps)
    cuts, _, width = gates_ref.shape
    scale = lax.rsqrt(squares / (cuts * width) + norm_eps)
    gate, up = gate * scale, up * scale
    activated = ((up + 1.0) * gate * jax.nn.sigmoid(glu_alpha * gate)).astype(jnp.bfloat16)
    activated_ref[...] = activated
    for k in range(steps):
        given_ref[k] = dot(activated, downs_ref[origin(k, True)], NN).astype(jnp.bfloat16)


def expert_kept_kernel(activated_ref, downs_ref, kept_ref):
    for k in range(kept_ref.shape[0]):
        kept_ref[k] = dot(activated_ref[...], downs_ref[origin(k, False)], NN).astype(jnp.bfloat16)


def add_cores_kernel(kept_ref, given_ref, *out_refs):
    half = out_refs[0].shape[0]
    for i, out_ref in enumerate(out_refs):
        rows = slice(i % 2 * half, (i % 2 + 1) * half)
        total = kept_ref[i // 2, rows].astype(jnp.float32) + given_ref[i // 2, rows].astype(jnp.float32)
        out_ref[...] = total.astype(jnp.bfloat16)


def add_chips_kernel(steps, *refs):
    total = sum(r[...].astype(jnp.float32) for r in refs[:steps])
    for k, out_ref in enumerate(refs[steps:]):
        out_ref[...] = total[k * CAP : (k + 1) * CAP].astype(jnp.bfloat16)


def combine_kernel(live, *refs):
    blocks = refs[:live]
    mix_hi_ref, mix_lo_ref, resid_ref, out_ref, rows_ref = refs[live:]
    me = lax.axis_index("seq")
    for k in range(live):
        rows_ref[lax.bitwise_xor(me, live - 1 - k)] = blocks[k][...]
    rows = rows_ref[...].reshape(live * CAP, -1)
    mix = jnp.concatenate([mix_hi_ref[...], mix_lo_ref[...]], axis=0)
    mixed = dot(jnp.concatenate([rows, rows], axis=0), mix, TN)
    out_ref[...] = (resid_ref[...].astype(jnp.float32) + mixed).astype(jnp.bfloat16)


def swap(block, axis, mask):
    return lax.ppermute(block, axis, [(i, i ^ mask) for i in range(lax.axis_size(axis))])


def from_chips(block):
    return [swap(block, "cuts", CORES * k) for k in range(1, lax.axis_size("cuts") // CORES)]


def from_sibling(block):
    return swap(block, "cuts", 1)


def after(arrays, others):
    return lax.optimization_barrier((arrays, others))[0]


def shards(
    queries,
    keyvals,
    preceding_keyvalues,
    attention_sink_logits,
    residual,
    w_out,
    norm_gain,
    expert_ids,
    route_weights,
    w_gate,
    w_up,
    w_down,
):
    toks, feats = residual.shape
    size = lax.axis_size("seq")
    live = w_gate.shape[0] * size
    cuts = lax.axis_size("cuts")
    steps = cuts // CORES
    slots = live * CAP
    head_rows = queries.shape[1]
    heads = head_rows // HEAD_SIZE
    width = norm_gain.shape[0]
    hidden = w_gate.shape[2]

    tail = keyvals[toks - KEYS_SEEN :]
    rim = lax.ppermute(tail, "seq", [(i, (i + 1) % size) for i in range(size)])
    loads = (queries, keyvals, preceding_keyvalues, w_out.T, residual.T)
    q, kv, before, w_t, residual_t, placing, mix_hi, mix_lo, sinks, late = call(
        functools.partial(first_kernel, live),
        (
            *(bf16(*a.shape) for a in loads),
            *(bf16(slots, toks),) * 3,
            jax.ShapeDtypeStruct((heads, KEYS_SEEN), jnp.float32),
            bf16(head_rows, toks - KEYS_SEEN),
        ),
        n_in=8,
        scratch=[
            pltpu.VMEM(expert_ids.T.shape, jnp.int32),
            pltpu.VMEM(expert_ids.T.shape, jnp.float32),
            pltpu.SMEM(attention_sink_logits.shape, jnp.float32),
            pltpu.SemaphoreType.DMA((8,)),
        ],
        hbm=range(8),
        flops=4 * toks * SPAN * head_rows,
        moved=2 * (w_out.size + residual.size + queries.size),
    )(*(in_hbm(a) for a in (expert_ids.T, route_weights.T, attention_sink_logits, *loads)))
    attended, rows = call(
        second_kernel,
        (bf16(head_rows, toks), bf16(slots, head_rows)),
        n_in=7,
        flops=2 * toks * SPAN * head_rows,
        moved=2 * queries.size,
    )(q, kv, before, rim, sinks, late, placing)

    chip_rows = from_chips(rows)
    total = jax.ShapeDtypeStruct((slots, feats), jnp.float32)
    part = dict(flops=slots * w_out.size // 2, moved=w_out.size // 2)
    own = call(functools.partial(rows_own_kernel, steps), total, n_in=4, **part)(
        rows, w_t, residual_t, placing
    )
    sibling_rows = from_sibling(rows)
    places = [steps, *range(1, steps)]
    spread = functools.partial(
        call, spread_kernel, bf16(cuts, hidden, feats), n_in=1, moved=4 * w_gate.size
    )
    gates = spread()(after(w_gate[0].T, rows))
    chip_rows = after(chip_rows, (own, gates))
    relayed_rows = [from_sibling(b) for b in chip_rows]
    chips = call(functools.partial(rows_more_kernel, places, steps), total, n_in=steps + 2, **part)(
        sibling_rows, *chip_rows, own, w_t
    )
    outgoing = call(
        functools.partial(rows_last_kernel, steps),
        (bf16(CAP, feats),) * live,
        n_in=steps + 1,
        scratch=[pltpu.VMEM((live, CAP, feats), jnp.bfloat16)],
        **part,
    )(*relayed_rows, chips, w_t)

    arrived = [swap(outgoing[k], "seq", k) for k in range(live - 1, 0, -1)] + [outgoing[0]]

    ups = spread()(after(w_up[0].T, outgoing[0]))
    gains = call(spread_gain_kernel, jax.ShapeDtypeStruct((cuts, 1, feats), jnp.float32), n_in=1)(norm_gain)
    sums = (
        *(jax.ShapeDtypeStruct((slots, hidden), jnp.float32),) * 2,
        jax.ShapeDtypeStruct((slots, KEYS_SEEN), jnp.float32),
    )
    part = dict(flops=slots * w_gate.size, moved=w_gate.size)
    stacked = call(stack_kernel, bf16(slots, feats), n_in=live)(*after(arrived, (ups, gains)))
    chip_rows = from_chips(stacked)
    own = call(functools.partial(expert_own_kernel, steps), sums, n_in=4, **part)(stacked, gains, gates, ups)
    sibling_rows = from_sibling(stacked)
    downs = spread()(after(w_down[0], stacked))
    chip_blocks = from_chips(after(attended, outgoing[0]))
    blocks = [attended, *chip_blocks]
    blocks += [from_sibling(b) for b in after(blocks, stacked)]
    chip_rows = after(chip_rows, (own, downs))
    relayed_rows = [from_sibling(b) for b in chip_rows]
    chips = call(functools.partial(expert_more_kernel, places, steps), sums, n_in=steps + 6, **part)(
        sibling_rows, *chip_rows, *own, gains, gates, ups
    )
    given, activated = call(
        functools.partial(expert_last_kernel, steps),
        (bf16(steps, slots, feats), bf16(slots, hidden)),
        n_in=steps + 6,
        **part,
    )(*relayed_rows, *chips, gains, gates, ups, downs)
    kept = call(expert_kept_kernel, bf16(steps, slots, feats), n_in=2, **part)(activated, downs)
    resid = call(
        functools.partial(project_kernel, steps),
        bf16(feats, toks),
        n_in=cuts + 2,
        flops=2 * toks * w_out.size,
        moved=2 * w_out.size,
    )(*blocks, w_t, residual_t)

    sums = call(add_cores_kernel, (bf16(slots // 2, feats),) * (2 * steps), n_in=2)(
        kept, swap(given, "cuts", 1)
    )
    returned, added = [], []
    for half in range(2):
        parts = [sums[half]] + [swap(sums[2 * k + half], "cuts", CORES * k) for k in range(1, steps)]
        added = call(functools.partial(add_chips_kernel, steps), (bf16(CAP, feats),) * (live // 2), n_in=steps)(
            *after(parts, added)
        )
        for block in added:
            k = live - 1 - len(returned)
            returned.append(swap(block, "seq", k) if k else block)
    out = call(
        functools.partial(combine_kernel, live),
        bf16(feats, toks),
        n_in=live + 3,
        scratch=[pltpu.VMEM((live, CAP, feats), jnp.bfloat16)],
    )(*returned, mix_hi, mix_lo, resid)
    return out.T


def solution(mesh):
    placed = (
        P(("groups", "seq"), "cuts"),
        P(("groups", "seq"), "cuts"),
        P("groups", "cuts"),
        P("cuts"),
        P(("groups", "seq"), "cuts"),
        P(None, "cuts"),
        P(),
        P(("groups", "seq"), None),
        P(("groups", "seq"), None),
        P("seq", None, "cuts"),
        P("seq", None, "cuts"),
        P("seq", "cuts", None),
    )
    return jax.shard_map(
        shards, mesh=mesh, in_specs=placed, out_specs=P(("groups", "seq"), "cuts"), check_vma=False
    )
```

```python
import functools
import math

import jax
import jax.numpy as jnp
from jax import lax
from jax.experimental import pallas as pl
from jax.experimental.pallas import tpu as pltpu
from jax.sharding import PartitionSpec as P

HEAD_SIZE = 64
KEYS_SEEN = 128
PAIR = 2 * HEAD_SIZE
SPAN = 2 * KEYS_SEEN
CAP = 16
CORES = 2

norm_eps = 1e-05
glu_alpha = 1.702

NT = (((1,), (1,)), ((), ()))
NN = (((1,), (0,)), ((), ()))
TN = (((0,), (0,)), ((), ()))
VMEM_LIMIT = 32 * 1024 * 1024


def dot(a, b, dims):
    return lax.dot_general(a, b, dims, preferred_element_type=jnp.float32)


def call(kernel, outs, n_in, scratch=(), hbm=(), smem=(), flops=0, moved=0):
    spaces = [pltpu.HBM if i in hbm else pltpu.SMEM if i in smem else pltpu.VMEM for i in range(n_in)]
    return pl.pallas_call(
        kernel,
        out_shape=outs,
        in_specs=[pl.BlockSpec(memory_space=space) for space in spaces],
        out_specs=jax.tree.map(lambda _: pl.BlockSpec(memory_space=pltpu.VMEM), outs),
        scratch_shapes=list(scratch),
        compiler_params=pltpu.CompilerParams(vmem_limit_bytes=VMEM_LIMIT),
        cost_estimate=pl.CostEstimate(flops=flops, bytes_accessed=moved, transcendentals=0),
    )


def in_hbm(array):
    return pltpu.with_memory_space_constraint(array, pltpu.HBM)


def bf16(*shape):
    return jax.ShapeDtypeStruct(shape, jnp.bfloat16)


def split_pair(both):
    both = both.astype(jnp.float32)
    low = lax.broadcasted_iota(jnp.int32, both.shape, 1) < HEAD_SIZE
    turned = pltpu.roll(both, HEAD_SIZE, 1)
    keys = jnp.concatenate([jnp.where(low, both, 0.0), jnp.where(low, 0.0, turned)], axis=0)
    values = jnp.concatenate([jnp.where(low, turned, 0.0), jnp.where(low, 0.0, both)], axis=0)
    return keys.astype(jnp.bfloat16), values.astype(jnp.bfloat16)


def score(pairs, keys, allowed):
    scores = dot(keys, jnp.concatenate(pairs, axis=0), NT) * (HEAD_SIZE**-0.5 * math.log2(math.e))
    allowed = jnp.concatenate([allowed] * len(pairs), axis=1)
    span = allowed.shape[0]
    return [jnp.where(allowed, scores[i * span : (i + 1) * span], -jnp.inf) for i in range(2)]


def sink_row(sinks, i, pairs):
    return jnp.concatenate([sinks[2 * p + i] for p in range(pairs)], axis=1)


def attend_block(pairs, both, sinks, allowed):
    keys, values = split_pair(both)
    probs = []
    for i, part in enumerate(score(pairs, keys, allowed)):
        sink = sink_row(sinks, i, len(pairs))
        peak = jnp.maximum(jnp.max(part, axis=0, keepdims=True), sink)
        terms = jnp.exp2(part - peak)
        denom = jnp.sum(terms, axis=0, keepdims=True) + jnp.exp2(sink - peak)
        probs.append((terms * (1.0 / denom)).astype(jnp.bfloat16))
    return dot(values, jnp.concatenate(probs, axis=0), TN).astype(jnp.bfloat16)


def group_queries(q_ref, g, groups, block):
    per_group = q_ref.shape[1] // PAIR // groups
    first = g * per_group
    toks = slice(block * KEYS_SEEN, (block + 1) * KEYS_SEEN)
    pairs = [q_ref[toks, (first + p) * PAIR : (first + p + 1) * PAIR] for p in range(per_group)]
    return first, pairs


def store_pairs(mixed, first, out_ref, lanes):
    for p in range(mixed.shape[1] // KEYS_SEEN):
        rows = slice((first + p) * PAIR, (first + p + 1) * PAIR)
        out_ref[rows, lanes] = mixed[:, p * KEYS_SEEN : (p + 1) * KEYS_SEEN]


def key_query(span):
    key = lax.broadcasted_iota(jnp.int32, (span, KEYS_SEEN), 0)
    return key, lax.broadcasted_iota(jnp.int32, (span, KEYS_SEEN), 1)


def per_head(pair):
    return jnp.concatenate([jnp.broadcast_to(row, (HEAD_SIZE, row.shape[1])) for row in pair], axis=0)


def fill_tables(live, ids, weights, placing_ref, mix_hi_ref, mix_lo_ref):
    toks = ids.shape[1]
    chosen = jnp.concatenate(
        [jnp.max((ids == e).astype(jnp.float32), axis=0, keepdims=True) for e in range(live)], axis=0
    )
    earlier = lax.broadcasted_iota(jnp.int32, (toks, toks), 0)
    later = lax.broadcasted_iota(jnp.int32, (toks, toks), 1)
    strict = (earlier < later).astype(jnp.bfloat16)
    before = dot(chosen.astype(jnp.bfloat16), strict, NN)
    slot = lax.broadcasted_iota(jnp.int32, (CAP, toks), 0).astype(jnp.float32)
    for e in range(live):
        weight = jnp.sum(jnp.where(ids == e, weights, 0.0), axis=0, keepdims=True)
        fills = (before[e : e + 1] == slot) & (chosen[e : e + 1] > 0.0)
        mix = jnp.where(fills, weight, 0.0)
        hi = mix.astype(jnp.bfloat16)
        rows = slice(e * CAP, (e + 1) * CAP)
        placing_ref[rows] = fills.astype(jnp.bfloat16)
        mix_hi_ref[rows] = hi
        mix_lo_ref[rows] = (mix - hi.astype(jnp.float32)).astype(jnp.bfloat16)


def first_kernel(live, *refs):
    loaded, held = refs[:8], refs[8:13]
    placing_ref, mix_hi_ref, mix_lo_ref, sinks_out, late_ref, rows_ref, mixed_ref, peaks_ref, sums_ref = refs[13:22]
    ids_ref, weights_ref, sinks_ref, sems = refs[22:]
    targets = (ids_ref, weights_ref, sinks_ref, *held)
    copies = [pltpu.make_async_copy(*pair, sems.at[i]) for i, pair in enumerate(zip(loaded, targets))]
    for copy in copies:
        copy.start()
    q_ref, kv_ref = held[:2]
    for copy in copies[:2]:
        copy.wait()
    fill_tables(live, ids_ref[...], weights_ref[...], placing_ref, mix_hi_ref, mix_lo_ref)
    for copy in copies[2:5]:
        copy.wait()
    heads = sinks_ref.shape[0]
    sinks = [jnp.full((1, KEYS_SEEN), sinks_ref[h], jnp.float32) * math.log2(math.e) for h in range(heads)]
    sinks_out[...] = jnp.concatenate(sinks, axis=0)
    groups = kv_ref.shape[1] // PAIR
    key, query = key_query(SPAN)
    allowed = (key > query) & (key <= query + KEYS_SEEN)
    for b in range(1, q_ref.shape[0] // KEYS_SEEN):
        span = slice((b - 1) * KEYS_SEEN, (b + 1) * KEYS_SEEN)
        for g in range(groups):
            first, pairs = group_queries(q_ref, g, groups, b)
            part = sinks[2 * first : 2 * (first + len(pairs))]
            mixed = attend_block(pairs, kv_ref[span, g * PAIR : (g + 1) * PAIR], part, allowed)
            store_pairs(mixed, first, late_ref, slice((b - 1) * KEYS_SEEN, b * KEYS_SEEN))
    key, query = key_query(KEYS_SEEN)
    for g in range(groups):
        _, pairs = group_queries(q_ref, g, groups, 0)
        keys, values = split_pair(kv_ref[:KEYS_SEEN, g * PAIR : (g + 1) * PAIR])
        terms = []
        for i, part in enumerate(score(pairs, keys, key <= query)):
            peak = jnp.max(part, axis=0, keepdims=True)
            terms.append(jnp.exp2(part - peak))
            peaks_ref[2 * g + i : 2 * g + i + 1] = peak
            sums_ref[2 * g + i : 2 * g + i + 1] = jnp.sum(terms[-1], axis=0, keepdims=True)
        mixed_ref[g] = dot(values, jnp.concatenate(terms, axis=0).astype(jnp.bfloat16), TN)
    rows_ref[...] = dot(placing_ref[:, KEYS_SEEN:], late_ref[...], NT)
    for copy in copies[5:]:
        copy.wait()


def second_kernel(q_ref, before_ref, rim_ref, sinks_ref, late_ref, placing_ref, *refs):
    late_rows_ref, mixed_ref, peaks_ref, sums_ref, all_ref, rows_ref = refs
    rim = jnp.where(lax.axis_index("seq") == 0, before_ref[...], rim_ref[...])
    groups = mixed_ref.shape[0]
    key, query = key_query(KEYS_SEEN)
    for g in range(groups):
        first, pairs = group_queries(q_ref, g, groups, 0)
        sinks = [sinks_ref[h : h + 1] for h in range(2 * first, 2 * (first + len(pairs)))]
        keys, values = split_pair(rim[:, g * PAIR : (g + 1) * PAIR])
        terms, scales, inverses = [], [], []
        for i, part in enumerate(score(pairs, keys, key > query)):
            sink = sink_row(sinks, i, len(pairs))
            own_peak = peaks_ref[2 * g + i : 2 * g + i + 1]
            peak = jnp.maximum(jnp.max(part, axis=0, keepdims=True), jnp.maximum(own_peak, sink))
            scale = jnp.exp2(own_peak - peak)
            terms.append(jnp.exp2(part - peak))
            denom = jnp.sum(terms[-1], axis=0, keepdims=True) + jnp.exp2(sink - peak)
            denom += sums_ref[2 * g + i : 2 * g + i + 1] * scale
            inverses.append(1.0 / denom)
            scales.append(scale)
        mixed = dot(values, jnp.concatenate(terms, axis=0).astype(jnp.bfloat16), TN)
        mixed = (mixed + mixed_ref[g] * per_head(scales)) * per_head(inverses)
        store_pairs(mixed.astype(jnp.bfloat16), first, all_ref, slice(0, KEYS_SEEN))
    rows = late_rows_ref[...] + dot(placing_ref[:, :KEYS_SEEN], all_ref[:, :KEYS_SEEN], NT)
    rows_ref[...] = rows.astype(jnp.bfloat16)
    all_ref[:, KEYS_SEEN:] = late_ref[...]


def origin(k, sibling):
    me = lax.axis_index("cuts")
    return lax.bitwise_xor(me, CORES * k + (1 if sibling else 0))


def add_products(total, places, blocks, w_ref, steps, dims, swapped=False):
    width = blocks[0].shape[0 if swapped else 1] if blocks else 0
    for i, block in zip(places, blocks):
        at = pl.multiple_of(origin(i % steps, i >= steps) * width, 128)
        w = w_ref[:, pl.ds(at, width)]
        total += dot(w, block[...], dims) if swapped else dot(block[...], w, dims)
    return total


def rows_own_kernel(steps, rows_ref, w_ref, residual_ref, placing_ref, total_ref):
    total = dot(placing_ref[...], residual_ref[...], NT)
    total_ref[...] = add_products(total, [0], [rows_ref], w_ref, steps, NT)


def rows_more_kernel(places, steps, *refs):
    blocks, (before_ref, w_ref, total_ref) = refs[:-3], refs[-3:]
    total_ref[...] = add_products(before_ref[...], places, blocks, w_ref, steps, NT)


def rows_last_kernel(steps, *refs):
    blocks, (before_ref, w_ref) = refs[: steps - 1], refs[steps - 1 : steps + 1]
    outgoing, rows_ref = refs[steps + 1 : -1], refs[-1]
    total = add_products(before_ref[...], range(steps + 1, 2 * steps), blocks, w_ref, steps, NT)
    rows_ref[...] = total.astype(jnp.bfloat16).reshape(rows_ref.shape)
    me = lax.axis_index("seq")
    for k, out_ref in enumerate(outgoing):
        out_ref[...] = rows_ref[lax.bitwise_xor(me, k)]


def stack_kernel(*refs):
    for i, block in enumerate(refs[:-1]):
        refs[-1][i * CAP : (i + 1) * CAP] = block[...]


def project_kernel(steps, *refs):
    blocks = refs[: 2 * steps]
    w_ref, residual_ref, resid_ref = refs[2 * steps :]
    total = residual_ref[...].astype(jnp.float32)
    total = add_products(total, range(2 * steps), blocks, w_ref, steps, NN, True)
    resid_ref[...] = total.astype(jnp.bfloat16)


def spread_kernel(source_ref, blocks_ref):
    cuts, _, width = blocks_ref.shape
    for p in range(cuts):
        blocks_ref[p] = source_ref[:, p * width : (p + 1) * width]


def spread_gain_kernel(gain_ref, blocks_ref):
    cuts, _, width = blocks_ref.shape
    gain = gain_ref[...].reshape(1, cuts * width)
    for p in range(cuts):
        blocks_ref[p] = gain[:, p * width : (p + 1) * width]


def add_features(sums, places, blocks, gains_ref, gates_ref, ups_ref, steps):
    gate, up, squares = sums
    for i, block in zip(places, blocks):
        p = origin(i % steps, i >= steps)
        wide = block[...].astype(jnp.float32)
        squares += jnp.sum(wide * wide, axis=1, keepdims=True)
        rows = (wide * gains_ref[p]).astype(jnp.bfloat16)
        gate += dot(rows, gates_ref[p], NT)
        up += dot(rows, ups_ref[p], NT)
    return gate, up, squares


def store_sums(sums, refs):
    for ref, value in zip(refs, sums):
        ref[...] = jnp.broadcast_to(value, ref.shape)


def expert_own_kernel(steps, block_ref, gains_ref, gates_ref, ups_ref, *out_refs):
    zeros = jnp.zeros(out_refs[0].shape, jnp.float32)
    sums = (zeros, zeros, jnp.zeros((zeros.shape[0], 1), jnp.float32))
    store_sums(add_features(sums, [0], [block_ref], gains_ref, gates_ref, ups_ref, steps), out_refs)


def expert_more_kernel(places, steps, *refs):
    blocks, refs = refs[:-9], refs[-9:]
    sums = (refs[0][...], refs[1][...], refs[2][:, :1])
    store_sums(add_features(sums, places, blocks, *refs[3:6], steps), refs[6:])


def expert_last_kernel(steps, *refs):
    blocks, refs = refs[: steps - 1], refs[steps - 1 :]
    sums = (refs[0][...], refs[1][...], refs[2][:, :1])
    gains_ref, gates_ref, ups_ref, downs_ref, given_ref, activated_ref = refs[3:]
    places = range(steps + 1, 2 * steps)
    gate, up, squares = add_features(sums, places, blocks, gains_ref, gates_ref, ups_ref, steps)
    cuts, _, width = gates_ref.shape
    scale = lax.rsqrt(squares / (cuts * width) + norm_eps)
    gate, up = gate * scale, up * scale
    activated = ((up + 1.0) * gate * jax.nn.sigmoid(glu_alpha * gate)).astype(jnp.bfloat16)
    activated_ref[...] = activated
    for k in range(steps):
        given_ref[k] = dot(activated, downs_ref[origin(k, True)], NN).astype(jnp.bfloat16)


def expert_kept_kernel(activated_ref, downs_ref, kept_ref):
    for k in range(kept_ref.shape[0]):
        kept_ref[k] = dot(activated_ref[...], downs_ref[origin(k, False)], NN).astype(jnp.bfloat16)


def add_cores_kernel(kept_ref, given_ref, *out_refs):
    half = out_refs[0].shape[0]
    for i, out_ref in enumerate(out_refs):
        rows = slice(i % 2 * half, (i % 2 + 1) * half)
        total = kept_ref[i // 2, rows].astype(jnp.float32) + given_ref[i // 2, rows].astype(jnp.float32)
        out_ref[...] = total.astype(jnp.bfloat16)


def add_chips_kernel(steps, *refs):
    total = sum(r[...].astype(jnp.float32) for r in refs[:steps])
    for k, out_ref in enumerate(refs[steps:]):
        out_ref[...] = total[k * CAP : (k + 1) * CAP].astype(jnp.bfloat16)


def combine_kernel(live, *refs):
    blocks = refs[:live]
    mix_hi_ref, mix_lo_ref, resid_ref, out_ref, rows_ref = refs[live:]
    me = lax.axis_index("seq")
    for k in range(live):
        rows_ref[lax.bitwise_xor(me, live - 1 - k)] = blocks[k][...]
    rows = rows_ref[...].reshape(live * CAP, -1)
    mixed = dot(rows, mix_hi_ref[...], TN) + dot(rows, mix_lo_ref[...], TN)
    out_ref[...] = (resid_ref[...].astype(jnp.float32) + mixed).astype(jnp.bfloat16)


def swap(block, axis, mask):
    return lax.ppermute(block, axis, [(i, i ^ mask) for i in range(lax.axis_size(axis))])


def from_chips(block):
    return [swap(block, "cuts", CORES * k) for k in range(1, lax.axis_size("cuts") // CORES)]


def from_sibling(block):
    return swap(block, "cuts", 1)


def after(arrays, others):
    return lax.optimization_barrier((arrays, others))[0]


def shards(
    queries,
    keyvals,
    preceding_keyvalues,
    attention_sink_logits,
    residual,
    w_out,
    norm_gain,
    expert_ids,
    route_weights,
    w_gate,
    w_up,
    w_down,
):
    toks, feats = residual.shape
    size = lax.axis_size("seq")
    live = w_gate.shape[0] * size
    cuts = lax.axis_size("cuts")
    steps = cuts // CORES
    slots = live * CAP
    head_rows = queries.shape[1]
    heads = head_rows // HEAD_SIZE
    width = norm_gain.shape[0]
    hidden = w_gate.shape[2]

    tail = keyvals[toks - KEYS_SEEN :]
    rim = lax.ppermute(tail, "seq", [(i, (i + 1) % size) for i in range(size)])
    loads = (queries, keyvals, preceding_keyvalues, w_out.T, residual.T)
    groups = keyvals.shape[1] // PAIR
    across = head_rows // PAIR // groups * KEYS_SEEN
    part_sums = jax.ShapeDtypeStruct((2 * groups, across), jnp.float32)
    q, _, before, w_t, residual_t, placing, mix_hi, mix_lo, sinks, late, *parts = call(
        functools.partial(first_kernel, live),
        (
            *(bf16(*a.shape) for a in loads),
            *(bf16(slots, toks),) * 3,
            jax.ShapeDtypeStruct((heads, KEYS_SEEN), jnp.float32),
            bf16(head_rows, toks - KEYS_SEEN),
            jax.ShapeDtypeStruct((slots, head_rows), jnp.float32),
            jax.ShapeDtypeStruct((groups, PAIR, across), jnp.float32),
            part_sums,
            part_sums,
        ),
        n_in=8,
        scratch=[
            pltpu.VMEM(expert_ids.T.shape, jnp.int32),
            pltpu.VMEM(expert_ids.T.shape, jnp.float32),
            pltpu.SMEM(attention_sink_logits.shape, jnp.float32),
            pltpu.SemaphoreType.DMA((8,)),
        ],
        hbm=range(8),
        flops=4 * toks * SPAN * head_rows,
        moved=2 * (w_out.size + residual.size + queries.size),
    )(*(in_hbm(a) for a in (expert_ids.T, route_weights.T, attention_sink_logits, *loads)))
    attended, rows = call(
        second_kernel,
        (bf16(head_rows, toks), bf16(slots, head_rows)),
        n_in=10,
        flops=2 * toks * SPAN * head_rows,
        moved=2 * queries.size,
    )(q, before, rim, sinks, late, placing, *parts)

    chip_rows = from_chips(rows)
    total = jax.ShapeDtypeStruct((slots, feats), jnp.float32)
    part = dict(flops=slots * w_out.size // 2, moved=w_out.size // 2)
    own = call(functools.partial(rows_own_kernel, steps), total, n_in=4, **part)(
        rows, w_t, residual_t, placing
    )
    sibling_rows = from_sibling(rows)
    places = [steps, *range(1, steps)]
    spread = functools.partial(
        call, spread_kernel, bf16(cuts, hidden, feats), n_in=1, moved=4 * w_gate.size
    )
    gates = spread()(after(w_gate[0].T, rows))
    chip_rows = after(chip_rows, (own, gates))
    relayed_rows = [from_sibling(b) for b in chip_rows]
    chips = call(functools.partial(rows_more_kernel, places, steps), total, n_in=steps + 2, **part)(
        sibling_rows, *chip_rows, own, w_t
    )
    outgoing = call(
        functools.partial(rows_last_kernel, steps),
        (bf16(CAP, feats),) * live,
        n_in=steps + 1,
        scratch=[pltpu.VMEM((live, CAP, feats), jnp.bfloat16)],
        **part,
    )(*relayed_rows, chips, w_t)

    arrived = [swap(outgoing[k], "seq", k) for k in range(live - 1, 0, -1)] + [outgoing[0]]

    ups = spread()(after(w_up[0].T, outgoing[0]))
    gains = call(spread_gain_kernel, jax.ShapeDtypeStruct((cuts, 1, feats), jnp.float32), n_in=1)(norm_gain)
    sums = (
        *(jax.ShapeDtypeStruct((slots, hidden), jnp.float32),) * 2,
        jax.ShapeDtypeStruct((slots, KEYS_SEEN), jnp.float32),
    )
    part = dict(flops=slots * w_gate.size, moved=w_gate.size)
    stacked = call(stack_kernel, bf16(slots, feats), n_in=live)(*after(arrived, (ups, gains)))
    chip_rows = from_chips(stacked)
    own = call(functools.partial(expert_own_kernel, steps), sums, n_in=4, **part)(stacked, gains, gates, ups)
    sibling_rows = from_sibling(stacked)
    downs = spread()(after(w_down[0], stacked))
    chip_blocks = from_chips(after(attended, gates))
    blocks = [attended, *chip_blocks]
    blocks += [from_sibling(b) for b in blocks]
    chip_rows = after(chip_rows, (own, downs))
    relayed_rows = [from_sibling(b) for b in chip_rows]
    chips = call(functools.partial(expert_more_kernel, places, steps), sums, n_in=steps + 6, **part)(
        sibling_rows, *chip_rows, *own, gains, gates, ups
    )
    given, activated = call(
        functools.partial(expert_last_kernel, steps),
        (bf16(steps, slots, feats), bf16(slots, hidden)),
        n_in=steps + 6,
        **part,
    )(*relayed_rows, *chips, gains, gates, ups, downs)
    kept = call(expert_kept_kernel, bf16(steps, slots, feats), n_in=2, **part)(activated, downs)
    resid = call(
        functools.partial(project_kernel, steps),
        bf16(feats, toks),
        n_in=cuts + 2,
        flops=2 * toks * w_out.size,
        moved=2 * w_out.size,
    )(*blocks, w_t, residual_t)

    sums = call(add_cores_kernel, (bf16(slots // 2, feats),) * (2 * steps), n_in=2)(
        kept, swap(given, "cuts", 1)
    )
    returned = []
    for half in range(2):
        parts = [sums[half]] + [swap(sums[2 * k + half], "cuts", CORES * k) for k in range(1, steps)]
        blocks = call(functools.partial(add_chips_kernel, steps), (bf16(CAP, feats),) * (live // 2), n_in=steps)(
            *parts
        )
        for block in blocks:
            k = live - 1 - len(returned)
            returned.append(swap(block, "seq", k) if k else block)
    out = call(
        functools.partial(combine_kernel, live),
        bf16(feats, toks),
        n_in=live + 3,
        scratch=[pltpu.VMEM((live, CAP, feats), jnp.bfloat16)],
    )(*returned, mix_hi, mix_lo, resid)
    return out.T


def solution(mesh):
    placed = (
        P(("groups", "seq"), "cuts"),
        P(("groups", "seq"), "cuts"),
        P("groups", "cuts"),
        P("cuts"),
        P(("groups", "seq"), "cuts"),
        P(None, "cuts"),
        P(),
        P(("groups", "seq"), None),
        P(("groups", "seq"), None),
        P("seq", None, "cuts"),
        P("seq", None, "cuts"),
        P("seq", "cuts", None),
    )
    return jax.shard_map(
        shards, mesh=mesh, in_specs=placed, out_specs=P(("groups", "seq"), "cuts"), check_vma=False
    )
```

```python
import functools
import math

import jax
import jax.numpy as jnp
from jax import lax
from jax.experimental import pallas as pl
from jax.experimental.pallas import tpu as pltpu
from jax.sharding import PartitionSpec as P

HEAD_SIZE = 64
KEYS_SEEN = 128
PAIR = 2 * HEAD_SIZE
SPAN = 2 * KEYS_SEEN
CAP = 16
CORES = 2

norm_eps = 1e-05
glu_alpha = 1.702

NT = (((1,), (1,)), ((), ()))
NN = (((1,), (0,)), ((), ()))
TN = (((0,), (0,)), ((), ()))
VMEM_LIMIT = 32 * 1024 * 1024


def dot(a, b, dims):
    return lax.dot_general(a, b, dims, preferred_element_type=jnp.float32)


def call(kernel, outs, n_in, scratch=(), hbm=(), smem=(), flops=0, moved=0):
    spaces = [pltpu.HBM if i in hbm else pltpu.SMEM if i in smem else pltpu.VMEM for i in range(n_in)]
    return pl.pallas_call(
        kernel,
        out_shape=outs,
        in_specs=[pl.BlockSpec(memory_space=space) for space in spaces],
        out_specs=jax.tree.map(lambda _: pl.BlockSpec(memory_space=pltpu.VMEM), outs),
        scratch_shapes=list(scratch),
        compiler_params=pltpu.CompilerParams(vmem_limit_bytes=VMEM_LIMIT),
        cost_estimate=pl.CostEstimate(flops=flops, bytes_accessed=moved, transcendentals=0),
    )


def in_hbm(array):
    return pltpu.with_memory_space_constraint(array, pltpu.HBM)


def bf16(*shape):
    return jax.ShapeDtypeStruct(shape, jnp.bfloat16)


def split_pair(both):
    both = both.astype(jnp.float32)
    low = lax.broadcasted_iota(jnp.int32, both.shape, 1) < HEAD_SIZE
    turned = pltpu.roll(both, HEAD_SIZE, 1)
    keys = jnp.concatenate([jnp.where(low, both, 0.0), jnp.where(low, 0.0, turned)], axis=0)
    values = jnp.concatenate([jnp.where(low, turned, 0.0), jnp.where(low, 0.0, both)], axis=0)
    return keys.astype(jnp.bfloat16), values.astype(jnp.bfloat16)


def score(pairs, keys, allowed):
    scores = dot(keys, jnp.concatenate(pairs, axis=0), NT) * (HEAD_SIZE**-0.5 * math.log2(math.e))
    allowed = jnp.concatenate([allowed] * len(pairs), axis=1)
    span = allowed.shape[0]
    return [jnp.where(allowed, scores[i * span : (i + 1) * span], -jnp.inf) for i in range(2)]


def sink_row(sinks, i, pairs):
    return jnp.concatenate([sinks[2 * p + i] for p in range(pairs)], axis=1)


def attend_block(pairs, both, sinks, allowed):
    keys, values = split_pair(both)
    probs = []
    for i, part in enumerate(score(pairs, keys, allowed)):
        sink = sink_row(sinks, i, len(pairs))
        peak = jnp.maximum(jnp.max(part, axis=0, keepdims=True), sink)
        terms = jnp.exp2(part - peak)
        denom = jnp.sum(terms, axis=0, keepdims=True) + jnp.exp2(sink - peak)
        probs.append((terms * (1.0 / denom)).astype(jnp.bfloat16))
    return dot(values, jnp.concatenate(probs, axis=0), TN).astype(jnp.bfloat16)


def group_queries(q_ref, g, groups, block):
    per_group = q_ref.shape[1] // PAIR // groups
    first = g * per_group
    toks = slice(block * KEYS_SEEN, (block + 1) * KEYS_SEEN)
    pairs = [q_ref[toks, (first + p) * PAIR : (first + p + 1) * PAIR] for p in range(per_group)]
    return first, pairs


def store_pairs(mixed, first, out_ref, lanes):
    for p in range(mixed.shape[1] // KEYS_SEEN):
        rows = slice((first + p) * PAIR, (first + p + 1) * PAIR)
        out_ref[rows, lanes] = mixed[:, p * KEYS_SEEN : (p + 1) * KEYS_SEEN]


def key_query(span):
    key = lax.broadcasted_iota(jnp.int32, (span, KEYS_SEEN), 0)
    return key, lax.broadcasted_iota(jnp.int32, (span, KEYS_SEEN), 1)


def per_head(pair):
    return jnp.concatenate([jnp.broadcast_to(row, (HEAD_SIZE, row.shape[1])) for row in pair], axis=0)


def fill_tables(live, ids, weights, placing_ref, mix_hi_ref, mix_lo_ref):
    toks = ids.shape[1]
    chosen = jnp.concatenate(
        [jnp.max((ids == e).astype(jnp.float32), axis=0, keepdims=True) for e in range(live)], axis=0
    )
    earlier = lax.broadcasted_iota(jnp.int32, (toks, toks), 0)
    later = lax.broadcasted_iota(jnp.int32, (toks, toks), 1)
    strict = (earlier < later).astype(jnp.bfloat16)
    before = dot(chosen.astype(jnp.bfloat16), strict, NN)
    slot = lax.broadcasted_iota(jnp.int32, (CAP, toks), 0).astype(jnp.float32)
    for e in range(live):
        weight = jnp.sum(jnp.where(ids == e, weights, 0.0), axis=0, keepdims=True)
        fills = (before[e : e + 1] == slot) & (chosen[e : e + 1] > 0.0)
        mix = jnp.where(fills, weight, 0.0)
        hi = mix.astype(jnp.bfloat16)
        rows = slice(e * CAP, (e + 1) * CAP)
        placing_ref[rows] = fills.astype(jnp.bfloat16)
        mix_hi_ref[rows] = hi
        mix_lo_ref[rows] = (mix - hi.astype(jnp.float32)).astype(jnp.bfloat16)


def first_kernel(live, *refs):
    loaded, held = refs[:8], refs[8:13]
    placing_ref, mix_hi_ref, mix_lo_ref, sinks_out, late_ref, rows_ref, mixed_ref, peaks_ref, sums_ref = refs[13:22]
    ids_ref, weights_ref, sinks_ref, sems = refs[22:]
    targets = (ids_ref, weights_ref, sinks_ref, *held)
    copies = [pltpu.make_async_copy(*pair, sems.at[i]) for i, pair in enumerate(zip(loaded, targets))]
    for copy in copies:
        copy.start()
    q_ref, kv_ref = held[:2]
    for copy in copies[:2]:
        copy.wait()
    fill_tables(live, ids_ref[...], weights_ref[...], placing_ref, mix_hi_ref, mix_lo_ref)
    for copy in copies[2:5]:
        copy.wait()
    heads = sinks_ref.shape[0]
    sinks = [jnp.full((1, KEYS_SEEN), sinks_ref[h], jnp.float32) * math.log2(math.e) for h in range(heads)]
    sinks_out[...] = jnp.concatenate(sinks, axis=0)
    groups = kv_ref.shape[1] // PAIR
    key, query = key_query(SPAN)
    allowed = (key > query) & (key <= query + KEYS_SEEN)
    for b in range(1, q_ref.shape[0] // KEYS_SEEN):
        span = slice((b - 1) * KEYS_SEEN, (b + 1) * KEYS_SEEN)
        for g in range(groups):
            first, pairs = group_queries(q_ref, g, groups, b)
            part = sinks[2 * first : 2 * (first + len(pairs))]
            mixed = attend_block(pairs, kv_ref[span, g * PAIR : (g + 1) * PAIR], part, allowed)
            store_pairs(mixed, first, late_ref, slice((b - 1) * KEYS_SEEN, b * KEYS_SEEN))
    key, query = key_query(KEYS_SEEN)
    for g in range(groups):
        _, pairs = group_queries(q_ref, g, groups, 0)
        keys, values = split_pair(kv_ref[:KEYS_SEEN, g * PAIR : (g + 1) * PAIR])
        terms = []
        for i, part in enumerate(score(pairs, keys, key <= query)):
            peak = jnp.max(part, axis=0, keepdims=True)
            terms.append(jnp.exp2(part - peak))
            peaks_ref[2 * g + i : 2 * g + i + 1] = peak
            sums_ref[2 * g + i : 2 * g + i + 1] = jnp.sum(terms[-1], axis=0, keepdims=True)
        mixed_ref[g] = dot(values, jnp.concatenate(terms, axis=0).astype(jnp.bfloat16), TN)
    rows_ref[...] = dot(placing_ref[:, KEYS_SEEN:], late_ref[...], NT)
    for copy in copies[5:]:
        copy.wait()


def second_kernel(q_ref, before_ref, rim_ref, sinks_ref, late_ref, placing_ref, *refs):
    late_rows_ref, mixed_ref, peaks_ref, sums_ref, all_ref, rows_ref = refs
    rim = jnp.where(lax.axis_index("seq") == 0, before_ref[...], rim_ref[...])
    groups = mixed_ref.shape[0]
    key, query = key_query(KEYS_SEEN)
    for g in range(groups):
        first, pairs = group_queries(q_ref, g, groups, 0)
        sinks = [sinks_ref[h : h + 1] for h in range(2 * first, 2 * (first + len(pairs)))]
        keys, values = split_pair(rim[:, g * PAIR : (g + 1) * PAIR])
        terms, scales, inverses = [], [], []
        for i, part in enumerate(score(pairs, keys, key > query)):
            sink = sink_row(sinks, i, len(pairs))
            own_peak = peaks_ref[2 * g + i : 2 * g + i + 1]
            peak = jnp.maximum(jnp.max(part, axis=0, keepdims=True), jnp.maximum(own_peak, sink))
            scale = jnp.exp2(own_peak - peak)
            terms.append(jnp.exp2(part - peak))
            denom = jnp.sum(terms[-1], axis=0, keepdims=True) + jnp.exp2(sink - peak)
            denom += sums_ref[2 * g + i : 2 * g + i + 1] * scale
            inverses.append(1.0 / denom)
            scales.append(scale)
        mixed = dot(values, jnp.concatenate(terms, axis=0).astype(jnp.bfloat16), TN)
        mixed = (mixed + mixed_ref[g] * per_head(scales)) * per_head(inverses)
        store_pairs(mixed.astype(jnp.bfloat16), first, all_ref, slice(0, KEYS_SEEN))
    rows = late_rows_ref[...] + dot(placing_ref[:, :KEYS_SEEN], all_ref[:, :KEYS_SEEN], NT)
    rows_ref[...] = rows.astype(jnp.bfloat16)
    all_ref[:, KEYS_SEEN:] = late_ref[...]


def origin(k, sibling):
    me = lax.axis_index("cuts")
    return lax.bitwise_xor(me, CORES * k + (1 if sibling else 0))


def add_products(total, places, blocks, w_ref, steps, dims, swapped=False):
    width = blocks[0].shape[0 if swapped else 1] if blocks else 0
    for i, block in zip(places, blocks):
        at = pl.multiple_of(origin(i % steps, i >= steps) * width, 128)
        w = w_ref[:, pl.ds(at, width)]
        total += dot(w, block[...], dims) if swapped else dot(block[...], w, dims)
    return total


def rows_own_kernel(steps, rows_ref, w_ref, residual_ref, placing_ref, total_ref):
    total = dot(placing_ref[...], residual_ref[...], NT)
    total_ref[...] = add_products(total, [0], [rows_ref], w_ref, steps, NT)


def rows_more_kernel(places, steps, *refs):
    blocks, (before_ref, w_ref, total_ref) = refs[:-3], refs[-3:]
    total_ref[...] = add_products(before_ref[...], places, blocks, w_ref, steps, NT)


def rows_last_kernel(steps, *refs):
    blocks, (before_ref, w_ref) = refs[: steps - 1], refs[steps - 1 : steps + 1]
    outgoing, rows_ref = refs[steps + 1 : -1], refs[-1]
    total = add_products(before_ref[...], range(1, steps), blocks, w_ref, steps, NT)
    rows_ref[...] = total.astype(jnp.bfloat16).reshape(rows_ref.shape)
    me = lax.axis_index("seq")
    for k, out_ref in enumerate(outgoing):
        out_ref[...] = rows_ref[lax.bitwise_xor(me, k)]


def stack_kernel(*refs):
    for i, block in enumerate(refs[:-1]):
        refs[-1][i * CAP : (i + 1) * CAP] = block[...]


def project_kernel(steps, *refs):
    blocks = refs[: 2 * steps]
    w_ref, residual_ref, resid_ref = refs[2 * steps :]
    total = residual_ref[...].astype(jnp.float32)
    total = add_products(total, range(2 * steps), blocks, w_ref, steps, NN, True)
    resid_ref[...] = total.astype(jnp.bfloat16)


def spread_kernel(source_ref, blocks_ref):
    cuts, _, width = blocks_ref.shape
    for p in range(cuts):
        blocks_ref[p] = source_ref[:, p * width : (p + 1) * width]


def spread_gain_kernel(gain_ref, blocks_ref):
    cuts, _, width = blocks_ref.shape
    gain = gain_ref[...].reshape(1, cuts * width)
    for p in range(cuts):
        blocks_ref[p] = gain[:, p * width : (p + 1) * width]


def add_features(sums, places, blocks, gains_ref, gates_ref, ups_ref, steps):
    gate, up, squares = sums
    for i, block in zip(places, blocks):
        p = origin(i % steps, i >= steps)
        wide = block[...].astype(jnp.float32)
        squares += jnp.sum(wide * wide, axis=1, keepdims=True)
        rows = (wide * gains_ref[p]).astype(jnp.bfloat16)
        gate += dot(rows, gates_ref[p], NT)
        up += dot(rows, ups_ref[p], NT)
    return gate, up, squares


def store_sums(sums, refs):
    for ref, value in zip(refs, sums):
        ref[...] = jnp.broadcast_to(value, ref.shape)


def expert_own_kernel(steps, block_ref, gains_ref, gates_ref, ups_ref, *out_refs):
    zeros = jnp.zeros(out_refs[0].shape, jnp.float32)
    sums = (zeros, zeros, jnp.zeros((zeros.shape[0], 1), jnp.float32))
    store_sums(add_features(sums, [steps], [block_ref], gains_ref, gates_ref, ups_ref, steps), out_refs)


def expert_more_kernel(places, steps, *refs):
    blocks, refs = refs[:-9], refs[-9:]
    sums = (refs[0][...], refs[1][...], refs[2][:, :1])
    store_sums(add_features(sums, places, blocks, *refs[3:6], steps), refs[6:])


def expert_last_kernel(steps, *refs):
    blocks, refs = refs[: steps - 1], refs[steps - 1 :]
    sums = (refs[0][...], refs[1][...], refs[2][:, :1])
    gains_ref, gates_ref, ups_ref, downs_ref, given_ref, activated_ref = refs[3:]
    places = range(steps + 1, 2 * steps)
    gate, up, squares = add_features(sums, places, blocks, gains_ref, gates_ref, ups_ref, steps)
    cuts, _, width = gates_ref.shape
    scale = lax.rsqrt(squares / (cuts * width) + norm_eps)
    gate, up = gate * scale, up * scale
    activated = ((up + 1.0) * gate * jax.nn.sigmoid(glu_alpha * gate)).astype(jnp.bfloat16)
    activated_ref[...] = activated
    for k in range(steps):
        given_ref[k] = dot(activated, downs_ref[origin(k, k > 0)], NN).astype(jnp.bfloat16)


def expert_kept_kernel(activated_ref, downs_ref, kept_ref):
    for k in range(kept_ref.shape[0]):
        kept_ref[k] = dot(activated_ref[...], downs_ref[origin(k, k == 0)], NN).astype(jnp.bfloat16)


def add_cores_kernel(kept_ref, given_ref, *out_refs):
    half = out_refs[0].shape[0]
    for i, out_ref in enumerate(out_refs):
        rows = slice(i % 2 * half, (i % 2 + 1) * half)
        total = kept_ref[i // 2, rows].astype(jnp.float32) + given_ref[i // 2, rows].astype(jnp.float32)
        out_ref[...] = total.astype(jnp.bfloat16)


def add_chips_kernel(steps, *refs):
    total = sum(r[...].astype(jnp.float32) for r in refs[:steps])
    for k, out_ref in enumerate(refs[steps:]):
        out_ref[...] = total[k * CAP : (k + 1) * CAP].astype(jnp.bfloat16)


def combine_kernel(live, *refs):
    blocks = refs[:live]
    mix_hi_ref, mix_lo_ref, resid_ref, out_ref, rows_ref = refs[live:]
    me = lax.axis_index("seq")
    for k in range(live):
        rows_ref[lax.bitwise_xor(me, live - 1 - k)] = blocks[k][...]
    rows = rows_ref[...].reshape(live * CAP, -1)
    mixed = dot(rows, mix_hi_ref[...], TN) + dot(rows, mix_lo_ref[...], TN)
    out_ref[...] = (resid_ref[...].astype(jnp.float32) + mixed).astype(jnp.bfloat16)


def swap(block, axis, mask):
    return lax.ppermute(block, axis, [(i, i ^ mask) for i in range(lax.axis_size(axis))])


def to_chip(block, k):
    return swap(block, "cuts", CORES * k + 1)


def from_chips(block):
    return [to_chip(block, k) for k in range(1, lax.axis_size("cuts") // CORES)]


def to_seq(block, k):
    size = lax.axis_size("seq") * lax.axis_size("cuts")
    mask = k * lax.axis_size("cuts") + 1
    return lax.ppermute(block, ("seq", "cuts"), [(i, i ^ mask) for i in range(size)])


def from_sibling(block):
    return swap(block, "cuts", 1)


def after(arrays, others):
    return lax.optimization_barrier((arrays, others))[0]


def shards(
    queries,
    keyvals,
    preceding_keyvalues,
    attention_sink_logits,
    residual,
    w_out,
    norm_gain,
    expert_ids,
    route_weights,
    w_gate,
    w_up,
    w_down,
):
    toks, feats = residual.shape
    size = lax.axis_size("seq")
    live = w_gate.shape[0] * size
    cuts = lax.axis_size("cuts")
    steps = cuts // CORES
    slots = live * CAP
    head_rows = queries.shape[1]
    heads = head_rows // HEAD_SIZE
    width = norm_gain.shape[0]
    hidden = w_gate.shape[2]

    tail = keyvals[toks - KEYS_SEEN :]
    rim = lax.ppermute(tail, "seq", [(i, (i + 1) % size) for i in range(size)])
    loads = (queries, keyvals, preceding_keyvalues, w_out.T, residual.T)
    groups = keyvals.shape[1] // PAIR
    across = head_rows // PAIR // groups * KEYS_SEEN
    part_sums = jax.ShapeDtypeStruct((2 * groups, across), jnp.float32)
    q, _, before, w_t, residual_t, placing, mix_hi, mix_lo, sinks, late, *parts = call(
        functools.partial(first_kernel, live),
        (
            *(bf16(*a.shape) for a in loads),
            *(bf16(slots, toks),) * 3,
            jax.ShapeDtypeStruct((heads, KEYS_SEEN), jnp.float32),
            bf16(head_rows, toks - KEYS_SEEN),
            jax.ShapeDtypeStruct((slots, head_rows), jnp.float32),
            jax.ShapeDtypeStruct((groups, PAIR, across), jnp.float32),
            part_sums,
            part_sums,
        ),
        n_in=8,
        scratch=[
            pltpu.VMEM(expert_ids.T.shape, jnp.int32),
            pltpu.VMEM(expert_ids.T.shape, jnp.float32),
            pltpu.SMEM(attention_sink_logits.shape, jnp.float32),
            pltpu.SemaphoreType.DMA((8,)),
        ],
        hbm=range(8),
        flops=4 * toks * SPAN * head_rows,
        moved=2 * (w_out.size + residual.size + queries.size),
    )(*(in_hbm(a) for a in (expert_ids.T, route_weights.T, attention_sink_logits, *loads)))
    attended, rows = call(
        second_kernel,
        (bf16(head_rows, toks), bf16(slots, head_rows)),
        n_in=10,
        flops=2 * toks * SPAN * head_rows,
        moved=2 * queries.size,
    )(q, before, rim, sinks, late, placing, *parts)

    chip_rows = from_chips(rows)
    total = jax.ShapeDtypeStruct((slots, feats), jnp.float32)
    part = dict(flops=slots * w_out.size // 2, moved=w_out.size // 2)
    own = call(functools.partial(rows_own_kernel, steps), total, n_in=4, **part)(
        rows, w_t, residual_t, placing
    )
    sibling_rows = from_sibling(rows)
    places = range(steps, 2 * steps)
    spread = functools.partial(
        call, spread_kernel, bf16(cuts, hidden, feats), n_in=1, moved=4 * w_gate.size
    )
    gates = spread()(after(w_gate[0].T, rows))
    chip_rows = after(chip_rows, (own, gates))
    relayed_rows = [from_sibling(b) for b in chip_rows]
    chips = call(functools.partial(rows_more_kernel, places, steps), total, n_in=steps + 2, **part)(
        sibling_rows, *chip_rows, own, w_t
    )
    outgoing = call(
        functools.partial(rows_last_kernel, steps),
        (bf16(CAP, feats),) * live,
        n_in=steps + 1,
        scratch=[pltpu.VMEM((live, CAP, feats), jnp.bfloat16)],
        **part,
    )(*relayed_rows, chips, w_t)

    arrived = [to_seq(outgoing[k], k) for k in range(live - 1, -1, -1)]

    ups = spread()(after(w_up[0].T, outgoing[0]))
    gains = call(spread_gain_kernel, jax.ShapeDtypeStruct((cuts, 1, feats), jnp.float32), n_in=1)(norm_gain)
    sums = (
        *(jax.ShapeDtypeStruct((slots, hidden), jnp.float32),) * 2,
        jax.ShapeDtypeStruct((slots, KEYS_SEEN), jnp.float32),
    )
    part = dict(flops=slots * w_gate.size, moved=w_gate.size)
    stacked = call(stack_kernel, bf16(slots, feats), n_in=live)(*after(arrived, (ups, gains)))
    chip_rows = from_chips(stacked)
    own = call(functools.partial(expert_own_kernel, steps), sums, n_in=4, **part)(stacked, gains, gates, ups)
    sibling_rows = from_sibling(stacked)
    downs = spread()(after(w_down[0], stacked))
    chip_blocks = from_chips(after(attended, gates))
    sibling_block, *relayed_blocks = [from_sibling(b) for b in (attended, *chip_blocks)]
    blocks = [attended, *relayed_blocks, sibling_block, *chip_blocks]
    chip_rows = after(chip_rows, (own, downs))
    relayed_rows = [from_sibling(b) for b in chip_rows]
    chips = call(functools.partial(expert_more_kernel, range(steps), steps), sums, n_in=steps + 6, **part)(
        sibling_rows, *chip_rows, *own, gains, gates, ups
    )
    given, activated = call(
        functools.partial(expert_last_kernel, steps),
        (bf16(steps, slots, feats), bf16(slots, hidden)),
        n_in=steps + 6,
        **part,
    )(*relayed_rows, *chips, gains, gates, ups, downs)
    kept = call(expert_kept_kernel, bf16(steps, slots, feats), n_in=2, **part)(activated, downs)
    resid = call(
        functools.partial(project_kernel, steps),
        bf16(feats, toks),
        n_in=cuts + 2,
        flops=2 * toks * w_out.size,
        moved=2 * w_out.size,
    )(*blocks, w_t, residual_t)

    sums = call(add_cores_kernel, (bf16(slots // 2, feats),) * (2 * steps), n_in=2)(
        kept, swap(given, "cuts", 1)
    )
    returned = []
    for half in range(2):
        parts = [sums[half]] + [to_chip(sums[2 * k + half], k) for k in range(1, steps)]
        blocks = call(functools.partial(add_chips_kernel, steps), (bf16(CAP, feats),) * (live // 2), n_in=steps)(
            *parts
        )
        for block in blocks:
            returned.append(to_seq(block, live - 1 - len(returned)))
    out = call(
        functools.partial(combine_kernel, live),
        bf16(feats, toks),
        n_in=live + 3,
        scratch=[pltpu.VMEM((live, CAP, feats), jnp.bfloat16)],
    )(*returned, mix_hi, mix_lo, resid)
    return out.T


def solution(mesh):
    placed = (
        P(("groups", "seq"), "cuts"),
        P(("groups", "seq"), "cuts"),
        P("groups", "cuts"),
        P("cuts"),
        P(("groups", "seq"), "cuts"),
        P(None, "cuts"),
        P(),
        P(("groups", "seq"), None),
        P(("groups", "seq"), None),
        P("seq", None, "cuts"),
        P("seq", None, "cuts"),
        P("seq", "cuts", None),
    )
    return jax.shard_map(
        shards, mesh=mesh, in_specs=placed, out_specs=P(("groups", "seq"), "cuts"), check_vma=False
    )
```

```python
import functools
import math

import jax
import jax.numpy as jnp
from jax import lax
from jax.experimental import pallas as pl
from jax.experimental.pallas import tpu as pltpu
from jax.sharding import PartitionSpec as P

HEAD_SIZE = 64
KEYS_SEEN = 128
PAIR = 2 * HEAD_SIZE
SPAN = 2 * KEYS_SEEN
CAP = 16
CORES = 2

norm_eps = 1e-05
glu_alpha = 1.702

NT = (((1,), (1,)), ((), ()))
NN = (((1,), (0,)), ((), ()))
TN = (((0,), (0,)), ((), ()))
VMEM_LIMIT = 32 * 1024 * 1024


def dot(a, b, dims):
    return lax.dot_general(a, b, dims, preferred_element_type=jnp.float32)


def call(kernel, outs, n_in, scratch=(), hbm=(), out_space=pltpu.VMEM, flops=0, moved=0):
    spaces = [pltpu.HBM if i in hbm else pltpu.VMEM for i in range(n_in)]
    return pl.pallas_call(
        kernel,
        out_shape=outs,
        in_specs=[pl.BlockSpec(memory_space=space) for space in spaces],
        out_specs=jax.tree.map(lambda _: pl.BlockSpec(memory_space=out_space), outs),
        scratch_shapes=list(scratch),
        compiler_params=pltpu.CompilerParams(vmem_limit_bytes=VMEM_LIMIT),
        cost_estimate=pl.CostEstimate(flops=flops, bytes_accessed=moved, transcendentals=0),
    )


def in_hbm(array):
    return pltpu.with_memory_space_constraint(array, pltpu.HBM)


def bf16(*shape):
    return jax.ShapeDtypeStruct(shape, jnp.bfloat16)


def split_pair(both):
    both = both.astype(jnp.float32)
    low = lax.broadcasted_iota(jnp.int32, both.shape, 1) < HEAD_SIZE
    turned = pltpu.roll(both, HEAD_SIZE, 1)
    keys = jnp.concatenate([jnp.where(low, both, 0.0), jnp.where(low, 0.0, turned)], axis=0)
    values = jnp.concatenate([jnp.where(low, turned, 0.0), jnp.where(low, 0.0, both)], axis=0)
    return keys.astype(jnp.bfloat16), values.astype(jnp.bfloat16)


def score(pairs, keys, allowed):
    scores = dot(keys, jnp.concatenate(pairs, axis=0), NT) * (HEAD_SIZE**-0.5 * math.log2(math.e))
    allowed = jnp.concatenate([allowed] * len(pairs), axis=1)
    span = allowed.shape[0]
    return [jnp.where(allowed, scores[i * span : (i + 1) * span], -jnp.inf) for i in range(2)]


def sink_row(sinks, i, pairs):
    return jnp.concatenate([sinks[2 * p + i] for p in range(pairs)], axis=1)


def attend_block(pairs, both, sinks, allowed):
    keys, values = split_pair(both)
    probs = []
    for i, part in enumerate(score(pairs, keys, allowed)):
        sink = sink_row(sinks, i, len(pairs))
        peak = jnp.maximum(jnp.max(part, axis=0, keepdims=True), sink)
        terms = jnp.exp2(part - peak)
        denom = jnp.sum(terms, axis=0, keepdims=True) + jnp.exp2(sink - peak)
        probs.append((terms * (1.0 / denom)).astype(jnp.bfloat16))
    return dot(values, jnp.concatenate(probs, axis=0), TN).astype(jnp.bfloat16)


def group_queries(q_ref, g, groups, block):
    per_group = q_ref.shape[1] // PAIR // groups
    first = g * per_group
    toks = slice(block * KEYS_SEEN, (block + 1) * KEYS_SEEN)
    pairs = [q_ref[toks, (first + p) * PAIR : (first + p + 1) * PAIR] for p in range(per_group)]
    return first, pairs


def store_pairs(mixed, first, out_ref, lanes):
    for p in range(mixed.shape[1] // KEYS_SEEN):
        rows = slice((first + p) * PAIR, (first + p + 1) * PAIR)
        out_ref[rows, lanes] = mixed[:, p * KEYS_SEEN : (p + 1) * KEYS_SEEN]


def key_query(span):
    key = lax.broadcasted_iota(jnp.int32, (span, KEYS_SEEN), 0)
    return key, lax.broadcasted_iota(jnp.int32, (span, KEYS_SEEN), 1)


def per_head(pair):
    return jnp.concatenate([jnp.broadcast_to(row, (HEAD_SIZE, row.shape[1])) for row in pair], axis=0)


def fill_tables(live, ids, weights, placing_ref, mix_hi_ref, mix_lo_ref):
    toks = ids.shape[1]
    chosen = jnp.concatenate(
        [jnp.max((ids == e).astype(jnp.float32), axis=0, keepdims=True) for e in range(live)], axis=0
    )
    earlier = lax.broadcasted_iota(jnp.int32, (toks, toks), 0)
    later = lax.broadcasted_iota(jnp.int32, (toks, toks), 1)
    strict = (earlier < later).astype(jnp.bfloat16)
    before = dot(chosen.astype(jnp.bfloat16), strict, NN)
    slot = lax.broadcasted_iota(jnp.int32, (CAP, toks), 0).astype(jnp.float32)
    for e in range(live):
        weight = jnp.sum(jnp.where(ids == e, weights, 0.0), axis=0, keepdims=True)
        fills = (before[e : e + 1] == slot) & (chosen[e : e + 1] > 0.0)
        mix = jnp.where(fills, weight, 0.0)
        hi = mix.astype(jnp.bfloat16)
        rows = slice(e * CAP, (e + 1) * CAP)
        placing_ref[rows] = fills.astype(jnp.bfloat16)
        mix_hi_ref[rows] = hi
        mix_lo_ref[rows] = (mix - hi.astype(jnp.float32)).astype(jnp.bfloat16)


def first_kernel(live, *refs):
    loaded, held = refs[:8], refs[8:13]
    placing_ref, mix_hi_ref, mix_lo_ref, sinks_out, late_ref, rows_ref, mixed_ref, peaks_ref, sums_ref = refs[13:22]
    ids_ref, weights_ref, sinks_ref, sems = refs[22:]
    targets = (ids_ref, weights_ref, sinks_ref, *held)
    copies = [pltpu.make_async_copy(*pair, sems.at[i]) for i, pair in enumerate(zip(loaded, targets))]
    for copy in copies:
        copy.start()
    q_ref, kv_ref = held[:2]
    for copy in copies[:2]:
        copy.wait()
    fill_tables(live, ids_ref[...], weights_ref[...], placing_ref, mix_hi_ref, mix_lo_ref)
    for copy in copies[2:5]:
        copy.wait()
    heads = sinks_ref.shape[0]
    sinks = [jnp.full((1, KEYS_SEEN), sinks_ref[h], jnp.float32) * math.log2(math.e) for h in range(heads)]
    sinks_out[...] = jnp.concatenate(sinks, axis=0)
    groups = kv_ref.shape[1] // PAIR
    key, query = key_query(SPAN)
    allowed = (key > query) & (key <= query + KEYS_SEEN)
    for b in range(1, q_ref.shape[0] // KEYS_SEEN):
        span = slice((b - 1) * KEYS_SEEN, (b + 1) * KEYS_SEEN)
        for g in range(groups):
            first, pairs = group_queries(q_ref, g, groups, b)
            part = sinks[2 * first : 2 * (first + len(pairs))]
            mixed = attend_block(pairs, kv_ref[span, g * PAIR : (g + 1) * PAIR], part, allowed)
            store_pairs(mixed, first, late_ref, slice((b - 1) * KEYS_SEEN, b * KEYS_SEEN))
    key, query = key_query(KEYS_SEEN)
    for g in range(mixed_ref.shape[0]):
        _, pairs = group_queries(q_ref, g, groups, 0)
        keys, values = split_pair(kv_ref[:KEYS_SEEN, g * PAIR : (g + 1) * PAIR])
        terms = []
        for i, part in enumerate(score(pairs, keys, key <= query)):
            peak = jnp.max(part, axis=0, keepdims=True)
            terms.append(jnp.exp2(part - peak))
            peaks_ref[2 * g + i : 2 * g + i + 1] = peak
            sums_ref[2 * g + i : 2 * g + i + 1] = jnp.sum(terms[-1], axis=0, keepdims=True)
        mixed_ref[g] = dot(values, jnp.concatenate(terms, axis=0).astype(jnp.bfloat16), TN)
    rows_ref[...] = dot(placing_ref[:, KEYS_SEEN:], late_ref[...], NT)
    for copy in copies[5:]:
        copy.wait()


def second_kernel(q_ref, kv_ref, before_ref, rim_ref, sinks_ref, late_ref, placing_ref, *refs):
    late_rows_ref, mixed_ref, peaks_ref, sums_ref, all_ref, rows_ref = refs
    rim = jnp.where(lax.axis_index("seq") == 0, before_ref[...], rim_ref[...])
    groups = rim.shape[1] // PAIR
    key, query = key_query(SPAN)
    allowed = (key > query) & (key <= query + KEYS_SEEN)
    key, query = key_query(KEYS_SEEN)
    for g in range(groups):
        first, pairs = group_queries(q_ref, g, groups, 0)
        sinks = [sinks_ref[h : h + 1] for h in range(2 * first, 2 * (first + len(pairs)))]
        lanes = slice(g * PAIR, (g + 1) * PAIR)
        if g >= mixed_ref.shape[0]:
            both = jnp.concatenate([rim[:, lanes], kv_ref[:KEYS_SEEN, lanes]], axis=0)
            store_pairs(attend_block(pairs, both, sinks, allowed), first, all_ref, slice(0, KEYS_SEEN))
            continue
        keys, values = split_pair(rim[:, lanes])
        terms, scales, inverses = [], [], []
        for i, part in enumerate(score(pairs, keys, key > query)):
            sink = sink_row(sinks, i, len(pairs))
            own_peak = peaks_ref[2 * g + i : 2 * g + i + 1]
            peak = jnp.maximum(jnp.max(part, axis=0, keepdims=True), jnp.maximum(own_peak, sink))
            scale = jnp.exp2(own_peak - peak)
            terms.append(jnp.exp2(part - peak))
            denom = jnp.sum(terms[-1], axis=0, keepdims=True) + jnp.exp2(sink - peak)
            denom += sums_ref[2 * g + i : 2 * g + i + 1] * scale
            inverses.append(1.0 / denom)
            scales.append(scale)
        mixed = dot(values, jnp.concatenate(terms, axis=0).astype(jnp.bfloat16), TN)
        mixed = (mixed + mixed_ref[g] * per_head(scales)) * per_head(inverses)
        store_pairs(mixed.astype(jnp.bfloat16), first, all_ref, slice(0, KEYS_SEEN))
    rows = late_rows_ref[...] + dot(placing_ref[:, :KEYS_SEEN], all_ref[:, :KEYS_SEEN], NT)
    rows_ref[...] = rows.astype(jnp.bfloat16)
    all_ref[:, KEYS_SEEN:] = late_ref[...]


def origin(k, sibling):
    me = lax.axis_index("cuts")
    return lax.bitwise_xor(me, CORES * k + (1 if sibling else 0))


def add_products(total, places, blocks, w_ref, steps, dims, swapped=False):
    width = blocks[0].shape[0 if swapped else 1] if blocks else 0
    for i, block in zip(places, blocks):
        at = pl.multiple_of(origin(i % steps, i >= steps) * width, 128)
        w = w_ref[:, pl.ds(at, width)]
        total += dot(w, block[...], dims) if swapped else dot(block[...], w, dims)
    return total


def rows_own_kernel(steps, rows_ref, w_ref, residual_ref, placing_ref, total_ref):
    total = dot(placing_ref[...], residual_ref[...], NT)
    total_ref[...] = add_products(total, [0], [rows_ref], w_ref, steps, NT)


def rows_more_kernel(places, steps, *refs):
    blocks, (before_ref, w_ref, total_ref) = refs[:-3], refs[-3:]
    total_ref[...] = add_products(before_ref[...], places, blocks, w_ref, steps, NT)


def rows_last_kernel(steps, *refs):
    blocks, (before_ref, w_ref) = refs[: steps - 1], refs[steps - 1 : steps + 1]
    outgoing, rows_ref = refs[steps + 1 : -1], refs[-1]
    total = add_products(before_ref[...], range(1, steps), blocks, w_ref, steps, NT)
    rows_ref[...] = total.astype(jnp.bfloat16).reshape(rows_ref.shape)
    me = lax.axis_index("seq")
    for k, out_ref in enumerate(outgoing):
        out_ref[...] = rows_ref[lax.bitwise_xor(me, k)]


def stack_kernel(*refs):
    for i, block in enumerate(refs[:-1]):
        refs[-1][i * CAP : (i + 1) * CAP] = block[...]


def project_kernel(steps, *refs):
    blocks = refs[: 2 * steps]
    w_ref, residual_ref, resid_ref = refs[2 * steps :]
    total = residual_ref[...].astype(jnp.float32)
    total = add_products(total, range(2 * steps), blocks, w_ref, steps, NN, True)
    resid_ref[...] = total.astype(jnp.bfloat16)


def spread_kernel(source_ref, blocks_ref):
    cuts, _, width = blocks_ref.shape
    for p in range(cuts):
        blocks_ref[p] = source_ref[:, p * width : (p + 1) * width]


def spread_gain_kernel(gain_ref, blocks_ref):
    cuts, _, width = blocks_ref.shape
    gain = gain_ref[...].reshape(1, cuts * width)
    for p in range(cuts):
        blocks_ref[p] = gain[:, p * width : (p + 1) * width]


def add_features(sums, places, blocks, gains_ref, gates_ref, ups_ref, steps):
    gate, up, squares = sums
    for i, block in zip(places, blocks):
        p = origin(i % steps, i >= steps)
        wide = block[...].astype(jnp.float32)
        squares += jnp.sum(wide * wide, axis=1, keepdims=True)
        rows = (wide * gains_ref[p]).astype(jnp.bfloat16)
        gate += dot(rows, gates_ref[p], NT)
        up += dot(rows, ups_ref[p], NT)
    return gate, up, squares


def store_sums(sums, refs):
    for ref, value in zip(refs, sums):
        ref[...] = jnp.broadcast_to(value, ref.shape)


def expert_own_kernel(steps, block_ref, gains_ref, gates_ref, ups_ref, *out_refs):
    zeros = jnp.zeros(out_refs[0].shape, jnp.float32)
    sums = (zeros, zeros, jnp.zeros((zeros.shape[0], 1), jnp.float32))
    store_sums(add_features(sums, [steps], [block_ref], gains_ref, gates_ref, ups_ref, steps), out_refs)


def expert_more_kernel(places, steps, *refs):
    blocks, refs = refs[:-9], refs[-9:]
    sums = (refs[0][...], refs[1][...], refs[2][:, :1])
    store_sums(add_features(sums, places, blocks, *refs[3:6], steps), refs[6:])


def expert_last_kernel(steps, *refs):
    blocks, refs = refs[: steps - 1], refs[steps - 1 :]
    sums = (refs[0][...], refs[1][...], refs[2][:, :1])
    gains_ref, gates_ref, ups_ref, downs_ref, given_ref, activated_ref = refs[3:]
    places = range(steps + 1, 2 * steps)
    gate, up, squares = add_features(sums, places, blocks, gains_ref, gates_ref, ups_ref, steps)
    cuts, _, width = gates_ref.shape
    scale = lax.rsqrt(squares / (cuts * width) + norm_eps)
    gate, up = gate * scale, up * scale
    activated = ((up + 1.0) * gate * jax.nn.sigmoid(glu_alpha * gate)).astype(jnp.bfloat16)
    activated_ref[...] = activated
    for k in range(steps):
        given_ref[k] = dot(activated, downs_ref[origin(k, k > 0)], NN).astype(jnp.bfloat16)


def expert_kept_kernel(activated_ref, downs_ref, kept_ref):
    for k in range(kept_ref.shape[0]):
        kept_ref[k] = dot(activated_ref[...], downs_ref[origin(k, k == 0)], NN).astype(jnp.bfloat16)


def add_cores_kernel(kept_ref, given_ref, *out_refs):
    half = out_refs[0].shape[0]
    for i, out_ref in enumerate(out_refs):
        rows = slice(i % 2 * half, (i % 2 + 1) * half)
        total = kept_ref[i // 2, rows].astype(jnp.float32) + given_ref[i // 2, rows].astype(jnp.float32)
        out_ref[...] = total.astype(jnp.bfloat16)


def add_chips_kernel(steps, *refs):
    total = sum(r[...].astype(jnp.float32) for r in refs[:steps])
    for k, out_ref in enumerate(refs[steps:]):
        out_ref[...] = total[k * CAP : (k + 1) * CAP].astype(jnp.bfloat16)


def combine_kernel(live, parts, *refs):
    blocks = refs[:live]
    mix_hi_ref, mix_lo_ref, resid_ref, out_ref, rows_ref, held_ref, sems = refs[live:]
    me = lax.axis_index("seq")
    for k in range(live):
        rows_ref[lax.bitwise_xor(me, live - 1 - k)] = blocks[k][...]
    rows = rows_ref[...].reshape(live * CAP, -1)
    rows = jnp.concatenate([rows, rows], axis=0)
    mix = jnp.concatenate([mix_hi_ref[...], mix_lo_ref[...]], axis=0)
    copies = []
    for i, (start, stop) in enumerate(parts):
        part = slice(start, stop)
        mixed = dot(rows[:, part], mix, TN)
        held_ref[part] = (resid_ref[part].astype(jnp.float32) + mixed).astype(jnp.bfloat16)
        copies.append(pltpu.make_async_copy(held_ref.at[part], out_ref.at[part], sems.at[i]))
        copies[-1].start()
    for copy in copies:
        copy.wait()


def swap(block, axis, mask):
    return lax.ppermute(block, axis, [(i, i ^ mask) for i in range(lax.axis_size(axis))])


def to_chip(block, k):
    return swap(block, "cuts", CORES * k + 1)


def from_chips(block):
    return [to_chip(block, k) for k in range(1, lax.axis_size("cuts") // CORES)]


def to_seq(block, k):
    size = lax.axis_size("seq") * lax.axis_size("cuts")
    mask = k * lax.axis_size("cuts") + 1
    return lax.ppermute(block, ("seq", "cuts"), [(i, i ^ mask) for i in range(size)])


def from_sibling(block):
    return swap(block, "cuts", 1)


def after(arrays, others):
    return lax.optimization_barrier((arrays, others))[0]


def shards(
    queries,
    keyvals,
    preceding_keyvalues,
    attention_sink_logits,
    residual,
    w_out,
    norm_gain,
    expert_ids,
    route_weights,
    w_gate,
    w_up,
    w_down,
):
    toks, feats = residual.shape
    size = lax.axis_size("seq")
    live = w_gate.shape[0] * size
    cuts = lax.axis_size("cuts")
    steps = cuts // CORES
    slots = live * CAP
    head_rows = queries.shape[1]
    heads = head_rows // HEAD_SIZE
    width = norm_gain.shape[0]
    hidden = w_gate.shape[2]

    tail = keyvals[toks - KEYS_SEEN :]
    rim = lax.ppermute(tail, "seq", [(i, (i + 1) % size) for i in range(size)])
    loads = (queries, keyvals, preceding_keyvalues, w_out.T, residual.T)
    groups = keyvals.shape[1] // PAIR
    across = head_rows // PAIR // groups * KEYS_SEEN
    early = (groups + 1) // 2
    part_sums = jax.ShapeDtypeStruct((2 * early, across), jnp.float32)
    q, kv, before, w_t, residual_t, placing, mix_hi, mix_lo, sinks, late, *parts = call(
        functools.partial(first_kernel, live),
        (
            *(bf16(*a.shape) for a in loads),
            *(bf16(slots, toks),) * 3,
            jax.ShapeDtypeStruct((heads, KEYS_SEEN), jnp.float32),
            bf16(head_rows, toks - KEYS_SEEN),
            jax.ShapeDtypeStruct((slots, head_rows), jnp.float32),
            jax.ShapeDtypeStruct((early, PAIR, across), jnp.float32),
            part_sums,
            part_sums,
        ),
        n_in=8,
        scratch=[
            pltpu.VMEM(expert_ids.T.shape, jnp.int32),
            pltpu.VMEM(expert_ids.T.shape, jnp.float32),
            pltpu.SMEM(attention_sink_logits.shape, jnp.float32),
            pltpu.SemaphoreType.DMA((8,)),
        ],
        hbm=range(8),
        flops=4 * toks * SPAN * head_rows,
        moved=2 * (w_out.size + residual.size + queries.size),
    )(*(in_hbm(a) for a in (expert_ids.T, route_weights.T, attention_sink_logits, *loads)))
    attended, rows = call(
        second_kernel,
        (bf16(head_rows, toks), bf16(slots, head_rows)),
        n_in=11,
        flops=2 * toks * SPAN * head_rows,
        moved=2 * queries.size,
    )(q, kv, before, rim, sinks, late, placing, *parts)

    chip_rows = from_chips(rows)
    total = jax.ShapeDtypeStruct((slots, feats), jnp.float32)
    part = dict(flops=slots * w_out.size // 2, moved=w_out.size // 2)
    own = call(functools.partial(rows_own_kernel, steps), total, n_in=4, **part)(
        rows, w_t, residual_t, placing
    )
    sibling_rows = from_sibling(rows)
    places = range(steps, 2 * steps)
    spread = functools.partial(
        call, spread_kernel, bf16(cuts, hidden, feats), n_in=1, moved=4 * w_gate.size
    )
    gates = spread()(after(w_gate[0].T, rows))
    chip_rows = after(chip_rows, (own, gates))
    relayed_rows = [from_sibling(b) for b in chip_rows]
    chips = call(functools.partial(rows_more_kernel, places, steps), total, n_in=steps + 2, **part)(
        sibling_rows, *chip_rows, own, w_t
    )
    outgoing = call(
        functools.partial(rows_last_kernel, steps),
        (bf16(CAP, feats),) * live,
        n_in=steps + 1,
        scratch=[pltpu.VMEM((live, CAP, feats), jnp.bfloat16)],
        **part,
    )(*relayed_rows, chips, w_t)

    arrived = [to_seq(outgoing[k], k) for k in range(live - 1, -1, -1)]

    ups = spread()(after(w_up[0].T, outgoing[0]))
    gains = call(spread_gain_kernel, jax.ShapeDtypeStruct((cuts, 1, feats), jnp.float32), n_in=1)(norm_gain)
    sums = (
        *(jax.ShapeDtypeStruct((slots, hidden), jnp.float32),) * 2,
        jax.ShapeDtypeStruct((slots, KEYS_SEEN), jnp.float32),
    )
    part = dict(flops=slots * w_gate.size, moved=w_gate.size)
    stacked = call(stack_kernel, bf16(slots, feats), n_in=live)(*after(arrived, (ups, gains)))
    chip_rows = from_chips(stacked)
    own = call(functools.partial(expert_own_kernel, steps), sums, n_in=4, **part)(stacked, gains, gates, ups)
    sibling_rows = from_sibling(stacked)
    downs = spread()(after(w_down[0], stacked))
    chip_blocks = from_chips(after(attended, gates))
    sibling_block, *relayed_blocks = [from_sibling(b) for b in (attended, *chip_blocks)]
    blocks = [attended, *relayed_blocks, sibling_block, *chip_blocks]
    chip_rows = after(chip_rows, (own, downs))
    relayed_rows = [from_sibling(b) for b in chip_rows]
    chips = call(functools.partial(expert_more_kernel, range(steps), steps), sums, n_in=steps + 6, **part)(
        sibling_rows, *chip_rows, *own, gains, gates, ups
    )
    given, activated = call(
        functools.partial(expert_last_kernel, steps),
        (bf16(steps, slots, feats), bf16(slots, hidden)),
        n_in=steps + 6,
        **part,
    )(*relayed_rows, *chips, gains, gates, ups, downs)
    kept = call(expert_kept_kernel, bf16(steps, slots, feats), n_in=2, **part)(activated, downs)
    resid = call(
        functools.partial(project_kernel, steps),
        bf16(feats, toks),
        n_in=cuts + 2,
        flops=2 * toks * w_out.size,
        moved=2 * w_out.size,
    )(*blocks, w_t, residual_t)

    sums = call(add_cores_kernel, (bf16(slots // 2, feats),) * (2 * steps), n_in=2)(
        kept, swap(given, "cuts", 1)
    )
    returned = []
    for half in range(2):
        parts = [sums[half]] + [to_chip(sums[2 * k + half], k) for k in range(1, steps)]
        blocks = call(functools.partial(add_chips_kernel, steps), (bf16(CAP, feats),) * (live // 2), n_in=steps)(
            *parts
        )
        for block in blocks:
            returned.append(to_seq(block, live - 1 - len(returned)))
    bounds = [*range(0, feats, SPAN), feats] if feats % 16 == 0 else [0, feats]
    parts = list(zip(bounds[:-1], bounds[1:]))
    out = call(
        functools.partial(combine_kernel, live, parts),
        bf16(feats, toks),
        n_in=live + 3,
        scratch=[
            pltpu.VMEM((live, CAP, feats), jnp.bfloat16),
            pltpu.VMEM((feats, toks), jnp.bfloat16),
            pltpu.SemaphoreType.DMA((len(parts),)),
        ],
        out_space=pltpu.HBM,
    )(*returned, mix_hi, mix_lo, resid)
    return out.T


def solution(mesh):
    placed = (
        P(("groups", "seq"), "cuts"),
        P(("groups", "seq"), "cuts"),
        P("groups", "cuts"),
        P("cuts"),
        P(("groups", "seq"), "cuts"),
        P(None, "cuts"),
        P(),
        P(("groups", "seq"), None),
        P(("groups", "seq"), None),
        P("seq", None, "cuts"),
        P("seq", None, "cuts"),
        P("seq", "cuts", None),
    )
    return jax.shard_map(
        shards, mesh=mesh, in_specs=placed, out_specs=P(("groups", "seq"), "cuts"), check_vma=False
    )
```

```python
import functools
import math

import jax
import jax.numpy as jnp
from jax import lax
from jax.experimental import pallas as pl
from jax.experimental.pallas import tpu as pltpu
from jax.sharding import PartitionSpec as P

HEAD_SIZE = 64
KEYS_SEEN = 128
PAIR = 2 * HEAD_SIZE
SPAN = 2 * KEYS_SEEN
CAP = 16
CORES = 2

norm_eps = 1e-05
glu_alpha = 1.702

NT = (((1,), (1,)), ((), ()))
NN = (((1,), (0,)), ((), ()))
TN = (((0,), (0,)), ((), ()))
VMEM_LIMIT = 32 * 1024 * 1024


def dot(a, b, dims):
    return lax.dot_general(a, b, dims, preferred_element_type=jnp.float32)


def call(kernel, outs, n_in, scratch=(), hbm=(), out_space=pltpu.VMEM, flops=0, moved=0):
    spaces = [pltpu.HBM if i in hbm else pltpu.VMEM for i in range(n_in)]
    return pl.pallas_call(
        kernel,
        out_shape=outs,
        in_specs=[pl.BlockSpec(memory_space=space) for space in spaces],
        out_specs=jax.tree.map(lambda _: pl.BlockSpec(memory_space=out_space), outs),
        scratch_shapes=list(scratch),
        compiler_params=pltpu.CompilerParams(vmem_limit_bytes=VMEM_LIMIT),
        cost_estimate=pl.CostEstimate(flops=flops, bytes_accessed=moved, transcendentals=0),
    )


def in_hbm(array):
    return pltpu.with_memory_space_constraint(array, pltpu.HBM)


def bf16(*shape):
    return jax.ShapeDtypeStruct(shape, jnp.bfloat16)


def split_pair(both):
    both = both.astype(jnp.float32)
    low = lax.broadcasted_iota(jnp.int32, both.shape, 1) < HEAD_SIZE
    turned = pltpu.roll(both, HEAD_SIZE, 1)
    keys = jnp.concatenate([jnp.where(low, both, 0.0), jnp.where(low, 0.0, turned)], axis=0)
    values = jnp.concatenate([jnp.where(low, turned, 0.0), jnp.where(low, 0.0, both)], axis=0)
    return keys.astype(jnp.bfloat16), values.astype(jnp.bfloat16)


def score(pairs, keys, allowed):
    scores = dot(keys, jnp.concatenate(pairs, axis=0), NT) * (HEAD_SIZE**-0.5 * math.log2(math.e))
    allowed = jnp.concatenate([allowed] * len(pairs), axis=1)
    span = allowed.shape[0]
    return [jnp.where(allowed, scores[i * span : (i + 1) * span], -jnp.inf) for i in range(2)]


def sink_row(sinks, i, pairs):
    return jnp.concatenate([sinks[2 * p + i] for p in range(pairs)], axis=1)


def attend_block(pairs, both, sinks, allowed):
    keys, values = split_pair(both)
    probs = []
    for i, part in enumerate(score(pairs, keys, allowed)):
        sink = sink_row(sinks, i, len(pairs))
        peak = jnp.maximum(jnp.max(part, axis=0, keepdims=True), sink)
        terms = jnp.exp2(part - peak)
        denom = jnp.sum(terms, axis=0, keepdims=True) + jnp.exp2(sink - peak)
        probs.append((terms * (1.0 / denom)).astype(jnp.bfloat16))
    return dot(values, jnp.concatenate(probs, axis=0), TN).astype(jnp.bfloat16)


def group_queries(q_ref, g, groups, block):
    per_group = q_ref.shape[1] // PAIR // groups
    first = g * per_group
    toks = slice(block * KEYS_SEEN, (block + 1) * KEYS_SEEN)
    pairs = [q_ref[toks, (first + p) * PAIR : (first + p + 1) * PAIR] for p in range(per_group)]
    return first, pairs


def store_pairs(mixed, first, out_ref, lanes):
    for p in range(mixed.shape[1] // KEYS_SEEN):
        rows = slice((first + p) * PAIR, (first + p + 1) * PAIR)
        out_ref[rows, lanes] = mixed[:, p * KEYS_SEEN : (p + 1) * KEYS_SEEN]


def key_query(span):
    key = lax.broadcasted_iota(jnp.int32, (span, KEYS_SEEN), 0)
    return key, lax.broadcasted_iota(jnp.int32, (span, KEYS_SEEN), 1)


def per_head(pair):
    return jnp.concatenate([jnp.broadcast_to(row, (HEAD_SIZE, row.shape[1])) for row in pair], axis=0)


def fill_tables(live, ids, weights, placing_ref, mix_hi_ref, mix_lo_ref):
    toks = ids.shape[1]
    chosen = jnp.concatenate(
        [jnp.max((ids == e).astype(jnp.float32), axis=0, keepdims=True) for e in range(live)], axis=0
    )
    earlier = lax.broadcasted_iota(jnp.int32, (toks, toks), 0)
    later = lax.broadcasted_iota(jnp.int32, (toks, toks), 1)
    strict = (earlier < later).astype(jnp.bfloat16)
    before = dot(chosen.astype(jnp.bfloat16), strict, NN)
    slot = lax.broadcasted_iota(jnp.int32, (CAP, toks), 0).astype(jnp.float32)
    for e in range(live):
        weight = jnp.sum(jnp.where(ids == e, weights, 0.0), axis=0, keepdims=True)
        fills = (before[e : e + 1] == slot) & (chosen[e : e + 1] > 0.0)
        mix = jnp.where(fills, weight, 0.0)
        hi = mix.astype(jnp.bfloat16)
        rows = slice(e * CAP, (e + 1) * CAP)
        placing_ref[rows] = fills.astype(jnp.bfloat16)
        mix_hi_ref[rows] = hi
        mix_lo_ref[rows] = (mix - hi.astype(jnp.float32)).astype(jnp.bfloat16)


def first_kernel(live, *refs):
    loaded, held = refs[:8], refs[8:13]
    placing_ref, mix_hi_ref, mix_lo_ref, sinks_out, late_ref, rows_ref, mixed_ref, peaks_ref, sums_ref = refs[13:22]
    ids_ref, weights_ref, sinks_ref, sems = refs[22:]
    targets = (ids_ref, weights_ref, sinks_ref, *held)
    copies = [pltpu.make_async_copy(*pair, sems.at[i]) for i, pair in enumerate(zip(loaded, targets))]
    for copy in copies:
        copy.start()
    q_ref, kv_ref = held[:2]
    for copy in copies[:2]:
        copy.wait()
    fill_tables(live, ids_ref[...], weights_ref[...], placing_ref, mix_hi_ref, mix_lo_ref)
    for copy in copies[2:5]:
        copy.wait()
    heads = sinks_ref.shape[0]
    sinks = [jnp.full((1, KEYS_SEEN), sinks_ref[h], jnp.float32) * math.log2(math.e) for h in range(heads)]
    sinks_out[...] = jnp.concatenate(sinks, axis=0)
    groups = kv_ref.shape[1] // PAIR
    key, query = key_query(SPAN)
    allowed = (key > query) & (key <= query + KEYS_SEEN)
    for b in range(1, q_ref.shape[0] // KEYS_SEEN):
        span = slice((b - 1) * KEYS_SEEN, (b + 1) * KEYS_SEEN)
        for g in range(groups):
            first, pairs = group_queries(q_ref, g, groups, b)
            part = sinks[2 * first : 2 * (first + len(pairs))]
            mixed = attend_block(pairs, kv_ref[span, g * PAIR : (g + 1) * PAIR], part, allowed)
            store_pairs(mixed, first, late_ref, slice((b - 1) * KEYS_SEEN, b * KEYS_SEEN))
    key, query = key_query(KEYS_SEEN)
    for g in range(mixed_ref.shape[0]):
        _, pairs = group_queries(q_ref, g, groups, 0)
        keys, values = split_pair(kv_ref[:KEYS_SEEN, g * PAIR : (g + 1) * PAIR])
        terms = []
        for i, part in enumerate(score(pairs, keys, key <= query)):
            peak = jnp.max(part, axis=0, keepdims=True)
            terms.append(jnp.exp2(part - peak))
            peaks_ref[2 * g + i : 2 * g + i + 1] = peak
            sums_ref[2 * g + i : 2 * g + i + 1] = jnp.sum(terms[-1], axis=0, keepdims=True)
        mixed_ref[g] = dot(values, jnp.concatenate(terms, axis=0).astype(jnp.bfloat16), TN)
    rows_ref[...] = dot(placing_ref[:, KEYS_SEEN:], late_ref[...], NT)
    for copy in copies[5:]:
        copy.wait()


def second_kernel(q_ref, kv_ref, before_ref, rim_ref, sinks_ref, late_ref, placing_ref, *refs):
    late_rows_ref, mixed_ref, peaks_ref, sums_ref, all_ref, rows_ref = refs
    rim = jnp.where(lax.axis_index("seq") == 0, before_ref[...], rim_ref[...])
    groups = rim.shape[1] // PAIR
    key, query = key_query(SPAN)
    allowed = (key > query) & (key <= query + KEYS_SEEN)
    key, query = key_query(KEYS_SEEN)
    for g in range(groups):
        first, pairs = group_queries(q_ref, g, groups, 0)
        sinks = [sinks_ref[h : h + 1] for h in range(2 * first, 2 * (first + len(pairs)))]
        lanes = slice(g * PAIR, (g + 1) * PAIR)
        if g >= mixed_ref.shape[0]:
            both = jnp.concatenate([rim[:, lanes], kv_ref[:KEYS_SEEN, lanes]], axis=0)
            store_pairs(attend_block(pairs, both, sinks, allowed), first, all_ref, slice(0, KEYS_SEEN))
            continue
        keys, values = split_pair(rim[:, lanes])
        terms, scales, inverses = [], [], []
        for i, part in enumerate(score(pairs, keys, key > query)):
            sink = sink_row(sinks, i, len(pairs))
            own_peak = peaks_ref[2 * g + i : 2 * g + i + 1]
            peak = jnp.maximum(jnp.max(part, axis=0, keepdims=True), jnp.maximum(own_peak, sink))
            scale = jnp.exp2(own_peak - peak)
            terms.append(jnp.exp2(part - peak))
            denom = jnp.sum(terms[-1], axis=0, keepdims=True) + jnp.exp2(sink - peak)
            denom += sums_ref[2 * g + i : 2 * g + i + 1] * scale
            inverses.append(1.0 / denom)
            scales.append(scale)
        mixed = dot(values, jnp.concatenate(terms, axis=0).astype(jnp.bfloat16), TN)
        mixed = (mixed + mixed_ref[g] * per_head(scales)) * per_head(inverses)
        store_pairs(mixed.astype(jnp.bfloat16), first, all_ref, slice(0, KEYS_SEEN))
    rows = late_rows_ref[...] + dot(placing_ref[:, :KEYS_SEEN], all_ref[:, :KEYS_SEEN], NT)
    rows_ref[...] = rows.astype(jnp.bfloat16)
    all_ref[:, KEYS_SEEN:] = late_ref[...]


def origin(k, sibling):
    me = lax.axis_index("cuts")
    return lax.bitwise_xor(me, CORES * k + (1 if sibling else 0))


def add_products(total, places, blocks, w_ref, steps, dims, swapped=False):
    width = blocks[0].shape[0 if swapped else 1] if blocks else 0
    for i, block in zip(places, blocks):
        at = pl.multiple_of(origin(i % steps, i >= steps) * width, 128)
        w = w_ref[:, pl.ds(at, width)]
        total += dot(w, block[...], dims) if swapped else dot(block[...], w, dims)
    return total


def rows_own_kernel(steps, rows_ref, w_ref, residual_ref, placing_ref, total_ref):
    total = dot(placing_ref[...], residual_ref[...], NT)
    total_ref[...] = add_products(total, [0], [rows_ref], w_ref, steps, NT)


def rows_more_kernel(places, steps, *refs):
    blocks, (before_ref, w_ref, total_ref) = refs[:-3], refs[-3:]
    total_ref[...] = add_products(before_ref[...], places, blocks, w_ref, steps, NT)


def rows_last_kernel(steps, *refs):
    blocks, (before_ref, w_ref) = refs[: steps - 1], refs[steps - 1 : steps + 1]
    outgoing, rows_ref = refs[steps + 1 : -1], refs[-1]
    total = add_products(before_ref[...], range(1, steps), blocks, w_ref, steps, NT)
    rows_ref[...] = total.astype(jnp.bfloat16).reshape(rows_ref.shape)
    me = lax.axis_index("seq")
    for k, out_ref in enumerate(outgoing):
        out_ref[...] = rows_ref[lax.bitwise_xor(me, k)]


def stack_kernel(*refs):
    for i, block in enumerate(refs[:-1]):
        refs[-1][i * CAP : (i + 1) * CAP] = block[...]


def project_kernel(steps, *refs):
    blocks = refs[: 2 * steps]
    w_ref, residual_ref, resid_ref = refs[2 * steps :]
    total = residual_ref[...].astype(jnp.float32)
    total = add_products(total, range(2 * steps), blocks, w_ref, steps, NN, True)
    resid_ref[...] = total.astype(jnp.bfloat16)


def spread_kernel(source_ref, blocks_ref):
    cuts, _, width = blocks_ref.shape
    for p in range(cuts):
        blocks_ref[p] = source_ref[:, p * width : (p + 1) * width]


def spread_gain_kernel(gain_ref, blocks_ref):
    cuts, _, width = blocks_ref.shape
    gain = gain_ref[...].reshape(1, cuts * width)
    for p in range(cuts):
        blocks_ref[p] = gain[:, p * width : (p + 1) * width]


def add_features(sums, places, blocks, gains_ref, gates_ref, ups_ref, steps):
    gate, up, squares = sums
    for i, block in zip(places, blocks):
        p = origin(i % steps, i >= steps)
        wide = block[...].astype(jnp.float32)
        squares += jnp.sum(wide * wide, axis=1, keepdims=True)
        rows = (wide * gains_ref[p]).astype(jnp.bfloat16)
        gate += dot(rows, gates_ref[p], NT)
        up += dot(rows, ups_ref[p], NT)
    return gate, up, squares


def store_sums(sums, refs):
    for ref, value in zip(refs, sums):
        ref[...] = jnp.broadcast_to(value, ref.shape)


def expert_own_kernel(steps, block_ref, gains_ref, gates_ref, ups_ref, *out_refs):
    zeros = jnp.zeros(out_refs[0].shape, jnp.float32)
    sums = (zeros, zeros, jnp.zeros((zeros.shape[0], 1), jnp.float32))
    store_sums(add_features(sums, [steps], [block_ref], gains_ref, gates_ref, ups_ref, steps), out_refs)


def expert_more_kernel(places, steps, *refs):
    blocks, refs = refs[:-9], refs[-9:]
    sums = (refs[0][...], refs[1][...], refs[2][:, :1])
    store_sums(add_features(sums, places, blocks, *refs[3:6], steps), refs[6:])


def expert_last_kernel(steps, *refs):
    blocks, refs = refs[: steps - 1], refs[steps - 1 :]
    sums = (refs[0][...], refs[1][...], refs[2][:, :1])
    gains_ref, gates_ref, ups_ref, downs_ref, given_ref, activated_ref = refs[3:]
    places = range(1, steps)
    gate, up, squares = add_features(sums, places, blocks, gains_ref, gates_ref, ups_ref, steps)
    cuts, _, width = gates_ref.shape
    scale = lax.rsqrt(squares / (cuts * width) + norm_eps)
    gate, up = gate * scale, up * scale
    activated = ((up + 1.0) * gate * jax.nn.sigmoid(glu_alpha * gate)).astype(jnp.bfloat16)
    activated_ref[...] = activated
    for k in range(steps):
        given_ref[k] = dot(activated, downs_ref[origin(k, k > 0)], NN).astype(jnp.bfloat16)


def expert_kept_kernel(activated_ref, downs_ref, kept_ref):
    for k in range(kept_ref.shape[0]):
        kept_ref[k] = dot(activated_ref[...], downs_ref[origin(k, k == 0)], NN).astype(jnp.bfloat16)


def add_cores_kernel(kept_ref, given_ref, *out_refs):
    half = out_refs[0].shape[0]
    for i, out_ref in enumerate(out_refs):
        rows = slice(i % 2 * half, (i % 2 + 1) * half)
        total = kept_ref[i // 2, rows].astype(jnp.float32) + given_ref[i // 2, rows].astype(jnp.float32)
        out_ref[...] = total.astype(jnp.bfloat16)


def add_chips_kernel(steps, *refs):
    total = sum(r[...].astype(jnp.float32) for r in refs[:steps])
    for k, out_ref in enumerate(refs[steps:]):
        out_ref[...] = total[k * CAP : (k + 1) * CAP].astype(jnp.bfloat16)


def combine_kernel(live, parts, *refs):
    blocks = refs[:live]
    mix_hi_ref, mix_lo_ref, resid_ref, out_ref, rows_ref, held_ref, sems = refs[live:]
    me = lax.axis_index("seq")
    for k in range(live):
        rows_ref[lax.bitwise_xor(me, live - 1 - k)] = blocks[k][...]
    rows = rows_ref[...].reshape(live * CAP, -1)
    rows = jnp.concatenate([rows, rows], axis=0)
    mix = jnp.concatenate([mix_hi_ref[...], mix_lo_ref[...]], axis=0)
    copies = []
    for i, (start, stop) in enumerate(parts):
        part = slice(start, stop)
        mixed = dot(rows[:, part], mix, TN)
        held_ref[part] = (resid_ref[part].astype(jnp.float32) + mixed).astype(jnp.bfloat16)
        copies.append(pltpu.make_async_copy(held_ref.at[part], out_ref.at[part], sems.at[i]))
        copies[-1].start()
    for copy in copies:
        copy.wait()


def swap(block, axis, mask):
    return lax.ppermute(block, axis, [(i, i ^ mask) for i in range(lax.axis_size(axis))])


def to_chip(block, k, other=True):
    return swap(block, "cuts", CORES * k + other)


def from_chips(block, other=True):
    return [to_chip(block, k, other) for k in range(1, lax.axis_size("cuts") // CORES)]


def to_seq(block, k):
    size = lax.axis_size("seq") * lax.axis_size("cuts")
    mask = k * lax.axis_size("cuts") + 1
    return lax.ppermute(block, ("seq", "cuts"), [(i, i ^ mask) for i in range(size)])


def from_sibling(block):
    return swap(block, "cuts", 1)


def after(arrays, others):
    return lax.optimization_barrier((arrays, others))[0]


def shards(
    queries,
    keyvals,
    preceding_keyvalues,
    attention_sink_logits,
    residual,
    w_out,
    norm_gain,
    expert_ids,
    route_weights,
    w_gate,
    w_up,
    w_down,
):
    toks, feats = residual.shape
    size = lax.axis_size("seq")
    live = w_gate.shape[0] * size
    cuts = lax.axis_size("cuts")
    steps = cuts // CORES
    slots = live * CAP
    head_rows = queries.shape[1]
    heads = head_rows // HEAD_SIZE
    width = norm_gain.shape[0]
    hidden = w_gate.shape[2]

    tail = keyvals[toks - KEYS_SEEN :]
    rim = lax.ppermute(tail, "seq", [(i, (i + 1) % size) for i in range(size)])
    loads = (queries, keyvals, preceding_keyvalues, w_out.T, residual.T)
    groups = keyvals.shape[1] // PAIR
    across = head_rows // PAIR // groups * KEYS_SEEN
    early = (groups + 1) // 2
    part_sums = jax.ShapeDtypeStruct((2 * early, across), jnp.float32)
    q, kv, before, w_t, residual_t, placing, mix_hi, mix_lo, sinks, late, *parts = call(
        functools.partial(first_kernel, live),
        (
            *(bf16(*a.shape) for a in loads),
            *(bf16(slots, toks),) * 3,
            jax.ShapeDtypeStruct((heads, KEYS_SEEN), jnp.float32),
            bf16(head_rows, toks - KEYS_SEEN),
            jax.ShapeDtypeStruct((slots, head_rows), jnp.float32),
            jax.ShapeDtypeStruct((early, PAIR, across), jnp.float32),
            part_sums,
            part_sums,
        ),
        n_in=8,
        scratch=[
            pltpu.VMEM(expert_ids.T.shape, jnp.int32),
            pltpu.VMEM(expert_ids.T.shape, jnp.float32),
            pltpu.SMEM(attention_sink_logits.shape, jnp.float32),
            pltpu.SemaphoreType.DMA((8,)),
        ],
        hbm=range(8),
        flops=4 * toks * SPAN * head_rows,
        moved=2 * (w_out.size + residual.size + queries.size),
    )(*(in_hbm(a) for a in (expert_ids.T, route_weights.T, attention_sink_logits, *loads)))
    attended, rows = call(
        second_kernel,
        (bf16(head_rows, toks), bf16(slots, head_rows)),
        n_in=11,
        flops=2 * toks * SPAN * head_rows,
        moved=2 * queries.size,
    )(q, kv, before, rim, sinks, late, placing, *parts)

    chip_rows = from_chips(rows)
    total = jax.ShapeDtypeStruct((slots, feats), jnp.float32)
    part = dict(flops=slots * w_out.size // 2, moved=w_out.size // 2)
    own = call(functools.partial(rows_own_kernel, steps), total, n_in=4, **part)(
        rows, w_t, residual_t, placing
    )
    sibling_rows = from_sibling(rows)
    places = range(steps, 2 * steps)
    spread = functools.partial(
        call, spread_kernel, bf16(cuts, hidden, feats), n_in=1, moved=4 * w_gate.size
    )
    gates = spread()(after(w_gate[0].T, rows))
    chip_rows = after(chip_rows, (own, gates))
    relayed_rows = [from_sibling(b) for b in chip_rows]
    chips = call(functools.partial(rows_more_kernel, places, steps), total, n_in=steps + 2, **part)(
        sibling_rows, *chip_rows, own, w_t
    )
    outgoing = call(
        functools.partial(rows_last_kernel, steps),
        (bf16(CAP, feats),) * live,
        n_in=steps + 1,
        scratch=[pltpu.VMEM((live, CAP, feats), jnp.bfloat16)],
        **part,
    )(*relayed_rows, chips, w_t)

    arrived = [to_seq(outgoing[k], k) for k in range(live - 1, -1, -1)]

    ups = spread()(after(w_up[0].T, outgoing[0]))
    gains = call(spread_gain_kernel, jax.ShapeDtypeStruct((cuts, 1, feats), jnp.float32), n_in=1)(norm_gain)
    sums = (
        *(jax.ShapeDtypeStruct((slots, hidden), jnp.float32),) * 2,
        jax.ShapeDtypeStruct((slots, KEYS_SEEN), jnp.float32),
    )
    part = dict(flops=slots * w_gate.size, moved=w_gate.size)
    stacked = call(stack_kernel, bf16(slots, feats), n_in=live)(*after(arrived, (ups, gains)))
    chip_rows = from_chips(stacked, False)
    own = call(functools.partial(expert_own_kernel, steps), sums, n_in=4, **part)(stacked, gains, gates, ups)
    sibling_rows = from_sibling(stacked)
    downs = spread()(after(w_down[0], stacked))
    chip_blocks = from_chips(after(attended, gates))
    sibling_block, *relayed_blocks = [from_sibling(b) for b in (attended, *chip_blocks)]
    blocks = [attended, *relayed_blocks, sibling_block, *chip_blocks]
    chip_rows = after(chip_rows, (own, downs))
    relayed_rows = [from_sibling(b) for b in chip_rows]
    chips = call(functools.partial(expert_more_kernel, [0, *range(steps + 1, 2 * steps)], steps), sums, n_in=steps + 6, **part)(
        sibling_rows, *chip_rows, *own, gains, gates, ups
    )
    given, activated = call(
        functools.partial(expert_last_kernel, steps),
        (bf16(steps, slots, feats), bf16(slots, hidden)),
        n_in=steps + 6,
        **part,
    )(*relayed_rows, *chips, gains, gates, ups, downs)
    kept = call(expert_kept_kernel, bf16(steps, slots, feats), n_in=2, **part)(activated, downs)
    resid = call(
        functools.partial(project_kernel, steps),
        bf16(feats, toks),
        n_in=cuts + 2,
        flops=2 * toks * w_out.size,
        moved=2 * w_out.size,
    )(*blocks, w_t, residual_t)

    sums = call(add_cores_kernel, (bf16(slots // 2, feats),) * (2 * steps), n_in=2)(
        kept, swap(given, "cuts", 1)
    )
    returned = []
    for half in range(2):
        parts = [sums[half]] + [to_chip(sums[2 * k + half], k) for k in range(1, steps)]
        blocks = call(functools.partial(add_chips_kernel, steps), (bf16(CAP, feats),) * (live // 2), n_in=steps)(
            *parts
        )
        for block in blocks:
            returned.append(to_seq(block, live - 1 - len(returned)))
    bounds = [*range(0, feats, SPAN), feats] if feats % 16 == 0 else [0, feats]
    parts = list(zip(bounds[:-1], bounds[1:]))
    out = call(
        functools.partial(combine_kernel, live, parts),
        bf16(feats, toks),
        n_in=live + 3,
        scratch=[
            pltpu.VMEM((live, CAP, feats), jnp.bfloat16),
            pltpu.VMEM((feats, toks), jnp.bfloat16),
            pltpu.SemaphoreType.DMA((len(parts),)),
        ],
        out_space=pltpu.HBM,
    )(*returned, mix_hi, mix_lo, resid)
    return out.T


def solution(mesh):
    placed = (
        P(("groups", "seq"), "cuts"),
        P(("groups", "seq"), "cuts"),
        P("groups", "cuts"),
        P("cuts"),
        P(("groups", "seq"), "cuts"),
        P(None, "cuts"),
        P(),
        P(("groups", "seq"), None),
        P(("groups", "seq"), None),
        P("seq", None, "cuts"),
        P("seq", None, "cuts"),
        P("seq", "cuts", None),
    )
    return jax.shard_map(
        shards, mesh=mesh, in_specs=placed, out_specs=P(("groups", "seq"), "cuts"), check_vma=False
    )
```

```python
import functools
import math

import jax
import jax.numpy as jnp
from jax import lax
from jax.experimental import pallas as pl
from jax.experimental.pallas import tpu as pltpu
from jax.sharding import PartitionSpec as P

HEAD_SIZE = 64
KEYS_SEEN = 128
PAIR = 2 * HEAD_SIZE
SPAN = 2 * KEYS_SEEN
CAP = 16
CORES = 2

norm_eps = 1e-05
glu_alpha = 1.702

NT = (((1,), (1,)), ((), ()))
NN = (((1,), (0,)), ((), ()))
TN = (((0,), (0,)), ((), ()))
VMEM_LIMIT = 32 * 1024 * 1024


def dot(a, b, dims):
    return lax.dot_general(a, b, dims, preferred_element_type=jnp.float32)


def call(kernel, outs, n_in, scratch=(), hbm=(), out_space=pltpu.VMEM, flops=0, moved=0):
    spaces = [pltpu.HBM if i in hbm else pltpu.VMEM for i in range(n_in)]
    return pl.pallas_call(
        kernel,
        out_shape=outs,
        in_specs=[pl.BlockSpec(memory_space=space) for space in spaces],
        out_specs=jax.tree.map(lambda _: pl.BlockSpec(memory_space=out_space), outs),
        scratch_shapes=list(scratch),
        compiler_params=pltpu.CompilerParams(vmem_limit_bytes=VMEM_LIMIT),
        cost_estimate=pl.CostEstimate(flops=flops, bytes_accessed=moved, transcendentals=0),
    )


def in_hbm(array):
    return pltpu.with_memory_space_constraint(array, pltpu.HBM)


def bf16(*shape):
    return jax.ShapeDtypeStruct(shape, jnp.bfloat16)


def split_pair(both):
    both = both.astype(jnp.float32)
    low = lax.broadcasted_iota(jnp.int32, both.shape, 1) < HEAD_SIZE
    turned = pltpu.roll(both, HEAD_SIZE, 1)
    keys = jnp.concatenate([jnp.where(low, both, 0.0), jnp.where(low, 0.0, turned)], axis=0)
    values = jnp.concatenate([jnp.where(low, turned, 0.0), jnp.where(low, 0.0, both)], axis=0)
    return keys.astype(jnp.bfloat16), values.astype(jnp.bfloat16)


def score(pairs, keys, allowed):
    scores = dot(keys, jnp.concatenate(pairs, axis=0), NT) * (HEAD_SIZE**-0.5 * math.log2(math.e))
    allowed = jnp.concatenate([allowed] * len(pairs), axis=1)
    span = allowed.shape[0]
    return [jnp.where(allowed, scores[i * span : (i + 1) * span], -jnp.inf) for i in range(2)]


def sink_row(sinks, i, pairs):
    return jnp.concatenate([sinks[2 * p + i] for p in range(pairs)], axis=1)


def attend_block(pairs, both, sinks, allowed):
    keys, values = split_pair(both)
    probs = []
    for i, part in enumerate(score(pairs, keys, allowed)):
        sink = sink_row(sinks, i, len(pairs))
        peak = jnp.maximum(jnp.max(part, axis=0, keepdims=True), sink)
        terms = jnp.exp2(part - peak)
        denom = jnp.sum(terms, axis=0, keepdims=True) + jnp.exp2(sink - peak)
        probs.append((terms * (1.0 / denom)).astype(jnp.bfloat16))
    return dot(values, jnp.concatenate(probs, axis=0), TN).astype(jnp.bfloat16)


def group_queries(q_ref, g, groups, block):
    per_group = q_ref.shape[1] // PAIR // groups
    first = g * per_group
    toks = slice(block * KEYS_SEEN, (block + 1) * KEYS_SEEN)
    pairs = [q_ref[toks, (first + p) * PAIR : (first + p + 1) * PAIR] for p in range(per_group)]
    return first, pairs


def store_pairs(mixed, first, out_ref, lanes):
    for p in range(mixed.shape[1] // KEYS_SEEN):
        rows = slice((first + p) * PAIR, (first + p + 1) * PAIR)
        out_ref[rows, lanes] = mixed[:, p * KEYS_SEEN : (p + 1) * KEYS_SEEN]


def key_query(span):
    key = lax.broadcasted_iota(jnp.int32, (span, KEYS_SEEN), 0)
    return key, lax.broadcasted_iota(jnp.int32, (span, KEYS_SEEN), 1)


def per_head(pair):
    return jnp.concatenate([jnp.broadcast_to(row, (HEAD_SIZE, row.shape[1])) for row in pair], axis=0)


def tail_kernel(rows_ref, tail_ref, sem):
    copy = pltpu.make_async_copy(rows_ref.at[rows_ref.shape[0] - KEYS_SEEN :], tail_ref, sem)
    copy.start()
    copy.wait()


def fill_tables(live, ids, weights, placing_ref, mix_hi_ref, mix_lo_ref):
    toks = ids.shape[1]
    chosen = jnp.concatenate(
        [jnp.max((ids == e).astype(jnp.float32), axis=0, keepdims=True) for e in range(live)], axis=0
    )
    earlier = lax.broadcasted_iota(jnp.int32, (toks, toks), 0)
    later = lax.broadcasted_iota(jnp.int32, (toks, toks), 1)
    strict = (earlier < later).astype(jnp.bfloat16)
    before = dot(chosen.astype(jnp.bfloat16), strict, NN)
    slot = lax.broadcasted_iota(jnp.int32, (CAP, toks), 0).astype(jnp.float32)
    for e in range(live):
        weight = jnp.sum(jnp.where(ids == e, weights, 0.0), axis=0, keepdims=True)
        fills = (before[e : e + 1] == slot) & (chosen[e : e + 1] > 0.0)
        mix = jnp.where(fills, weight, 0.0)
        hi = mix.astype(jnp.bfloat16)
        rows = slice(e * CAP, (e + 1) * CAP)
        placing_ref[rows] = fills.astype(jnp.bfloat16)
        mix_hi_ref[rows] = hi
        mix_lo_ref[rows] = (mix - hi.astype(jnp.float32)).astype(jnp.bfloat16)


def first_kernel(live, *refs):
    loaded, held = refs[:8], refs[8:13]
    placing_ref, mix_hi_ref, mix_lo_ref, sinks_out, late_ref, rows_ref, mixed_ref, peaks_ref, sums_ref = refs[13:22]
    ids_ref, weights_ref, sinks_ref, sems = refs[22:]
    targets = (ids_ref, weights_ref, sinks_ref, *held)
    copies = [pltpu.make_async_copy(*pair, sems.at[i]) for i, pair in enumerate(zip(loaded, targets))]
    for copy in copies:
        copy.start()
    q_ref, kv_ref = held[:2]
    for copy in copies[:2]:
        copy.wait()
    fill_tables(live, ids_ref[...], weights_ref[...], placing_ref, mix_hi_ref, mix_lo_ref)
    for copy in copies[2:5]:
        copy.wait()
    heads = sinks_ref.shape[0]
    sinks = [jnp.full((1, KEYS_SEEN), sinks_ref[h], jnp.float32) * math.log2(math.e) for h in range(heads)]
    sinks_out[...] = jnp.concatenate(sinks, axis=0)
    groups = kv_ref.shape[1] // PAIR
    key, query = key_query(SPAN)
    allowed = (key > query) & (key <= query + KEYS_SEEN)
    for b in range(1, q_ref.shape[0] // KEYS_SEEN):
        span = slice((b - 1) * KEYS_SEEN, (b + 1) * KEYS_SEEN)
        for g in range(groups):
            first, pairs = group_queries(q_ref, g, groups, b)
            part = sinks[2 * first : 2 * (first + len(pairs))]
            mixed = attend_block(pairs, kv_ref[span, g * PAIR : (g + 1) * PAIR], part, allowed)
            store_pairs(mixed, first, late_ref, slice((b - 1) * KEYS_SEEN, b * KEYS_SEEN))
    key, query = key_query(KEYS_SEEN)
    for g in range(mixed_ref.shape[0]):
        _, pairs = group_queries(q_ref, g, groups, 0)
        keys, values = split_pair(kv_ref[:KEYS_SEEN, g * PAIR : (g + 1) * PAIR])
        terms = []
        for i, part in enumerate(score(pairs, keys, key <= query)):
            peak = jnp.max(part, axis=0, keepdims=True)
            terms.append(jnp.exp2(part - peak))
            peaks_ref[2 * g + i : 2 * g + i + 1] = peak
            sums_ref[2 * g + i : 2 * g + i + 1] = jnp.sum(terms[-1], axis=0, keepdims=True)
        mixed_ref[g] = dot(values, jnp.concatenate(terms, axis=0).astype(jnp.bfloat16), TN)
    rows_ref[...] = dot(placing_ref[:, KEYS_SEEN:], late_ref[...], NT)
    for copy in copies[5:]:
        copy.wait()


def second_kernel(q_ref, kv_ref, before_ref, rim_ref, sinks_ref, late_ref, placing_ref, *refs):
    late_rows_ref, mixed_ref, peaks_ref, sums_ref, all_ref, rows_ref = refs
    rim = jnp.where(lax.axis_index("seq") == 0, before_ref[...], rim_ref[...])
    groups = rim.shape[1] // PAIR
    key, query = key_query(SPAN)
    allowed = (key > query) & (key <= query + KEYS_SEEN)
    key, query = key_query(KEYS_SEEN)
    for g in range(groups):
        first, pairs = group_queries(q_ref, g, groups, 0)
        sinks = [sinks_ref[h : h + 1] for h in range(2 * first, 2 * (first + len(pairs)))]
        lanes = slice(g * PAIR, (g + 1) * PAIR)
        if g >= mixed_ref.shape[0]:
            both = jnp.concatenate([rim[:, lanes], kv_ref[:KEYS_SEEN, lanes]], axis=0)
            store_pairs(attend_block(pairs, both, sinks, allowed), first, all_ref, slice(0, KEYS_SEEN))
            continue
        keys, values = split_pair(rim[:, lanes])
        terms, scales, inverses = [], [], []
        for i, part in enumerate(score(pairs, keys, key > query)):
            sink = sink_row(sinks, i, len(pairs))
            own_peak = peaks_ref[2 * g + i : 2 * g + i + 1]
            peak = jnp.maximum(jnp.max(part, axis=0, keepdims=True), jnp.maximum(own_peak, sink))
            scale = jnp.exp2(own_peak - peak)
            terms.append(jnp.exp2(part - peak))
            denom = jnp.sum(terms[-1], axis=0, keepdims=True) + jnp.exp2(sink - peak)
            denom += sums_ref[2 * g + i : 2 * g + i + 1] * scale
            inverses.append(1.0 / denom)
            scales.append(scale)
        mixed = dot(values, jnp.concatenate(terms, axis=0).astype(jnp.bfloat16), TN)
        mixed = (mixed + mixed_ref[g] * per_head(scales)) * per_head(inverses)
        store_pairs(mixed.astype(jnp.bfloat16), first, all_ref, slice(0, KEYS_SEEN))
    rows = late_rows_ref[...] + dot(placing_ref[:, :KEYS_SEEN], all_ref[:, :KEYS_SEEN], NT)
    rows_ref[...] = rows.astype(jnp.bfloat16)
    all_ref[:, KEYS_SEEN:] = late_ref[...]


def origin(k, sibling):
    me = lax.axis_index("cuts")
    return lax.bitwise_xor(me, CORES * k + (1 if sibling else 0))


def add_products(total, places, blocks, w_ref, steps, dims, swapped=False):
    width = blocks[0].shape[0 if swapped else 1] if blocks else 0
    for i, block in zip(places, blocks):
        at = pl.multiple_of(origin(i % steps, i >= steps) * width, 128)
        w = w_ref[:, pl.ds(at, width)]
        total += dot(w, block[...], dims) if swapped else dot(block[...], w, dims)
    return total


def rows_own_kernel(steps, rows_ref, w_ref, residual_ref, placing_ref, total_ref):
    total = dot(placing_ref[...], residual_ref[...], NT)
    total_ref[...] = add_products(total, [0], [rows_ref], w_ref, steps, NT)


def rows_more_kernel(places, steps, *refs):
    blocks, (before_ref, w_ref, total_ref) = refs[:-3], refs[-3:]
    total_ref[...] = add_products(before_ref[...], places, blocks, w_ref, steps, NT)


def rows_last_kernel(steps, *refs):
    blocks, (before_ref, w_ref) = refs[: steps - 1], refs[steps - 1 : steps + 1]
    outgoing, rows_ref = refs[steps + 1 : -1], refs[-1]
    total = add_products(before_ref[...], range(1, steps), blocks, w_ref, steps, NT)
    rows_ref[...] = total.astype(jnp.bfloat16).reshape(rows_ref.shape)
    me = lax.axis_index("seq")
    for k, out_ref in enumerate(outgoing):
        out_ref[...] = rows_ref[lax.bitwise_xor(me, k)]


def stack_kernel(*refs):
    for i, block in enumerate(refs[:-1]):
        refs[-1][i * CAP : (i + 1) * CAP] = block[...]


def project_kernel(steps, *refs):
    blocks = refs[: 2 * steps]
    w_ref, residual_ref, resid_ref = refs[2 * steps :]
    total = residual_ref[...].astype(jnp.float32)
    total = add_products(total, range(2 * steps), blocks, w_ref, steps, NN, True)
    resid_ref[...] = total.astype(jnp.bfloat16)


def spread_kernel(source_ref, blocks_ref):
    cuts, _, width = blocks_ref.shape
    for p in range(cuts):
        blocks_ref[p] = source_ref[:, p * width : (p + 1) * width]


def spread_gain_kernel(gain_ref, blocks_ref):
    cuts, _, width = blocks_ref.shape
    gain = gain_ref[...].reshape(1, cuts * width)
    for p in range(cuts):
        blocks_ref[p] = gain[:, p * width : (p + 1) * width]


def add_features(sums, places, blocks, gains_ref, gates_ref, ups_ref, steps):
    gate, up, squares = sums
    for i, block in zip(places, blocks):
        p = origin(i % steps, i >= steps)
        wide = block[...].astype(jnp.float32)
        squares += jnp.sum(wide * wide, axis=1, keepdims=True)
        rows = (wide * gains_ref[p]).astype(jnp.bfloat16)
        gate += dot(rows, gates_ref[p], NT)
        up += dot(rows, ups_ref[p], NT)
    return gate, up, squares


def store_sums(sums, refs):
    for ref, value in zip(refs, sums):
        ref[...] = jnp.broadcast_to(value, ref.shape)


def expert_own_kernel(steps, block_ref, gains_ref, gates_ref, ups_ref, *out_refs):
    zeros = jnp.zeros(out_refs[0].shape, jnp.float32)
    sums = (zeros, zeros, jnp.zeros((zeros.shape[0], 1), jnp.float32))
    store_sums(add_features(sums, [steps], [block_ref], gains_ref, gates_ref, ups_ref, steps), out_refs)


def expert_more_kernel(places, steps, *refs):
    blocks, refs = refs[:-9], refs[-9:]
    sums = (refs[0][...], refs[1][...], refs[2][:, :1])
    store_sums(add_features(sums, places, blocks, *refs[3:6], steps), refs[6:])


def expert_last_kernel(steps, *refs):
    blocks, refs = refs[: steps - 1], refs[steps - 1 :]
    sums = (refs[0][...], refs[1][...], refs[2][:, :1])
    gains_ref, gates_ref, ups_ref, downs_ref, given_ref, activated_ref = refs[3:]
    places = range(1, steps)
    gate, up, squares = add_features(sums, places, blocks, gains_ref, gates_ref, ups_ref, steps)
    cuts, _, width = gates_ref.shape
    scale = lax.rsqrt(squares / (cuts * width) + norm_eps)
    gate, up = gate * scale, up * scale
    activated = ((up + 1.0) * gate * jax.nn.sigmoid(glu_alpha * gate)).astype(jnp.bfloat16)
    activated_ref[...] = activated
    for k in range(1, steps):
        given_ref[k - 1] = dot(activated, downs_ref[origin(k, True)], NN).astype(jnp.bfloat16)


def expert_rest_kernel(activated_ref, downs_ref, far_ref, near_ref, given_ref):
    for k in range(1, far_ref.shape[0] + 1):
        far_ref[k - 1] = dot(activated_ref[...], downs_ref[origin(k, False)], NN).astype(jnp.bfloat16)
    near_ref[0] = dot(activated_ref[...], downs_ref[origin(0, True)], NN).astype(jnp.bfloat16)
    given_ref[0] = dot(activated_ref[...], downs_ref[origin(0, False)], NN).astype(jnp.bfloat16)


def add_cores_kernel(kept_ref, given_ref, *out_refs):
    half = out_refs[0].shape[0]
    for i, out_ref in enumerate(out_refs):
        rows = slice(i % 2 * half, (i % 2 + 1) * half)
        total = kept_ref[i // 2, rows].astype(jnp.float32) + given_ref[i // 2, rows].astype(jnp.float32)
        out_ref[...] = total.astype(jnp.bfloat16)


def add_chips_kernel(steps, *refs):
    total = sum(r[...].astype(jnp.float32) for r in refs[:steps])
    for k, out_ref in enumerate(refs[steps:]):
        out_ref[...] = total[k * CAP : (k + 1) * CAP].astype(jnp.bfloat16)


def combine_kernel(live, parts, *refs):
    blocks = refs[:live]
    mix_hi_ref, mix_lo_ref, resid_ref, out_ref, rows_ref, held_ref, sems = refs[live:]
    me = lax.axis_index("seq")
    for k in range(live):
        rows_ref[lax.bitwise_xor(me, live - 1 - k)] = blocks[k][...]
    rows = rows_ref[...].reshape(live * CAP, -1)
    rows = jnp.concatenate([rows, rows], axis=0)
    mix = jnp.concatenate([mix_hi_ref[...], mix_lo_ref[...]], axis=0)
    copies = []
    for i, (start, stop) in enumerate(parts):
        part = slice(start, stop)
        mixed = dot(rows[:, part], mix, TN)
        held_ref[part] = (resid_ref[part].astype(jnp.float32) + mixed).astype(jnp.bfloat16)
        copies.append(pltpu.make_async_copy(held_ref.at[part], out_ref.at[part], sems.at[i]))
        copies[-1].start()
    for copy in copies:
        copy.wait()


def swap(block, axis, mask):
    return lax.ppermute(block, axis, [(i, i ^ mask) for i in range(lax.axis_size(axis))])


def to_chip(block, k, other=True):
    return swap(block, "cuts", CORES * k + other)


def from_chips(block, other=True):
    return [to_chip(block, k, other) for k in range(1, lax.axis_size("cuts") // CORES)]


def to_seq(block, k):
    size = lax.axis_size("seq") * lax.axis_size("cuts")
    mask = k * lax.axis_size("cuts") + 1
    return lax.ppermute(block, ("seq", "cuts"), [(i, i ^ mask) for i in range(size)])


def from_sibling(block):
    return swap(block, "cuts", 1)


def after(arrays, others):
    return lax.optimization_barrier((arrays, others))[0]


def shards(
    queries,
    keyvals,
    preceding_keyvalues,
    attention_sink_logits,
    residual,
    w_out,
    norm_gain,
    expert_ids,
    route_weights,
    w_gate,
    w_up,
    w_down,
):
    toks, feats = residual.shape
    size = lax.axis_size("seq")
    live = w_gate.shape[0] * size
    cuts = lax.axis_size("cuts")
    steps = cuts // CORES
    slots = live * CAP
    head_rows = queries.shape[1]
    heads = head_rows // HEAD_SIZE
    width = norm_gain.shape[0]
    hidden = w_gate.shape[2]

    tail = call(
        tail_kernel, bf16(KEYS_SEEN, keyvals.shape[1]), n_in=1, hbm=(0,), scratch=[pltpu.SemaphoreType.DMA]
    )(in_hbm(keyvals))
    rim = lax.ppermute(tail, "seq", [(i, (i + 1) % size) for i in range(size)])
    loads = (queries, keyvals, preceding_keyvalues, w_out.T, residual.T)
    groups = keyvals.shape[1] // PAIR
    across = head_rows // PAIR // groups * KEYS_SEEN
    early = (groups + 1) // 2
    part_sums = jax.ShapeDtypeStruct((2 * early, across), jnp.float32)
    q, kv, before, w_t, residual_t, placing, mix_hi, mix_lo, sinks, late, *parts = call(
        functools.partial(first_kernel, live),
        (
            *(bf16(*a.shape) for a in loads),
            *(bf16(slots, toks),) * 3,
            jax.ShapeDtypeStruct((heads, KEYS_SEEN), jnp.float32),
            bf16(head_rows, toks - KEYS_SEEN),
            jax.ShapeDtypeStruct((slots, head_rows), jnp.float32),
            jax.ShapeDtypeStruct((early, PAIR, across), jnp.float32),
            part_sums,
            part_sums,
        ),
        n_in=8,
        scratch=[
            pltpu.VMEM(expert_ids.T.shape, jnp.int32),
            pltpu.VMEM(expert_ids.T.shape, jnp.float32),
            pltpu.SMEM(attention_sink_logits.shape, jnp.float32),
            pltpu.SemaphoreType.DMA((8,)),
        ],
        hbm=range(8),
        flops=4 * toks * SPAN * head_rows,
        moved=2 * (w_out.size + residual.size + queries.size),
    )(*(in_hbm(a) for a in (expert_ids.T, route_weights.T, attention_sink_logits, *loads)))
    attended, rows = call(
        second_kernel,
        (bf16(head_rows, toks), bf16(slots, head_rows)),
        n_in=11,
        flops=2 * toks * SPAN * head_rows,
        moved=2 * queries.size,
    )(q, kv, before, rim, sinks, late, placing, *parts)

    chip_rows = from_chips(rows)
    total = jax.ShapeDtypeStruct((slots, feats), jnp.float32)
    part = dict(flops=slots * w_out.size // 2, moved=w_out.size // 2)
    own = call(functools.partial(rows_own_kernel, steps), total, n_in=4, **part)(
        rows, w_t, residual_t, placing
    )
    sibling_rows = from_sibling(rows)
    places = range(steps, 2 * steps)
    spread = functools.partial(
        call, spread_kernel, bf16(cuts, hidden, feats), n_in=1, moved=4 * w_gate.size
    )
    gates = spread()(after(w_gate[0].T, rows))
    chip_rows = after(chip_rows, (own, gates))
    relayed_rows = [from_sibling(b) for b in chip_rows]
    chips = call(functools.partial(rows_more_kernel, places, steps), total, n_in=steps + 2, **part)(
        sibling_rows, *chip_rows, own, w_t
    )
    outgoing = call(
        functools.partial(rows_last_kernel, steps),
        (bf16(CAP, feats),) * live,
        n_in=steps + 1,
        scratch=[pltpu.VMEM((live, CAP, feats), jnp.bfloat16)],
        **part,
    )(*relayed_rows, chips, w_t)

    arrived = [to_seq(outgoing[k], k) for k in range(live - 1, -1, -1)]

    ups = spread()(after(w_up[0].T, outgoing[0]))
    gains = call(spread_gain_kernel, jax.ShapeDtypeStruct((cuts, 1, feats), jnp.float32), n_in=1)(norm_gain)
    sums = (
        *(jax.ShapeDtypeStruct((slots, hidden), jnp.float32),) * 2,
        jax.ShapeDtypeStruct((slots, KEYS_SEEN), jnp.float32),
    )
    part = dict(flops=slots * w_gate.size, moved=w_gate.size)
    stacked = call(stack_kernel, bf16(slots, feats), n_in=live)(*after(arrived, (ups, gains)))
    chip_rows = from_chips(stacked, False)
    own = call(functools.partial(expert_own_kernel, steps), sums, n_in=4, **part)(stacked, gains, gates, ups)
    sibling_rows = from_sibling(stacked)
    downs = spread()(after(w_down[0], stacked))
    chip_blocks = from_chips(after(attended, gates))
    sibling_block, *relayed_blocks = [from_sibling(b) for b in (attended, *chip_blocks)]
    blocks = [attended, *relayed_blocks, sibling_block, *chip_blocks]
    chip_rows = after(chip_rows, (own, downs))
    relayed_rows = [from_sibling(b) for b in chip_rows]
    chips = call(functools.partial(expert_more_kernel, [0, *range(steps + 1, 2 * steps)], steps), sums, n_in=steps + 6, **part)(
        sibling_rows, *chip_rows, *own, gains, gates, ups
    )
    given, activated = call(
        functools.partial(expert_last_kernel, steps),
        (bf16(steps - 1, slots, feats), bf16(slots, hidden)),
        n_in=steps + 6,
        **part,
    )(*relayed_rows, *chips, gains, gates, ups, downs)
    far, near, near_given = call(
        expert_rest_kernel, (bf16(steps - 1, slots, feats), *(bf16(1, slots, feats),) * 2), n_in=2, **part
    )(activated, downs)
    resid = call(
        functools.partial(project_kernel, steps),
        bf16(feats, toks),
        n_in=cuts + 2,
        flops=2 * toks * w_out.size,
        moved=2 * w_out.size,
    )(*blocks, w_t, residual_t)

    half = bf16(slots // 2, feats)
    far_sums = call(add_cores_kernel, (half,) * (2 * steps - 2), n_in=2)(far, from_sibling(given))
    near_sums = call(add_cores_kernel, (half,) * 2, n_in=2)(near, from_sibling(after(near_given, far_sums)))
    sums = [*near_sums, *far_sums]
    returned, blocks_before = [], []
    for half in range(2):
        parts = [sums[half]] + [to_chip(sums[2 * k + half], k) for k in range(1, steps)]
        blocks = call(functools.partial(add_chips_kernel, steps), (bf16(CAP, feats),) * (live // 2), n_in=steps)(
            *after(parts, blocks_before)
        )
        blocks_before = blocks
        for block in blocks:
            returned.append(to_seq(block, live - 1 - len(returned)))
    bounds = [*range(0, feats, SPAN), feats] if feats % 16 == 0 else [0, feats]
    parts = list(zip(bounds[:-1], bounds[1:]))
    out = call(
        functools.partial(combine_kernel, live, parts),
        bf16(feats, toks),
        n_in=live + 3,
        scratch=[
            pltpu.VMEM((live, CAP, feats), jnp.bfloat16),
            pltpu.VMEM((feats, toks), jnp.bfloat16),
            pltpu.SemaphoreType.DMA((len(parts),)),
        ],
        out_space=pltpu.HBM,
    )(*returned, mix_hi, mix_lo, resid)
    return out.T


def solution(mesh):
    placed = (
        P(("groups", "seq"), "cuts"),
        P(("groups", "seq"), "cuts"),
        P("groups", "cuts"),
        P("cuts"),
        P(("groups", "seq"), "cuts"),
        P(None, "cuts"),
        P(),
        P(("groups", "seq"), None),
        P(("groups", "seq"), None),
        P("seq", None, "cuts"),
        P("seq", None, "cuts"),
        P("seq", "cuts", None),
    )
    return jax.shard_map(
        shards, mesh=mesh, in_specs=placed, out_specs=P(("groups", "seq"), "cuts"), check_vma=False
    )
```

```python
import functools
import math

import jax
import jax.numpy as jnp
from jax import lax
from jax.experimental import pallas as pl
from jax.experimental.pallas import tpu as pltpu
from jax.sharding import PartitionSpec as P

HEAD_SIZE = 64
KEYS_SEEN = 128
PAIR = 2 * HEAD_SIZE
SPAN = 2 * KEYS_SEEN
CAP = 16
CORES = 2

norm_eps = 1e-05
glu_alpha = 1.702

NT = (((1,), (1,)), ((), ()))
NN = (((1,), (0,)), ((), ()))
TN = (((0,), (0,)), ((), ()))
VMEM_LIMIT = 32 * 1024 * 1024


def dot(a, b, dims):
    return lax.dot_general(a, b, dims, preferred_element_type=jnp.float32)


def call(kernel, outs, n_in, scratch=(), hbm=(), out_space=pltpu.VMEM, flops=0, moved=0):
    spaces = [pltpu.HBM if i in hbm else pltpu.VMEM for i in range(n_in)]
    return pl.pallas_call(
        kernel,
        out_shape=outs,
        in_specs=[pl.BlockSpec(memory_space=space) for space in spaces],
        out_specs=jax.tree.map(lambda _: pl.BlockSpec(memory_space=out_space), outs),
        scratch_shapes=list(scratch),
        compiler_params=pltpu.CompilerParams(vmem_limit_bytes=VMEM_LIMIT),
        cost_estimate=pl.CostEstimate(flops=flops, bytes_accessed=moved, transcendentals=0),
    )


def in_hbm(array):
    return pltpu.with_memory_space_constraint(array, pltpu.HBM)


def bf16(*shape):
    return jax.ShapeDtypeStruct(shape, jnp.bfloat16)


def split_pair(both):
    both = both.astype(jnp.float32)
    low = lax.broadcasted_iota(jnp.int32, both.shape, 1) < HEAD_SIZE
    turned = pltpu.roll(both, HEAD_SIZE, 1)
    keys = jnp.concatenate([jnp.where(low, both, 0.0), jnp.where(low, 0.0, turned)], axis=0)
    values = jnp.concatenate([jnp.where(low, turned, 0.0), jnp.where(low, 0.0, both)], axis=0)
    return keys.astype(jnp.bfloat16), values.astype(jnp.bfloat16)


def score(pairs, keys, allowed):
    scores = dot(keys, jnp.concatenate(pairs, axis=0), NT) * (HEAD_SIZE**-0.5 * math.log2(math.e))
    allowed = jnp.concatenate([allowed] * len(pairs), axis=1)
    span = allowed.shape[0]
    return [jnp.where(allowed, scores[i * span : (i + 1) * span], -jnp.inf) for i in range(2)]


def sink_row(sinks, i, pairs):
    return jnp.concatenate([sinks[2 * p + i] for p in range(pairs)], axis=1)


def attend_block(pairs, both, sinks, allowed):
    keys, values = split_pair(both)
    probs = []
    for i, part in enumerate(score(pairs, keys, allowed)):
        sink = sink_row(sinks, i, len(pairs))
        peak = jnp.maximum(jnp.max(part, axis=0, keepdims=True), sink)
        terms = jnp.exp2(part - peak)
        denom = jnp.sum(terms, axis=0, keepdims=True) + jnp.exp2(sink - peak)
        probs.append((terms * (1.0 / denom)).astype(jnp.bfloat16))
    return dot(values, jnp.concatenate(probs, axis=0), TN).astype(jnp.bfloat16)


def group_queries(q_ref, g, groups, block):
    per_group = q_ref.shape[1] // PAIR // groups
    first = g * per_group
    toks = slice(block * KEYS_SEEN, (block + 1) * KEYS_SEEN)
    pairs = [q_ref[toks, (first + p) * PAIR : (first + p + 1) * PAIR] for p in range(per_group)]
    return first, pairs


def store_pairs(mixed, first, out_ref, lanes):
    for p in range(mixed.shape[1] // KEYS_SEEN):
        rows = slice((first + p) * PAIR, (first + p + 1) * PAIR)
        out_ref[rows, lanes] = mixed[:, p * KEYS_SEEN : (p + 1) * KEYS_SEEN]


def key_query(span):
    key = lax.broadcasted_iota(jnp.int32, (span, KEYS_SEEN), 0)
    return key, lax.broadcasted_iota(jnp.int32, (span, KEYS_SEEN), 1)


def fill_tables(live, ids, weights, placing_ref, mix_hi_ref, mix_lo_ref):
    toks = ids.shape[1]
    chosen = jnp.concatenate(
        [jnp.max((ids == e).astype(jnp.float32), axis=0, keepdims=True) for e in range(live)], axis=0
    )
    earlier = lax.broadcasted_iota(jnp.int32, (toks, toks), 0)
    later = lax.broadcasted_iota(jnp.int32, (toks, toks), 1)
    strict = (earlier < later).astype(jnp.bfloat16)
    before = dot(chosen.astype(jnp.bfloat16), strict, NN)
    slot = lax.broadcasted_iota(jnp.int32, (CAP, toks), 0).astype(jnp.float32)
    for e in range(live):
        weight = jnp.sum(jnp.where(ids == e, weights, 0.0), axis=0, keepdims=True)
        fills = (before[e : e + 1] == slot) & (chosen[e : e + 1] > 0.0)
        mix = jnp.where(fills, weight, 0.0)
        hi = mix.astype(jnp.bfloat16)
        rows = slice(e * CAP, (e + 1) * CAP)
        placing_ref[rows] = fills.astype(jnp.bfloat16)
        mix_hi_ref[rows] = hi
        mix_lo_ref[rows] = (mix - hi.astype(jnp.float32)).astype(jnp.bfloat16)


def first_kernel(live, *refs):
    loaded, held = refs[:8], refs[8:13]
    placing_ref, mix_hi_ref, mix_lo_ref, sinks_out, late_ref, rows_ref = refs[13:19]
    ids_ref, weights_ref, sinks_ref, sems = refs[19:]
    targets = (ids_ref, weights_ref, sinks_ref, *held)
    copies = [pltpu.make_async_copy(*pair, sems.at[i]) for i, pair in enumerate(zip(loaded, targets))]
    for copy in copies:
        copy.start()
    q_ref, kv_ref = held[:2]
    for copy in copies[:2]:
        copy.wait()
    fill_tables(live, ids_ref[...], weights_ref[...], placing_ref, mix_hi_ref, mix_lo_ref)
    for copy in copies[2:5]:
        copy.wait()
    heads = sinks_ref.shape[0]
    sinks = [jnp.full((1, KEYS_SEEN), sinks_ref[h], jnp.float32) * math.log2(math.e) for h in range(heads)]
    sinks_out[...] = jnp.concatenate(sinks, axis=0)
    groups = kv_ref.shape[1] // PAIR
    key, query = key_query(SPAN)
    allowed = (key > query) & (key <= query + KEYS_SEEN)
    for b in range(1, q_ref.shape[0] // KEYS_SEEN):
        span = slice((b - 1) * KEYS_SEEN, (b + 1) * KEYS_SEEN)
        for g in range(groups):
            first, pairs = group_queries(q_ref, g, groups, b)
            part = sinks[2 * first : 2 * (first + len(pairs))]
            mixed = attend_block(pairs, kv_ref[span, g * PAIR : (g + 1) * PAIR], part, allowed)
            store_pairs(mixed, first, late_ref, slice((b - 1) * KEYS_SEEN, b * KEYS_SEEN))
    rows_ref[...] = dot(placing_ref[:, KEYS_SEEN:], late_ref[...], NT)
    for copy in copies[5:]:
        copy.wait()


def second_kernel(q_ref, kv_ref, before_ref, rim_ref, sinks_ref, late_ref, placing_ref, late_rows_ref, all_ref, rows_ref):
    rim = jnp.where(lax.axis_index("seq") == 0, before_ref[...], rim_ref[...])
    groups = rim.shape[1] // PAIR
    key, query = key_query(SPAN)
    allowed = (key > query) & (key <= query + KEYS_SEEN)
    for g in range(groups):
        first, pairs = group_queries(q_ref, g, groups, 0)
        sinks = [sinks_ref[h : h + 1] for h in range(2 * first, 2 * (first + len(pairs)))]
        lanes = slice(g * PAIR, (g + 1) * PAIR)
        both = jnp.concatenate([rim[:, lanes], kv_ref[:KEYS_SEEN, lanes]], axis=0)
        store_pairs(attend_block(pairs, both, sinks, allowed), first, all_ref, slice(0, KEYS_SEEN))
    rows = late_rows_ref[...] + dot(placing_ref[:, :KEYS_SEEN], all_ref[:, :KEYS_SEEN], NT)
    rows_ref[...] = rows.astype(jnp.bfloat16)
    all_ref[:, KEYS_SEEN:] = late_ref[...]


def origin(k, sibling):
    me = lax.axis_index("cuts")
    return lax.bitwise_xor(me, CORES * k + (1 if sibling else 0))


def add_products(total, places, blocks, w_ref, steps, dims, swapped=False):
    width = blocks[0].shape[0 if swapped else 1] if blocks else 0
    for i, block in zip(places, blocks):
        at = pl.multiple_of(origin(i % steps, i >= steps) * width, 128)
        w = w_ref[:, pl.ds(at, width)]
        total += dot(w, block[...], dims) if swapped else dot(block[...], w, dims)
    return total


def rows_own_kernel(steps, rows_ref, w_ref, residual_ref, placing_ref, total_ref):
    total = dot(placing_ref[...], residual_ref[...], NT)
    total_ref[...] = add_products(total, [0], [rows_ref], w_ref, steps, NT)


def rows_more_kernel(places, steps, *refs):
    blocks, (before_ref, w_ref, total_ref) = refs[:-3], refs[-3:]
    total_ref[...] = add_products(before_ref[...], places, blocks, w_ref, steps, NT)


def rows_last_kernel(steps, *refs):
    blocks, (before_ref, w_ref) = refs[: steps - 1], refs[steps - 1 : steps + 1]
    outgoing, rows_ref = refs[steps + 1 : -1], refs[-1]
    total = add_products(before_ref[...], range(1, steps), blocks, w_ref, steps, NT)
    rows_ref[...] = total.astype(jnp.bfloat16).reshape(rows_ref.shape)
    me = lax.axis_index("seq")
    for k, out_ref in enumerate(outgoing):
        out_ref[...] = rows_ref[lax.bitwise_xor(me, k)]


def stack_kernel(*refs):
    for i, block in enumerate(refs[:-1]):
        refs[-1][i * CAP : (i + 1) * CAP] = block[...]


def project_kernel(steps, *refs):
    blocks = refs[: 2 * steps]
    w_ref, residual_ref, resid_ref = refs[2 * steps :]
    total = residual_ref[...].astype(jnp.float32)
    total = add_products(total, range(2 * steps), blocks, w_ref, steps, NN, True)
    resid_ref[...] = total.astype(jnp.bfloat16)


def spread_kernel(source_ref, blocks_ref):
    cuts, _, width = blocks_ref.shape
    for p in range(cuts):
        blocks_ref[p] = source_ref[:, p * width : (p + 1) * width]


def spread_gain_kernel(gain_ref, blocks_ref):
    cuts, _, width = blocks_ref.shape
    gain = gain_ref[...].reshape(1, cuts * width)
    for p in range(cuts):
        blocks_ref[p] = gain[:, p * width : (p + 1) * width]


def expert_kernel(places, steps, *refs):
    blocks = refs[: 2 * steps]
    gains_ref, gates_ref, ups_ref, downs_ref, given_ref, activated_ref = refs[2 * steps :]
    wide = [block[...].astype(jnp.float32) for block in blocks]
    squares = sum(jnp.sum(block * block, axis=1, keepdims=True) for block in wide)
    scale = lax.rsqrt(squares / (len(blocks) * wide[0].shape[1]) + norm_eps)
    gate, up = 0.0, 0.0
    for i, block in zip(places, wide):
        p = origin(i % steps, i >= steps)
        rows = (block * scale * gains_ref[p]).astype(jnp.bfloat16)
        gate += dot(rows, gates_ref[p], NT)
        up += dot(rows, ups_ref[p], NT)
    activated = ((up + 1.0) * gate * jax.nn.sigmoid(glu_alpha * gate)).astype(jnp.bfloat16)
    activated_ref[...] = activated
    for k in range(steps):
        given_ref[k] = dot(activated, downs_ref[origin(k, k > 0)], NN).astype(jnp.bfloat16)


def expert_kept_kernel(activated_ref, downs_ref, kept_ref):
    for k in range(kept_ref.shape[0]):
        kept_ref[k] = dot(activated_ref[...], downs_ref[origin(k, k == 0)], NN).astype(jnp.bfloat16)


def add_cores_kernel(kept_ref, given_ref, *out_refs):
    half = out_refs[0].shape[0]
    for i, out_ref in enumerate(out_refs):
        rows = slice(i % 2 * half, (i % 2 + 1) * half)
        total = kept_ref[i // 2, rows].astype(jnp.float32) + given_ref[i // 2, rows].astype(jnp.float32)
        out_ref[...] = total.astype(out_ref.dtype)


def add_chips_kernel(steps, *refs):
    total = sum(r[...].astype(jnp.float32) for r in refs[:steps])
    for k, out_ref in enumerate(refs[steps:]):
        out_ref[...] = total[k * CAP : (k + 1) * CAP].astype(jnp.bfloat16)


def combine_kernel(live, parts, *refs):
    blocks = refs[:live]
    mix_hi_ref, mix_lo_ref, resid_ref, out_ref, rows_ref, held_ref, sems = refs[live:]
    me = lax.axis_index("seq")
    for k in range(live):
        rows_ref[lax.bitwise_xor(me, live - 1 - k)] = blocks[k][...]
    rows = rows_ref[...].reshape(live * CAP, -1)
    rows = jnp.concatenate([rows, rows], axis=0)
    mix = jnp.concatenate([mix_hi_ref[...], mix_lo_ref[...]], axis=0)
    copies = []
    for i, (start, stop) in enumerate(parts):
        part = slice(start, stop)
        mixed = dot(rows[:, part], mix, TN)
        held_ref[part] = (resid_ref[part].astype(jnp.float32) + mixed).astype(jnp.bfloat16)
        copies.append(pltpu.make_async_copy(held_ref.at[part], out_ref.at[part], sems.at[i]))
        copies[-1].start()
    for copy in copies:
        copy.wait()


def swap(block, axis, mask):
    return lax.ppermute(block, axis, [(i, i ^ mask) for i in range(lax.axis_size(axis))])


def to_chip(block, k, other=True):
    return swap(block, "cuts", CORES * k + other)


def from_chips(block, other=True):
    return [to_chip(block, k, other) for k in range(1, lax.axis_size("cuts") // CORES)]


def to_seq(block, k):
    size = lax.axis_size("seq") * lax.axis_size("cuts")
    mask = k * lax.axis_size("cuts") + 1
    return lax.ppermute(block, ("seq", "cuts"), [(i, i ^ mask) for i in range(size)])


def from_sibling(block):
    return swap(block, "cuts", 1)


def after(arrays, others):
    return lax.optimization_barrier((arrays, others))[0]


def shards(
    queries,
    keyvals,
    preceding_keyvalues,
    attention_sink_logits,
    residual,
    w_out,
    norm_gain,
    expert_ids,
    route_weights,
    w_gate,
    w_up,
    w_down,
):
    toks, feats = residual.shape
    size = lax.axis_size("seq")
    live = w_gate.shape[0] * size
    cuts = lax.axis_size("cuts")
    steps = cuts // CORES
    slots = live * CAP
    head_rows = queries.shape[1]
    heads = head_rows // HEAD_SIZE
    width = norm_gain.shape[0]
    hidden = w_gate.shape[2]

    tail = keyvals[toks - KEYS_SEEN :]
    rim = lax.ppermute(tail, "seq", [(i, (i + 1) % size) for i in range(size)])
    loads = (queries, keyvals, preceding_keyvalues, w_out.T, residual.T)
    q, kv, before, w_t, residual_t, placing, mix_hi, mix_lo, sinks, late, late_rows = call(
        functools.partial(first_kernel, live),
        (
            *(bf16(*a.shape) for a in loads),
            *(bf16(slots, toks),) * 3,
            jax.ShapeDtypeStruct((heads, KEYS_SEEN), jnp.float32),
            bf16(head_rows, toks - KEYS_SEEN),
            jax.ShapeDtypeStruct((slots, head_rows), jnp.float32),
        ),
        n_in=8,
        scratch=[
            pltpu.VMEM(expert_ids.T.shape, jnp.int32),
            pltpu.VMEM(expert_ids.T.shape, jnp.float32),
            pltpu.SMEM(attention_sink_logits.shape, jnp.float32),
            pltpu.SemaphoreType.DMA((8,)),
        ],
        hbm=range(8),
        flops=4 * toks * SPAN * head_rows,
        moved=2 * (w_out.size + residual.size + queries.size),
    )(*(in_hbm(a) for a in (expert_ids.T, route_weights.T, attention_sink_logits, *loads)))
    attended, rows = call(
        second_kernel,
        (bf16(head_rows, toks), bf16(slots, head_rows)),
        n_in=8,
        flops=2 * toks * SPAN * head_rows,
        moved=2 * queries.size,
    )(q, kv, before, rim, sinks, late, placing, late_rows)

    chip_rows = from_chips(rows)
    total = jax.ShapeDtypeStruct((slots, feats), jnp.float32)
    part = dict(flops=slots * w_out.size // 2, moved=w_out.size // 2)
    own = call(functools.partial(rows_own_kernel, steps), total, n_in=4, **part)(
        rows, w_t, residual_t, placing
    )
    sibling_rows = from_sibling(rows)
    places = range(steps, 2 * steps)
    spread = functools.partial(
        call, spread_kernel, bf16(cuts, hidden, feats), n_in=1, moved=4 * w_gate.size
    )
    gates = spread()(after(w_gate[0].T, rows))
    chip_rows = after(chip_rows, (own, gates))
    relayed_rows = [from_sibling(b) for b in chip_rows]
    chips = call(functools.partial(rows_more_kernel, places, steps), total, n_in=steps + 2, **part)(
        sibling_rows, *chip_rows, own, w_t
    )
    outgoing = call(
        functools.partial(rows_last_kernel, steps),
        (bf16(CAP, feats),) * live,
        n_in=steps + 1,
        scratch=[pltpu.VMEM((live, CAP, feats), jnp.bfloat16)],
        **part,
    )(*relayed_rows, chips, w_t)

    arrived = [to_seq(outgoing[k], k) for k in range(live - 1, -1, -1)]

    ups = spread()(after(w_up[0].T, outgoing[0]))
    gains = call(spread_gain_kernel, jax.ShapeDtypeStruct((cuts, 1, feats), jnp.float32), n_in=1)(norm_gain)
    part = dict(flops=slots * w_gate.size, moved=w_gate.size)
    stacked = call(stack_kernel, bf16(slots, feats), n_in=live)(*after(arrived, (ups, gains)))
    chip_rows = from_chips(stacked, False)
    sibling_rows = from_sibling(stacked)
    downs = spread()(after(w_down[0], stacked))
    chip_blocks = from_chips(after(attended, gates))
    sibling_block, *relayed_blocks = [from_sibling(b) for b in (attended, *chip_blocks)]
    blocks = [attended, *relayed_blocks, sibling_block, *chip_blocks]
    chip_rows = after(chip_rows, downs)
    relayed_rows = [from_sibling(b) for b in chip_rows]
    given, activated = call(
        functools.partial(expert_kernel, [steps, 0, *range(steps + 1, 2 * steps), *range(1, steps)], steps),
        (bf16(steps, slots, feats), bf16(slots, hidden)),
        n_in=cuts + 4,
        **part,
    )(stacked, sibling_rows, *chip_rows, *relayed_rows, gains, gates, ups, downs)
    kept = call(expert_kept_kernel, bf16(steps, slots, feats), n_in=2, **part)(activated, downs)
    resid = call(
        functools.partial(project_kernel, steps),
        bf16(feats, toks),
        n_in=cuts + 2,
        flops=2 * toks * w_out.size,
        moved=2 * w_out.size,
    )(*blocks, w_t, residual_t)

    half = jax.ShapeDtypeStruct((slots // 2, feats), jnp.float32)
    sums = call(add_cores_kernel, (half,) * 2 + (bf16(slots // 2, feats),) * (2 * steps - 2), n_in=2)(
        kept, swap(given, "cuts", 1)
    )
    returned = []
    for half in range(2):
        parts = [sums[half]] + [to_chip(sums[2 * k + half], k) for k in range(1, steps)]
        blocks = call(functools.partial(add_chips_kernel, steps), (bf16(CAP, feats),) * (live // 2), n_in=steps)(
            *parts
        )
        for block in blocks:
            returned.append(to_seq(block, live - 1 - len(returned)))
    bounds = [*range(0, feats, SPAN), feats] if feats % 16 == 0 else [0, feats]
    parts = list(zip(bounds[:-1], bounds[1:]))
    out = call(
        functools.partial(combine_kernel, live, parts),
        bf16(feats, toks),
        n_in=live + 3,
        scratch=[
            pltpu.VMEM((live, CAP, feats), jnp.bfloat16),
            pltpu.VMEM((feats, toks), jnp.bfloat16),
            pltpu.SemaphoreType.DMA((len(parts),)),
        ],
        out_space=pltpu.HBM,
    )(*returned, mix_hi, mix_lo, resid)
    return out.T


def solution(mesh):
    placed = (
        P(("groups", "seq"), "cuts"),
        P(("groups", "seq"), "cuts"),
        P("groups", "cuts"),
        P("cuts"),
        P(("groups", "seq"), "cuts"),
        P(None, "cuts"),
        P(),
        P(("groups", "seq"), None),
        P(("groups", "seq"), None),
        P("seq", None, "cuts"),
        P("seq", None, "cuts"),
        P("seq", "cuts", None),
    )
    return jax.shard_map(
        shards, mesh=mesh, in_specs=placed, out_specs=P(("groups", "seq"), "cuts"), check_vma=False
    )
```

```python
import functools
import math

import jax
import jax.numpy as jnp
from jax import lax
from jax.experimental import pallas as pl
from jax.experimental.pallas import tpu as pltpu
from jax.sharding import PartitionSpec as P

HEAD_SIZE = 64
KEYS_SEEN = 128
PAIR = 2 * HEAD_SIZE
SPAN = 2 * KEYS_SEEN
CAP = 16
CORES = 2

norm_eps = 1e-05
glu_alpha = 1.702

NT = (((1,), (1,)), ((), ()))
NN = (((1,), (0,)), ((), ()))
TN = (((0,), (0,)), ((), ()))
VMEM_LIMIT = 32 * 1024 * 1024


def dot(a, b, dims):
    return lax.dot_general(a, b, dims, preferred_element_type=jnp.float32)


def call(kernel, outs, n_in, scratch=(), hbm=(), out_space=pltpu.VMEM, flops=0, moved=0):
    spaces = [pltpu.HBM if i in hbm else pltpu.VMEM for i in range(n_in)]
    return pl.pallas_call(
        kernel,
        out_shape=outs,
        in_specs=[pl.BlockSpec(memory_space=space) for space in spaces],
        out_specs=jax.tree.map(lambda _: pl.BlockSpec(memory_space=out_space), outs),
        scratch_shapes=list(scratch),
        compiler_params=pltpu.CompilerParams(vmem_limit_bytes=VMEM_LIMIT),
        cost_estimate=pl.CostEstimate(flops=flops, bytes_accessed=moved, transcendentals=0),
    )


def in_hbm(array):
    return pltpu.with_memory_space_constraint(array, pltpu.HBM)


def bf16(*shape):
    return jax.ShapeDtypeStruct(shape, jnp.bfloat16)


def split_pair(both):
    both = both.astype(jnp.float32)
    low = lax.broadcasted_iota(jnp.int32, both.shape, 1) < HEAD_SIZE
    turned = pltpu.roll(both, HEAD_SIZE, 1)
    keys = jnp.concatenate([jnp.where(low, both, 0.0), jnp.where(low, 0.0, turned)], axis=0)
    values = jnp.concatenate([jnp.where(low, turned, 0.0), jnp.where(low, 0.0, both)], axis=0)
    return keys.astype(jnp.bfloat16), values.astype(jnp.bfloat16)


def score(pairs, keys, allowed):
    scores = dot(keys, jnp.concatenate(pairs, axis=0), NT) * (HEAD_SIZE**-0.5 * math.log2(math.e))
    allowed = jnp.concatenate([allowed] * len(pairs), axis=1)
    span = allowed.shape[0]
    return [jnp.where(allowed, scores[i * span : (i + 1) * span], -jnp.inf) for i in range(2)]


def sink_row(sinks, i, pairs):
    return jnp.concatenate([sinks[2 * p + i] for p in range(pairs)], axis=1)


def attend_block(pairs, both, sinks, allowed):
    keys, values = split_pair(both)
    probs = []
    for i, part in enumerate(score(pairs, keys, allowed)):
        sink = sink_row(sinks, i, len(pairs))
        peak = jnp.maximum(jnp.max(part, axis=0, keepdims=True), sink)
        terms = jnp.exp2(part - peak)
        denom = jnp.sum(terms, axis=0, keepdims=True) + jnp.exp2(sink - peak)
        probs.append((terms * (1.0 / denom)).astype(jnp.bfloat16))
    return dot(values, jnp.concatenate(probs, axis=0), TN).astype(jnp.bfloat16)


def group_queries(q_ref, g, groups, block):
    per_group = q_ref.shape[1] // PAIR // groups
    first = g * per_group
    toks = slice(block * KEYS_SEEN, (block + 1) * KEYS_SEEN)
    pairs = [q_ref[toks, (first + p) * PAIR : (first + p + 1) * PAIR] for p in range(per_group)]
    return first, pairs


def store_pairs(mixed, first, out_ref, lanes):
    for p in range(mixed.shape[1] // KEYS_SEEN):
        rows = slice((first + p) * PAIR, (first + p + 1) * PAIR)
        out_ref[rows, lanes] = mixed[:, p * KEYS_SEEN : (p + 1) * KEYS_SEEN]


def key_query(span):
    key = lax.broadcasted_iota(jnp.int32, (span, KEYS_SEEN), 0)
    return key, lax.broadcasted_iota(jnp.int32, (span, KEYS_SEEN), 1)


def fill_tables(live, ids, weights, placing_ref, mix_hi_ref, mix_lo_ref):
    toks = ids.shape[1]
    chosen = jnp.concatenate(
        [jnp.max((ids == e).astype(jnp.float32), axis=0, keepdims=True) for e in range(live)], axis=0
    )
    earlier = lax.broadcasted_iota(jnp.int32, (toks, toks), 0)
    later = lax.broadcasted_iota(jnp.int32, (toks, toks), 1)
    strict = (earlier < later).astype(jnp.bfloat16)
    before = dot(chosen.astype(jnp.bfloat16), strict, NN)
    slot = lax.broadcasted_iota(jnp.int32, (CAP, toks), 0).astype(jnp.float32)
    for e in range(live):
        weight = jnp.sum(jnp.where(ids == e, weights, 0.0), axis=0, keepdims=True)
        fills = (before[e : e + 1] == slot) & (chosen[e : e + 1] > 0.0)
        mix = jnp.where(fills, weight, 0.0)
        hi = mix.astype(jnp.bfloat16)
        rows = slice(e * CAP, (e + 1) * CAP)
        placing_ref[rows] = fills.astype(jnp.bfloat16)
        mix_hi_ref[rows] = hi
        mix_lo_ref[rows] = (mix - hi.astype(jnp.float32)).astype(jnp.bfloat16)


def first_kernel(live, *refs):
    loaded, held = refs[:8], refs[8:13]
    placing_ref, mix_hi_ref, mix_lo_ref, sinks_out, late_ref, rows_ref = refs[13:19]
    ids_ref, weights_ref, sinks_ref, sems = refs[19:]
    targets = (ids_ref, weights_ref, sinks_ref, *held)
    copies = [pltpu.make_async_copy(*pair, sems.at[i]) for i, pair in enumerate(zip(loaded, targets))]
    for copy in copies:
        copy.start()
    q_ref, kv_ref = held[:2]
    for copy in copies[:2]:
        copy.wait()
    fill_tables(live, ids_ref[...], weights_ref[...], placing_ref, mix_hi_ref, mix_lo_ref)
    for copy in copies[2:5]:
        copy.wait()
    heads = sinks_ref.shape[0]
    sinks = [jnp.full((1, KEYS_SEEN), sinks_ref[h], jnp.float32) * math.log2(math.e) for h in range(heads)]
    sinks_out[...] = jnp.concatenate(sinks, axis=0)
    groups = kv_ref.shape[1] // PAIR
    key, query = key_query(SPAN)
    allowed = (key > query) & (key <= query + KEYS_SEEN)
    for b in range(1, q_ref.shape[0] // KEYS_SEEN):
        span = slice((b - 1) * KEYS_SEEN, (b + 1) * KEYS_SEEN)
        for g in range(groups):
            first, pairs = group_queries(q_ref, g, groups, b)
            part = sinks[2 * first : 2 * (first + len(pairs))]
            mixed = attend_block(pairs, kv_ref[span, g * PAIR : (g + 1) * PAIR], part, allowed)
            store_pairs(mixed, first, late_ref, slice((b - 1) * KEYS_SEEN, b * KEYS_SEEN))
    rows_ref[...] = dot(placing_ref[:, KEYS_SEEN:], late_ref[...], NT)
    for copy in copies[5:]:
        copy.wait()


def second_kernel(q_ref, kv_ref, before_ref, rim_ref, sinks_ref, late_ref, placing_ref, late_rows_ref, all_ref, rows_ref):
    rim = jnp.where(lax.axis_index("seq") == 0, before_ref[...], rim_ref[...])
    groups = rim.shape[1] // PAIR
    key, query = key_query(SPAN)
    allowed = (key > query) & (key <= query + KEYS_SEEN)
    for g in range(groups):
        first, pairs = group_queries(q_ref, g, groups, 0)
        sinks = [sinks_ref[h : h + 1] for h in range(2 * first, 2 * (first + len(pairs)))]
        lanes = slice(g * PAIR, (g + 1) * PAIR)
        both = jnp.concatenate([rim[:, lanes], kv_ref[:KEYS_SEEN, lanes]], axis=0)
        store_pairs(attend_block(pairs, both, sinks, allowed), first, all_ref, slice(0, KEYS_SEEN))
    rows = late_rows_ref[...] + dot(placing_ref[:, :KEYS_SEEN], all_ref[:, :KEYS_SEEN], NT)
    rows_ref[...] = rows.astype(jnp.bfloat16)
    all_ref[:, KEYS_SEEN:] = late_ref[...]


def origin(k, sibling):
    me = lax.axis_index("cuts")
    return lax.bitwise_xor(me, CORES * k + (1 if sibling else 0))


def add_products(total, places, blocks, w_ref, steps, dims, swapped=False):
    width = blocks[0].shape[0 if swapped else 1] if blocks else 0
    for i, block in zip(places, blocks):
        at = pl.multiple_of(origin(i % steps, i >= steps) * width, 128)
        w = w_ref[:, pl.ds(at, width)]
        total += dot(w, block[...], dims) if swapped else dot(block[...], w, dims)
    return total


def rows_own_kernel(steps, rows_ref, w_ref, residual_ref, placing_ref, total_ref):
    total = dot(placing_ref[...], residual_ref[...], NT)
    total_ref[...] = add_products(total, [0], [rows_ref], w_ref, steps, NT)


def rows_more_kernel(places, steps, *refs):
    blocks, (before_ref, w_ref, total_ref) = refs[:-3], refs[-3:]
    total_ref[...] = add_products(before_ref[...], places, blocks, w_ref, steps, NT)


def rows_last_kernel(steps, *refs):
    blocks, (before_ref, w_ref) = refs[: steps - 1], refs[steps - 1 : steps + 1]
    outgoing, rows_ref = refs[steps + 1 : -1], refs[-1]
    total = add_products(before_ref[...], range(1, steps), blocks, w_ref, steps, NT)
    rows_ref[...] = total.astype(jnp.bfloat16).reshape(rows_ref.shape)
    me = lax.axis_index("seq")
    for k, out_ref in enumerate(outgoing):
        out_ref[...] = rows_ref[lax.bitwise_xor(me, k)]


def stack_kernel(*refs):
    for i, block in enumerate(refs[:-1]):
        refs[-1][i * CAP : (i + 1) * CAP] = block[...]


def project_kernel(steps, *refs):
    blocks = refs[: 2 * steps]
    w_ref, residual_ref, resid_ref = refs[2 * steps :]
    total = residual_ref[...].astype(jnp.float32)
    total = add_products(total, range(2 * steps), blocks, w_ref, steps, NN, True)
    resid_ref[...] = total.astype(jnp.bfloat16)


def spread_kernel(source_ref, blocks_ref):
    cuts, _, width = blocks_ref.shape
    for p in range(cuts):
        blocks_ref[p] = source_ref[:, p * width : (p + 1) * width]


def spread_gain_kernel(gain_ref, blocks_ref):
    cuts, _, width = blocks_ref.shape
    gain = gain_ref[...].reshape(1, cuts * width)
    for p in range(cuts):
        blocks_ref[p] = gain[:, p * width : (p + 1) * width]


def squares_kernel(mine_ref, theirs_ref, squares_ref):
    wide = [ref[...].astype(jnp.float32) for ref in (mine_ref, theirs_ref)]
    squares = sum(jnp.sum(block * block, axis=1, keepdims=True) for block in wide)
    squares_ref[...] = jnp.broadcast_to(squares, squares_ref.shape)


def add_features(gate, up, scale, places, blocks, gains_ref, gates_ref, ups_ref, steps):
    for i, block in zip(places, blocks):
        p = origin(i % steps, i >= steps)
        rows = (block[...].astype(jnp.float32) * scale * gains_ref[p]).astype(jnp.bfloat16)
        gate += dot(rows, gates_ref[p], NT)
        up += dot(rows, ups_ref[p], NT)
    return gate, up


def expert_most_kernel(places, steps, *refs):
    blocks, squares = refs[: steps + 1], refs[steps + 1 : 2 * steps + 1]
    gains_ref, gates_ref, ups_ref, gate_ref, up_ref, scale_ref = refs[2 * steps + 1 :]
    features = 2 * steps * blocks[0].shape[1]
    scale = lax.rsqrt(sum(ref[...] for ref in squares) / features + norm_eps)
    scale_ref[...] = scale
    sums = add_features(0.0, 0.0, scale[:, :1], places, blocks, gains_ref, gates_ref, ups_ref, steps)
    gate_ref[...], up_ref[...] = sums


def expert_last_kernel(steps, *refs):
    blocks, refs = refs[: steps - 1], refs[steps - 1 :]
    gate_ref, up_ref, scale_ref, gains_ref, gates_ref, ups_ref, downs_ref, given_ref, activated_ref = refs
    gate, up = add_features(
        gate_ref[...], up_ref[...], scale_ref[:, :1], range(1, steps), blocks, gains_ref, gates_ref, ups_ref, steps
    )
    activated = ((up + 1.0) * gate * jax.nn.sigmoid(glu_alpha * gate)).astype(jnp.bfloat16)
    activated_ref[...] = activated
    for k in range(steps):
        given_ref[k] = dot(activated, downs_ref[origin(k, k > 0)], NN).astype(jnp.bfloat16)


def expert_kept_kernel(activated_ref, downs_ref, kept_ref):
    for k in range(kept_ref.shape[0]):
        kept_ref[k] = dot(activated_ref[...], downs_ref[origin(k, k == 0)], NN).astype(jnp.bfloat16)


def add_cores_kernel(kept_ref, given_ref, *out_refs):
    half = out_refs[0].shape[0]
    for i, out_ref in enumerate(out_refs):
        rows = slice(i % 2 * half, (i % 2 + 1) * half)
        total = kept_ref[i // 2, rows].astype(jnp.float32) + given_ref[i // 2, rows].astype(jnp.float32)
        out_ref[...] = total.astype(out_ref.dtype)


def add_chips_kernel(steps, *refs):
    total = sum(r[...].astype(jnp.float32) for r in refs[:steps])
    for k, out_ref in enumerate(refs[steps:]):
        out_ref[...] = total[k * CAP : (k + 1) * CAP].astype(jnp.bfloat16)


def combine_kernel(live, parts, *refs):
    blocks = refs[:live]
    mix_hi_ref, mix_lo_ref, resid_ref, out_ref, rows_ref, held_ref, sems = refs[live:]
    me = lax.axis_index("seq")
    for k in range(live):
        rows_ref[lax.bitwise_xor(me, live - 1 - k)] = blocks[k][...]
    rows = rows_ref[...].reshape(live * CAP, -1)
    rows = jnp.concatenate([rows, rows], axis=0)
    mix = jnp.concatenate([mix_hi_ref[...], mix_lo_ref[...]], axis=0)
    copies = []
    for i, (start, stop) in enumerate(parts):
        part = slice(start, stop)
        mixed = dot(rows[:, part], mix, TN)
        held_ref[part] = (resid_ref[part].astype(jnp.float32) + mixed).astype(jnp.bfloat16)
        copies.append(pltpu.make_async_copy(held_ref.at[part], out_ref.at[part], sems.at[i]))
        copies[-1].start()
    for copy in copies:
        copy.wait()


def swap(block, axis, mask):
    return lax.ppermute(block, axis, [(i, i ^ mask) for i in range(lax.axis_size(axis))])


def to_chip(block, k, other=True):
    return swap(block, "cuts", CORES * k + other)


def from_chips(block, other=True):
    return [to_chip(block, k, other) for k in range(1, lax.axis_size("cuts") // CORES)]


def to_seq(block, k):
    size = lax.axis_size("seq") * lax.axis_size("cuts")
    mask = k * lax.axis_size("cuts") + 1
    return lax.ppermute(block, ("seq", "cuts"), [(i, i ^ mask) for i in range(size)])


def from_sibling(block):
    return swap(block, "cuts", 1)


def after(arrays, others):
    return lax.optimization_barrier((arrays, others))[0]


def shards(
    queries,
    keyvals,
    preceding_keyvalues,
    attention_sink_logits,
    residual,
    w_out,
    norm_gain,
    expert_ids,
    route_weights,
    w_gate,
    w_up,
    w_down,
):
    toks, feats = residual.shape
    size = lax.axis_size("seq")
    live = w_gate.shape[0] * size
    cuts = lax.axis_size("cuts")
    steps = cuts // CORES
    slots = live * CAP
    head_rows = queries.shape[1]
    heads = head_rows // HEAD_SIZE
    width = norm_gain.shape[0]
    hidden = w_gate.shape[2]

    tail = keyvals[toks - KEYS_SEEN :]
    rim = lax.ppermute(tail, "seq", [(i, (i + 1) % size) for i in range(size)])
    loads = (queries, keyvals, preceding_keyvalues, w_out.T, residual.T)
    q, kv, before, w_t, residual_t, placing, mix_hi, mix_lo, sinks, late, late_rows = call(
        functools.partial(first_kernel, live),
        (
            *(bf16(*a.shape) for a in loads),
            *(bf16(slots, toks),) * 3,
            jax.ShapeDtypeStruct((heads, KEYS_SEEN), jnp.float32),
            bf16(head_rows, toks - KEYS_SEEN),
            jax.ShapeDtypeStruct((slots, head_rows), jnp.float32),
        ),
        n_in=8,
        scratch=[
            pltpu.VMEM(expert_ids.T.shape, jnp.int32),
            pltpu.VMEM(expert_ids.T.shape, jnp.float32),
            pltpu.SMEM(attention_sink_logits.shape, jnp.float32),
            pltpu.SemaphoreType.DMA((8,)),
        ],
        hbm=range(8),
        flops=4 * toks * SPAN * head_rows,
        moved=2 * (w_out.size + residual.size + queries.size),
    )(*(in_hbm(a) for a in (expert_ids.T, route_weights.T, attention_sink_logits, *loads)))
    attended, rows = call(
        second_kernel,
        (bf16(head_rows, toks), bf16(slots, head_rows)),
        n_in=8,
        flops=2 * toks * SPAN * head_rows,
        moved=2 * queries.size,
    )(q, kv, before, rim, sinks, late, placing, late_rows)

    chip_rows = from_chips(rows)
    total = jax.ShapeDtypeStruct((slots, feats), jnp.float32)
    part = dict(flops=slots * w_out.size // 2, moved=w_out.size // 2)
    own = call(functools.partial(rows_own_kernel, steps), total, n_in=4, **part)(
        rows, w_t, residual_t, placing
    )
    sibling_rows = from_sibling(rows)
    places = range(steps, 2 * steps)
    spread = functools.partial(
        call, spread_kernel, bf16(cuts, hidden, feats), n_in=1, moved=4 * w_gate.size
    )
    gates = spread()(after(w_gate[0].T, rows))
    chip_rows = after(chip_rows, (own, gates))
    relayed_rows = [from_sibling(b) for b in chip_rows]
    chips = call(functools.partial(rows_more_kernel, places, steps), total, n_in=steps + 2, **part)(
        sibling_rows, *chip_rows, own, w_t
    )
    outgoing = call(
        functools.partial(rows_last_kernel, steps),
        (bf16(CAP, feats),) * live,
        n_in=steps + 1,
        scratch=[pltpu.VMEM((live, CAP, feats), jnp.bfloat16)],
        **part,
    )(*relayed_rows, chips, w_t)

    arrived = [to_seq(outgoing[k], k) for k in range(live - 1, -1, -1)]

    ups = spread()(after(w_up[0].T, outgoing[0]))
    gains = call(spread_gain_kernel, jax.ShapeDtypeStruct((cuts, 1, feats), jnp.float32), n_in=1)(norm_gain)
    part = dict(flops=slots * w_gate.size, moved=w_gate.size)
    stacked = call(stack_kernel, bf16(slots, feats), n_in=live)(*after(arrived, (ups, gains)))
    chip_rows = from_chips(stacked, False)
    sibling_rows = from_sibling(stacked)
    downs = spread()(after(w_down[0], stacked))
    chip_blocks = from_chips(after(attended, gates))
    sibling_block, *relayed_blocks = [from_sibling(b) for b in (attended, *chip_blocks)]
    blocks = [attended, *relayed_blocks, sibling_block, *chip_blocks]
    row_sums = jax.ShapeDtypeStruct((slots, KEYS_SEEN), jnp.float32)
    squares = call(squares_kernel, row_sums, n_in=2)(stacked, sibling_rows)
    chip_squares = from_chips(squares)
    chip_rows = after(chip_rows, (downs, chip_squares))
    relayed_rows = [from_sibling(b) for b in chip_rows]
    sums = jax.ShapeDtypeStruct((slots, hidden), jnp.float32)
    most = call(
        functools.partial(expert_most_kernel, [steps, 0, *range(steps + 1, 2 * steps)], steps),
        (sums, sums, row_sums),
        n_in=2 * steps + 4,
        **part,
    )(stacked, sibling_rows, *chip_rows, squares, *chip_squares, gains, gates, ups)
    given, activated = call(
        functools.partial(expert_last_kernel, steps),
        (bf16(steps, slots, feats), bf16(slots, hidden)),
        n_in=steps + 6,
        **part,
    )(*relayed_rows, *most, gains, gates, ups, downs)
    kept = call(expert_kept_kernel, bf16(steps, slots, feats), n_in=2, **part)(activated, downs)
    resid = call(
        functools.partial(project_kernel, steps),
        bf16(feats, toks),
        n_in=cuts + 2,
        flops=2 * toks * w_out.size,
        moved=2 * w_out.size,
    )(*blocks, w_t, residual_t)

    half = jax.ShapeDtypeStruct((slots // 2, feats), jnp.float32)
    sums = call(add_cores_kernel, (half,) * 2 + (bf16(slots // 2, feats),) * (2 * steps - 2), n_in=2)(
        kept, swap(given, "cuts", 1)
    )
    returned = []
    for half in range(2):
        parts = [sums[half]] + [to_chip(sums[2 * k + half], k) for k in range(1, steps)]
        blocks = call(functools.partial(add_chips_kernel, steps), (bf16(CAP, feats),) * (live // 2), n_in=steps)(
            *parts
        )
        for block in blocks:
            returned.append(to_seq(block, live - 1 - len(returned)))
    bounds = [*range(0, feats, SPAN), feats] if feats % 16 == 0 else [0, feats]
    parts = list(zip(bounds[:-1], bounds[1:]))
    out = call(
        functools.partial(combine_kernel, live, parts),
        bf16(feats, toks),
        n_in=live + 3,
        scratch=[
            pltpu.VMEM((live, CAP, feats), jnp.bfloat16),
            pltpu.VMEM((feats, toks), jnp.bfloat16),
            pltpu.SemaphoreType.DMA((len(parts),)),
        ],
        out_space=pltpu.HBM,
    )(*returned, mix_hi, mix_lo, resid)
    return out.T


def solution(mesh):
    placed = (
        P(("groups", "seq"), "cuts"),
        P(("groups", "seq"), "cuts"),
        P("groups", "cuts"),
        P("cuts"),
        P(("groups", "seq"), "cuts"),
        P(None, "cuts"),
        P(),
        P(("groups", "seq"), None),
        P(("groups", "seq"), None),
        P("seq", None, "cuts"),
        P("seq", None, "cuts"),
        P("seq", "cuts", None),
    )
    return jax.shard_map(
        shards, mesh=mesh, in_specs=placed, out_specs=P(("groups", "seq"), "cuts"), check_vma=False
    )
```

```python
import functools
import math

import jax
import jax.numpy as jnp
from jax import lax
from jax.experimental import pallas as pl
from jax.experimental.pallas import tpu as pltpu
from jax.sharding import PartitionSpec as P

HEAD_SIZE = 64
KEYS_SEEN = 128
PAIR = 2 * HEAD_SIZE
SPAN = 2 * KEYS_SEEN
CAP = 16
CORES = 2

norm_eps = 1e-05
glu_alpha = 1.702

NT = (((1,), (1,)), ((), ()))
NN = (((1,), (0,)), ((), ()))
TN = (((0,), (0,)), ((), ()))
VMEM_LIMIT = 32 * 1024 * 1024


def dot(a, b, dims):
    return lax.dot_general(a, b, dims, preferred_element_type=jnp.float32)


def call(kernel, outs, n_in, scratch=(), hbm=(), out_space=pltpu.VMEM, flops=0, moved=0):
    spaces = [pltpu.HBM if i in hbm else pltpu.VMEM for i in range(n_in)]
    return pl.pallas_call(
        kernel,
        out_shape=outs,
        in_specs=[pl.BlockSpec(memory_space=space) for space in spaces],
        out_specs=jax.tree.map(lambda _: pl.BlockSpec(memory_space=out_space), outs),
        scratch_shapes=list(scratch),
        compiler_params=pltpu.CompilerParams(vmem_limit_bytes=VMEM_LIMIT),
        cost_estimate=pl.CostEstimate(flops=flops, bytes_accessed=moved, transcendentals=0),
    )


def in_hbm(array):
    return pltpu.with_memory_space_constraint(array, pltpu.HBM)


def bf16(*shape):
    return jax.ShapeDtypeStruct(shape, jnp.bfloat16)


def split_pair(both):
    both = both.astype(jnp.float32)
    low = lax.broadcasted_iota(jnp.int32, both.shape, 1) < HEAD_SIZE
    turned = pltpu.roll(both, HEAD_SIZE, 1)
    keys = jnp.concatenate([jnp.where(low, both, 0.0), jnp.where(low, 0.0, turned)], axis=0)
    values = jnp.concatenate([jnp.where(low, turned, 0.0), jnp.where(low, 0.0, both)], axis=0)
    return keys.astype(jnp.bfloat16), values.astype(jnp.bfloat16)


def score(pairs, keys, allowed):
    scores = dot(keys, jnp.concatenate(pairs, axis=0), NT) * (HEAD_SIZE**-0.5 * math.log2(math.e))
    allowed = jnp.concatenate([allowed] * len(pairs), axis=1)
    span = allowed.shape[0]
    return [jnp.where(allowed, scores[i * span : (i + 1) * span], -jnp.inf) for i in range(2)]


def sink_row(sinks, i, pairs):
    return jnp.concatenate([sinks[2 * p + i] for p in range(pairs)], axis=1)


def attend_block(pairs, both, sinks, allowed):
    keys, values = split_pair(both)
    probs = []
    for i, part in enumerate(score(pairs, keys, allowed)):
        sink = sink_row(sinks, i, len(pairs))
        peak = jnp.maximum(jnp.max(part, axis=0, keepdims=True), sink)
        terms = jnp.exp2(part - peak)
        denom = jnp.sum(terms, axis=0, keepdims=True) + jnp.exp2(sink - peak)
        probs.append((terms * (1.0 / denom)).astype(jnp.bfloat16))
    return dot(values, jnp.concatenate(probs, axis=0), TN).astype(jnp.bfloat16)


def group_queries(q_ref, g, groups, block):
    per_group = q_ref.shape[1] // PAIR // groups
    first = g * per_group
    toks = slice(block * KEYS_SEEN, (block + 1) * KEYS_SEEN)
    pairs = [q_ref[toks, (first + p) * PAIR : (first + p + 1) * PAIR] for p in range(per_group)]
    return first, pairs


def store_pairs(mixed, first, out_ref, lanes):
    for p in range(mixed.shape[1] // KEYS_SEEN):
        rows = slice((first + p) * PAIR, (first + p + 1) * PAIR)
        out_ref[rows, lanes] = mixed[:, p * KEYS_SEEN : (p + 1) * KEYS_SEEN]


def key_query(span):
    key = lax.broadcasted_iota(jnp.int32, (span, KEYS_SEEN), 0)
    return key, lax.broadcasted_iota(jnp.int32, (span, KEYS_SEEN), 1)


def fill_tables(live, ids, weights, placing_ref, mix_hi_ref, mix_lo_ref):
    toks = ids.shape[1]
    chosen = jnp.concatenate(
        [jnp.max((ids == e).astype(jnp.float32), axis=0, keepdims=True) for e in range(live)], axis=0
    )
    earlier = lax.broadcasted_iota(jnp.int32, (toks, toks), 0)
    later = lax.broadcasted_iota(jnp.int32, (toks, toks), 1)
    strict = (earlier < later).astype(jnp.bfloat16)
    before = dot(chosen.astype(jnp.bfloat16), strict, NN)
    slot = lax.broadcasted_iota(jnp.int32, (CAP, toks), 0).astype(jnp.float32)
    for e in range(live):
        weight = jnp.sum(jnp.where(ids == e, weights, 0.0), axis=0, keepdims=True)
        fills = (before[e : e + 1] == slot) & (chosen[e : e + 1] > 0.0)
        mix = jnp.where(fills, weight, 0.0)
        hi = mix.astype(jnp.bfloat16)
        rows = slice(e * CAP, (e + 1) * CAP)
        placing_ref[rows] = fills.astype(jnp.bfloat16)
        mix_hi_ref[rows] = hi
        mix_lo_ref[rows] = (mix - hi.astype(jnp.float32)).astype(jnp.bfloat16)


def first_kernel(live, *refs):
    loaded, held = refs[:8], refs[8:13]
    placing_ref, mix_hi_ref, mix_lo_ref, sinks_out, late_ref, rows_ref = refs[13:19]
    ids_ref, weights_ref, sinks_ref, sems = refs[19:]
    targets = (ids_ref, weights_ref, sinks_ref, *held)
    copies = [pltpu.make_async_copy(*pair, sems.at[i]) for i, pair in enumerate(zip(loaded, targets))]
    for copy in copies:
        copy.start()
    q_ref, kv_ref = held[:2]
    for copy in copies[:2]:
        copy.wait()
    fill_tables(live, ids_ref[...], weights_ref[...], placing_ref, mix_hi_ref, mix_lo_ref)
    for copy in copies[2:5]:
        copy.wait()
    heads = sinks_ref.shape[0]
    sinks = [jnp.full((1, KEYS_SEEN), sinks_ref[h], jnp.float32) * math.log2(math.e) for h in range(heads)]
    sinks_out[...] = jnp.concatenate(sinks, axis=0)
    groups = kv_ref.shape[1] // PAIR
    key, query = key_query(SPAN)
    allowed = (key > query) & (key <= query + KEYS_SEEN)
    for b in range(1, q_ref.shape[0] // KEYS_SEEN):
        span = slice((b - 1) * KEYS_SEEN, (b + 1) * KEYS_SEEN)
        for g in range(groups):
            first, pairs = group_queries(q_ref, g, groups, b)
            part = sinks[2 * first : 2 * (first + len(pairs))]
            mixed = attend_block(pairs, kv_ref[span, g * PAIR : (g + 1) * PAIR], part, allowed)
            store_pairs(mixed, first, late_ref, slice((b - 1) * KEYS_SEEN, b * KEYS_SEEN))
    rows_ref[...] = dot(placing_ref[:, KEYS_SEEN:], late_ref[...], NT)
    for copy in copies[5:]:
        copy.wait()


def second_kernel(q_ref, kv_ref, before_ref, rim_ref, sinks_ref, late_ref, placing_ref, late_rows_ref, all_ref, rows_ref):
    rim = jnp.where(lax.axis_index("seq") == 0, before_ref[...], rim_ref[...])
    groups = rim.shape[1] // PAIR
    key, query = key_query(SPAN)
    allowed = (key > query) & (key <= query + KEYS_SEEN)
    for g in range(groups):
        first, pairs = group_queries(q_ref, g, groups, 0)
        sinks = [sinks_ref[h : h + 1] for h in range(2 * first, 2 * (first + len(pairs)))]
        lanes = slice(g * PAIR, (g + 1) * PAIR)
        both = jnp.concatenate([rim[:, lanes], kv_ref[:KEYS_SEEN, lanes]], axis=0)
        store_pairs(attend_block(pairs, both, sinks, allowed), first, all_ref, slice(0, KEYS_SEEN))
    rows = late_rows_ref[...] + dot(placing_ref[:, :KEYS_SEEN], all_ref[:, :KEYS_SEEN], NT)
    rows_ref[...] = rows.astype(jnp.bfloat16)
    all_ref[:, KEYS_SEEN:] = late_ref[...]


def origin(k, sibling):
    me = lax.axis_index("cuts")
    return lax.bitwise_xor(me, CORES * k + (1 if sibling else 0))


def add_products(total, places, blocks, w_ref, steps, dims, swapped=False):
    width = blocks[0].shape[0 if swapped else 1] if blocks else 0
    for i, block in zip(places, blocks):
        at = pl.multiple_of(origin(i % steps, i >= steps) * width, 128)
        w = w_ref[:, pl.ds(at, width)]
        total += dot(w, block[...], dims) if swapped else dot(block[...], w, dims)
    return total


def rows_own_kernel(steps, rows_ref, w_ref, residual_ref, placing_ref, total_ref):
    total = dot(placing_ref[...], residual_ref[...], NT)
    total_ref[...] = add_products(total, [0], [rows_ref], w_ref, steps, NT)


def rows_more_kernel(places, steps, *refs):
    blocks, (before_ref, w_ref, total_ref) = refs[:-3], refs[-3:]
    total_ref[...] = add_products(before_ref[...], places, blocks, w_ref, steps, NT)


def rows_last_kernel(steps, *refs):
    blocks, (before_ref, w_ref) = refs[: steps - 1], refs[steps - 1 : steps + 1]
    outgoing, rows_ref = refs[steps + 1 : -1], refs[-1]
    total = add_products(before_ref[...], range(1, steps), blocks, w_ref, steps, NT)
    rows_ref[...] = total.astype(jnp.bfloat16).reshape(rows_ref.shape)
    me = lax.axis_index("seq")
    for k, out_ref in enumerate(outgoing):
        out_ref[...] = rows_ref[lax.bitwise_xor(me, k)]


def stack_kernel(*refs):
    for i, block in enumerate(refs[:-1]):
        refs[-1][i * CAP : (i + 1) * CAP] = block[...]


def project_kernel(steps, *refs):
    blocks = refs[: 2 * steps]
    w_ref, residual_ref, resid_ref = refs[2 * steps :]
    total = residual_ref[...].astype(jnp.float32)
    total = add_products(total, range(2 * steps), blocks, w_ref, steps, NN, True)
    resid_ref[...] = total.astype(jnp.bfloat16)


def spread_kernel(source_ref, blocks_ref):
    cuts, _, width = blocks_ref.shape
    for p in range(cuts):
        blocks_ref[p] = source_ref[:, p * width : (p + 1) * width]


def spread_pair_kernel(start, gate_ref, up_ref, blocks_ref):
    cuts, _, width = blocks_ref.shape
    hidden = gate_ref.shape[0]
    for p in range(cuts):
        blocks_ref[p, :hidden] = gate_ref[:, p * width : (p + 1) * width]
        blocks_ref[p, hidden:start] = jnp.zeros((start - hidden, width), jnp.bfloat16)
        blocks_ref[p, start:] = up_ref[:, p * width : (p + 1) * width]


def spread_gain_kernel(gain_ref, blocks_ref):
    cuts, _, width = blocks_ref.shape
    gain = gain_ref[...].reshape(1, cuts * width)
    for p in range(cuts):
        blocks_ref[p] = gain[:, p * width : (p + 1) * width]


def squares_kernel(mine_ref, theirs_ref, squares_ref):
    wide = [ref[...].astype(jnp.float32) for ref in (mine_ref, theirs_ref)]
    squares = sum(jnp.sum(block * block, axis=1, keepdims=True) for block in wide)
    squares_ref[...] = jnp.broadcast_to(squares, squares_ref.shape)


def add_features(total, scale, places, blocks, gains_ref, weights_ref, steps):
    for i, block in zip(places, blocks):
        p = origin(i % steps, i >= steps)
        rows = (block[...].astype(jnp.float32) * scale * gains_ref[p]).astype(jnp.bfloat16)
        total += dot(rows, weights_ref[p], NT)
    return total


def expert_most_kernel(places, steps, *refs):
    blocks, squares = refs[: steps + 1], refs[steps + 1 : 2 * steps + 1]
    gains_ref, weights_ref, total_ref, scale_ref = refs[2 * steps + 1 :]
    features = 2 * steps * blocks[0].shape[1]
    scale = lax.rsqrt(sum(ref[...] for ref in squares) / features + norm_eps)
    scale_ref[...] = scale
    total_ref[...] = add_features(0.0, scale[:, :1], places, blocks, gains_ref, weights_ref, steps)


def expert_last_kernel(steps, *refs):
    blocks, refs = refs[: steps - 1], refs[steps - 1 :]
    total_ref, scale_ref, gains_ref, weights_ref, downs_ref, given_ref, activated_ref = refs
    scale = scale_ref[:, :1]
    total = add_features(total_ref[...], scale, range(1, steps), blocks, gains_ref, weights_ref, steps)
    hidden = activated_ref.shape[1]
    gate, up = total[:, :hidden], total[:, total.shape[1] - hidden :]
    activated = ((up + 1.0) * gate * jax.nn.sigmoid(glu_alpha * gate)).astype(jnp.bfloat16)
    activated_ref[...] = activated
    for k in range(steps):
        given_ref[k] = dot(activated, downs_ref[origin(k, k > 0)], NN).astype(jnp.bfloat16)


def expert_kept_kernel(activated_ref, downs_ref, kept_ref):
    for k in range(kept_ref.shape[0]):
        kept_ref[k] = dot(activated_ref[...], downs_ref[origin(k, k == 0)], NN).astype(jnp.bfloat16)


def add_cores_kernel(kept_ref, given_ref, *out_refs):
    half = out_refs[0].shape[0]
    for i, out_ref in enumerate(out_refs):
        rows = slice(i % 2 * half, (i % 2 + 1) * half)
        total = kept_ref[i // 2, rows].astype(jnp.float32) + given_ref[i // 2, rows].astype(jnp.float32)
        out_ref[...] = total.astype(out_ref.dtype)


def add_chips_kernel(steps, *refs):
    total = sum(r[...].astype(jnp.float32) for r in refs[:steps])
    for k, out_ref in enumerate(refs[steps:]):
        out_ref[...] = total[k * CAP : (k + 1) * CAP].astype(jnp.bfloat16)


def combine_kernel(live, parts, *refs):
    blocks = refs[:live]
    mix_hi_ref, mix_lo_ref, resid_ref, out_ref, rows_ref, held_ref, sems = refs[live:]
    me = lax.axis_index("seq")
    for k in range(live):
        rows_ref[lax.bitwise_xor(me, live - 1 - k)] = blocks[k][...]
    rows = rows_ref[...].reshape(live * CAP, -1)
    rows = jnp.concatenate([rows, rows], axis=0)
    mix = jnp.concatenate([mix_hi_ref[...], mix_lo_ref[...]], axis=0)
    copies = []
    for i, (start, stop) in enumerate(parts):
        part = slice(start, stop)
        mixed = dot(rows[:, part], mix, TN)
        held_ref[part] = (resid_ref[part].astype(jnp.float32) + mixed).astype(jnp.bfloat16)
        copies.append(pltpu.make_async_copy(held_ref.at[part], out_ref.at[part], sems.at[i]))
        copies[-1].start()
    for copy in copies:
        copy.wait()


def swap(block, axis, mask):
    return lax.ppermute(block, axis, [(i, i ^ mask) for i in range(lax.axis_size(axis))])


def to_chip(block, k, other=True):
    return swap(block, "cuts", CORES * k + other)


def from_chips(block, other=True):
    return [to_chip(block, k, other) for k in range(1, lax.axis_size("cuts") // CORES)]


def to_seq(block, k):
    size = lax.axis_size("seq") * lax.axis_size("cuts")
    mask = k * lax.axis_size("cuts") + 1
    return lax.ppermute(block, ("seq", "cuts"), [(i, i ^ mask) for i in range(size)])


def from_sibling(block):
    return swap(block, "cuts", 1)


def after(arrays, others):
    return lax.optimization_barrier((arrays, others))[0]


def shards(
    queries,
    keyvals,
    preceding_keyvalues,
    attention_sink_logits,
    residual,
    w_out,
    norm_gain,
    expert_ids,
    route_weights,
    w_gate,
    w_up,
    w_down,
):
    toks, feats = residual.shape
    size = lax.axis_size("seq")
    live = w_gate.shape[0] * size
    cuts = lax.axis_size("cuts")
    steps = cuts // CORES
    slots = live * CAP
    head_rows = queries.shape[1]
    heads = head_rows // HEAD_SIZE
    width = norm_gain.shape[0]
    hidden = w_gate.shape[2]

    tail = keyvals[toks - KEYS_SEEN :]
    rim = lax.ppermute(tail, "seq", [(i, (i + 1) % size) for i in range(size)])
    loads = (queries, keyvals, preceding_keyvalues, w_out.T, residual.T)
    q, kv, before, w_t, residual_t, placing, mix_hi, mix_lo, sinks, late, late_rows = call(
        functools.partial(first_kernel, live),
        (
            *(bf16(*a.shape) for a in loads),
            *(bf16(slots, toks),) * 3,
            jax.ShapeDtypeStruct((heads, KEYS_SEEN), jnp.float32),
            bf16(head_rows, toks - KEYS_SEEN),
            jax.ShapeDtypeStruct((slots, head_rows), jnp.float32),
        ),
        n_in=8,
        scratch=[
            pltpu.VMEM(expert_ids.T.shape, jnp.int32),
            pltpu.VMEM(expert_ids.T.shape, jnp.float32),
            pltpu.SMEM(attention_sink_logits.shape, jnp.float32),
            pltpu.SemaphoreType.DMA((8,)),
        ],
        hbm=range(8),
        flops=4 * toks * SPAN * head_rows,
        moved=2 * (w_out.size + residual.size + queries.size),
    )(*(in_hbm(a) for a in (expert_ids.T, route_weights.T, attention_sink_logits, *loads)))
    attended, rows = call(
        second_kernel,
        (bf16(head_rows, toks), bf16(slots, head_rows)),
        n_in=8,
        flops=2 * toks * SPAN * head_rows,
        moved=2 * queries.size,
    )(q, kv, before, rim, sinks, late, placing, late_rows)

    chip_rows = from_chips(rows)
    total = jax.ShapeDtypeStruct((slots, feats), jnp.float32)
    part = dict(flops=slots * w_out.size // 2, moved=w_out.size // 2)
    own = call(functools.partial(rows_own_kernel, steps), total, n_in=4, **part)(
        rows, w_t, residual_t, placing
    )
    sibling_rows = from_sibling(rows)
    places = range(steps, 2 * steps)
    spread = functools.partial(
        call, spread_kernel, bf16(cuts, hidden, feats), n_in=1, moved=4 * w_gate.size
    )
    downs = spread()(after(w_down[0], rows))
    chip_rows = after(chip_rows, (own, downs))
    relayed_rows = [from_sibling(b) for b in chip_rows]
    chips = call(functools.partial(rows_more_kernel, places, steps), total, n_in=steps + 2, **part)(
        sibling_rows, *chip_rows, own, w_t
    )
    outgoing = call(
        functools.partial(rows_last_kernel, steps),
        (bf16(CAP, feats),) * live,
        n_in=steps + 1,
        scratch=[pltpu.VMEM((live, CAP, feats), jnp.bfloat16)],
        **part,
    )(*relayed_rows, chips, w_t)

    arrived = [to_seq(outgoing[k], k) for k in range(live - 1, -1, -1)]

    start = -(-hidden // 128) * 128
    weights = call(
        functools.partial(spread_pair_kernel, start),
        bf16(cuts, start + hidden, feats),
        n_in=2,
        moved=4 * w_gate.size,
    )(*after((w_gate[0].T, w_up[0].T), outgoing[0]))
    gains = call(spread_gain_kernel, jax.ShapeDtypeStruct((cuts, 1, feats), jnp.float32), n_in=1)(norm_gain)
    part = dict(flops=slots * w_gate.size, moved=w_gate.size)
    stacked = call(stack_kernel, bf16(slots, feats), n_in=live)(*after(arrived, (weights, gains)))
    chip_rows = from_chips(stacked, False)
    sibling_rows = from_sibling(stacked)
    chip_blocks = from_chips(after(attended, downs))
    sibling_block, *relayed_blocks = [from_sibling(b) for b in (attended, *chip_blocks)]
    blocks = [attended, *relayed_blocks, sibling_block, *chip_blocks]
    row_sums = jax.ShapeDtypeStruct((slots, KEYS_SEEN), jnp.float32)
    squares = call(squares_kernel, row_sums, n_in=2)(stacked, sibling_rows)
    chip_squares = from_chips(squares)
    chip_rows = after(chip_rows, chip_squares)
    relayed_rows = [from_sibling(b) for b in chip_rows]
    sums = jax.ShapeDtypeStruct((slots, start + hidden), jnp.float32)
    most = call(
        functools.partial(expert_most_kernel, [steps, 0, *range(steps + 1, 2 * steps)], steps),
        (sums, row_sums),
        n_in=2 * steps + 3,
        **part,
    )(stacked, sibling_rows, *chip_rows, squares, *chip_squares, gains, weights)
    given, activated = call(
        functools.partial(expert_last_kernel, steps),
        (bf16(steps, slots, feats), bf16(slots, hidden)),
        n_in=steps + 4,
        **part,
    )(*relayed_rows, *most, gains, weights, downs)
    kept = call(expert_kept_kernel, bf16(steps, slots, feats), n_in=2, **part)(activated, downs)
    resid = call(
        functools.partial(project_kernel, steps),
        bf16(feats, toks),
        n_in=cuts + 2,
        flops=2 * toks * w_out.size,
        moved=2 * w_out.size,
    )(*blocks, w_t, residual_t)

    half = jax.ShapeDtypeStruct((slots // 2, feats), jnp.float32)
    sums = call(add_cores_kernel, (half,) * 2 + (bf16(slots // 2, feats),) * (2 * steps - 2), n_in=2)(
        kept, swap(given, "cuts", 1)
    )
    returned = []
    for half in range(2):
        parts = [sums[half]] + [to_chip(sums[2 * k + half], k) for k in range(1, steps)]
        blocks = call(functools.partial(add_chips_kernel, steps), (bf16(CAP, feats),) * (live // 2), n_in=steps)(
            *parts
        )
        for block in blocks:
            returned.append(to_seq(block, live - 1 - len(returned)))
    bounds = [*range(0, feats, SPAN), feats] if feats % 16 == 0 else [0, feats]
    parts = list(zip(bounds[:-1], bounds[1:]))
    out = call(
        functools.partial(combine_kernel, live, parts),
        bf16(feats, toks),
        n_in=live + 3,
        scratch=[
            pltpu.VMEM((live, CAP, feats), jnp.bfloat16),
            pltpu.VMEM((feats, toks), jnp.bfloat16),
            pltpu.SemaphoreType.DMA((len(parts),)),
        ],
        out_space=pltpu.HBM,
    )(*returned, mix_hi, mix_lo, resid)
    return out.T


def solution(mesh):
    placed = (
        P(("groups", "seq"), "cuts"),
        P(("groups", "seq"), "cuts"),
        P("groups", "cuts"),
        P("cuts"),
        P(("groups", "seq"), "cuts"),
        P(None, "cuts"),
        P(),
        P(("groups", "seq"), None),
        P(("groups", "seq"), None),
        P("seq", None, "cuts"),
        P("seq", None, "cuts"),
        P("seq", "cuts", None),
    )
    return jax.shard_map(
        shards, mesh=mesh, in_specs=placed, out_specs=P(("groups", "seq"), "cuts"), check_vma=False
    )
```

```python
import functools
import math

import jax
import jax.numpy as jnp
from jax import lax
from jax.experimental import pallas as pl
from jax.experimental.pallas import tpu as pltpu
from jax.sharding import PartitionSpec as P

HEAD_SIZE = 64
KEYS_SEEN = 128
PAIR = 2 * HEAD_SIZE
SPAN = 2 * KEYS_SEEN
CAP = 16
CORES = 2

norm_eps = 1e-05
glu_alpha = 1.702

NT = (((1,), (1,)), ((), ()))
NN = (((1,), (0,)), ((), ()))
TN = (((0,), (0,)), ((), ()))
VMEM_LIMIT = 32 * 1024 * 1024


def dot(a, b, dims):
    return lax.dot_general(a, b, dims, preferred_element_type=jnp.float32)


def call(kernel, outs, n_in, scratch=(), hbm=(), out_space=pltpu.VMEM, flops=0, moved=0):
    spaces = [pltpu.HBM if i in hbm else pltpu.VMEM for i in range(n_in)]
    return pl.pallas_call(
        kernel,
        out_shape=outs,
        in_specs=[pl.BlockSpec(memory_space=space) for space in spaces],
        out_specs=jax.tree.map(lambda _: pl.BlockSpec(memory_space=out_space), outs),
        scratch_shapes=list(scratch),
        compiler_params=pltpu.CompilerParams(vmem_limit_bytes=VMEM_LIMIT),
        cost_estimate=pl.CostEstimate(flops=flops, bytes_accessed=moved, transcendentals=0),
    )


def in_hbm(array):
    return pltpu.with_memory_space_constraint(array, pltpu.HBM)


def bf16(*shape):
    return jax.ShapeDtypeStruct(shape, jnp.bfloat16)


def split_pair(both):
    both = both.astype(jnp.float32)
    low = lax.broadcasted_iota(jnp.int32, both.shape, 1) < HEAD_SIZE
    turned = pltpu.roll(both, HEAD_SIZE, 1)
    keys = jnp.concatenate([jnp.where(low, both, 0.0), jnp.where(low, 0.0, turned)], axis=0)
    values = jnp.concatenate([jnp.where(low, turned, 0.0), jnp.where(low, 0.0, both)], axis=0)
    return keys.astype(jnp.bfloat16), values.astype(jnp.bfloat16)


def score(pairs, keys, allowed):
    scores = dot(keys, jnp.concatenate(pairs, axis=0), NT) * (HEAD_SIZE**-0.5 * math.log2(math.e))
    allowed = jnp.concatenate([allowed] * len(pairs), axis=1)
    span = allowed.shape[0]
    return [jnp.where(allowed, scores[i * span : (i + 1) * span], -jnp.inf) for i in range(2)]


def sink_row(sinks, i, pairs):
    return jnp.concatenate([sinks[2 * p + i] for p in range(pairs)], axis=1)


def attend_block(pairs, both, sinks, allowed):
    keys, values = split_pair(both)
    probs = []
    for i, part in enumerate(score(pairs, keys, allowed)):
        sink = sink_row(sinks, i, len(pairs))
        peak = jnp.maximum(jnp.max(part, axis=0, keepdims=True), sink)
        terms = jnp.exp2(part - peak)
        denom = jnp.sum(terms, axis=0, keepdims=True) + jnp.exp2(sink - peak)
        probs.append((terms * (1.0 / denom)).astype(jnp.bfloat16))
    return dot(values, jnp.concatenate(probs, axis=0), TN).astype(jnp.bfloat16)


def group_queries(q_ref, g, groups, block):
    per_group = q_ref.shape[1] // PAIR // groups
    first = g * per_group
    toks = slice(block * KEYS_SEEN, (block + 1) * KEYS_SEEN)
    pairs = [q_ref[toks, (first + p) * PAIR : (first + p + 1) * PAIR] for p in range(per_group)]
    return first, pairs


def store_pairs(mixed, first, out_ref, lanes):
    for p in range(mixed.shape[1] // KEYS_SEEN):
        rows = slice((first + p) * PAIR, (first + p + 1) * PAIR)
        out_ref[rows, lanes] = mixed[:, p * KEYS_SEEN : (p + 1) * KEYS_SEEN]


def key_query(span):
    key = lax.broadcasted_iota(jnp.int32, (span, KEYS_SEEN), 0)
    return key, lax.broadcasted_iota(jnp.int32, (span, KEYS_SEEN), 1)


def fill_tables(live, ids, weights, placing_ref, mix_hi_ref, mix_lo_ref):
    toks = ids.shape[1]
    chosen = jnp.concatenate(
        [jnp.max((ids == e).astype(jnp.float32), axis=0, keepdims=True) for e in range(live)], axis=0
    )
    earlier = lax.broadcasted_iota(jnp.int32, (toks, toks), 0)
    later = lax.broadcasted_iota(jnp.int32, (toks, toks), 1)
    strict = (earlier < later).astype(jnp.bfloat16)
    before = dot(chosen.astype(jnp.bfloat16), strict, NN)
    slot = lax.broadcasted_iota(jnp.int32, (CAP, toks), 0).astype(jnp.float32)
    for e in range(live):
        weight = jnp.sum(jnp.where(ids == e, weights, 0.0), axis=0, keepdims=True)
        fills = (before[e : e + 1] == slot) & (chosen[e : e + 1] > 0.0)
        mix = jnp.where(fills, weight, 0.0)
        hi = mix.astype(jnp.bfloat16)
        rows = slice(e * CAP, (e + 1) * CAP)
        placing_ref[rows] = fills.astype(jnp.bfloat16)
        mix_hi_ref[rows] = hi
        mix_lo_ref[rows] = (mix - hi.astype(jnp.float32)).astype(jnp.bfloat16)


def first_kernel(live, *refs):
    loaded, held = refs[:8], refs[8:13]
    placing_ref, mix_hi_ref, mix_lo_ref, sinks_out, late_ref, rows_ref = refs[13:19]
    ids_ref, weights_ref, sinks_ref, sems = refs[19:]
    targets = (ids_ref, weights_ref, sinks_ref, *held)
    copies = [pltpu.make_async_copy(*pair, sems.at[i]) for i, pair in enumerate(zip(loaded, targets))]
    for copy in copies:
        copy.start()
    q_ref, kv_ref = held[:2]
    for copy in copies[:2]:
        copy.wait()
    fill_tables(live, ids_ref[...], weights_ref[...], placing_ref, mix_hi_ref, mix_lo_ref)
    for copy in copies[2:5]:
        copy.wait()
    heads = sinks_ref.shape[0]
    sinks = [jnp.full((1, KEYS_SEEN), sinks_ref[h], jnp.float32) * math.log2(math.e) for h in range(heads)]
    sinks_out[...] = jnp.concatenate(sinks, axis=0)
    groups = kv_ref.shape[1] // PAIR
    key, query = key_query(SPAN)
    allowed = (key > query) & (key <= query + KEYS_SEEN)
    for b in range(1, q_ref.shape[0] // KEYS_SEEN):
        span = slice((b - 1) * KEYS_SEEN, (b + 1) * KEYS_SEEN)
        for g in range(groups):
            first, pairs = group_queries(q_ref, g, groups, b)
            part = sinks[2 * first : 2 * (first + len(pairs))]
            mixed = attend_block(pairs, kv_ref[span, g * PAIR : (g + 1) * PAIR], part, allowed)
            store_pairs(mixed, first, late_ref, slice((b - 1) * KEYS_SEEN, b * KEYS_SEEN))
    rows_ref[...] = dot(placing_ref[:, KEYS_SEEN:], late_ref[...], NT)
    for copy in copies[5:]:
        copy.wait()


def second_kernel(q_ref, kv_ref, before_ref, rim_ref, sinks_ref, late_ref, placing_ref, late_rows_ref, all_ref, rows_ref):
    rim = jnp.where(lax.axis_index("seq") == 0, before_ref[...], rim_ref[...])
    groups = rim.shape[1] // PAIR
    key, query = key_query(SPAN)
    allowed = (key > query) & (key <= query + KEYS_SEEN)
    for g in range(groups):
        first, pairs = group_queries(q_ref, g, groups, 0)
        sinks = [sinks_ref[h : h + 1] for h in range(2 * first, 2 * (first + len(pairs)))]
        lanes = slice(g * PAIR, (g + 1) * PAIR)
        both = jnp.concatenate([rim[:, lanes], kv_ref[:KEYS_SEEN, lanes]], axis=0)
        store_pairs(attend_block(pairs, both, sinks, allowed), first, all_ref, slice(0, KEYS_SEEN))
    rows = late_rows_ref[...] + dot(placing_ref[:, :KEYS_SEEN], all_ref[:, :KEYS_SEEN], NT)
    rows_ref[...] = rows.astype(jnp.bfloat16)
    all_ref[:, KEYS_SEEN:] = late_ref[...]


def origin(k, sibling):
    me = lax.axis_index("cuts")
    return lax.bitwise_xor(me, CORES * k + (1 if sibling else 0))


def add_products(total, places, blocks, w_ref, steps, dims, swapped=False):
    width = blocks[0].shape[0 if swapped else 1] if blocks else 0
    for i, block in zip(places, blocks):
        at = pl.multiple_of(origin(i % steps, i >= steps) * width, 128)
        w = w_ref[:, pl.ds(at, width)]
        total += dot(w, block[...], dims) if swapped else dot(block[...], w, dims)
    return total


def rows_own_kernel(steps, rows_ref, w_ref, residual_ref, placing_ref, total_ref):
    total = dot(placing_ref[...], residual_ref[...], NT)
    total_ref[...] = add_products(total, [0], [rows_ref], w_ref, steps, NT)


def rows_more_kernel(places, steps, *refs):
    blocks, (before_ref, w_ref, total_ref) = refs[:-3], refs[-3:]
    total_ref[...] = add_products(before_ref[...], places, blocks, w_ref, steps, NT)


def rows_last_kernel(steps, *refs):
    blocks, (before_ref, w_ref) = refs[: steps - 1], refs[steps - 1 : steps + 1]
    outgoing, rows_ref = refs[steps + 1 : -1], refs[-1]
    total = add_products(before_ref[...], range(1, steps), blocks, w_ref, steps, NT)
    rows_ref[...] = total.astype(jnp.bfloat16).reshape(rows_ref.shape)
    me = lax.axis_index("seq")
    for k, out_ref in enumerate(outgoing):
        out_ref[...] = rows_ref[lax.bitwise_xor(me, k)]


def stack_kernel(*refs):
    for i, block in enumerate(refs[:-1]):
        refs[-1][i * CAP : (i + 1) * CAP] = block[...]


def project_kernel(steps, *refs):
    blocks = refs[: 2 * steps]
    w_ref, residual_ref, resid_ref = refs[2 * steps :]
    total = residual_ref[...].astype(jnp.float32)
    total = add_products(total, range(2 * steps), blocks, w_ref, steps, NN, True)
    resid_ref[...] = total.astype(jnp.bfloat16)


def spread_kernel(source_ref, blocks_ref):
    cuts, _, width = blocks_ref.shape
    for p in range(cuts):
        blocks_ref[p] = source_ref[:, p * width : (p + 1) * width]


def spread_gain_kernel(gain_ref, blocks_ref):
    cuts, _, width = blocks_ref.shape
    gain = gain_ref[...].reshape(1, cuts * width)
    for p in range(cuts):
        blocks_ref[p] = gain[:, p * width : (p + 1) * width]


def squares_kernel(mine_ref, theirs_ref, squares_ref):
    wide = [ref[...].astype(jnp.float32) for ref in (mine_ref, theirs_ref)]
    squares = sum(jnp.sum(block * block, axis=1, keepdims=True) for block in wide)
    squares_ref[...] = jnp.broadcast_to(squares, squares_ref.shape)


def add_features(gate, up, scale, places, blocks, gains_ref, gates_ref, ups_ref, steps):
    for i, block in zip(places, blocks):
        p = origin(i % steps, i >= steps)
        rows = (block[...].astype(jnp.float32) * scale * gains_ref[p]).astype(jnp.bfloat16)
        gate += dot(rows, gates_ref[p], NT)
        up += dot(rows, ups_ref[p], NT)
    return gate, up


def expert_most_kernel(places, steps, *refs):
    blocks, squares = refs[: steps + 1], refs[steps + 1 : 2 * steps + 1]
    gains_ref, gates_ref, ups_ref, gate_ref, up_ref, scale_ref = refs[2 * steps + 1 :]
    features = 2 * steps * blocks[0].shape[1]
    scale = lax.rsqrt(sum(ref[...] for ref in squares) / features + norm_eps)
    scale_ref[...] = scale
    sums = add_features(0.0, 0.0, scale[:, :1], places, blocks, gains_ref, gates_ref, ups_ref, steps)
    gate_ref[...], up_ref[...] = sums


def expert_last_kernel(steps, *refs):
    blocks, refs = refs[: steps - 1], refs[steps - 1 :]
    gate_ref, up_ref, scale_ref, gains_ref, gates_ref, ups_ref, downs_ref, given_ref, activated_ref = refs
    gate, up = add_features(
        gate_ref[...], up_ref[...], scale_ref[:, :1], range(steps + 1, 2 * steps), blocks, gains_ref, gates_ref, ups_ref, steps
    )
    activated = ((up + 1.0) * gate * jax.nn.sigmoid(glu_alpha * gate)).astype(jnp.bfloat16)
    activated_ref[...] = activated
    for k in range(steps):
        given_ref[k] = dot(activated, downs_ref[origin(k, k > 0)], NN).astype(jnp.bfloat16)


def expert_kept_kernel(activated_ref, downs_ref, kept_ref):
    for k in range(kept_ref.shape[0]):
        kept_ref[k] = dot(activated_ref[...], downs_ref[origin(k, k == 0)], NN).astype(jnp.bfloat16)


def add_cores_kernel(kept_ref, given_ref, *out_refs):
    half = out_refs[0].shape[0]
    for i, out_ref in enumerate(out_refs):
        rows = slice(i % 2 * half, (i % 2 + 1) * half)
        total = kept_ref[i // 2, rows].astype(jnp.float32) + given_ref[i // 2, rows].astype(jnp.float32)
        out_ref[...] = total.astype(out_ref.dtype)


def add_chips_kernel(steps, *refs):
    total = sum(r[...].astype(jnp.float32) for r in refs[:steps])
    for k, out_ref in enumerate(refs[steps:]):
        out_ref[...] = total[k * CAP : (k + 1) * CAP].astype(jnp.bfloat16)


def combine_kernel(live, parts, *refs):
    blocks = refs[:live]
    mix_hi_ref, mix_lo_ref, resid_ref, out_ref, rows_ref, held_ref, sems = refs[live:]
    me = lax.axis_index("seq")
    for k in range(live):
        rows_ref[lax.bitwise_xor(me, live - 1 - k)] = blocks[k][...]
    rows = rows_ref[...].reshape(live * CAP, -1)
    rows = jnp.concatenate([rows, rows], axis=0)
    mix = jnp.concatenate([mix_hi_ref[...], mix_lo_ref[...]], axis=0)
    copies = []
    for i, (start, stop) in enumerate(parts):
        part = slice(start, stop)
        mixed = dot(rows[:, part], mix, TN)
        held_ref[part] = (resid_ref[part].astype(jnp.float32) + mixed).astype(jnp.bfloat16)
        copies.append(pltpu.make_async_copy(held_ref.at[part], out_ref.at[part], sems.at[i]))
        copies[-1].start()
    for copy in copies:
        copy.wait()


def swap(block, axis, mask):
    return lax.ppermute(block, axis, [(i, i ^ mask) for i in range(lax.axis_size(axis))])


def to_chip(block, k, other=True):
    return swap(block, "cuts", CORES * k + other)


def from_chips(block, other=True):
    return [to_chip(block, k, other) for k in range(1, lax.axis_size("cuts") // CORES)]


def to_seq(block, k):
    size = lax.axis_size("seq") * lax.axis_size("cuts")
    mask = k * lax.axis_size("cuts") + 1
    return lax.ppermute(block, ("seq", "cuts"), [(i, i ^ mask) for i in range(size)])


def from_sibling(block):
    return swap(block, "cuts", 1)


def after(arrays, others):
    return lax.optimization_barrier((arrays, others))[0]


def shards(
    queries,
    keyvals,
    preceding_keyvalues,
    attention_sink_logits,
    residual,
    w_out,
    norm_gain,
    expert_ids,
    route_weights,
    w_gate,
    w_up,
    w_down,
):
    toks, feats = residual.shape
    size = lax.axis_size("seq")
    live = w_gate.shape[0] * size
    cuts = lax.axis_size("cuts")
    steps = cuts // CORES
    slots = live * CAP
    head_rows = queries.shape[1]
    heads = head_rows // HEAD_SIZE
    width = norm_gain.shape[0]
    hidden = w_gate.shape[2]

    tail = keyvals[toks - KEYS_SEEN :]
    rim = lax.ppermute(tail, "seq", [(i, (i + 1) % size) for i in range(size)])
    loads = (queries, keyvals, preceding_keyvalues, w_out.T, residual.T)
    q, kv, before, w_t, residual_t, placing, mix_hi, mix_lo, sinks, late, late_rows = call(
        functools.partial(first_kernel, live),
        (
            *(bf16(*a.shape) for a in loads),
            *(bf16(slots, toks),) * 3,
            jax.ShapeDtypeStruct((heads, KEYS_SEEN), jnp.float32),
            bf16(head_rows, toks - KEYS_SEEN),
            jax.ShapeDtypeStruct((slots, head_rows), jnp.float32),
        ),
        n_in=8,
        scratch=[
            pltpu.VMEM(expert_ids.T.shape, jnp.int32),
            pltpu.VMEM(expert_ids.T.shape, jnp.float32),
            pltpu.SMEM(attention_sink_logits.shape, jnp.float32),
            pltpu.SemaphoreType.DMA((8,)),
        ],
        hbm=range(8),
        flops=4 * toks * SPAN * head_rows,
        moved=2 * (w_out.size + residual.size + queries.size),
    )(*(in_hbm(a) for a in (expert_ids.T, route_weights.T, attention_sink_logits, *loads)))
    attended, rows = call(
        second_kernel,
        (bf16(head_rows, toks), bf16(slots, head_rows)),
        n_in=8,
        flops=2 * toks * SPAN * head_rows,
        moved=2 * queries.size,
    )(q, kv, before, rim, sinks, late, placing, late_rows)

    chip_rows = from_chips(rows)
    total = jax.ShapeDtypeStruct((slots, feats), jnp.float32)
    part = dict(flops=slots * w_out.size // 2, moved=w_out.size // 2)
    own = call(functools.partial(rows_own_kernel, steps), total, n_in=4, **part)(
        rows, w_t, residual_t, placing
    )
    sibling_rows = from_sibling(rows)
    places = range(steps, 2 * steps)
    spread = functools.partial(
        call, spread_kernel, bf16(cuts, hidden, feats), n_in=1, moved=4 * w_gate.size
    )
    gates = spread()(after(w_gate[0].T, rows))
    chip_rows = after(chip_rows, (own, gates))
    relayed_rows = [from_sibling(b) for b in chip_rows]
    chips = call(functools.partial(rows_more_kernel, places, steps), total, n_in=steps + 2, **part)(
        sibling_rows, *chip_rows, own, w_t
    )
    outgoing = call(
        functools.partial(rows_last_kernel, steps),
        (bf16(CAP, feats),) * live,
        n_in=steps + 1,
        scratch=[pltpu.VMEM((live, CAP, feats), jnp.bfloat16)],
        **part,
    )(*relayed_rows, chips, w_t)

    arrived = [to_seq(outgoing[k], k) for k in range(live - 1, -1, -1)]

    ups = spread()(after(w_up[0].T, outgoing[0]))
    gains = call(spread_gain_kernel, jax.ShapeDtypeStruct((cuts, 1, feats), jnp.float32), n_in=1)(norm_gain)
    part = dict(flops=slots * w_gate.size, moved=w_gate.size)
    stacked = call(stack_kernel, bf16(slots, feats), n_in=live)(*after(arrived, (ups, gains)))
    chip_rows = from_chips(stacked)
    sibling_rows = from_sibling(stacked)
    downs = spread()(after(w_down[0], stacked))
    chip_blocks = from_chips(after(attended, gates))
    sibling_block, *relayed_blocks = [from_sibling(b) for b in (attended, *chip_blocks)]
    blocks = [attended, *relayed_blocks, sibling_block, *chip_blocks]
    row_sums = jax.ShapeDtypeStruct((slots, KEYS_SEEN), jnp.float32)
    squares = call(squares_kernel, row_sums, n_in=2)(stacked, sibling_rows)
    chip_squares = from_chips(squares)
    chip_rows = after(chip_rows, (downs, chip_squares))
    relayed_rows = [from_sibling(b) for b in chip_rows]
    sums = jax.ShapeDtypeStruct((slots, hidden), jnp.float32)
    most = call(
        functools.partial(expert_most_kernel, [steps, 0, *range(1, steps)], steps),
        (sums, sums, row_sums),
        n_in=2 * steps + 4,
        **part,
    )(stacked, sibling_rows, *chip_rows, squares, *chip_squares, gains, gates, ups)
    given, activated = call(
        functools.partial(expert_last_kernel, steps),
        (bf16(steps, slots, feats), bf16(slots, hidden)),
        n_in=steps + 6,
        **part,
    )(*relayed_rows, *most, gains, gates, ups, downs)
    kept = call(expert_kept_kernel, bf16(steps, slots, feats), n_in=2, **part)(activated, downs)
    resid = call(
        functools.partial(project_kernel, steps),
        bf16(feats, toks),
        n_in=cuts + 2,
        flops=2 * toks * w_out.size,
        moved=2 * w_out.size,
    )(*blocks, w_t, residual_t)

    half = jax.ShapeDtypeStruct((slots // 2, feats), jnp.float32)
    sums = call(add_cores_kernel, (half,) * 2 + (bf16(slots // 2, feats),) * (2 * steps - 2), n_in=2)(
        kept, swap(given, "cuts", 1)
    )
    returned = []
    for half in range(2):
        parts = [sums[half]] + [to_chip(sums[2 * k + half], k) for k in range(1, steps)]
        blocks = call(functools.partial(add_chips_kernel, steps), (bf16(CAP, feats),) * (live // 2), n_in=steps)(
            *parts
        )
        for block in blocks:
            returned.append(to_seq(block, live - 1 - len(returned)))
    bounds = [*range(0, feats, SPAN), feats] if feats % 16 == 0 else [0, feats]
    parts = list(zip(bounds[:-1], bounds[1:]))
    out = call(
        functools.partial(combine_kernel, live, parts),
        bf16(feats, toks),
        n_in=live + 3,
        scratch=[
            pltpu.VMEM((live, CAP, feats), jnp.bfloat16),
            pltpu.VMEM((feats, toks), jnp.bfloat16),
            pltpu.SemaphoreType.DMA((len(parts),)),
        ],
        out_space=pltpu.HBM,
    )(*returned, mix_hi, mix_lo, resid)
    return out.T


def solution(mesh):
    placed = (
        P(("groups", "seq"), "cuts"),
        P(("groups", "seq"), "cuts"),
        P("groups", "cuts"),
        P("cuts"),
        P(("groups", "seq"), "cuts"),
        P(None, "cuts"),
        P(),
        P(("groups", "seq"), None),
        P(("groups", "seq"), None),
        P("seq", None, "cuts"),
        P("seq", None, "cuts"),
        P("seq", "cuts", None),
    )
    return jax.shard_map(
        shards, mesh=mesh, in_specs=placed, out_specs=P(("groups", "seq"), "cuts"), check_vma=False
    )
```
